32 devices in a mesh: dp: 8 (over z, x), tensor: 4 (over y, core).
Axes of the slice: x: 2, y: 2, z: 4, core: 2. Of those that a mesh axis runs over, the one named last changes fastest.
Arguments:
- tokens: bfloat16 [448, 257, 384], P(('dp', 'tensor')), may hold values from -6 to 6
- image_mask: int32 [448], P(('dp', 'tensor')), may hold values 0 or 1
- patch_mask: int32 [448, 256], P(('dp', 'tensor')), may hold values 0 or 1
- first_gain: bfloat16 [384], replicated, may hold values from 0.5 to 1.5
- first_shift: bfloat16 [384], replicated, may hold values from -1.75 to 1.75
- attend_weight: bfloat16 [384, 1152], replicated, may hold values from -0.4375 to 0.4375
- attend_bias: bfloat16 [2, 384], replicated, may hold values from -1.75 to 1.75
- merge_weight: bfloat16 [384, 384], replicated, may hold values from -0.875 to 0.875
- merge_bias: bfloat16 [384], replicated, may hold values from -1.75 to 1.75
- second_gain: bfloat16 [384], replicated, may hold values from 0.5 to 1.5
- second_shift: bfloat16 [384], replicated, may hold values from -1.75 to 1.75
- up_weight: bfloat16 [384, 1536], P(None, 'tensor'), may hold values from -0.3125 to 0.3125
- up_bias: bfloat16 [1536], P('tensor'), may hold values from -1.75 to 1.75
- down_weight: bfloat16 [1536, 384], P('tensor'), may hold values from -0.15625 to 0.15625
- down_bias: bfloat16 [384], replicated, may hold values from -1.75 to 1.75
- cotangent: bfloat16 [448, 257, 384], P(('dp', 'tensor')), may hold values from -6 to 6
Outputs:
- output: bfloat16 [448, 257, 384], P(('dp', 'tensor'))
- input_grad: bfloat16 [448, 257, 384], P(('dp', 'tensor'))
- first_gain_grad: float32 [384], replicated
- first_shift_grad: float32 [384], replicated
- attend_weight_grad: float32 [384, 1152], replicated
- attend_bias_grad: float32 [2, 384], replicated
- merge_weight_grad: float32 [384, 384], replicated
- merge_bias_grad: float32 [384], replicated
- second_gain_grad: float32 [384], replicated
- second_shift_grad: float32 [384], replicated
- up_weight_grad: float32 [384, 1536], P(None, 'tensor')
- up_bias_grad: float32 [1536], P('tensor')
- down_weight_grad: float32 [1536, 384], P('tensor')
- down_bias_grad: float32 [384], replicated
The draws below stay inside these ranges and needn't reach their ends.
All inputs are finite; a program needn't handle non-finite values. No bound on the sum of `image_mask` or of `patch_mask` on one device may be relied on, other than what follows from the above.
Results may differ from the reference program's by a relative error of at most 0.012.
The reference program's roundings to bfloat16 on the way count: a program that leaves them out, or rounds other values in their place, can miss the bound.
Values may be sent and summed in bfloat16 or wider, within the bound.
A program may use at most 256 MiB of HBM per device.

```python
import math
import jax
import jax.numpy as jnp
from jax import lax

D = 384
HEADS = 6
HEAD = 64
FF = 1536
PATCHES = 256
SEQ = 257
IMAGES = 448


def touch_ends(values, stream_key, smallest, top_value):
    index_at = [jax.random.randint(jax.random.fold_in(stream_key, axis), (), 0, length) for axis, length in enumerate(values.shape)]
    main_axis = values.shape.index(max(values.shape))
    beside = index_at[:main_axis] + [(index_at[main_axis] + 1) % values.shape[main_axis]] + index_at[main_axis + 1:]
    return values.at[tuple(index_at)].set(smallest).at[tuple(beside)].set(top_value)


def levels(stream_key, dims, shards, low, high):
    def one(axis_at, blocks):
        steps = jax.random.uniform(jax.random.fold_in(jax.random.fold_in(stream_key, 6), axis_at), (blocks,), jnp.float32, low / len(shards), high / len(shards))
        return jnp.repeat(jnp.exp(steps), dims[axis_at] // blocks).reshape((-1,) + (1,) * (len(dims) - axis_at - 1))

    gain = one(*shards[0])
    for cut in shards[1:]:
        gain = gain * one(*cut)
    return gain


def scatter_about(stream_key, shape, deviation, reach, cuts=(), dtype=jnp.bfloat16):
    factor_of = levels(stream_key, shape, cuts, -0.22, 0.18) if cuts else 1.0
    entries = jax.random.normal(stream_key, shape, jnp.float32) * deviation * factor_of
    return jnp.minimum(jnp.maximum(entries, -reach), reach).astype(dtype)


def setup_inputs(seed: int = 0) -> dict:
    streams_of = jax.random.split(jax.random.key(seed), 17)
    return {
        "tokens": scatter_about(streams_of[0], (IMAGES, SEQ, D), 1.0, 6.0, ((0, 32),)),
        "image_mask": touch_ends((jax.random.randint(streams_of[1], (IMAGES,), 0, 4) < 3).astype(jnp.int32), jax.random.fold_in(streams_of[1], 1), 0, 1),
        "patch_mask": touch_ends((jax.random.randint(streams_of[2], (IMAGES, PATCHES), 0, 4) < 3).astype(jnp.int32), jax.random.fold_in(streams_of[2], 1), 0, 1),
        "first_gain": jnp.clip(1.0 + 0.1 * jax.random.normal(streams_of[3], (D,), jnp.float32), 0.5, 1.5).astype(jnp.bfloat16),
        "first_shift": scatter_about(streams_of[4], (D,), 0.3, 1.75),
        "attend_weight": scatter_about(streams_of[5], (D, 3 * D), (D // 2) ** -0.5, 0.4375),
        "attend_bias": scatter_about(streams_of[6], (2, D), 0.3, 1.75),
        "merge_weight": scatter_about(streams_of[7], (D, D), (D // 8) ** -0.5, 0.875),
        "merge_bias": scatter_about(streams_of[8], (D,), 0.3, 1.75),
        "second_gain": jnp.clip(1.0 + 0.1 * jax.random.normal(streams_of[9], (D,), jnp.float32), 0.5, 1.5).astype(jnp.bfloat16),
        "second_shift": scatter_about(streams_of[10], (D,), 0.3, 1.75),
        "up_weight": scatter_about(streams_of[11], (D, FF), D ** -0.5, 0.3125, ((1, 4),)),
        "up_bias": scatter_about(streams_of[12], (FF,), 0.3, 1.75, ((0, 4),)),
        "down_weight": scatter_about(streams_of[13], (FF, D), FF ** -0.5, 0.15625, ((0, 4),)),
        "down_bias": scatter_about(streams_of[14], (D,), 0.3, 1.75),
        "cotangent": scatter_about(streams_of[15], (IMAGES, SEQ, D), 1.0, 6.0, ((0, 32),)),
    }


@jax.custom_vjp
def low(v):
    return lax.optimization_barrier(v.astype(jnp.bfloat16)).astype(jnp.float32)

@jax.custom_vjp
def low_back(v):
    return v

def low_keep(v):
    return (low(v), None)

def low_pass(kept, grad):
    return (grad,)

def back_keep(v):
    return (v, None)

def back_low(kept, grad):
    return (low(grad),)
low.defvjp(low_keep, low_pass)
low_back.defvjp(back_keep, back_low)
epsilon = 1e-06
neg_large = -1e+30
highest = lax.Precision.HIGHEST

def layer_norm(values, norm_gain, norm_shift):
    center = values - lax.optimization_barrier(jnp.mean(values, axis=-1, keepdims=True))
    spread = lax.optimization_barrier(jnp.mean(center * center, axis=-1, keepdims=True))
    return center * lax.rsqrt(spread + epsilon) * norm_gain + norm_shift

def product(left, right):
    return jnp.dot(left, right, precision=highest)

def block_forward(inputs, live_image, live_keys, params):
    first_gain, first_shift, attend_weight, attend_bias, merge_weight, merge_bias, second_gain, second_shift, up_weight, up_bias, down_weight, down_bias = params
    image_count, seq_len, features = inputs.shape
    score_scale = HEAD ** (-0.5)
    live_rows = live_image[:, None, None]
    first_in = low(layer_norm(inputs, first_gain, first_shift))
    bias_full = jnp.concatenate([attend_bias[0], jnp.zeros_like(attend_bias[0]), attend_bias[1]])
    packed = product(first_in, attend_weight) + bias_full
    queries = low(low_back(packed[..., :features])).reshape(image_count, seq_len, HEADS, HEAD)
    key_rows = low(low_back(packed[..., features:2 * features])).reshape(image_count, seq_len, HEADS, HEAD)
    value_rows = low(low_back(packed[..., 2 * features:])).reshape(image_count, seq_len, HEADS, HEAD)
    scores = low_back(jnp.einsum('gqhe,gkhe->ghqk', queries, key_rows, precision=highest) * score_scale)
    scores = jnp.where(live_keys[:, None, None, :], scores, neg_large)
    row_peak = lax.optimization_barrier(jnp.max(scores, axis=-1, keepdims=True))
    raised = jnp.exp(scores - row_peak)
    attn_weights = raised / lax.optimization_barrier(jnp.sum(raised, axis=-1, keepdims=True))
    mixed_heads = jnp.einsum('ghqk,gkhe->gqhe', low(attn_weights), value_rows, precision=highest)
    attended = low(low_back(mixed_heads.reshape(image_count, seq_len, features)))
    branch = low_back(product(attended, merge_weight) + merge_bias)
    hidden = inputs + live_rows * branch
    second_in = low(layer_norm(hidden, second_gain, second_shift))
    pre_act = low_back(product(second_in, up_weight) + up_bias)
    activated = low(jax.nn.gelu(pre_act, approximate=False))
    result = low_back(product(activated, down_weight) + down_bias)
    return hidden + live_rows * result

def reference(tokens, image_mask, patch_mask, first_gain, first_shift, attend_weight, attend_bias, merge_weight, merge_bias, second_gain, second_shift, up_weight, up_bias, down_weight, down_bias, cotangent):
    params = tuple((weight.astype(jnp.float32) for weight in (first_gain, first_shift, attend_weight, attend_bias, merge_weight, merge_bias, second_gain, second_shift, up_weight, up_bias, down_weight, down_bias)))
    group_size = math.gcd(IMAGES, 16)
    blocks = IMAGES // group_size
    inputs = tokens.astype(jnp.float32).reshape(blocks, group_size, SEQ, D)
    grads_in = cotangent.astype(jnp.float32).reshape(blocks, group_size, SEQ, D)
    live = image_mask.astype(jnp.float32).reshape(blocks, group_size)
    key_live = jnp.concatenate([jnp.ones((IMAGES, 1), jnp.bool_), patch_mask == 1], axis=1)
    key_live = key_live.reshape(blocks, group_size, SEQ)

    def step(totals, block_args):
        tok_block, live_block, key_block, cot_block = block_args

        def forward(values, weights):
            return block_forward(values, live_block, key_block, weights)
        out_block, back = jax.vjp(forward, tok_block, params)
        grad_block, grad_params = back(cot_block)
        totals = jax.tree.map(jnp.add, totals, grad_params)
        return (totals, (out_block.astype(jnp.bfloat16), grad_block.astype(jnp.bfloat16)))
    zeros = jax.tree.map(jnp.zeros_like, params)
    totals, (outputs, grads) = lax.scan(step, zeros, (inputs, live, key_live, grads_in))
    return (outputs.reshape(IMAGES, SEQ, D), grads.reshape(IMAGES, SEQ, D), totals[0], totals[1], totals[2], totals[3], totals[4], totals[5], totals[6], totals[7], totals[8], totals[9], totals[10], totals[11])
```

```python
import functools

import jax
import jax.numpy as jnp
from jax import lax
from jax.experimental import pallas as pl
from jax.experimental.pallas import tpu as pltpu
from jax.sharding import PartitionSpec as P

HEADS = 6
HEAD = 64
MAIN = 256
EPS = 1e-06
MASKED = -1e30
f32, bf16 = jnp.float32, jnp.bfloat16

NN = ((1,), (0,))
NT = ((1,), (1,))
TN = ((0,), (0,))


def dot(left, right, dims=NN):
    return lax.dot_general(left, right, (dims, ((), ())), preferred_element_type=f32)


def rows_where(index, value, rows, dtype):
    columns = value.shape[-1]
    at = lax.broadcasted_iota(jnp.int32, (rows, columns), 0)
    return jnp.where(at == index, value, 0.0).astype(dtype)


def wide(column, width):
    return jnp.concatenate([column] * (width // 128), axis=1)


def as_column(row):
    return jnp.broadcast_to(row, (128, row.shape[1])).T


def norm_columns(values):
    center = values - jnp.mean(values, axis=0, keepdims=True)
    scale = lax.rsqrt(jnp.mean(center * center, axis=0, keepdims=True) + EPS)
    return center * scale, scale


def norm_rows(values):
    center = values - jnp.mean(values, axis=1, keepdims=True)
    scale = lax.rsqrt(jnp.mean(center * center, axis=1, keepdims=True) + EPS)
    return center * scale, scale


def norm_back(grad, normed, scale, axis):
    mean_grad = jnp.mean(grad, axis=axis, keepdims=True)
    mean_both = jnp.mean(grad * normed, axis=axis, keepdims=True)
    return scale * (grad - mean_grad - normed * mean_both)


def gelu_both(pre):
    curve = 0.5 + 0.5 * lax.erf(pre * 0.7071067811865476)
    bell = 0.3989422804014327 * jnp.exp(-0.5 * pre * pre)
    return pre * curve, curve + pre * bell


def head_rows(rows, features):
    at = lax.broadcasted_iota(jnp.int32, (rows, features), 0)
    head = lax.broadcasted_iota(jnp.int32, (rows, features), 1) // HEAD
    return jnp.where(at == head, 1.0, 0.0)


def lane_live(live_ref, first, count):
    flags = [
        jnp.full((1, MAIN), live_ref[first + g].astype(f32)) for g in range(count)
    ]
    return jnp.concatenate(flags, axis=1)


def row_live(live_ref, count, rows):
    at = lax.broadcasted_iota(jnp.int32, (rows, 1), 0)
    flags = jnp.zeros((rows, 1), f32)
    for image in range(count):
        flags = jnp.where(at == image, live_ref[image].astype(f32), flags)
    return flags


def take_left(left_ref, to_ref, count):
    to_ref[...] = jnp.zeros_like(to_ref)
    for image in range(count):
        to_ref[image : image + 1, :] = left_ref[image].astype(f32)[0:1, :]


def attend_kernel(
    count, group,
    tok, left, pmask, live, vec, aw, mw,
    fi_out, qkv_out, probs_out, edge_out, inv_out, lp_out, lself_out, att_out, hid_out,
    fil_out, qkvl_out, attl_out, hidl_out,
    awt, mwt, fia, atta, cols, peaks, xl, qkvl, attl,
):
    step = pl.program_id(0)
    features = aw.shape[0]
    packed = aw.shape[1]
    rows = xl.shape[0]
    heads = head_rows(rows, features)

    @pl.when(step == 0)
    def _():
        for part in range(3):
            span = slice(part * features, (part + 1) * features)
            block = aw[:, span].astype(f32).T
            awt[span, :features] = (block * (HEAD**-0.5 if part == 0 else 1.0)).astype(bf16)
            if part == 1:
                bias = jnp.zeros((1, features), f32)
            else:
                bias = vec[2:3, :] * (HEAD**-0.5) if part == 0 else vec[3:4, :]
            awt[span, features:] = rows_where(0, bias, 128, f32).T.astype(bf16)
        mwt[:, :features] = mw[...].astype(f32).T.astype(bf16)
        mwt[:, features:] = rows_where(0, vec[4:5, :], 128, f32).T.astype(bf16)
        ones = rows_where(0, jnp.ones((1, fia.shape[1]), f32), 128, bf16)
        fia[features:, :] = ones
        atta[features:, :] = ones
        cols[0] = as_column(vec[0:1, :])
        cols[1] = as_column(vec[1:2, :])
        peaks[...] = jnp.zeros_like(peaks)
        take_left(left, xl, count)
        normed, _ = norm_rows(xl[...])
        fil = (normed * vec[0:1, :] + vec[1:2, :]).astype(bf16)
        fil_out[...] = fil.astype(f32)
        bias = jnp.concatenate([vec[2:3, :], jnp.zeros((1, features), f32), vec[3:4, :]], axis=1)
        rounded = (dot(fil, aw[...]) + bias).astype(bf16).astype(f32)
        at = lax.broadcasted_iota(jnp.int32, (1, packed), 1)
        qkvl[...] = rounded * jnp.where(at < features, HEAD**-0.5, 1.0)
        qkvl_out[...] = qkvl[...]
        attl[...] = jnp.zeros_like(attl)

    tokens = jnp.concatenate([tok[g].astype(f32).T for g in range(group)], axis=1)
    width = group * MAIN
    normed, _ = norm_columns(tokens)
    fi = (normed * wide(cols[0], width) + wide(cols[1], width)).astype(bf16)
    fia[:features, :] = fi
    qkv = dot(awt[...], fia[...]).astype(bf16)
    one_row = rows_where(0, jnp.ones((1, MAIN), f32), 16, bf16)
    for g in range(group):
        image = step * group + g
        lanes = slice(g * MAIN, (g + 1) * MAIN)
        fi_out[g] = fi[:, lanes]
        qt = qkv[:features, lanes]
        kt = qkv[features : 2 * features, lanes]
        vt = qkv[2 * features :, lanes]
        qkv_out[g] = qkv[:, lanes]
        qkv_row = qkvl[pl.ds(image, 1), :]
        ql, kl, vl = (qkv_row[:, p * features : (p + 1) * features] for p in range(3))
        qlb, klb, vlb = ((heads * v).astype(bf16) for v in (ql, kl, vl))

        key_bias = jnp.where(pmask[pl.ds(image, 1), :] == 1, 0.0, MASKED)
        moved = pltpu.roll(key_bias, 1, axis=1)
        left_bias = moved[:, 0:1]
        at = lax.broadcasted_iota(jnp.int32, moved.shape, 1)
        main_bias = jnp.where(at == 0, 0.0, moved)
        bias_rows = rows_where(0, main_bias, 16, bf16)

        slk = dot(klb, qt) + left_bias
        outs = []
        for h in range(HEADS):
            span = slice(h * HEAD, (h + 1) * HEAD)
            scores = dot(
                jnp.concatenate([kt[span], bias_rows], axis=0),
                jnp.concatenate([qt[span], one_row], axis=0),
                TN,
            )
            peak = jnp.maximum(jnp.max(scores, axis=0, keepdims=True), slk[h : h + 1, :])
            raised = jnp.exp(scores - peak).astype(bf16)
            probs_out[g, h] = raised
            peaks[g, h : h + 1, :] = peak
            outs.append(dot(jnp.concatenate([vt[span], one_row], axis=0), raised))
        edge = jnp.exp(slk - peaks[g])
        edge_out[g] = edge
        added = dot(vlb, edge.astype(bf16), TN)
        for h in range(HEADS):
            span = slice(h * HEAD, (h + 1) * HEAD)
            inv = 1.0 / (outs[h][HEAD : HEAD + 1, :] + edge[h : h + 1, :])
            inv_out[g, h : h + 1, :] = inv
            mixed = ((outs[h][:HEAD, :] + added[span]) * inv).astype(bf16)
            atta[span, lanes] = mixed
            att_out[g, span, :] = mixed

        sl = dot(qlb, kt) + main_bias
        self_score = jnp.sum(heads * (ql * kl), axis=1, keepdims=True) + left_bias
        peak = jnp.maximum(jnp.max(sl, axis=1, keepdims=True), self_score)
        raised = jnp.exp(sl - peak)
        raised_self = jnp.exp(self_score - peak)
        inv = 1.0 / (jnp.sum(raised, axis=1, keepdims=True) + raised_self)
        lp = raised * inv
        lself = raised_self * inv
        lp_out[g] = lp
        lself_out[g] = jnp.broadcast_to(lself, (rows, 128))
        mixed = dot(lp.astype(bf16), vt, NT) + lself * vl
        attl[pl.ds(image, 1), :] = jnp.sum(mixed * heads, axis=0, keepdims=True).astype(bf16).astype(f32)

    branch = dot(mwt[...], atta[...])
    hidden = tokens + lane_live(live, step * group, group) * branch
    for g in range(group):
        hid_out[g] = hidden[:, g * MAIN : (g + 1) * MAIN]

    @pl.when(step == pl.num_programs(0) - 1)
    def _():
        attl_out[...] = attl[...]
        branch = dot(attl[...].astype(bf16), mw[...]) + vec[4:5, :]
        hidl_out[...] = xl[...] + row_live(live, count, rows) * branch


def feed_kernel(
    count, group,
    hid, att, cot, cleft, live, vec, hidl, attl, upw, upb, dnw,
    out, gh_out, ga_out, ghl_out, gal_out, up_acc, down_acc, merge_acc, sums_out,
    upt, dnt, sia, atta, act, gpre, gb, cols, gsum, xl, outl,
):
    step = pl.program_id(0)
    features, hidden_units = upw.shape
    rows = xl.shape[0]
    width = group * MAIN
    part = 384

    @pl.when(step == 0)
    def _():
        for at in range(0, hidden_units, part):
            span = slice(at, at + part)
            upt[span, :features] = upw[:, span].astype(f32).T.astype(bf16)
            upt[span, features:] = rows_where(0, upb[0:1, span].astype(f32), 128, f32).T.astype(bf16)
            dnt[:, span] = dnw[span, :].astype(f32).T.astype(bf16)
        ones = rows_where(0, jnp.ones((1, width), f32), 128, bf16)
        sia[features:, :] = ones
        atta[features:, :] = ones
        cols[0] = as_column(vec[5:6, :])
        cols[1] = as_column(vec[6:7, :])
        cols[2] = as_column(vec[7:8, :])
        gsum[...] = jnp.zeros_like(gsum)
        take_left(cleft, xl, count)
        alive = row_live(live, count, rows)
        normed, scale = norm_rows(hidl[...])
        si = (normed * vec[5:6, :] + vec[6:7, :]).astype(bf16)
        pre = dot(si, upw[...]) + upb[0:1, :].astype(f32)
        value, slope = gelu_both(pre)
        value = value.astype(bf16)
        outl[...] = hidl[...] + alive * (dot(value, dnw[...]) + vec[7:8, :])
        grad_branch = (alive * xl[...]).astype(bf16)
        grad_pre = (dot(grad_branch, dnw[...], NT) * slope).astype(bf16)
        grad_second = dot(grad_pre, upw[...], NT)
        grad_hidden = xl[...] + norm_back(grad_second * vec[5:6, :], normed, scale, 1)
        ghl_out[...] = grad_hidden
        grad_attn = (alive * grad_hidden).astype(bf16)
        gal_out[...] = grad_attn.astype(f32)
        one = jnp.ones((rows, 16), bf16)
        up_acc[...] = dot(jnp.concatenate([si.astype(f32), one.astype(f32)], axis=1).astype(bf16), grad_pre, TN)
        down_acc[...] = dot(grad_branch, value, TN)
        merge_acc[...] = dot(
            jnp.concatenate([attl[...], one.astype(f32)], axis=1).astype(bf16), grad_attn, TN
        )
        sums_out[...] = jnp.zeros_like(sums_out)
        sums_out[0:1, :] = jnp.sum(grad_second * normed, axis=0, keepdims=True)
        sums_out[1:2, :] = jnp.sum(grad_second, axis=0, keepdims=True)
        sums_out[2:3, :] = jnp.sum(grad_branch.astype(f32), axis=0, keepdims=True)

    alive = lane_live(live, step * group, group)
    hidden = jnp.concatenate([hid[g] for g in range(group)], axis=1)
    normed, scale = norm_columns(hidden)
    sia[:features, :] = (normed * wide(cols[0], width) + wide(cols[1], width)).astype(bf16)
    cotangent = jnp.concatenate([cot[g].astype(f32).T for g in range(group)], axis=1)
    gb[...] = (cotangent * alive).astype(bf16)
    for at in range(0, hidden_units, part):
        span = slice(at, at + part)
        pre = dot(upt[span, :], sia[...])
        grad_act = dot(dnw[span, :], gb[...])
        value, slope = gelu_both(pre)
        act[span, :] = value.astype(bf16)
        gpre[span, :] = (grad_act * slope).astype(bf16)
    reduced = dot(dnt[...], act[...])
    grad_second = dot(upw[...], gpre[...])
    result = hidden + alive * (reduced + wide(cols[2], width))
    up_acc[...] += dot(sia[: up_acc.shape[0], :], gpre[...], NT)
    down_acc[...] += dot(gb[...], act[...], NT)
    grad_hidden = cotangent + norm_back(grad_second * wide(cols[0], width), normed, scale, 0)
    grad_attn = (alive * grad_hidden).astype(bf16)
    both = grad_second * normed
    for at in range(0, width, 128):
        gsum[0] += both[:, at : at + 128]
        gsum[1] += grad_second[:, at : at + 128]
    sums_out[2:3, :] += dot(jnp.ones((16, width), bf16), gb[...], NT)[0:1, :]
    for g in range(group):
        lanes = slice(g * MAIN, (g + 1) * MAIN)
        image = step * group + g
        gh_out[g] = grad_hidden[:, lanes]
        ga_out[g] = grad_attn[:, lanes]
        atta[:features, lanes] = att[g]
        out[g, :MAIN, :] = result[:, lanes].T.astype(bf16)
        out[g, MAIN : MAIN + 1, :] = outl[pl.ds(image, 1), :].astype(bf16)
    merge_acc[...] += dot(atta[: merge_acc.shape[0], :], grad_attn, NT)

    @pl.when(step == pl.num_programs(0) - 1)
    def _():
        sums_out[0:1, :] += jnp.sum(gsum[0].T, axis=0, keepdims=True)
        sums_out[1:2, :] += jnp.sum(gsum[1].T, axis=0, keepdims=True)


def attend_back_kernel(
    count, group,
    qkv, probs, edge, inv, lp, lself, att, ga, fi, fil, qkvl, attl, gal, mw,
    gp_out, gpl_out, acc,
    fia, gpa, gml, dots, gmleft, gpl,
):
    step = pl.program_id(0)
    features = mw.shape[0]
    rows = gal.shape[0]
    heads = head_rows(rows, features)

    @pl.when(step == 0)
    def _():
        fia[features:, :] = rows_where(0, jnp.ones((1, fia.shape[1]), f32), 16, bf16)
        acc[...] = jnp.zeros_like(acc)
        dots[...] = jnp.zeros_like(dots)
        gmleft[...] = dot(gal[...].astype(bf16), mw[...], NT).astype(bf16).astype(f32)
        gpl[...] = jnp.zeros_like(gpl)

    at16 = lax.broadcasted_iota(jnp.int32, (16, MAIN), 0)
    minus = jnp.where(at16 < 2, -1.0, 0.0).astype(bf16)
    for g in range(group):
        image = step * group + g
        lanes = slice(g * MAIN, (g + 1) * MAIN)
        qt = qkv[g, :features, :]
        kt = qkv[g, features : 2 * features, :]
        vt = qkv[g, 2 * features :, :]
        fia[:features, lanes] = fi[g]
        grad_mixed = dot(mw[...], ga[g]).astype(bf16).astype(f32)
        both = grad_mixed * att[g].astype(f32)
        edge_f = edge[g]
        tails = []
        for h in range(HEADS):
            span = slice(h * HEAD, (h + 1) * HEAD)
            row_inv = inv[g, h : h + 1, :]
            gml[span, lanes] = (grad_mixed[span] * row_inv).astype(bf16)
            row_dot = jnp.sum(both[span], axis=0, keepdims=True) * row_inv
            dots[g, h : h + 1, :] = row_dot
            high = row_dot.astype(bf16).astype(f32)
            tails.append(
                jnp.where(at16 == 0, high, jnp.where(at16 == 1, row_dot - high, 0.0)).astype(bf16)
            )

        qkv_row = qkvl[pl.ds(image, 1), :]
        ql, kl, vl = (qkv_row[:, p * features : (p + 1) * features] for p in range(3))
        qlb, klb, vlb = ((heads * v).astype(bf16) for v in (ql, kl, vl))
        scaled = gml[:, lanes]
        edge_grad = (edge_f * (dot(vlb, scaled) - dots[g])).astype(bf16)
        grad_kl = jnp.sum(dot(edge_grad, qt, NT) * heads, axis=0, keepdims=True)
        grad_vl = jnp.sum(dot(edge_f.astype(bf16), scaled, NT) * heads, axis=0, keepdims=True)
        gm_row = gmleft[pl.ds(image, 1), :]
        gmb = (heads * gm_row).astype(bf16)
        row_dot = jnp.sum(heads * (gm_row * attl[pl.ds(image, 1), :]), axis=1, keepdims=True)
        left_grad = (lp[g] * (dot(gmb, vt) - row_dot)).astype(bf16)
        self_prob = lself[g][:, 0:1]
        self_grad = self_prob * (jnp.sum(heads * (gm_row * vl), axis=1, keepdims=True) - row_dot)
        self_grad = self_grad.astype(bf16).astype(f32)
        self_row = jnp.sum(heads * self_grad, axis=0, keepdims=True)
        prob_row = jnp.sum(heads * self_prob.astype(bf16).astype(f32), axis=0, keepdims=True)
        grad_ql = jnp.sum(dot(left_grad, kt, NT) * heads, axis=0, keepdims=True) + self_row * kl
        grad_kl = grad_kl + self_row * ql
        grad_vl = grad_vl + prob_row * gm_row
        gpl[pl.ds(image, 1), :] = (
            jnp.concatenate([grad_ql * HEAD**-0.5, grad_kl, grad_vl], axis=1).astype(bf16).astype(f32)
        )
        add_q = dot(klb, edge_grad, TN)
        add_k = dot(qlb, left_grad, TN)
        add_v = dot(gmb, lp[g].astype(bf16), TN)
        for h in range(HEADS):
            span = slice(h * HEAD, (h + 1) * HEAD)
            raised = probs[g, h]
            change = dot(
                jnp.concatenate([vt[span], minus], axis=0),
                jnp.concatenate([scaled[span], tails[h]], axis=0),
                TN,
            )
            score_grad = raised * change.astype(bf16)
            grad_q = (dot(kt[span], score_grad) + add_q[span]) * HEAD**-0.5
            grad_k = dot(qt[span], score_grad, NT) + add_k[span]
            grad_v = dot(scaled[span], raised, NT) + add_v[span]
            for p, grad in enumerate((grad_q, grad_k, grad_v)):
                to = slice(p * features + h * HEAD, p * features + (h + 1) * HEAD)
                rounded = grad.astype(bf16)
                gpa[to, lanes] = rounded
                gp_out[g, to, :] = rounded
    acc[...] += dot(fia[...], gpa[...], NT)

    @pl.when(step == pl.num_programs(0) - 1)
    def _():
        gpl_out[...] = gpl[...]
        one = jnp.ones((rows, 16), f32)
        acc[...] += dot(
            jnp.concatenate([fil[...], one], axis=1).astype(bf16), gpl[...].astype(bf16), TN
        )


def first_back_kernel(
    count, group,
    tok, left, gp, gh, gpl, ghl, vec, aw,
    out, sums_out,
    cols, gsum, xl, outl,
):
    step = pl.program_id(0)
    width = group * MAIN

    @pl.when(step == 0)
    def _():
        cols[...] = as_column(vec[0:1, :])
        gsum[...] = jnp.zeros_like(gsum)
        take_left(left, xl, count)
        normed, scale = norm_rows(xl[...])
        grad_first = dot(gpl[...].astype(bf16), aw[...], NT)
        outl[...] = ghl[...] + norm_back(grad_first * vec[0:1, :], normed, scale, 1)
        sums_out[...] = jnp.zeros_like(sums_out)
        sums_out[0:1, :] = jnp.sum(grad_first * normed, axis=0, keepdims=True)
        sums_out[1:2, :] = jnp.sum(grad_first, axis=0, keepdims=True)

    tokens = jnp.concatenate([tok[g].astype(f32).T for g in range(group)], axis=1)
    normed, scale = norm_columns(tokens)
    packed = jnp.concatenate([gp[g] for g in range(group)], axis=1)
    grad_first = dot(aw[...], packed)
    grad = norm_back(grad_first * wide(cols[...], width), normed, scale, 0)
    both = grad_first * normed
    for at in range(0, width, 128):
        gsum[0] += both[:, at : at + 128]
        gsum[1] += grad_first[:, at : at + 128]
    for g in range(group):
        image = step * group + g
        result = gh[g] + grad[:, g * MAIN : (g + 1) * MAIN]
        out[g, :MAIN, :] = result.T.astype(bf16)
        out[g, MAIN : MAIN + 1, :] = outl[pl.ds(image, 1), :].astype(bf16)

    @pl.when(step == pl.num_programs(0) - 1)
    def _():
        sums_out[0:1, :] += jnp.sum(gsum[0].T, axis=0, keepdims=True)
        sums_out[1:2, :] += jnp.sum(gsum[1].T, axis=0, keepdims=True)


def per_step(group, *dims):
    return pl.BlockSpec((group, *dims), lambda i: (i,) + (0,) * len(dims))


def whole(*dims):
    return pl.BlockSpec(dims, lambda i: (0,) * len(dims))


LIVE = pl.BlockSpec(memory_space=pltpu.SMEM)


def params():
    return pltpu.CompilerParams(vmem_limit_bytes=58 * 2**20, dimension_semantics=("arbitrary",))


def shape(dtype, *dims):
    return jax.ShapeDtypeStruct(dims, dtype)


def shards(
    tokens, image_mask, patch_mask, first_gain, first_shift, attend_weight, attend_bias,
    merge_weight, merge_bias, second_gain, second_shift, up_weight, up_bias, down_weight,
    down_bias, cotangent,
):
    n, seq, d = tokens.shape
    packed = attend_weight.shape[1]
    rows = -(-n // 16) * 16
    group = 2 if n % 2 == 0 else 1
    steps = n // group
    width = group * MAIN
    left = pl.BlockSpec((n, 16, d), lambda i: (0, MAIN // 16, 0))
    vec = jnp.stack(
        [
            v.astype(f32)
            for v in (
                first_gain, first_shift, attend_bias[0], attend_bias[1], merge_bias,
                second_gain, second_shift, down_bias,
            )
        ]
    )
    up_all = lax.all_gather(up_weight, "tensor", axis=1, tiled=True)
    down_all = lax.all_gather(down_weight, "tensor", axis=0, tiled=True)
    up_bias_all = lax.all_gather(up_bias, "tensor", axis=0, tiled=True)[None, :]
    units = up_all.shape[1]

    main = per_step(group, d, MAIN)
    token_in = per_step(group, MAIN, d)
    token_out = per_step(group, seq, d)
    edge = per_step(group, rows, MAIN)
    fi, qkv, probs, edges, invs, lp, lself, att, hid, fil, qkvl, attl, hidl = pl.pallas_call(
        functools.partial(attend_kernel, n, group),
        grid=(steps,),
        in_specs=[token_in, left, whole(n, MAIN), LIVE, whole(8, d), whole(d, packed), whole(d, d)],
        out_specs=[
            main, per_step(group, packed, MAIN), per_step(group, HEADS, MAIN, MAIN), edge, edge, edge,
            per_step(group, rows, 128), main, main,
            whole(rows, d), whole(rows, packed), whole(rows, d), whole(rows, d),
        ],
        out_shape=[
            shape(bf16, n, d, MAIN), shape(bf16, n, packed, MAIN), shape(bf16, n, HEADS, MAIN, MAIN),
            shape(f32, n, rows, MAIN), shape(f32, n, rows, MAIN), shape(f32, n, rows, MAIN),
            shape(f32, n, rows, 128), shape(bf16, n, d, MAIN), shape(f32, n, d, MAIN),
            shape(f32, rows, d), shape(f32, rows, packed), shape(f32, rows, d), shape(f32, rows, d),
        ],
        scratch_shapes=[
            pltpu.VMEM((packed, d + 128), bf16), pltpu.VMEM((d, d + 128), bf16),
            pltpu.VMEM((d + 128, width), bf16), pltpu.VMEM((d + 128, width), bf16),
            pltpu.VMEM((2, d, 128), f32), pltpu.VMEM((group, rows, MAIN), f32),
            pltpu.VMEM((rows, d), f32), pltpu.VMEM((rows, packed), f32), pltpu.VMEM((rows, d), f32),
        ],
        compiler_params=params(),
        name="attend",
    )(tokens, tokens, patch_mask, image_mask, vec, attend_weight, merge_weight)

    output, gh, ga, ghl, gal, up_acc, down_acc, merge_acc, second_sums = pl.pallas_call(
        functools.partial(feed_kernel, n, group),
        grid=(steps,),
        in_specs=[
            main, main, token_in, left, LIVE, whole(8, d), whole(rows, d), whole(rows, d),
            whole(d, units), whole(1, units), whole(units, d),
        ],
        out_specs=[
            token_out, main, main, whole(rows, d), whole(rows, d),
            whole(d + 16, units), whole(d, units), whole(d + 16, d), whole(8, d),
        ],
        out_shape=[
            shape(bf16, n, seq, d), shape(f32, n, d, MAIN), shape(bf16, n, d, MAIN),
            shape(f32, rows, d), shape(f32, rows, d),
            shape(f32, d + 16, units), shape(f32, d, units), shape(f32, d + 16, d), shape(f32, 8, d),
        ],
        scratch_shapes=[
            pltpu.VMEM((units, d + 128), bf16), pltpu.VMEM((d, units), bf16),
            pltpu.VMEM((d + 128, width), bf16), pltpu.VMEM((d + 128, width), bf16),
            pltpu.VMEM((units, width), bf16), pltpu.VMEM((units, width), bf16),
            pltpu.VMEM((d, width), bf16), pltpu.VMEM((3, d, 128), f32), pltpu.VMEM((2, d, 128), f32),
            pltpu.VMEM((rows, d), f32), pltpu.VMEM((rows, d), f32),
        ],
        compiler_params=params(),
        name="feed",
    )(hid, att, cotangent, cotangent, image_mask, vec, hidl, attl, up_all, up_bias_all, down_all)

    feed_sums = lax.psum((up_acc, down_acc, merge_acc, second_sums), ("dp", "tensor"))

    gp, gpl, attend_acc = pl.pallas_call(
        functools.partial(attend_back_kernel, n, group),
        grid=(steps,),
        in_specs=[
            per_step(group, packed, MAIN), per_step(group, HEADS, MAIN, MAIN), edge, edge, edge,
            per_step(group, rows, 128), main, main, main,
            whole(rows, d), whole(rows, packed), whole(rows, d), whole(rows, d), whole(d, d),
        ],
        out_specs=[per_step(group, packed, MAIN), whole(rows, packed), whole(d + 16, packed)],
        out_shape=[shape(bf16, n, packed, MAIN), shape(f32, rows, packed), shape(f32, d + 16, packed)],
        scratch_shapes=[
            pltpu.VMEM((d + 16, width), bf16), pltpu.VMEM((packed, width), bf16),
            pltpu.VMEM((d, width), bf16), pltpu.VMEM((group, rows, MAIN), f32),
            pltpu.VMEM((rows, d), f32), pltpu.VMEM((rows, packed), f32),
        ],
        compiler_params=params(),
        name="attend_back",
    )(qkv, probs, edges, invs, lp, lself, att, ga, fi, fil, qkvl, attl, gal, merge_weight)

    input_grad, first_sums = pl.pallas_call(
        functools.partial(first_back_kernel, n, group),
        grid=(steps,),
        in_specs=[
            token_in, left, per_step(group, packed, MAIN), main, whole(rows, packed), whole(rows, d),
            whole(8, d), whole(d, packed),
        ],
        out_specs=[token_out, whole(8, d)],
        out_shape=[shape(bf16, n, seq, d), shape(f32, 8, d)],
        scratch_shapes=[
            pltpu.VMEM((d, 128), f32), pltpu.VMEM((2, d, 128), f32),
            pltpu.VMEM((rows, d), f32), pltpu.VMEM((rows, d), f32),
        ],
        compiler_params=params(),
        name="first_back",
    )(tokens, tokens, gp, gh, gpl, ghl, vec, attend_weight)

    attend_acc, first_sums = lax.psum((attend_acc, first_sums), ("dp", "tensor"))
    up_acc, down_acc, merge_acc, second_sums = feed_sums
    share = up_weight.shape[1]
    offset = lax.axis_index("tensor") * share
    up_grad = lax.dynamic_slice_in_dim(up_acc, offset, share, 1)
    down_grad = lax.dynamic_slice_in_dim(down_acc, offset, share, 1).T
    return (
        output,
        input_grad,
        first_sums[0],
        first_sums[1],
        attend_acc[:d],
        jnp.stack([attend_acc[d, :d], attend_acc[d, 2 * d :]]),
        merge_acc[:d],
        merge_acc[d],
        second_sums[0],
        second_sums[1],
        up_grad[:d],
        up_grad[d],
        down_grad,
        second_sums[2],
    )


def solution(mesh):
    split = ("dp", "tensor")
    in_specs = (
        P(split, None, None), P(split), P(split, None), P(), P(), P(), P(), P(), P(), P(), P(),
        P(None, "tensor"), P("tensor"), P("tensor", None), P(), P(split, None, None),
    )
    out_specs = (
        P(split, None, None), P(split, None, None), P(), P(), P(), P(), P(), P(), P(), P(),
        P(None, "tensor"), P("tensor"), P("tensor", None), P(),
    )
    return jax.shard_map(shards, mesh=mesh, in_specs=in_specs, out_specs=out_specs, check_vma=False)
```

```python
import functools

import jax
import jax.numpy as jnp
from jax import lax
from jax.experimental import pallas as pl
from jax.experimental.pallas import tpu as pltpu
from jax.sharding import PartitionSpec as P

HEADS = 6
HEAD = 64
MAIN = 256
EPS = 1e-06
MASKED = -1e30
f32, bf16 = jnp.float32, jnp.bfloat16

NN = ((1,), (0,))
NT = ((1,), (1,))
TN = ((0,), (0,))


def dot(left, right, dims=NN):
    return lax.dot_general(left, right, (dims, ((), ())), preferred_element_type=f32)


def rows_where(index, value, rows, dtype):
    columns = value.shape[-1]
    at = lax.broadcasted_iota(jnp.int32, (rows, columns), 0)
    return jnp.where(at == index, value, 0.0).astype(dtype)


def wide(column, width):
    return jnp.concatenate([column] * (width // 128), axis=1)


def as_column(row):
    return jnp.broadcast_to(row, (128, row.shape[1])).T


def norm_columns(values):
    center = values - jnp.mean(values, axis=0, keepdims=True)
    scale = lax.rsqrt(jnp.mean(center * center, axis=0, keepdims=True) + EPS)
    return center * scale, scale


def norm_rows(values):
    center = values - jnp.mean(values, axis=1, keepdims=True)
    scale = lax.rsqrt(jnp.mean(center * center, axis=1, keepdims=True) + EPS)
    return center * scale, scale


def norm_back(grad, normed, scale, axis):
    mean_grad = jnp.mean(grad, axis=axis, keepdims=True)
    mean_both = jnp.mean(grad * normed, axis=axis, keepdims=True)
    return scale * (grad - mean_grad - normed * mean_both)


def gelu_both(pre):
    curve = 0.5 + 0.5 * lax.erf(pre * 0.7071067811865476)
    bell = 0.3989422804014327 * jnp.exp(-0.5 * pre * pre)
    return pre * curve, curve + pre * bell


def head_rows(rows, features):
    at = lax.broadcasted_iota(jnp.int32, (rows, features), 0)
    head = lax.broadcasted_iota(jnp.int32, (rows, features), 1) // HEAD
    return jnp.where(at == head, 1.0, 0.0)


def lane_live(live_ref, first, count):
    flags = [
        jnp.full((1, MAIN), live_ref[first + g].astype(f32)) for g in range(count)
    ]
    return jnp.concatenate(flags, axis=1)


def row_live(live_ref, count, rows):
    at = lax.broadcasted_iota(jnp.int32, (rows, 1), 0)
    flags = jnp.zeros((rows, 1), f32)
    for image in range(count):
        flags = jnp.where(at == image, live_ref[image].astype(f32), flags)
    return flags


def take_left(left_ref, to_ref, count):
    to_ref[...] = jnp.zeros_like(to_ref)
    for image in range(count):
        to_ref[image : image + 1, :] = left_ref[image].astype(f32)[0:1, :]


class Sums:
    def __init__(self, mesh_sizes, streams, rows, shared):
        self.dp, self.tensor = mesh_sizes
        self.far = self.dp // 2
        self.streams, self.rows, self.shared = streams, rows, shared
        self.copies = 2 + 3 + 2 + 2 * (self.far - 1) + 1 + 3

    def scratch(self):
        s, r, far = self.streams, self.rows, self.far
        vm = lambda *dims: pltpu.VMEM((s, *dims, 128), bf16)
        return [
            vm(2, r), vm(2, r), vm(r // 2), vm(2, r // 4), vm(2, r // 4),
            vm(r // 2), vm(max(far - 1, 1), r // 2 // far), vm(2, r // 2),
            vm(4, self.shared[1]),
            pltpu.SemaphoreType.DMA((s, self.copies)), pltpu.SemaphoreType.DMA((s, self.copies)),
        ]

    def bind(self, send, refs):
        self.send = send
        (self.work, self.r1, self.r2y, self.r2x, self.r3, self.cur, self.r4, self.fin, self.out,
         self.ss, self.rs) = refs
        self.me_dp, self.me_t = lax.axis_index("dp"), lax.axis_index("tensor")
        self.x = lax.rem(self.me_dp, 2)
        self.z = self.me_dp // 2

    def peer(self, kind, j=1):
        if kind == "t":
            t = self.me_t
            flip0 = t + 1 - 2 * lax.rem(t, 2) if j & 1 else t
            high = flip0 // 2
            flipped = flip0 + 2 - 4 * lax.rem(high, 2) if j & 2 else flip0
            return (self.me_dp, flipped)
        if kind == "x":
            return (self.me_dp + 1 - 2 * self.x, self.me_t)
        return (lax.rem(self.z + j, self.far) * 2 + self.x, self.me_t)

    def peers(self):
        found = [self.peer("t", j) for j in (1, 2, 3)] + [self.peer("x")]
        return found + [self.peer("z", j) for j in range(1, self.far)]

    def greet(self):
        barrier = pltpu.get_barrier_semaphore()
        for peer in self.peers():
            pl.semaphore_signal(barrier, inc=1, device_id=peer, device_id_type=pl.DeviceIdType.MESH)

    def meet(self):
        pl.semaphore_wait(pltpu.get_barrier_semaphore(), len(self.peers()))

    def copy(self, s, index, src, dst, peer):
        return pltpu.make_async_remote_copy(
            src_ref=src, dst_ref=dst, send_sem=self.ss.at[s, index], recv_sem=self.rs.at[s, index],
            device_id=peer, device_id_type=pl.DeviceIdType.MESH,
        )

    def copies_of(self, phase, s):
        half, part = self.rows // 2, self.rows // 4
        chunk = half // self.far
        t, x, z = self.me_t, self.x, self.z
        cp = functools.partial(self.copy, s)
        if phase == 1:
            core = self.peer("t", 1)
            return [
                cp(0, self.send.at[s, core[1]], self.r1.at[s, 0], core),
                cp(1, self.send.at[s, self.peer("t", 3)[1]], self.r1.at[s, 1], core),
            ]
        if phase == 2:
            other = pl.ds(pl.multiple_of(half + (1 - x) * part, 16), part)
            return [
                cp(2, self.work.at[s, 1, pl.ds(0, half)], self.r2y.at[s], self.peer("t", 2)),
                cp(3, self.work.at[s, 0, other], self.r2x.at[s, 0], self.peer("x")),
                cp(4, self.work.at[s, 1, other], self.r2x.at[s, 1], self.peer("x")),
            ]
        if phase == 3:
            other = pl.ds(pl.multiple_of((1 - x) * part, 16), part)
            mine = pl.ds(pl.multiple_of(half + x * part, 16), part)
            return [
                cp(5, self.work.at[s, 0, other], self.r3.at[s, 0], self.peer("x")),
                cp(6, self.work.at[s, 1, mine], self.r3.at[s, 1], self.peer("t", 2)),
            ]
        found = []
        if phase == 4:
            for j in range(1, self.far):
                place = lax.rem(z + j, self.far)
                src = self.cur.at[s, pl.ds(pl.multiple_of(place * chunk, 16), chunk)]
                found.append(cp(6 + j, src, self.r4.at[s, j - 1], self.peer("z", j)))
        if phase == 5:
            mine = pl.ds(pl.multiple_of(z * chunk, 16), chunk)
            for j in range(1, self.far):
                ref = self.fin.at[s, x, mine]
                found.append(cp(5 + self.far + j, ref, ref, self.peer("z", j)))
        if phase == 6:
            ref = self.fin.at[s, x]
            found.append(cp(5 + 2 * self.far, ref, ref, self.peer("x")))
        if phase == 7:
            for j in (1, 2, 3):
                src = self.out.at[s, t]
                found.append(cp(5 + 2 * self.far + j, src, src, self.peer("t", j)))
        return found

    def start(self, phase, s):
        for copy in self.copies_of(phase, s):
            copy.start()

    def finish(self, phase, s):
        for copy in self.copies_of(phase, s):
            copy.wait()
        half, part = self.rows // 2, self.rows // 4
        chunk = half // self.far
        t, x, z = self.me_t, self.x, self.z

        def plus(*parts):
            total = parts[0].astype(f32)
            for one in parts[1:]:
                total = total + one.astype(f32)
            return total.astype(bf16)

        if phase == 1:
            self.work[s, 0] = plus(self.send[s, t], self.r1[s, 0])
            self.work[s, 1] = plus(self.send[s, self.peer("t", 2)[1]], self.r1[s, 1])
        if phase == 2:
            self.work[s, 0, :half] = plus(self.work[s, 0, :half], self.r2y[s])
            mine = pl.ds(pl.multiple_of(half + x * part, 16), part)
            for q in range(2):
                self.work[s, q, mine] = plus(self.work[s, q, mine], self.r2x[s, q])
        if phase == 3:
            mine = pl.ds(pl.multiple_of(x * part, 16), part)
            self.cur[s, :part] = plus(self.work[s, 0, mine], self.r3[s, 0])
            mine = pl.ds(pl.multiple_of(half + x * part, 16), part)
            self.cur[s, part:] = plus(self.work[s, 0, mine], self.r3[s, 1])
        if phase == 4:
            mine = pl.ds(pl.multiple_of(z * chunk, 16), chunk)
            self.fin[s, x, mine] = plus(
                self.cur[s, mine], *(self.r4[s, j - 1] for j in range(1, self.far))
            )
        if phase == 6:
            first, count = self.shared
            first = first - self.rows // 2
            side, first = first // part, first % part
            self.out[s, t] = self.fin[s, side, part + first : part + first + count]

    def advance(self, phase, s):
        self.finish(phase, s)
        if phase < 7:
            self.start(phase + 1, s)

    def quarter_rows(self, s, first, count):
        half, part = self.rows // 2, self.rows // 4
        pieces, at = [], first
        while at < first + count:
            block = at // part
            end = min(first + count, (block + 1) * part)
            low = (block // 2) * part + at - block * part
            pieces.append(self.fin[s, block % 2, low : low + end - at].astype(f32))
            at = end
        return pieces[0] if len(pieces) == 1 else jnp.concatenate(pieces, axis=0)


def attend_kernel(
    count, group,
    tok, left, pmask, live, vec, aw, mw,
    fi_out, qkv_out, probs_out, edge_out, inv_out, lp_out, lself_out, att_out, hid_out,
    fil_out, qkvl_out, attl_out, hidl_out,
    awt, mwt, fia, atta, cols, peaks, xl, qkvl, attl,
):
    step = pl.program_id(0)
    features = aw.shape[0]
    packed = aw.shape[1]
    rows = xl.shape[0]
    heads = head_rows(rows, features)

    @pl.when(step == 0)
    def _():
        for part in range(3):
            span = slice(part * features, (part + 1) * features)
            block = aw[:, span].astype(f32).T
            awt[span, :features] = (block * (HEAD**-0.5 if part == 0 else 1.0)).astype(bf16)
            if part == 1:
                bias = jnp.zeros((1, features), f32)
            else:
                bias = vec[2:3, :] * (HEAD**-0.5) if part == 0 else vec[3:4, :]
            awt[span, features:] = rows_where(0, bias, 128, f32).T.astype(bf16)
        mwt[:, :features] = mw[...].astype(f32).T.astype(bf16)
        mwt[:, features:] = rows_where(0, vec[4:5, :], 128, f32).T.astype(bf16)
        ones = rows_where(0, jnp.ones((1, fia.shape[1]), f32), 128, bf16)
        fia[features:, :] = ones
        atta[features:, :] = ones
        cols[0] = as_column(vec[0:1, :])
        cols[1] = as_column(vec[1:2, :])
        peaks[...] = jnp.zeros_like(peaks)
        take_left(left, xl, count)
        normed, _ = norm_rows(xl[...])
        fil = (normed * vec[0:1, :] + vec[1:2, :]).astype(bf16)
        fil_out[...] = fil.astype(f32)
        bias = jnp.concatenate([vec[2:3, :], jnp.zeros((1, features), f32), vec[3:4, :]], axis=1)
        rounded = (dot(fil, aw[...]) + bias).astype(bf16).astype(f32)
        at = lax.broadcasted_iota(jnp.int32, (1, packed), 1)
        qkvl[...] = rounded * jnp.where(at < features, HEAD**-0.5, 1.0)
        qkvl_out[...] = qkvl[...]
        attl[...] = jnp.zeros_like(attl)

    tokens = jnp.concatenate([tok[g].astype(f32).T for g in range(group)], axis=1)
    width = group * MAIN
    normed, _ = norm_columns(tokens)
    fi = (normed * wide(cols[0], width) + wide(cols[1], width)).astype(bf16)
    fia[:features, :] = fi
    qkv = dot(awt[...], fia[...]).astype(bf16)
    one_row = rows_where(0, jnp.ones((1, MAIN), f32), 16, bf16)
    for g in range(group):
        image = step * group + g
        lanes = slice(g * MAIN, (g + 1) * MAIN)
        fi_out[g] = fi[:, lanes]
        qt = qkv[:features, lanes]
        kt = qkv[features : 2 * features, lanes]
        vt = qkv[2 * features :, lanes]
        qkv_out[g] = qkv[:, lanes]
        qkv_row = qkvl[pl.ds(image, 1), :]
        ql, kl, vl = (qkv_row[:, p * features : (p + 1) * features] for p in range(3))
        qlb, klb, vlb = ((heads * v).astype(bf16) for v in (ql, kl, vl))

        key_bias = jnp.where(pmask[pl.ds(image, 1), :] == 1, 0.0, MASKED)
        moved = pltpu.roll(key_bias, 1, axis=1)
        left_bias = moved[:, 0:1]
        at = lax.broadcasted_iota(jnp.int32, moved.shape, 1)
        main_bias = jnp.where(at == 0, 0.0, moved)
        bias_rows = rows_where(0, main_bias, 16, bf16)

        slk = dot(klb, qt) + left_bias
        outs = []
        for h in range(HEADS):
            span = slice(h * HEAD, (h + 1) * HEAD)
            scores = dot(
                jnp.concatenate([kt[span], bias_rows], axis=0),
                jnp.concatenate([qt[span], one_row], axis=0),
                TN,
            )
            peak = jnp.maximum(jnp.max(scores, axis=0, keepdims=True), slk[h : h + 1, :])
            raised = jnp.exp(scores - peak).astype(bf16)
            probs_out[g, h] = raised
            peaks[g, h : h + 1, :] = peak
            outs.append(dot(jnp.concatenate([vt[span], one_row], axis=0), raised))
        edge = jnp.exp(slk - peaks[g])
        edge_out[g] = edge
        added = dot(vlb, edge.astype(bf16), TN)
        for h in range(HEADS):
            span = slice(h * HEAD, (h + 1) * HEAD)
            inv = 1.0 / (outs[h][HEAD : HEAD + 1, :] + edge[h : h + 1, :])
            inv_out[g, h : h + 1, :] = inv
            mixed = ((outs[h][:HEAD, :] + added[span]) * inv).astype(bf16)
            atta[span, lanes] = mixed
            att_out[g, span, :] = mixed

        sl = dot(qlb, kt) + main_bias
        self_score = jnp.sum(heads * (ql * kl), axis=1, keepdims=True) + left_bias
        peak = jnp.maximum(jnp.max(sl, axis=1, keepdims=True), self_score)
        raised = jnp.exp(sl - peak)
        raised_self = jnp.exp(self_score - peak)
        inv = 1.0 / (jnp.sum(raised, axis=1, keepdims=True) + raised_self)
        lp = raised * inv
        lself = raised_self * inv
        lp_out[g] = lp
        lself_out[g] = jnp.broadcast_to(lself, (rows, 128))
        mixed = dot(lp.astype(bf16), vt, NT) + lself * vl
        attl[pl.ds(image, 1), :] = jnp.sum(mixed * heads, axis=0, keepdims=True).astype(bf16).astype(f32)

    branch = dot(mwt[...], atta[...])
    hidden = tokens + lane_live(live, step * group, group) * branch
    for g in range(group):
        hid_out[g] = hidden[:, g * MAIN : (g + 1) * MAIN]

    @pl.when(step == pl.num_programs(0) - 1)
    def _():
        attl_out[...] = attl[...]
        branch = dot(attl[...].astype(bf16), mw[...]) + vec[4:5, :]
        hidl_out[...] = xl[...] + row_live(live, count, rows) * branch


def feed_kernel(
    count, group,
    hid, att, cot, cleft, live, vec, hidl, attl, upw, upb, dnw,
    out, gh_out, ga_out, ghl_out, gal_out, send,
    upt, dnt, sia, atta, act, gpre, gb, cols, gsum, xl, outl, up_acc, down_acc, merge_acc, sums_out,
):
    step = pl.program_id(0)
    features, hidden_units = upw.shape
    rows = xl.shape[0]
    width = group * MAIN
    part = 384

    @pl.when(step == 0)
    def _():
        for at in range(0, hidden_units, part):
            span = slice(at, at + part)
            upt[span, :features] = upw[:, span].astype(f32).T.astype(bf16)
            upt[span, features:] = rows_where(0, upb[0:1, span].astype(f32), 128, f32).T.astype(bf16)
            dnt[:, span] = dnw[span, :].astype(f32).T.astype(bf16)
        ones = rows_where(0, jnp.ones((1, width), f32), 128, bf16)
        sia[features:, :] = ones
        atta[features:, :] = ones
        cols[0] = as_column(vec[5:6, :])
        cols[1] = as_column(vec[6:7, :])
        cols[2] = as_column(vec[7:8, :])
        gsum[...] = jnp.zeros_like(gsum)
        take_left(cleft, xl, count)
        alive = row_live(live, count, rows)
        normed, scale = norm_rows(hidl[...])
        si = (normed * vec[5:6, :] + vec[6:7, :]).astype(bf16)
        pre = dot(si, upw[...]) + upb[0:1, :].astype(f32)
        value, slope = gelu_both(pre)
        value = value.astype(bf16)
        outl[...] = hidl[...] + alive * (dot(value, dnw[...]) + vec[7:8, :])
        grad_branch = (alive * xl[...]).astype(bf16)
        grad_pre = (dot(grad_branch, dnw[...], NT) * slope).astype(bf16)
        grad_second = dot(grad_pre, upw[...], NT)
        grad_hidden = xl[...] + norm_back(grad_second * vec[5:6, :], normed, scale, 1)
        ghl_out[...] = grad_hidden
        grad_attn = (alive * grad_hidden).astype(bf16)
        gal_out[...] = grad_attn.astype(f32)
        one = jnp.ones((rows, 16), bf16)
        up_acc[...] = dot(jnp.concatenate([si.astype(f32), one.astype(f32)], axis=1).astype(bf16), grad_pre, TN)
        down_acc[...] = dot(grad_branch, value, TN)
        merge_acc[...] = dot(
            jnp.concatenate([attl[...], one.astype(f32)], axis=1).astype(bf16), grad_attn, TN
        )
        sums_out[...] = jnp.zeros_like(sums_out)
        sums_out[0:1, :] = jnp.sum(grad_second * normed, axis=0, keepdims=True)
        sums_out[1:2, :] = jnp.sum(grad_second, axis=0, keepdims=True)
        sums_out[2:3, :] = jnp.sum(grad_branch.astype(f32), axis=0, keepdims=True)

    alive = lane_live(live, step * group, group)
    hidden = jnp.concatenate([hid[g] for g in range(group)], axis=1)
    normed, scale = norm_columns(hidden)
    sia[:features, :] = (normed * wide(cols[0], width) + wide(cols[1], width)).astype(bf16)
    cotangent = jnp.concatenate([cot[g].astype(f32).T for g in range(group)], axis=1)
    gb[...] = (cotangent * alive).astype(bf16)
    for at in range(0, hidden_units, part):
        span = slice(at, at + part)
        pre = dot(upt[span, :], sia[...])
        grad_act = dot(dnw[span, :], gb[...])
        value, slope = gelu_both(pre)
        act[span, :] = value.astype(bf16)
        gpre[span, :] = (grad_act * slope).astype(bf16)
    reduced = dot(dnt[...], act[...])
    grad_second = dot(upw[...], gpre[...])
    result = hidden + alive * (reduced + wide(cols[2], width))
    up_acc[...] += dot(sia[: up_acc.shape[0], :], gpre[...], NT)
    down_acc[...] += dot(gb[...], act[...], NT)
    grad_hidden = cotangent + norm_back(grad_second * wide(cols[0], width), normed, scale, 0)
    grad_attn = (alive * grad_hidden).astype(bf16)
    both = grad_second * normed
    for at in range(0, width, 128):
        gsum[0] += both[:, at : at + 128]
        gsum[1] += grad_second[:, at : at + 128]
    sums_out[2:3, :] += dot(jnp.ones((16, width), bf16), gb[...], NT)[0:1, :]
    for g in range(group):
        lanes = slice(g * MAIN, (g + 1) * MAIN)
        image = step * group + g
        gh_out[g] = grad_hidden[:, lanes]
        ga_out[g] = grad_attn[:, lanes]
        atta[:features, lanes] = att[g]
        out[g, :MAIN, :] = result[:, lanes].T.astype(bf16)
        out[g, MAIN : MAIN + 1, :] = outl[pl.ds(image, 1), :].astype(bf16)
    merge_acc[...] += dot(atta[: merge_acc.shape[0], :], grad_attn, NT)

    @pl.when(step == pl.num_programs(0) - 1)
    def _():
        sums_out[0:1, :] += jnp.sum(gsum[0].T, axis=0, keepdims=True)
        sums_out[1:2, :] += jnp.sum(gsum[1].T, axis=0, keepdims=True)
        up_rows, merge_rows = up_acc.shape[0], merge_acc.shape[0]
        quarter = (merge_rows + 48) // 4
        used = up_rows + features + quarter
        shared = jnp.concatenate(
            [merge_acc[...], sums_out[...], jnp.zeros((40, features), f32)], axis=0
        ).astype(bf16)
        for s in range(send.shape[0]):
            for q in range(4):
                lanes = slice(q * features + s * 128, q * features + (s + 1) * 128)
                send[s, q, :up_rows] = up_acc[:, lanes].astype(bf16)
                send[s, q, up_rows : up_rows + features] = down_acc[:, lanes].astype(bf16)
                send[s, q, up_rows + features : used] = shared[
                    q * quarter : (q + 1) * quarter, s * 128 : (s + 1) * 128
                ]
                if used < send.shape[2]:
                    send[s, q, used:] = jnp.zeros((send.shape[2] - used, 128), bf16)


def attend_back_kernel(
    count, group, sums, plan,
    qkv, probs, edge, inv, lp, lself, att, ga, fi, fil, qkvl, attl, gal, mw, send,
    gp_out, gpl_out, acc, up_out, down_out, merge_out, rows_out,
    fia, gpa, gml, dots, gmleft, gpl, *comm,
):
    step = pl.program_id(0)
    sums.bind(send, comm)

    @pl.when(step == 0)
    def _():
        sums.greet()
        sums.meet()
        for s in range(sums.streams):
            sums.start(1, s)

    features = mw.shape[0]
    rows = gal.shape[0]
    heads = head_rows(rows, features)

    @pl.when(step == 0)
    def _():
        fia[features:, :] = rows_where(0, jnp.ones((1, fia.shape[1]), f32), 16, bf16)
        acc[...] = jnp.zeros_like(acc)
        dots[...] = jnp.zeros_like(dots)
        gmleft[...] = dot(gal[...].astype(bf16), mw[...], NT).astype(bf16).astype(f32)
        gpl[...] = jnp.zeros_like(gpl)

    at16 = lax.broadcasted_iota(jnp.int32, (16, MAIN), 0)
    minus = jnp.where(at16 < 2, -1.0, 0.0).astype(bf16)
    for g in range(group):
        for slot, phase, s in plan:
            if slot < count and slot % group == g:
                pl.when(step == slot // group)(functools.partial(sums.advance, phase, s))
        image = step * group + g
        lanes = slice(g * MAIN, (g + 1) * MAIN)
        qt = qkv[g, :features, :]
        kt = qkv[g, features : 2 * features, :]
        vt = qkv[g, 2 * features :, :]
        fia[:features, lanes] = fi[g]
        grad_mixed = dot(mw[...], ga[g]).astype(bf16).astype(f32)
        both = grad_mixed * att[g].astype(f32)
        edge_f = edge[g]
        tails = []
        for h in range(HEADS):
            span = slice(h * HEAD, (h + 1) * HEAD)
            row_inv = inv[g, h : h + 1, :]
            gml[span, lanes] = (grad_mixed[span] * row_inv).astype(bf16)
            row_dot = jnp.sum(both[span], axis=0, keepdims=True) * row_inv
            dots[g, h : h + 1, :] = row_dot
            high = row_dot.astype(bf16).astype(f32)
            tails.append(
                jnp.where(at16 == 0, high, jnp.where(at16 == 1, row_dot - high, 0.0)).astype(bf16)
            )

        qkv_row = qkvl[pl.ds(image, 1), :]
        ql, kl, vl = (qkv_row[:, p * features : (p + 1) * features] for p in range(3))
        qlb, klb, vlb = ((heads * v).astype(bf16) for v in (ql, kl, vl))
        scaled = gml[:, lanes]
        edge_grad = (edge_f * (dot(vlb, scaled) - dots[g])).astype(bf16)
        grad_kl = jnp.sum(dot(edge_grad, qt, NT) * heads, axis=0, keepdims=True)
        grad_vl = jnp.sum(dot(edge_f.astype(bf16), scaled, NT) * heads, axis=0, keepdims=True)
        gm_row = gmleft[pl.ds(image, 1), :]
        gmb = (heads * gm_row).astype(bf16)
        row_dot = jnp.sum(heads * (gm_row * attl[pl.ds(image, 1), :]), axis=1, keepdims=True)
        left_grad = (lp[g] * (dot(gmb, vt) - row_dot)).astype(bf16)
        self_prob = lself[g][:, 0:1]
        self_grad = self_prob * (jnp.sum(heads * (gm_row * vl), axis=1, keepdims=True) - row_dot)
        self_grad = self_grad.astype(bf16).astype(f32)
        self_row = jnp.sum(heads * self_grad, axis=0, keepdims=True)
        prob_row = jnp.sum(heads * self_prob.astype(bf16).astype(f32), axis=0, keepdims=True)
        grad_ql = jnp.sum(dot(left_grad, kt, NT) * heads, axis=0, keepdims=True) + self_row * kl
        grad_kl = grad_kl + self_row * ql
        grad_vl = grad_vl + prob_row * gm_row
        gpl[pl.ds(image, 1), :] = (
            jnp.concatenate([grad_ql * HEAD**-0.5, grad_kl, grad_vl], axis=1).astype(bf16).astype(f32)
        )
        add_q = dot(klb, edge_grad, TN)
        add_k = dot(qlb, left_grad, TN)
        add_v = dot(gmb, lp[g].astype(bf16), TN)
        for h in range(HEADS):
            span = slice(h * HEAD, (h + 1) * HEAD)
            raised = probs[g, h]
            change = dot(
                jnp.concatenate([vt[span], minus], axis=0),
                jnp.concatenate([scaled[span], tails[h]], axis=0),
                TN,
            )
            score_grad = raised * change.astype(bf16)
            grad_q = (dot(kt[span], score_grad) + add_q[span]) * HEAD**-0.5
            grad_k = dot(qt[span], score_grad, NT) + add_k[span]
            grad_v = dot(scaled[span], raised, NT) + add_v[span]
            for p, grad in enumerate((grad_q, grad_k, grad_v)):
                to = slice(p * features + h * HEAD, p * features + (h + 1) * HEAD)
                rounded = grad.astype(bf16)
                gpa[to, lanes] = rounded
                gp_out[g, to, :] = rounded
    acc[...] += dot(fia[...], gpa[...], NT)

    @pl.when(step == pl.num_programs(0) - 1)
    def _():
        gpl_out[...] = gpl[...]
        one = jnp.ones((rows, 16), f32)
        acc[...] += dot(
            jnp.concatenate([fil[...], one], axis=1).astype(bf16), gpl[...].astype(bf16), TN
        )
        for slot, phase, s in plan:
            if slot >= count:
                sums.advance(phase, s)
        for s in range(sums.streams):
            lanes = slice(s * 128, (s + 1) * 128)
            up_out[:, lanes] = sums.quarter_rows(s, 0, features)
            rows_out[8:16, lanes] = sums.quarter_rows(s, features, 16)[:8]
            down_out[lanes, :] = sums.quarter_rows(s, features + 16, features).T
            shared = jnp.concatenate([sums.out[s, q].astype(f32) for q in range(4)], axis=0)
            merge_out[:, lanes] = shared[:features]
            rows_out[16:24, lanes] = shared[features : features + 8]
            rows_out[:8, lanes] = shared[features + 16 : features + 24]


def first_back_kernel(
    count, group,
    tok, left, gp, gh, gpl, ghl, vec, aw,
    out, sums_out,
    cols, gsum, xl, outl,
):
    step = pl.program_id(0)
    width = group * MAIN

    @pl.when(step == 0)
    def _():
        cols[...] = as_column(vec[0:1, :])
        gsum[...] = jnp.zeros_like(gsum)
        take_left(left, xl, count)
        normed, scale = norm_rows(xl[...])
        grad_first = dot(gpl[...].astype(bf16), aw[...], NT)
        outl[...] = ghl[...] + norm_back(grad_first * vec[0:1, :], normed, scale, 1)
        sums_out[...] = jnp.zeros_like(sums_out)
        sums_out[0:1, :] = jnp.sum(grad_first * normed, axis=0, keepdims=True)
        sums_out[1:2, :] = jnp.sum(grad_first, axis=0, keepdims=True)

    tokens = jnp.concatenate([tok[g].astype(f32).T for g in range(group)], axis=1)
    normed, scale = norm_columns(tokens)
    packed = jnp.concatenate([gp[g] for g in range(group)], axis=1)
    grad_first = dot(aw[...], packed)
    grad = norm_back(grad_first * wide(cols[...], width), normed, scale, 0)
    both = grad_first * normed
    for at in range(0, width, 128):
        gsum[0] += both[:, at : at + 128]
        gsum[1] += grad_first[:, at : at + 128]
    for g in range(group):
        image = step * group + g
        result = gh[g] + grad[:, g * MAIN : (g + 1) * MAIN]
        out[g, :MAIN, :] = result.T.astype(bf16)
        out[g, MAIN : MAIN + 1, :] = outl[pl.ds(image, 1), :].astype(bf16)

    @pl.when(step == pl.num_programs(0) - 1)
    def _():
        sums_out[0:1, :] += jnp.sum(gsum[0].T, axis=0, keepdims=True)
        sums_out[1:2, :] += jnp.sum(gsum[1].T, axis=0, keepdims=True)


def per_step(group, *dims):
    return pl.BlockSpec((group, *dims), lambda i: (i,) + (0,) * len(dims))


def whole(*dims):
    return pl.BlockSpec(dims, lambda i: (0,) * len(dims))


LIVE = pl.BlockSpec(memory_space=pltpu.SMEM)


def params():
    return pltpu.CompilerParams(vmem_limit_bytes=58 * 2**20, dimension_semantics=("arbitrary",))


def shape(dtype, *dims):
    return jax.ShapeDtypeStruct(dims, dtype)


def shards(
    mesh_sizes, tokens, image_mask, patch_mask, first_gain, first_shift, attend_weight, attend_bias,
    merge_weight, merge_bias, second_gain, second_shift, up_weight, up_bias, down_weight,
    down_bias, cotangent,
):
    n, seq, d = tokens.shape
    packed = attend_weight.shape[1]
    rows = -(-n // 16) * 16
    group = 2 if n % 2 == 0 else 1
    steps = n // group
    width = group * MAIN
    left = pl.BlockSpec((n, 16, d), lambda i: (0, MAIN // 16, 0))
    vec = jnp.stack(
        [
            v.astype(f32)
            for v in (
                first_gain, first_shift, attend_bias[0], attend_bias[1], merge_bias,
                second_gain, second_shift, down_bias,
            )
        ]
    )
    up_all = lax.all_gather(up_weight, "tensor", axis=1, tiled=True)
    down_all = lax.all_gather(down_weight, "tensor", axis=0, tiled=True)
    up_bias_all = lax.all_gather(up_bias, "tensor", axis=0, tiled=True)[None, :]
    units = up_all.shape[1]

    main = per_step(group, d, MAIN)
    token_in = per_step(group, MAIN, d)
    token_out = per_step(group, seq, d)
    edge = per_step(group, rows, MAIN)
    fi, qkv, probs, edges, invs, lp, lself, att, hid, fil, qkvl, attl, hidl = pl.pallas_call(
        functools.partial(attend_kernel, n, group),
        grid=(steps,),
        in_specs=[token_in, left, whole(n, MAIN), LIVE, whole(8, d), whole(d, packed), whole(d, d)],
        out_specs=[
            main, per_step(group, packed, MAIN), per_step(group, HEADS, MAIN, MAIN), edge, edge, edge,
            per_step(group, rows, 128), main, main,
            whole(rows, d), whole(rows, packed), whole(rows, d), whole(rows, d),
        ],
        out_shape=[
            shape(bf16, n, d, MAIN), shape(bf16, n, packed, MAIN), shape(bf16, n, HEADS, MAIN, MAIN),
            shape(f32, n, rows, MAIN), shape(f32, n, rows, MAIN), shape(f32, n, rows, MAIN),
            shape(f32, n, rows, 128), shape(bf16, n, d, MAIN), shape(f32, n, d, MAIN),
            shape(f32, rows, d), shape(f32, rows, packed), shape(f32, rows, d), shape(f32, rows, d),
        ],
        scratch_shapes=[
            pltpu.VMEM((packed, d + 128), bf16), pltpu.VMEM((d, d + 128), bf16),
            pltpu.VMEM((d + 128, width), bf16), pltpu.VMEM((d + 128, width), bf16),
            pltpu.VMEM((2, d, 128), f32), pltpu.VMEM((group, rows, MAIN), f32),
            pltpu.VMEM((rows, d), f32), pltpu.VMEM((rows, packed), f32), pltpu.VMEM((rows, d), f32),
        ],
        compiler_params=params(),
        name="attend",
    )(tokens, tokens, patch_mask, image_mask, vec, attend_weight, merge_weight)

    rows_quarter = d + 16 + d + (d + 64) // 4
    unit = 16 * mesh_sizes[0]
    rows_quarter = -(-rows_quarter // unit) * unit
    sums = Sums(mesh_sizes, d // 128, rows_quarter, (2 * d + 16, (d + 64) // 4))
    plan = [(1 + s + 2 * (phase - 1), phase, s) for phase in range(1, 8) for s in range(sums.streams)]
    output, gh, ga, ghl, gal, send = pl.pallas_call(
        functools.partial(feed_kernel, n, group),
        grid=(steps,),
        in_specs=[
            main, main, token_in, left, LIVE, whole(8, d), whole(rows, d), whole(rows, d),
            whole(d, units), whole(1, units), whole(units, d),
        ],
        out_specs=[
            token_out, main, main, whole(rows, d), whole(rows, d),
            whole(sums.streams, 4, rows_quarter, 128),
        ],
        out_shape=[
            shape(bf16, n, seq, d), shape(f32, n, d, MAIN), shape(bf16, n, d, MAIN),
            shape(f32, rows, d), shape(f32, rows, d), shape(bf16, sums.streams, 4, rows_quarter, 128),
        ],
        scratch_shapes=[
            pltpu.VMEM((units, d + 128), bf16), pltpu.VMEM((d, units), bf16),
            pltpu.VMEM((d + 128, width), bf16), pltpu.VMEM((d + 128, width), bf16),
            pltpu.VMEM((units, width), bf16), pltpu.VMEM((units, width), bf16),
            pltpu.VMEM((d, width), bf16), pltpu.VMEM((3, d, 128), f32), pltpu.VMEM((2, d, 128), f32),
            pltpu.VMEM((rows, d), f32), pltpu.VMEM((rows, d), f32),
            pltpu.VMEM((d + 16, units), f32), pltpu.VMEM((d, units), f32), pltpu.VMEM((d + 16, d), f32),
            pltpu.VMEM((8, d), f32),
        ],
        compiler_params=params(),
        name="feed",
    )(hid, att, cotangent, cotangent, image_mask, vec, hidl, attl, up_all, up_bias_all, down_all)

    gp, gpl, attend_acc, up_grad, down_grad, merge_grad, row_grads = pl.pallas_call(
        functools.partial(attend_back_kernel, n, group, sums, plan),
        grid=(steps,),
        in_specs=[
            per_step(group, packed, MAIN), per_step(group, HEADS, MAIN, MAIN), edge, edge, edge,
            per_step(group, rows, 128), main, main, main,
            whole(rows, d), whole(rows, packed), whole(rows, d), whole(rows, d), whole(d, d),
            whole(sums.streams, 4, rows_quarter, 128),
        ],
        out_specs=[
            per_step(group, packed, MAIN), whole(rows, packed), whole(d + 16, packed),
            whole(d, d), whole(d, d), whole(d, d), whole(24, d),
        ],
        out_shape=[
            shape(bf16, n, packed, MAIN), shape(f32, rows, packed), shape(f32, d + 16, packed),
            shape(f32, d, d), shape(f32, d, d), shape(f32, d, d), shape(f32, 24, d),
        ],
        scratch_shapes=[
            pltpu.VMEM((d + 16, width), bf16), pltpu.VMEM((packed, width), bf16),
            pltpu.VMEM((d, width), bf16), pltpu.VMEM((group, rows, MAIN), f32),
            pltpu.VMEM((rows, d), f32), pltpu.VMEM((rows, packed), f32), *sums.scratch(),
        ],
        compiler_params=pltpu.CompilerParams(
            vmem_limit_bytes=58 * 2**20, dimension_semantics=("arbitrary",), collective_id=0,
            has_side_effects=True,
        ),
        name="attend_back",
    )(qkv, probs, edges, invs, lp, lself, att, ga, fi, fil, qkvl, attl, gal, merge_weight, send)

    input_grad, first_sums = pl.pallas_call(
        functools.partial(first_back_kernel, n, group),
        grid=(steps,),
        in_specs=[
            token_in, left, per_step(group, packed, MAIN), main, whole(rows, packed), whole(rows, d),
            whole(8, d), whole(d, packed),
        ],
        out_specs=[token_out, whole(8, d)],
        out_shape=[shape(bf16, n, seq, d), shape(f32, 8, d)],
        scratch_shapes=[
            pltpu.VMEM((d, 128), f32), pltpu.VMEM((2, d, 128), f32),
            pltpu.VMEM((rows, d), f32), pltpu.VMEM((rows, d), f32),
        ],
        compiler_params=params(),
        name="first_back",
    )(tokens, tokens, gp, gh, gpl, ghl, vec, attend_weight)

    attend_acc, first_sums = lax.psum((attend_acc, first_sums), ("dp", "tensor"))
    return (
        output,
        input_grad,
        first_sums[0],
        first_sums[1],
        attend_acc[:d],
        jnp.stack([attend_acc[d, :d], attend_acc[d, 2 * d :]]),
        merge_grad,
        row_grads[16],
        row_grads[0],
        row_grads[1],
        up_grad,
        row_grads[8],
        down_grad,
        row_grads[2],
    )


def solution(mesh):
    split = ("dp", "tensor")
    in_specs = (
        P(split, None, None), P(split), P(split, None), P(), P(), P(), P(), P(), P(), P(), P(),
        P(None, "tensor"), P("tensor"), P("tensor", None), P(), P(split, None, None),
    )
    out_specs = (
        P(split, None, None), P(split, None, None), P(), P(), P(), P(), P(), P(), P(), P(),
        P(None, "tensor"), P("tensor"), P("tensor", None), P(),
    )
    sizes = (mesh.shape["dp"], mesh.shape["tensor"])
    return jax.shard_map(functools.partial(shards, sizes), mesh=mesh, in_specs=in_specs, out_specs=out_specs, check_vma=False)
```

```python
import functools

import jax
import jax.numpy as jnp
from jax import lax
from jax.experimental import pallas as pl
from jax.experimental.pallas import tpu as pltpu
from jax.sharding import PartitionSpec as P

HEADS = 6
HEAD = 64
MAIN = 256
EPS = 1e-06
MASKED = -1e30
f32, bf16 = jnp.float32, jnp.bfloat16

NN = ((1,), (0,))
NT = ((1,), (1,))
TN = ((0,), (0,))


def dot(left, right, dims=NN):
    return lax.dot_general(left, right, (dims, ((), ())), preferred_element_type=f32)


def rows_where(index, value, rows, dtype):
    columns = value.shape[-1]
    at = lax.broadcasted_iota(jnp.int32, (rows, columns), 0)
    return jnp.where(at == index, value, 0.0).astype(dtype)


def wide(column, width):
    return jnp.concatenate([column] * (width // 128), axis=1)


def as_column(row):
    return jnp.broadcast_to(row, (128, row.shape[1])).T


def norm_columns(values):
    center = values - jnp.mean(values, axis=0, keepdims=True)
    scale = lax.rsqrt(jnp.mean(center * center, axis=0, keepdims=True) + EPS)
    return center * scale, scale


def norm_rows(values):
    center = values - jnp.mean(values, axis=1, keepdims=True)
    scale = lax.rsqrt(jnp.mean(center * center, axis=1, keepdims=True) + EPS)
    return center * scale, scale


def norm_back(grad, normed, scale, axis):
    mean_grad = jnp.mean(grad, axis=axis, keepdims=True)
    mean_both = jnp.mean(grad * normed, axis=axis, keepdims=True)
    return scale * (grad - mean_grad - normed * mean_both)


def gelu_both(pre):
    curve = 0.5 + 0.5 * lax.erf(pre * 0.7071067811865476)
    bell = 0.3989422804014327 * jnp.exp(-0.5 * pre * pre)
    return pre * curve, curve + pre * bell


def head_rows(rows, features):
    at = lax.broadcasted_iota(jnp.int32, (rows, features), 0)
    head = lax.broadcasted_iota(jnp.int32, (rows, features), 1) // HEAD
    return jnp.where(at == head, 1.0, 0.0)


def lane_live(live_ref, first, count):
    flags = [
        jnp.full((1, MAIN), live_ref[first + g].astype(f32)) for g in range(count)
    ]
    return jnp.concatenate(flags, axis=1)


def row_live(live_ref, count, rows):
    at = lax.broadcasted_iota(jnp.int32, (rows, 1), 0)
    flags = jnp.zeros((rows, 1), f32)
    for image in range(count):
        flags = jnp.where(at == image, live_ref[image].astype(f32), flags)
    return flags


def take_left(left_ref, to_ref, count):
    to_ref[...] = jnp.zeros_like(to_ref)
    for image in range(count):
        to_ref[image : image + 1, :] = left_ref[image].astype(f32)[0:1, :]


class Sums:
    def __init__(self, mesh_sizes, streams, rows, shared):
        self.dp, self.tensor = mesh_sizes
        self.far = self.dp // 2
        self.streams, self.rows, self.shared = streams, rows, shared
        self.copies = 2 + 3 + 2 + 2 * (self.far - 1) + 1 + 3

    def scratch(self):
        s, r, far = self.streams, self.rows, self.far
        vm = lambda *dims: pltpu.VMEM((s, *dims, 128), bf16)
        return [
            vm(2, r), vm(2, r), vm(r // 2), vm(2, r // 4), vm(2, r // 4),
            vm(r // 2), vm(max(far - 1, 1), r // 2 // far), vm(2, r // 2),
            vm(4, self.shared[1]),
            pltpu.SemaphoreType.DMA((s, self.copies)), pltpu.SemaphoreType.DMA((s, self.copies)),
        ]

    def bind(self, send, refs):
        self.send = send
        (self.work, self.r1, self.r2y, self.r2x, self.r3, self.cur, self.r4, self.fin, self.out,
         self.ss, self.rs) = refs
        self.me_dp, self.me_t = lax.axis_index("dp"), lax.axis_index("tensor")
        self.x = lax.rem(self.me_dp, 2)
        self.z = self.me_dp // 2

    def peer(self, kind, j=1):
        if kind == "t":
            t = self.me_t
            flip0 = t + 1 - 2 * lax.rem(t, 2) if j & 1 else t
            high = flip0 // 2
            flipped = flip0 + 2 - 4 * lax.rem(high, 2) if j & 2 else flip0
            return (self.me_dp, flipped)
        if kind == "x":
            return (self.me_dp + 1 - 2 * self.x, self.me_t)
        return (lax.rem(self.z + j, self.far) * 2 + self.x, self.me_t)

    def peers(self):
        found = [self.peer("t", j) for j in (1, 2, 3)] + [self.peer("x")]
        return found + [self.peer("z", j) for j in range(1, self.far)]

    def greet(self):
        barrier = pltpu.get_barrier_semaphore()
        for peer in self.peers():
            pl.semaphore_signal(barrier, inc=1, device_id=peer, device_id_type=pl.DeviceIdType.MESH)

    def meet(self):
        pl.semaphore_wait(pltpu.get_barrier_semaphore(), len(self.peers()))

    def copy(self, s, index, src, dst, peer):
        return pltpu.make_async_remote_copy(
            src_ref=src, dst_ref=dst, send_sem=self.ss.at[s, index], recv_sem=self.rs.at[s, index],
            device_id=peer, device_id_type=pl.DeviceIdType.MESH,
        )

    def copies_of(self, phase, s):
        half, part = self.rows // 2, self.rows // 4
        chunk = half // self.far
        t, x, z = self.me_t, self.x, self.z
        cp = functools.partial(self.copy, s)
        if phase == 1:
            core = self.peer("t", 1)
            return [
                cp(0, self.send.at[s, core[1]], self.r1.at[s, 0], core),
                cp(1, self.send.at[s, self.peer("t", 3)[1]], self.r1.at[s, 1], core),
            ]
        if phase == 2:
            other = pl.ds(pl.multiple_of(half + (1 - x) * part, 16), part)
            return [
                cp(2, self.work.at[s, 1, pl.ds(0, half)], self.r2y.at[s], self.peer("t", 2)),
                cp(3, self.work.at[s, 0, other], self.r2x.at[s, 0], self.peer("x")),
                cp(4, self.work.at[s, 1, other], self.r2x.at[s, 1], self.peer("x")),
            ]
        if phase == 3:
            other = pl.ds(pl.multiple_of((1 - x) * part, 16), part)
            mine = pl.ds(pl.multiple_of(half + x * part, 16), part)
            return [
                cp(5, self.work.at[s, 0, other], self.r3.at[s, 0], self.peer("x")),
                cp(6, self.work.at[s, 1, mine], self.r3.at[s, 1], self.peer("t", 2)),
            ]
        found = []
        if phase == 4:
            for j in range(1, self.far):
                place = lax.rem(z + j, self.far)
                src = self.cur.at[s, pl.ds(pl.multiple_of(place * chunk, 16), chunk)]
                found.append(cp(6 + j, src, self.r4.at[s, j - 1], self.peer("z", j)))
        if phase == 5:
            mine = pl.ds(pl.multiple_of(z * chunk, 16), chunk)
            for j in range(1, self.far):
                ref = self.fin.at[s, x, mine]
                found.append(cp(5 + self.far + j, ref, ref, self.peer("z", j)))
        if phase == 6:
            ref = self.fin.at[s, x]
            found.append(cp(5 + 2 * self.far, ref, ref, self.peer("x")))
        if phase == 7:
            for j in (1, 2, 3):
                src = self.out.at[s, t]
                found.append(cp(5 + 2 * self.far + j, src, src, self.peer("t", j)))
        return found

    def start(self, phase, s):
        for copy in self.copies_of(phase, s):
            copy.start()

    def finish(self, phase, s):
        for copy in self.copies_of(phase, s):
            copy.wait()
        half, part = self.rows // 2, self.rows // 4
        chunk = half // self.far
        t, x, z = self.me_t, self.x, self.z

        def plus(*parts):
            total = parts[0].astype(f32)
            for one in parts[1:]:
                total = total + one.astype(f32)
            return total.astype(bf16)

        if phase == 1:
            self.work[s, 0] = plus(self.send[s, t], self.r1[s, 0])
            self.work[s, 1] = plus(self.send[s, self.peer("t", 2)[1]], self.r1[s, 1])
        if phase == 2:
            self.work[s, 0, :half] = plus(self.work[s, 0, :half], self.r2y[s])
            mine = pl.ds(pl.multiple_of(half + x * part, 16), part)
            for q in range(2):
                self.work[s, q, mine] = plus(self.work[s, q, mine], self.r2x[s, q])
        if phase == 3:
            mine = pl.ds(pl.multiple_of(x * part, 16), part)
            self.cur[s, :part] = plus(self.work[s, 0, mine], self.r3[s, 0])
            mine = pl.ds(pl.multiple_of(half + x * part, 16), part)
            self.cur[s, part:] = plus(self.work[s, 0, mine], self.r3[s, 1])
        if phase == 4:
            mine = pl.ds(pl.multiple_of(z * chunk, 16), chunk)
            self.fin[s, x, mine] = plus(
                self.cur[s, mine], *(self.r4[s, j - 1] for j in range(1, self.far))
            )
        if phase == 6:
            first, count = self.shared
            first = first - self.rows // 2
            side, first = first // part, first % part
            self.out[s, t] = self.fin[s, side, part + first : part + first + count]

    def advance(self, phase, s):
        self.finish(phase, s)
        if phase < 7:
            self.start(phase + 1, s)

    def quarter_rows(self, s, first, count):
        half, part = self.rows // 2, self.rows // 4
        pieces, at = [], first
        while at < first + count:
            block = at // part
            end = min(first + count, (block + 1) * part)
            low = (block // 2) * part + at - block * part
            pieces.append(self.fin[s, block % 2, low : low + end - at].astype(f32))
            at = end
        return pieces[0] if len(pieces) == 1 else jnp.concatenate(pieces, axis=0)


class Spread:
    def __init__(self, mesh_sizes, streams, chunk):
        self.dp, self.tensor = mesh_sizes
        self.far = self.dp // 2
        self.streams, self.chunk = streams, chunk
        self.copies = 1 + 3 + (self.far - 1) + 3 + 1

    def scratch(self):
        s, c = self.streams, self.chunk
        vm = lambda *dims: pltpu.VMEM((s, *dims, 128), bf16)
        return [
            vm(8 * c), vm(4 * c), vm(4 * c), vm(3, c), vm(self.far, c), vm(8 * c),
            pltpu.SemaphoreType.DMA((s, self.copies)), pltpu.SemaphoreType.DMA((s, self.copies)),
        ]

    def bind(self, refs):
        self.send, self.r1, self.work, self.r2, self.r3, self.out, self.ss, self.rs = refs
        self.me_dp, self.me_t = lax.axis_index("dp"), lax.axis_index("tensor")
        self.x, self.z = lax.rem(self.me_dp, 2), self.me_dp // 2
        self.c, self.y = lax.rem(self.me_t, 2), self.me_t // 2
        self.place = 2 * self.y + self.x

    def plane(self, j):
        x = 1 - self.x if j & 1 else self.x
        y = 1 - self.y if j & 2 else self.y
        return (self.z * 2 + x, 2 * y + self.c), 2 * y + x

    def core(self):
        return (self.me_dp, 2 * self.y + 1 - self.c)

    def line(self, j):
        return (lax.rem(self.z + j, self.far) * 2 + self.x, self.me_t)

    def rows(self, first, count):
        return pl.ds(pl.multiple_of(first * self.chunk, 16), count * self.chunk)

    def copies_of(self, phase, s):
        def cp(index, src, dst, peer):
            return pltpu.make_async_remote_copy(
                src_ref=src, dst_ref=dst, send_sem=self.ss.at[s, index], recv_sem=self.rs.at[s, index],
                device_id=peer, device_id_type=pl.DeviceIdType.MESH,
            )

        if phase == 1:
            return [cp(0, self.send.at[s, self.rows(4 * (1 - self.c), 4)], self.r1.at[s], self.core())]
        found = []
        if phase == 2:
            for j in (1, 2, 3):
                peer, place = self.plane(j)
                found.append(cp(j, self.work.at[s, self.rows(place, 1)], self.r2.at[s, j - 1], peer))
        if phase == 3:
            for j in range(1, self.far):
                ref = self.r3.at[s, self.z]
                found.append(cp(3 + j, ref, ref, self.line(j)))
        mine = self.out.at[s, self.rows(4 * self.c + self.place, 1)]
        if phase == 4:
            for j in (1, 2, 3):
                found.append(cp(2 + self.far + j, mine, mine, self.plane(j)[0]))
        if phase == 5:
            ref = self.out.at[s, self.rows(4 * self.c, 4)]
            found.append(cp(6 + self.far, ref, ref, self.core()))
        return found

    def start(self, phase, s):
        for copy in self.copies_of(phase, s):
            copy.start()

    def advance(self, phase, s):
        for copy in self.copies_of(phase, s):
            copy.wait()
        if phase == 1:
            half = self.send[s, self.rows(4 * self.c, 4)].astype(f32)
            self.work[s] = (half + self.r1[s].astype(f32)).astype(bf16)
        if phase == 2:
            total = self.work[s, self.rows(self.place, 1)].astype(f32)
            for j in range(3):
                total = total + self.r2[s, j].astype(f32)
            self.r3[s, self.z] = total.astype(bf16)
        if phase == 3:
            total = self.r3[s, 0].astype(f32)
            for j in range(1, self.far):
                total = total + self.r3[s, j].astype(f32)
            self.out[s, self.rows(4 * self.c + self.place, 1)] = total.astype(bf16)
        if phase < 5:
            self.start(phase + 1, s)


def row_of(ref):
    return ref[...].astype(f32).reshape(1, ref.shape[0])


def parts_of(at, pair):
    return slice(pair * 384 + at * 128, pair * 384 + (at + 1) * 128)


def attend_kernel(
    count, group, steps,
    tok0, tok, left, pmask, live, gain, shift, abias, mbias, aw, mw,
    fi_out, qkv_out, probs_out, edge_out, inv_out, lp_out, lself_out, att_out, hid_out,
    fil_out, qkvl_out, attl_out, hidl_out,
    awt, mwt, fia, atta, cols, peaks, edges, qkv2, toks, xl, qkvl, attl,
):
    step = pl.program_id(0)
    features = aw.shape[0]
    packed = aw.shape[1]
    rows = xl.shape[0]
    width = group * MAIN
    pairs = HEADS // 2
    heads = head_rows(rows, features)

    def first_norm(block):
        tokens = jnp.concatenate([block[g].T for g in range(group)], axis=1)
        normed, _ = norm_columns(tokens.astype(f32))
        return tokens, (normed * wide(cols[0], width) + wide(cols[1], width)).astype(bf16)

    def project(slot, part):
        span = slice(part * features, (part + 1) * features)
        qkv2[slot, span, :] = dot(awt[span, :], fia[...]).astype(bf16)

    @pl.when(step == 0)
    def _():
        ab = abias[...].astype(f32)
        for pair in range(pairs):
            for at in range(3):
                cut = slice(at * features + pair * 128, at * features + (pair + 1) * 128)
                to = parts_of(at, pair)
                scale = HEAD**-0.5 if at == 0 else 1.0
                awt[to, :features] = (aw[:, cut].astype(f32).T * scale).astype(bf16)
                if at == 1:
                    bias = jnp.zeros((1, 128), f32)
                else:
                    bias = ab[at // 2 : at // 2 + 1, pair * 128 : (pair + 1) * 128] * scale
                awt[to, features:] = rows_where(0, bias, 128, f32).T.astype(bf16)
        mwt[:, :features] = mw[...].astype(f32).T.astype(bf16)
        mwt[:, features:] = rows_where(0, row_of(mbias), 128, f32).T.astype(bf16)
        ones = rows_where(0, jnp.ones((1, fia.shape[1]), f32), 128, bf16)
        fia[features:, :] = ones
        atta[features:, :] = ones
        cols[0] = as_column(row_of(gain))
        cols[1] = as_column(row_of(shift))
        peaks[...] = jnp.zeros_like(peaks)
        edges[...] = jnp.zeros_like(edges)
        take_left(left, xl, count)
        normed, _ = norm_rows(xl[...])
        fil = (normed * row_of(gain) + row_of(shift)).astype(bf16)
        fil_out[...] = fil.astype(f32)
        plain = dot(fil, aw[...])
        for pair in range(pairs):
            for at in range(3):
                cut = slice(at * features + pair * 128, at * features + (pair + 1) * 128)
                value = plain[:, cut]
                if at != 1:
                    value = value + ab[at // 2 : at // 2 + 1, pair * 128 : (pair + 1) * 128]
                value = value.astype(bf16).astype(f32)
                qkvl[:, parts_of(at, pair)] = value * (HEAD**-0.5) if at == 0 else value
        qkvl_out[...] = qkvl[...]
        attl[...] = jnp.zeros_like(attl)
        tokens, fi = first_norm(tok0)
        toks[0] = tokens
        fia[:features, :] = fi
        for part in range(3):
            project(0, part)

    def merge_branch():
        return dot(mwt[...], atta[...])

    def hidden_of(branch, index):
        tokens = toks[lax.rem(index, 3)].astype(f32)
        return tokens + lane_live(live, index * group, group) * branch

    @pl.when(step < steps)
    def _():
        edge_out[...] = jnp.zeros_like(edge_out)
        lp_out[...] = jnp.zeros_like(lp_out)
        lself_out[...] = jnp.zeros_like(lself_out)
        now, later = lax.rem(step, 2), lax.rem(step + 1, 2)
        one_row = rows_where(0, jnp.ones((1, MAIN), f32), 16, bf16)
        held = {}
        units = [(g, h) for g in range(group) for h in range(HEADS)]

        def lanes_of(g):
            return slice(g * MAIN, (g + 1) * MAIN)

        def part(at, g, h):
            low = (h // 2) * 384 + at * 128 + (h % 2) * HEAD
            return qkv2[now, low : low + HEAD, lanes_of(g)]

        def all_heads(at, g):
            return jnp.concatenate(
                [qkv2[now, parts_of(at, pair), lanes_of(g)] for pair in range(pairs)], axis=0
            )

        def begin(g):
            image = step * group + g
            row = qkvl[pl.ds(image, 1), :]
            ql, kl, vl = (
                jnp.concatenate([row[:, parts_of(at, pair)] for pair in range(pairs)], axis=1)
                for at in range(3)
            )
            key_bias = jnp.where(pmask[pl.ds(image, 1), :] == 1, 0.0, MASKED)
            moved = pltpu.roll(key_bias, 1, axis=1)
            at = lax.broadcasted_iota(jnp.int32, moved.shape, 1)
            main_bias = jnp.where(at == 0, 0.0, moved)
            left_bias = moved[:, 0:1]
            held["bias", g] = rows_where(0, main_bias, 16, bf16)
            held["vl", g] = vl
            held["slk", g] = dot((heads * kl).astype(bf16), all_heads(0, g)) + left_bias
            held["sl", g] = dot((heads * ql).astype(bf16), all_heads(1, g)) + main_bias
            held["self", g] = jnp.sum(heads * (ql * kl), axis=1, keepdims=True) + left_bias

        def left_query(g):
            sl, self_score = held.pop(("sl", g)), held.pop(("self", g))
            peak = jnp.maximum(jnp.max(sl, axis=1, keepdims=True), self_score)
            raised = jnp.exp(sl - peak)
            raised_self = jnp.exp(self_score - peak)
            inv = 1.0 / (jnp.sum(raised, axis=1, keepdims=True) + raised_self)
            lp = raised * inv
            lself = raised_self * inv
            for pair in range(pairs):
                lp_out[g, pair, 0:2, :] = lp[2 * pair : 2 * pair + 2, :]
                lself_out[g, pair, 0:2, :] = jnp.broadcast_to(lself[2 * pair : 2 * pair + 2, :], (2, 128))
            mixed = dot(lp.astype(bf16), all_heads(2, g), NT) + lself * held["vl", g]
            image = step * group + g
            attl[pl.ds(image, 1), :] = (
                jnp.sum(mixed * heads, axis=0, keepdims=True).astype(bf16).astype(f32)
            )

        def scores(g, h):
            held["s", g, h] = dot(
                jnp.concatenate([part(1, g, h), held["bias", g]], axis=0),
                jnp.concatenate([part(0, g, h), one_row], axis=0),
                TN,
            )

        def soften(g, h):
            value = held.pop(("s", g, h))
            slk = held["slk", g][h : h + 1, :]
            peak = jnp.maximum(jnp.max(value, axis=0, keepdims=True), slk)
            raised = jnp.exp(value - peak).astype(bf16)
            probs_out[g, h] = raised
            held["e", g, h] = raised
            edge = jnp.exp(slk - peak)
            held["edge", g, h] = edge
            edges[g, h : h + 1, :] = edge
            edge_out[g, h // 2, h % 2 : h % 2 + 1, :] = edge

        def mix(g, h):
            held["o", g, h] = dot(
                jnp.concatenate([part(2, g, h), one_row], axis=0), held.pop(("e", g, h))
            )

        def add_left(g):
            held["add", g] = dot((heads * held["vl", g]).astype(bf16), edges[g].astype(bf16), TN)

        def finish(g, h):
            out = held.pop(("o", g, h))
            span = slice(h * HEAD, (h + 1) * HEAD)
            inv = 1.0 / (out[HEAD : HEAD + 1, :] + held["edge", g, h])
            inv_out[g, h : h + 1, :] = inv
            mixed = ((out[:HEAD, :] + held["add", g][span]) * inv).astype(bf16)
            atta[span, lanes_of(g)] = mixed
            att_out[span, lanes_of(g)] = mixed

        count_units = len(units)
        for t in range(-2, count_units + 4):
            if t + 2 == 0:
                for g in range(group):
                    begin(g)
                held["branch"] = merge_branch()
            if 0 <= t + 2 < count_units:
                scores(*units[t + 2])
            if t == -1:
                hid_out[...] = hidden_of(held.pop("branch"), step - 1 + 3 * (1 - jnp.minimum(step, 1)))
                qkv_out[...] = qkv2[now]
                fi_out[:features, :] = fia[:features, :]
                fi_out[features:, :] = fia[features : features + 16, :]
                held["next"] = first_norm(tok)
            if t == 1:
                tokens, fi = held.pop("next")
                toks[lax.rem(step + 1, 3)] = tokens
                fia[:features, :] = fi
            if t in (2, 4, 6):
                project(later, (t - 2) // 2)
            if 0 <= t < count_units:
                soften(*units[t])
            if 0 <= t - 2 < count_units:
                mix(*units[t - 2])
            for g in range(group):
                if t == HEADS * g + 3:
                    left_query(g)
                if t == HEADS * (g + 1):
                    add_left(g)
                if t == HEADS * (g + 1) + 3:
                    for h in range(HEADS):
                        finish(g, h)

    @pl.when(step == steps)
    def _():
        hid_out[...] = hidden_of(merge_branch(), step - 1)
        attl_out[...] = attl[...]
        branch = dot(attl[...].astype(bf16), mw[...]) + row_of(mbias)
        hidl_out[...] = xl[...] + row_live(live, count, rows) * branch


def feed_kernel(
    count, group,
    hid, att, inv, cot, cleft, live, gain, shift, dbias, hidl, attl, upw, upb, dnw, mw,
    out, gh_out, gml_out, dots_out, ghl_out, gmleft_out, send,
    upt, dnt, sia, atta, act, gpre, gb, cols, gsum, xl, outl, up_acc, down_acc, merge_acc, sums_out,
):
    step = pl.program_id(0)
    features, hidden_units = upw.shape
    rows = xl.shape[0]
    width = group * MAIN
    part = 384

    @pl.when(step == 0)
    def _():
        gain_row, shift_row, dbias_row = row_of(gain), row_of(shift), row_of(dbias)
        for at in range(0, hidden_units, part):
            span = slice(at, at + part)
            upt[span, :features] = upw[:, span].astype(f32).T.astype(bf16)
            upt[span, features:] = rows_where(0, upb[0:1, span].astype(f32), 128, f32).T.astype(bf16)
            dnt[:, span] = dnw[span, :].astype(f32).T.astype(bf16)
        ones = rows_where(0, jnp.ones((1, width), f32), 128, bf16)
        sia[features:, :] = ones
        atta[features:, :] = ones
        cols[0] = as_column(gain_row)
        cols[1] = as_column(shift_row)
        cols[2] = as_column(dbias_row)
        gsum[...] = jnp.zeros_like(gsum)
        take_left(cleft, xl, count)
        alive = row_live(live, count, rows)
        normed, scale = norm_rows(hidl[...])
        si = (normed * gain_row + shift_row).astype(bf16)
        pre = dot(si, upw[...]) + upb[0:1, :].astype(f32)
        value, slope = gelu_both(pre)
        value = value.astype(bf16)
        outl[...] = hidl[...] + alive * (dot(value, dnw[...]) + dbias_row)
        grad_branch = (alive * xl[...]).astype(bf16)
        grad_pre = (dot(grad_branch, dnw[...], NT) * slope).astype(bf16)
        grad_second = dot(grad_pre, upw[...], NT)
        grad_hidden = xl[...] + norm_back(grad_second * gain_row, normed, scale, 1)
        ghl_out[...] = grad_hidden
        grad_attn = (alive * grad_hidden).astype(bf16)
        gmleft_out[...] = dot(grad_attn, mw[...], NT).astype(bf16).astype(f32)
        one = jnp.ones((rows, 16), f32)
        up_acc[...] = dot(jnp.concatenate([si.astype(f32), one], axis=1).astype(bf16), grad_pre, TN)
        down_acc[...] = dot(grad_branch, value, TN)
        merge_acc[...] = dot(jnp.concatenate([attl[...], one], axis=1).astype(bf16), grad_attn, TN)
        sums_out[...] = jnp.zeros_like(sums_out)
        sums_out[0:1, :] = jnp.sum(grad_second * normed, axis=0, keepdims=True)
        sums_out[1:2, :] = jnp.sum(grad_second, axis=0, keepdims=True)
        sums_out[2:3, :] = jnp.sum(grad_branch.astype(f32), axis=0, keepdims=True)

    alive = lane_live(live, step * group, group)
    hidden = hid[...]
    normed, scale = norm_columns(hidden)
    sia[:features, :] = (normed * wide(cols[0], width) + wide(cols[1], width)).astype(bf16)
    cotangent = jnp.concatenate([cot[g].T for g in range(group)], axis=1).astype(f32)
    gb[...] = (cotangent * alive).astype(bf16)
    pres, grads = {}, {}
    ready = hidden_units // part

    def into(c):
        span = slice(c * part, (c + 1) * part)
        pres[c] = dot(upt[span, :], sia[...])
        grads[c] = dot(dnw[span, :], gb[...])

    def through(c):
        span = slice(c * part, (c + 1) * part)
        value, slope = gelu_both(pres.pop(c))
        act[span, :] = value.astype(bf16)
        gpre[span, :] = (grads.pop(c) * slope).astype(bf16)

    into(0)
    for c in range(ready):
        if c + 1 < ready:
            into(c + 1)
        through(c)
    grad_second = dot(upw[...], gpre[...])
    reduced = dot(dnt[...], act[...])
    up_acc[...] += dot(sia[: up_acc.shape[0], :], gpre[...], NT)
    grad_hidden = cotangent + norm_back(grad_second * wide(cols[0], width), normed, scale, 0)
    gh_out[...] = grad_hidden
    grad_attn = (alive * grad_hidden).astype(bf16)
    grad_mixed = dot(mw[...], grad_attn)
    down_acc[...] += dot(gb[...], act[...], NT)
    result = hidden + alive * (reduced + wide(cols[2], width))
    for g in range(group):
        image = step * group + g
        out[g, :MAIN, :] = result[:, g * MAIN : (g + 1) * MAIN].astype(bf16).T
        out[g, MAIN : MAIN + 1, :] = outl[pl.ds(image, 1), :].astype(bf16)
    both = grad_second * normed
    for at in range(0, width, 128):
        gsum[0] += both[:, at : at + 128]
        gsum[1] += grad_second[:, at : at + 128]
    sums_out[2:3, :] += dot(jnp.ones((16, width), bf16), gb[...], NT)[0:1, :]
    atta[:features, :] = att[...]
    merge_acc[...] += dot(atta[: merge_acc.shape[0], :], grad_attn, NT)
    grad_mixed = grad_mixed.astype(bf16).astype(f32)
    both = grad_mixed * att[...].astype(f32)
    dots_out[...] = jnp.zeros_like(dots_out)
    for g in range(group):
        lanes = slice(g * MAIN, (g + 1) * MAIN)
        for h in range(HEADS):
            span = slice(h * HEAD, (h + 1) * HEAD)
            row_inv = inv[g, h : h + 1, :]
            gml_out[span, lanes] = (grad_mixed[span, lanes] * row_inv).astype(bf16)
            row_dot = jnp.sum(both[span, lanes], axis=0, keepdims=True) * row_inv
            dots_out[g, h // 2, h % 2 : h % 2 + 1, :] = row_dot

    @pl.when(step == pl.num_programs(0) - 1)
    def _():
        sums_out[0:1, :] += jnp.sum(gsum[0].T, axis=0, keepdims=True)
        sums_out[1:2, :] += jnp.sum(gsum[1].T, axis=0, keepdims=True)
        up_rows, merge_rows = up_acc.shape[0], merge_acc.shape[0]
        quarter = (merge_rows + 48) // 4
        used = up_rows + features + quarter
        shared = jnp.concatenate(
            [merge_acc[...], sums_out[...], jnp.zeros((40, features), f32)], axis=0
        ).astype(bf16)
        for s in range(send.shape[0]):
            for q in range(4):
                lanes = slice(q * features + s * 128, q * features + (s + 1) * 128)
                send[s, q, :up_rows] = up_acc[:, lanes].astype(bf16)
                send[s, q, up_rows : up_rows + features] = down_acc[:, lanes].astype(bf16)
                send[s, q, up_rows + features : used] = shared[
                    q * quarter : (q + 1) * quarter, s * 128 : (s + 1) * 128
                ]
                if used < send.shape[2]:
                    send[s, q, used:] = jnp.zeros((send.shape[2] - used, 128), bf16)


def back_kernel(
    count, group, steps, sums, spread, plan,
    qkv, probs, edge, lp, lself, gml, dots, fi, fil, qkvl, attl, gmleft, aw, send,
    tok, left, gh, ghl, gain, shift,
    out, attend_out, up_out, down_out, merge_out, rows_out,
    gpa, acc, gpl, awp, cols, xl, outl, *comm,
):
    step = pl.program_id(0)
    features = aw.shape[0]
    rows = xl.shape[0]
    pairs = HEADS // 2
    last = pairs * steps
    pair = lax.rem(step // steps, pairs)
    at_group = lax.rem(step, steps)
    used = len(sums.scratch())
    sums.bind(send, comm[:used])
    spread.bind(comm[used:])
    engines = {"sums": sums, "spread": spread}
    heads = head_rows(rows, 128)

    @pl.when(step == 0)
    def _():
        barrier = pltpu.get_barrier_semaphore()
        peers = sums.peers() + [spread.plane(3)[0]]
        for peer in peers:
            pl.semaphore_signal(barrier, inc=1, device_id=peer, device_id_type=pl.DeviceIdType.MESH)
        for part in range(pairs):
            for at in range(3):
                cut = slice(at * features + part * 128, at * features + (part + 1) * 128)
                awp[:, parts_of(at, part)] = aw[:, cut]
        cols[...] = as_column(row_of(gain))
        gpl[...] = jnp.zeros_like(gpl)
        pl.semaphore_wait(barrier, len(peers))
        for s in range(sums.streams):
            sums.start(1, s)

    for slot, name, phase, s in plan:
        if slot < last + steps:
            pl.when(step == slot)(functools.partial(engines[name].advance, phase, s))

    @pl.when(step < last)
    def _():
        at16 = lax.broadcasted_iota(jnp.int32, (16, MAIN), 0)
        minus = jnp.where(at16 < 2, -1.0, 0.0).astype(bf16)
        gp = gpa.at[at_group, pl.ds(pl.multiple_of(pair * 384, 128), 384)]
        held = {}
        units = [(g, r) for g in range(group) for r in range(2)]

        def lanes_of(g):
            return slice(g * MAIN, (g + 1) * MAIN)

        def part(at, r, g):
            return qkv[at * 128 + r * HEAD : at * 128 + (r + 1) * HEAD, lanes_of(g)]

        def both(at, g):
            return qkv[at * 128 : (at + 1) * 128, lanes_of(g)]

        def left_one(g):
            image = at_group * group + g
            row = qkvl[pl.ds(image, 1), :]
            ql, kl, vl = (row[:, at * 128 : (at + 1) * 128] for at in range(3))
            gm_row = gmleft[pl.ds(image, 1), :]
            row_dot = jnp.sum(heads * (gm_row * attl[pl.ds(image, 1), :]), axis=1, keepdims=True)
            self_prob = lself[g, 0][:, 0:1]
            self_grad = self_prob * (jnp.sum(heads * (gm_row * vl), axis=1, keepdims=True) - row_dot)
            self_grad = self_grad.astype(bf16).astype(f32)
            held["rows", g] = (ql, kl, vl, gm_row, row_dot, self_prob, self_grad)
            gmb = (heads * gm_row).astype(bf16)
            held["gmb", g] = gmb
            held["edge dp", g] = dot((heads * vl).astype(bf16), gml[:, lanes_of(g)])
            held["left dp", g] = dot(gmb, both(2, g))

        def left_two(g):
            ql, kl, vl, gm_row, row_dot, self_prob, self_grad = held["rows", g]
            edge_grad = (edge[g, 0] * (held.pop(("edge dp", g)) - dots[g, 0])).astype(bf16)
            left_grad = (lp[g, 0] * (held.pop(("left dp", g)) - row_dot)).astype(bf16)
            held["add", g] = (
                dot((heads * kl).astype(bf16), edge_grad, TN),
                dot((heads * ql).astype(bf16), left_grad, TN),
                dot(held.pop(("gmb", g)), lp[g, 0].astype(bf16), TN),
            )
            held["left", g] = (
                dot(left_grad, both(1, g), NT),
                dot(edge_grad, both(0, g), NT),
                dot(edge[g, 0].astype(bf16), gml[:, lanes_of(g)], NT),
            )

        def left_three(g):
            ql, kl, vl, gm_row, row_dot, self_prob, self_grad = held.pop(("rows", g))
            grad_ql, grad_kl, grad_vl = (
                jnp.sum(v * heads, axis=0, keepdims=True) for v in held.pop(("left", g))
            )
            self_row = jnp.sum(heads * self_grad, axis=0, keepdims=True)
            prob_row = jnp.sum(heads * self_prob.astype(bf16).astype(f32), axis=0, keepdims=True)
            image = at_group * group + g
            value = jnp.concatenate(
                [
                    (grad_ql + self_row * kl) * HEAD**-0.5,
                    grad_kl + self_row * ql,
                    grad_vl + prob_row * gm_row,
                ],
                axis=1,
            )
            gpl[pair, pl.ds(image, 1), :] = value.astype(bf16).astype(f32)

        def change(g, r):
            row_dot = dots[g, 0, r : r + 1, :]
            high = row_dot.astype(bf16).astype(f32)
            rest = jnp.where(at16 == 0, high, jnp.where(at16 == 1, row_dot - high, 0.0)).astype(bf16)
            held["z", g, r] = dot(
                jnp.concatenate([part(2, r, g), minus], axis=0),
                jnp.concatenate([gml[r * HEAD : (r + 1) * HEAD, lanes_of(g)], rest], axis=0),
                TN,
            )

        def scores(g, r):
            raised = probs[g, r]
            held["ds", g, r] = (raised.astype(f32) * held.pop(("z", g, r))).astype(bf16)
            held["v", g, r] = dot(gml[r * HEAD : (r + 1) * HEAD, lanes_of(g)], raised, NT)

        def grads(g, r):
            ds = held.pop(("ds", g, r))
            held["q", g, r] = dot(part(1, r, g), ds)
            held["k", g, r] = dot(part(0, r, g), ds, NT)

        def store(g, r):
            span = slice(r * HEAD, (r + 1) * HEAD)
            add_q, add_k, add_v = held["add", g]
            values = (
                (held.pop(("q", g, r)) + add_q[span]) * HEAD**-0.5,
                held.pop(("k", g, r)) + add_k[span],
                held.pop(("v", g, r)) + add_v[span],
            )
            for at, value in enumerate(values):
                gp[at * 128 + r * HEAD : at * 128 + (r + 1) * HEAD, lanes_of(g)] = value.astype(bf16)

        number = len(units)
        for t in range(-4, number + 4):
            for g in range(group):
                if t == 2 * g - 4:
                    left_one(g)
                if t == 2 * g - 2:
                    left_two(g)
                if t == 2 * g + 2:
                    left_three(g)
            if 0 <= t + 2 < number:
                change(*units[t + 2])
            if 0 <= t < number:
                scores(*units[t])
            if 0 <= t - 1 < number:
                grads(*units[t - 1])
            if 0 <= t - 3 < number:
                store(*units[t - 3])

        @pl.when(at_group == 0)
        def _():
            acc[...] = jnp.zeros_like(acc)

        acc[...] += dot(fi[...], gp[...], NT)

        @pl.when(at_group == steps - 1)
        def _():
            one = jnp.ones((rows, 16), f32)
            acc[...] += dot(
                jnp.concatenate([fil[...], one], axis=1).astype(bf16), gpl[pair].astype(bf16), TN
            )
            weight = awp[:, pl.ds(pl.multiple_of(pair * 384, 128), 384)].astype(f32)
            by_gain = weight * acc[:features, :]
            by_shift = weight * acc[features : features + 1, :]
            fold = lambda v: jnp.sum((v[:, :128] + v[:, 128:256] + v[:, 256:]).T, axis=0, keepdims=True)
            shift_row = fold(by_shift)
            gain_row = (fold(by_gain) - row_of(shift) * shift_row) / row_of(gain)
            block = features + 32
            for at in range(3):
                lanes = slice(at * 128, (at + 1) * 128)
                spread.send[pair, at * block : at * block + features + 16] = acc[:, lanes].astype(bf16)
                ends = rows_where(0, gain_row[:, lanes], 16, f32) + rows_where(1, shift_row[:, lanes], 16, f32)
                spread.send[pair, at * block + features + 16 : (at + 1) * block] = ends.astype(bf16)
            rest = spread.send.shape[1] - 3 * block
            if rest:
                spread.send[pair, 3 * block :] = jnp.zeros((rest, 128), bf16)
            spread.start(1, pair)

    @pl.when(step == last)
    def _():
        take_left(left, xl, count)
        normed, scale = norm_rows(xl[...])
        packed = jnp.concatenate([gpl[p] for p in range(pairs)], axis=1).astype(bf16)
        grad_first = dot(packed, awp[...], NT)
        outl[...] = ghl[...] + norm_back(grad_first * row_of(gain), normed, scale, 1)

    @pl.when(step >= last)
    def _():
        held = {}

        def product(g):
            held["grad", g] = dot(awp[...], gpa[at_group, :, g * MAIN : (g + 1) * MAIN])

        def norm(g):
            held["norm", g] = norm_columns(tok[g].T.astype(f32))

        def finish(g):
            normed, scale = held.pop(("norm", g))
            grad = norm_back(held.pop(("grad", g)) * wide(cols[...], MAIN), normed, scale, 0)
            result = gh[:, g * MAIN : (g + 1) * MAIN] + grad
            out[g, :MAIN, :] = result.astype(bf16).T
            image = at_group * group + g
            out[g, MAIN : MAIN + 1, :] = outl[pl.ds(image, 1), :].astype(bf16)

        product(0)
        norm(0)
        for g in range(group):
            if g + 1 < group:
                product(g + 1)
                norm(g + 1)
            finish(g)

    @pl.when(step == last + steps - 1)
    def _():
        for slot, name, phase, s in plan:
            if slot >= last + steps:
                engines[name].advance(phase, s)
        for s in range(sums.streams):
            lanes = slice(s * 128, (s + 1) * 128)
            up_out[:, lanes] = sums.quarter_rows(s, 0, features)
            rows_out[8:16, lanes] = sums.quarter_rows(s, features, 16)[:8]
            down_out[lanes, :] = sums.quarter_rows(s, features + 16, features).T
            shared = jnp.concatenate([sums.out[s, q].astype(f32) for q in range(4)], axis=0)
            merge_out[:, lanes] = shared[:features]
            rows_out[16:24, lanes] = shared[features : features + 8]
            rows_out[:8, lanes] = shared[features + 16 : features + 24]
        block = features + 32
        for at in range(3):
            total = jnp.zeros((16, 128), f32)
            for p in range(pairs):
                lanes = slice(at * features + p * 128, at * features + (p + 1) * 128)
                attend_out[:, lanes] = spread.out[p, at * block : at * block + features].astype(f32)
                total = total + spread.out[p, at * block + features + 16 : (at + 1) * block].astype(f32)
                if at != 1:
                    first = 32 + (at // 2) * 8
                    bias = spread.out[p, at * block + features : at * block + features + 16].astype(f32)
                    rows_out[first : first + 8, p * 128 : (p + 1) * 128] = bias[:8]
            rows_out[24:32, at * 128 : (at + 1) * 128] = total[:8]


def whole(*dims):
    return pl.BlockSpec(dims, lambda i: (0,) * len(dims))


def once(*dims):
    return pl.BlockSpec(dims, lambda i: (0,) * len(dims), pipeline_mode=pl.Buffered(1))


LIVE = pl.BlockSpec(memory_space=pltpu.SMEM)


def params(**more):
    return pltpu.CompilerParams(
        vmem_limit_bytes=60 * 2**20, dimension_semantics=("arbitrary",), **more
    )


def shape(dtype, *dims):
    return jax.ShapeDtypeStruct(dims, dtype)


def shards(
    mesh_sizes, tokens, image_mask, patch_mask, first_gain, first_shift, attend_weight, attend_bias,
    merge_weight, merge_bias, second_gain, second_shift, up_weight, up_bias, down_weight,
    down_bias, cotangent,
):
    n, seq, d = tokens.shape
    packed = attend_weight.shape[1]
    rows = -(-n // 16) * 16
    group = 2 if n % 2 == 0 else 1
    steps = n // group
    width = group * MAIN
    pairs = HEADS // 2
    total = n * MAIN
    left = pl.BlockSpec((n, 16, d), lambda i: (0, MAIN // 16, 0), pipeline_mode=pl.Buffered(1))
    up_all = lax.all_gather(up_weight, "tensor", axis=1, tiled=True)
    down_all = lax.all_gather(down_weight, "tensor", axis=0, tiled=True)
    up_bias_all = lax.all_gather(up_bias, "tensor", axis=0, tiled=True)[None, :]
    units = up_all.shape[1]

    here = lambda i: jnp.minimum(i, steps - 1)
    cols = lambda r: pl.BlockSpec((r, width), lambda i: (0, here(i)))
    images = lambda *dims: pl.BlockSpec((group, *dims), lambda i: (here(i),) + (0,) * len(dims))
    fi, qkv, probs, edges, invs, lp, lself, att, hid, fil, qkvl, attl, hidl = pl.pallas_call(
        functools.partial(attend_kernel, n, group, steps),
        grid=(steps + 1,),
        in_specs=[
            once(group, MAIN, d),
            pl.BlockSpec((group, MAIN, d), lambda i: (here(i + 1), 0, 0)),
            left, whole(n, MAIN), LIVE, whole(d), whole(d), whole(2, d), whole(d),
            once(d, packed), once(d, d),
        ],
        out_specs=[
            cols(d + 16), cols(packed), images(HEADS, MAIN, MAIN), images(pairs, 16, MAIN),
            images(16, MAIN), images(pairs, 16, MAIN), images(pairs, 16, 128), cols(d),
            pl.BlockSpec((d, width), lambda i: (0, jnp.maximum(i, 1) - 1)),
            whole(rows, d), whole(rows, packed), whole(rows, d), whole(rows, d),
        ],
        out_shape=[
            shape(bf16, d + 16, total), shape(bf16, packed, total), shape(bf16, n, HEADS, MAIN, MAIN),
            shape(f32, n, pairs, 16, MAIN), shape(f32, n, 16, MAIN), shape(f32, n, pairs, 16, MAIN),
            shape(f32, n, pairs, 16, 128), shape(bf16, d, total), shape(f32, d, total),
            shape(f32, rows, d), shape(f32, rows, packed), shape(f32, rows, d), shape(f32, rows, d),
        ],
        scratch_shapes=[
            pltpu.VMEM((packed, d + 128), bf16), pltpu.VMEM((d, d + 128), bf16),
            pltpu.VMEM((d + 128, width), bf16), pltpu.VMEM((d + 128, width), bf16),
            pltpu.VMEM((2, d, 128), f32), pltpu.VMEM((group, 16, MAIN), f32),
            pltpu.VMEM((group, 16, MAIN), f32), pltpu.VMEM((2, packed, width), bf16),
            pltpu.VMEM((3, d, width), bf16),
            pltpu.VMEM((rows, d), f32), pltpu.VMEM((rows, packed), f32), pltpu.VMEM((rows, d), f32),
        ],
        compiler_params=params(),
        name="attend",
    )(
        tokens, tokens, tokens, patch_mask, image_mask, first_gain, first_shift, attend_bias, merge_bias,
        attend_weight, merge_weight,
    )

    rows_quarter = d + 16 + d + (d + 64) // 4
    unit = 16 * mesh_sizes[0]
    rows_quarter = -(-rows_quarter // unit) * unit
    sums = Sums(mesh_sizes, d // 128, rows_quarter, (2 * d + 16, (d + 64) // 4))
    cols = lambda r: pl.BlockSpec((r, width), lambda i: (0, i))
    images = lambda *dims: pl.BlockSpec((group, *dims), lambda i: (i,) + (0,) * len(dims))
    output, gh, gml, dots, ghl, gmleft, send = pl.pallas_call(
        functools.partial(feed_kernel, n, group),
        grid=(steps,),
        in_specs=[
            cols(d), cols(d), images(16, MAIN), images(MAIN, d), left, LIVE, whole(d), whole(d), whole(d),
            whole(rows, d), whole(rows, d), once(d, units), whole(1, units), once(units, d), once(d, d),
        ],
        out_specs=[
            images(seq, d), cols(d), cols(d), images(pairs, 16, MAIN), whole(rows, d), whole(rows, d),
            once(sums.streams, 4, rows_quarter, 128),
        ],
        out_shape=[
            shape(bf16, n, seq, d), shape(f32, d, total), shape(bf16, d, total),
            shape(f32, n, pairs, 16, MAIN), shape(f32, rows, d), shape(f32, rows, d),
            shape(bf16, sums.streams, 4, rows_quarter, 128),
        ],
        scratch_shapes=[
            pltpu.VMEM((units, d + 128), bf16), pltpu.VMEM((d, units), bf16),
            pltpu.VMEM((d + 128, width), bf16), pltpu.VMEM((d + 128, width), bf16),
            pltpu.VMEM((units, width), bf16), pltpu.VMEM((units, width), bf16),
            pltpu.VMEM((d, width), bf16), pltpu.VMEM((3, d, 128), f32), pltpu.VMEM((2, d, 128), f32),
            pltpu.VMEM((rows, d), f32), pltpu.VMEM((rows, d), f32),
            pltpu.VMEM((d + 16, units), f32), pltpu.VMEM((d, units), f32), pltpu.VMEM((d + 16, d), f32),
            pltpu.VMEM((8, d), f32),
        ],
        compiler_params=params(),
        name="feed",
    )(
        hid, att, invs, cotangent, cotangent, image_mask, second_gain, second_shift, down_bias, hidl, attl,
        up_all, up_bias_all, down_all, merge_weight,
    )

    group = next(g for g in (7, 2, 1) if n % g == 0)
    steps = n // group
    width = group * MAIN
    last = pairs * steps
    chunk = -(-3 * (d + 32) // (8 * 16)) * 16
    spread = Spread(mesh_sizes, pairs, chunk)
    plan = [(min(phase, last + steps), "sums", phase, s) for phase in range(1, 8) for s in range(sums.streams)]
    for p in range(pairs):
        plan += [((p + 1) * steps + phase, "spread", phase, p) for phase in range(1, 6)]
    plan.sort(key=lambda item: item[0])
    early = lambda i: i - (i // last) * (i - (last - 1))
    late = lambda i: (i // last) * (i - last)
    by_pair = lambda r: pl.BlockSpec((r, width), lambda i: (early(i) // steps, early(i) % steps))
    of_pair = lambda *dims: pl.BlockSpec(
        (group, 1, *dims), lambda i: (early(i) % steps, early(i) // steps) + (0,) * len(dims)
    )
    pair_lanes = lambda w: pl.BlockSpec((rows, w), lambda i: (0, early(i) // steps))
    late_images = lambda *dims: pl.BlockSpec((group, *dims), lambda i: (late(i),) + (0,) * len(dims))
    input_grad, attend_grad, up_grad, down_grad, merge_grad, row_grads = pl.pallas_call(
        functools.partial(back_kernel, n, group, steps, sums, spread, plan),
        grid=(last + steps,),
        in_specs=[
            by_pair(3 * 128),
            pl.BlockSpec((group, 2, MAIN, MAIN), lambda i: (early(i) % steps, early(i) // steps, 0, 0)),
            of_pair(16, MAIN), of_pair(16, MAIN), of_pair(16, 128), by_pair(128), of_pair(16, MAIN),
            pl.BlockSpec((d + 16, width), lambda i: (0, early(i) % steps)),
            whole(rows, d), pair_lanes(384), pair_lanes(128), pair_lanes(128), once(d, packed),
            once(sums.streams, 4, rows_quarter, 128),
            late_images(MAIN, d), left, pl.BlockSpec((d, width), lambda i: (0, late(i))),
            whole(rows, d), whole(d), whole(d),
        ],
        out_specs=[
            late_images(seq, d), once(d, packed), once(d, d), once(d, d), once(d, d), whole(48, d),
        ],
        out_shape=[
            shape(bf16, n, seq, d), shape(f32, d, packed), shape(f32, d, d), shape(f32, d, d),
            shape(f32, d, d), shape(f32, 48, d),
        ],
        scratch_shapes=[
            pltpu.VMEM((steps, packed, width), bf16), pltpu.VMEM((d + 16, 384), f32),
            pltpu.VMEM((pairs, rows, 384), f32), pltpu.VMEM((d, packed), bf16), pltpu.VMEM((d, 128), f32),
            pltpu.VMEM((rows, d), f32), pltpu.VMEM((rows, d), f32), *sums.scratch(), *spread.scratch(),
        ],
        compiler_params=params(collective_id=0, has_side_effects=True),
        name="back",
    )(
        qkv, probs, edges, lp, lself, gml, dots, fi, fil, qkvl, attl, gmleft, attend_weight, send,
        tokens, tokens, gh, ghl, first_gain, first_shift,
    )
    return (
        output,
        input_grad,
        row_grads[24],
        row_grads[25],
        attend_grad,
        jnp.stack([row_grads[32], row_grads[40]]),
        merge_grad,
        row_grads[16],
        row_grads[0],
        row_grads[1],
        up_grad,
        row_grads[8],
        down_grad,
        row_grads[2],
    )


def solution(mesh):
    split = ("dp", "tensor")
    in_specs = (
        P(split, None, None), P(split), P(split, None), P(), P(), P(), P(), P(), P(), P(), P(),
        P(None, "tensor"), P("tensor"), P("tensor", None), P(), P(split, None, None),
    )
    out_specs = (
        P(split, None, None), P(split, None, None), P(), P(), P(), P(), P(), P(), P(), P(),
        P(None, "tensor"), P("tensor"), P("tensor", None), P(),
    )
    sizes = (mesh.shape["dp"], mesh.shape["tensor"])
    return jax.shard_map(functools.partial(shards, sizes), mesh=mesh, in_specs=in_specs, out_specs=out_specs, check_vma=False)
```

```python
import functools

import jax
import jax.numpy as jnp
from jax import lax
from jax.experimental import pallas as pl
from jax.experimental.pallas import tpu as pltpu
from jax.sharding import PartitionSpec as P

HEADS = 6
HEAD = 64
MAIN = 256
EPS = 1e-06
MASKED = -1e30
f32, bf16 = jnp.float32, jnp.bfloat16

NN = ((1,), (0,))
NT = ((1,), (1,))
TN = ((0,), (0,))


def dot(left, right, dims=NN):
    return lax.dot_general(left, right, (dims, ((), ())), preferred_element_type=f32)


def rows_where(index, value, rows, dtype):
    columns = value.shape[-1]
    at = lax.broadcasted_iota(jnp.int32, (rows, columns), 0)
    return jnp.where(at == index, value, 0.0).astype(dtype)


def wide(column, width):
    return jnp.concatenate([column] * (width // 128), axis=1)


def as_column(row):
    return jnp.broadcast_to(row, (128, row.shape[1])).T


def norm_columns(values):
    center = values - jnp.mean(values, axis=0, keepdims=True)
    scale = lax.rsqrt(jnp.mean(center * center, axis=0, keepdims=True) + EPS)
    return center * scale, scale


def norm_rows(values):
    center = values - jnp.mean(values, axis=1, keepdims=True)
    scale = lax.rsqrt(jnp.mean(center * center, axis=1, keepdims=True) + EPS)
    return center * scale, scale


def norm_back(grad, normed, scale, axis):
    mean_grad = jnp.mean(grad, axis=axis, keepdims=True)
    mean_both = jnp.mean(grad * normed, axis=axis, keepdims=True)
    return scale * (grad - mean_grad - normed * mean_both)


def gelu_both(pre):
    curve = 0.5 + 0.5 * lax.erf(pre * 0.7071067811865476)
    bell = 0.3989422804014327 * jnp.exp(-0.5 * pre * pre)
    return pre * curve, curve + pre * bell


def head_rows(rows, features):
    at = lax.broadcasted_iota(jnp.int32, (rows, features), 0)
    head = lax.broadcasted_iota(jnp.int32, (rows, features), 1) // HEAD
    return jnp.where(at == head, 1.0, 0.0)


def lane_live(live_ref, first, count):
    flags = [
        jnp.full((1, MAIN), live_ref[first + g].astype(f32)) for g in range(count)
    ]
    return jnp.concatenate(flags, axis=1)


def row_live(live_ref, count, rows):
    at = lax.broadcasted_iota(jnp.int32, (rows, 1), 0)
    flags = jnp.zeros((rows, 1), f32)
    for image in range(count):
        flags = jnp.where(at == image, live_ref[image].astype(f32), flags)
    return flags


def take_left(left_ref, to_ref, count):
    to_ref[...] = jnp.zeros_like(to_ref)
    for image in range(count):
        to_ref[image : image + 1, :] = left_ref[image].astype(f32)[0:1, :]


def flip(place, bits):
    if bits & 1:
        place = place + 1 - 2 * lax.rem(place, 2)
    if bits & 2:
        place = place + 2 - 4 * (place // 2)
    return place


def remote(src, dst, sends, recvs, index, peer):
    return pltpu.make_async_remote_copy(
        src_ref=src, dst_ref=dst, send_sem=sends.at[index], recv_sem=recvs.at[index],
        device_id=peer, device_id_type=pl.DeviceIdType.MESH,
    )


def greet(peers):
    barrier = pltpu.get_barrier_semaphore()
    for peer in peers:
        pl.semaphore_signal(barrier, inc=1, device_id=peer, device_id_type=pl.DeviceIdType.MESH)


def meet(peers):
    pl.semaphore_wait(pltpu.get_barrier_semaphore(), len(peers))


class Quarter:
    def __init__(self, dp, streams, rows):
        self.far = dp // 2
        self.streams, self.half = streams, rows // 2
        self.chunk = -(-self.half // (16 * self.far)) * 16
        self.padded = self.chunk * self.far
        self.copies = 3 + 2 * (self.far - 1)

    def scratch(self):
        s = self.streams
        vm = lambda *dims: pltpu.VMEM((s, *dims, 128), bf16)
        return [
            vm(2 * self.half), vm(2 * self.half), vm(self.half), vm(self.padded),
            vm(max(self.far - 1, 1), self.chunk), vm(2, self.padded),
            pltpu.SemaphoreType.DMA((s, self.copies)), pltpu.SemaphoreType.DMA((s, self.copies)),
        ]

    def bind(self, mine, beside, refs):
        self.mine, self.beside = mine, beside
        self.r1, self.work, self.r2, self.cur, self.r3, self.fin, self.sends, self.recvs = refs
        self.me_dp, self.me_t = lax.axis_index("dp"), lax.axis_index("tensor")
        self.x, self.z = lax.rem(self.me_dp, 2), self.me_dp // 2

    def line(self, j):
        return (lax.rem(self.z + j, self.far) * 2 + self.x, self.me_t)

    def copies_of(self, phase, s):
        across = (self.z * 2 + 1 - self.x, self.me_t)
        cp = lambda index, src, dst, peer: remote(src, dst, self.sends, self.recvs, (s, index), peer)
        if phase == 1:
            return [cp(0, self.beside.at[s], self.r1.at[s], (self.me_dp, flip(self.me_t, 1)))]
        if phase == 2:
            other = pl.ds(pl.multiple_of((1 - self.x) * self.half, 16), self.half)
            return [cp(1, self.work.at[s, other], self.r2.at[s], across)]
        found = []
        if phase == 3:
            for j in range(1, self.far):
                place = lax.rem(self.z + j, self.far)
                src = self.cur.at[s, pl.ds(pl.multiple_of(place * self.chunk, 16), self.chunk)]
                found.append(cp(1 + j, src, self.r3.at[s, j - 1], self.line(j)))
        if phase == 4:
            ref = self.fin.at[s, self.x, pl.ds(pl.multiple_of(self.z * self.chunk, 16), self.chunk)]
            for j in range(1, self.far):
                found.append(cp(self.far + j, ref, ref, self.line(j)))
        if phase == 5:
            ref = self.fin.at[s, self.x, pl.ds(0, self.half)]
            found.append(cp(2 * self.far, ref, ref, across))
        return found

    def start(self, phase, s):
        for copy in self.copies_of(phase, s):
            copy.start()

    def advance(self, phase, s):
        for copy in self.copies_of(phase, s):
            copy.wait()
        if phase == 1:
            self.work[s] = (self.mine[s].astype(f32) + self.r1[s].astype(f32)).astype(bf16)
        if phase == 2:
            kept = self.work[s, pl.ds(pl.multiple_of(self.x * self.half, 16), self.half)]
            self.cur[s, : self.half] = (kept.astype(f32) + self.r2[s].astype(f32)).astype(bf16)
            if self.padded > self.half:
                self.cur[s, self.half :] = jnp.zeros((self.padded - self.half, 128), bf16)
        if phase == 3:
            mine = pl.ds(pl.multiple_of(self.z * self.chunk, 16), self.chunk)
            total = self.cur[s, mine].astype(f32)
            for j in range(self.far - 1):
                total = total + self.r3[s, j].astype(f32)
            self.fin[s, self.x, mine] = total.astype(bf16)
        if phase < 5:
            self.start(phase + 1, s)


class Spread:
    def __init__(self, mesh_sizes, streams, chunk):
        self.dp, self.tensor = mesh_sizes
        self.far = self.dp // 2
        self.streams, self.chunk = streams, chunk
        self.copies = 1 + 3 + (self.far - 1) + 3 + 1

    def scratch(self):
        s, c = self.streams, self.chunk
        vm = lambda *dims: pltpu.VMEM((s, *dims, 128), bf16)
        return [
            vm(8 * c), vm(4 * c), vm(4 * c), vm(3, c), vm(self.far, c), vm(8 * c),
            pltpu.SemaphoreType.DMA((s, self.copies)), pltpu.SemaphoreType.DMA((s, self.copies)),
        ]

    def bind(self, refs):
        self.send, self.r1, self.work, self.r2, self.r3, self.out, self.ss, self.rs = refs
        self.me_dp, self.me_t = lax.axis_index("dp"), lax.axis_index("tensor")
        self.x, self.z = lax.rem(self.me_dp, 2), self.me_dp // 2
        self.c, self.y = lax.rem(self.me_t, 2), self.me_t // 2
        self.place = 2 * self.y + self.x

    def plane(self, j):
        x = 1 - self.x if j & 1 else self.x
        y = 1 - self.y if j & 2 else self.y
        return (self.z * 2 + x, 2 * y + self.c), 2 * y + x

    def core(self):
        return (self.me_dp, 2 * self.y + 1 - self.c)

    def line(self, j):
        return (lax.rem(self.z + j, self.far) * 2 + self.x, self.me_t)

    def rows(self, first, count):
        return pl.ds(pl.multiple_of(first * self.chunk, 16), count * self.chunk)

    def copies_of(self, phase, s):
        def cp(index, src, dst, peer):
            return pltpu.make_async_remote_copy(
                src_ref=src, dst_ref=dst, send_sem=self.ss.at[s, index], recv_sem=self.rs.at[s, index],
                device_id=peer, device_id_type=pl.DeviceIdType.MESH,
            )

        if phase == 1:
            return [cp(0, self.send.at[s, self.rows(4 * (1 - self.c), 4)], self.r1.at[s], self.core())]
        found = []
        if phase == 2:
            for j in (1, 2, 3):
                peer, place = self.plane(j)
                found.append(cp(j, self.work.at[s, self.rows(place, 1)], self.r2.at[s, j - 1], peer))
        if phase == 3:
            for j in range(1, self.far):
                ref = self.r3.at[s, self.z]
                found.append(cp(3 + j, ref, ref, self.line(j)))
        mine = self.out.at[s, self.rows(4 * self.c + self.place, 1)]
        if phase == 4:
            for j in (1, 2, 3):
                found.append(cp(2 + self.far + j, mine, mine, self.plane(j)[0]))
        if phase == 5:
            ref = self.out.at[s, self.rows(4 * self.c, 4)]
            found.append(cp(6 + self.far, ref, ref, self.core()))
        return found

    def start(self, phase, s):
        for copy in self.copies_of(phase, s):
            copy.start()

    def advance(self, phase, s):
        for copy in self.copies_of(phase, s):
            copy.wait()
        if phase == 1:
            half = self.send[s, self.rows(4 * self.c, 4)].astype(f32)
            self.work[s] = (half + self.r1[s].astype(f32)).astype(bf16)
        if phase == 2:
            total = self.work[s, self.rows(self.place, 1)].astype(f32)
            for j in range(3):
                total = total + self.r2[s, j].astype(f32)
            self.r3[s, self.z] = total.astype(bf16)
        if phase == 3:
            total = self.r3[s, 0].astype(f32)
            for j in range(1, self.far):
                total = total + self.r3[s, j].astype(f32)
            self.out[s, self.rows(4 * self.c + self.place, 1)] = total.astype(bf16)
        if phase < 5:
            self.start(phase + 1, s)


def row_of(ref):
    return ref[...].astype(f32).reshape(1, ref.shape[0])


def parts_of(at, pair):
    return slice(pair * 384 + at * 128, pair * 384 + (at + 1) * 128)


def attend_kernel(
    count, group, steps,
    tok0, tok, left, pmask, live, gain, shift, abias, mbias, aw, mw, up, ubias, down,
    fi_out, qkv_out, probs_out, edge_out, inv_out, lp_out, lself_out, att_out, hid_out,
    fil_out, qkvl_out, attl_out, hidl_out, wall, ball,
    awt, mwt, fia, atta, cols, edges, qkv2, toks, xl, qkvl, attl, brow, sends, recvs, own,
):
    step = pl.program_id(0)
    me_dp, me_t = lax.axis_index("dp"), lax.axis_index("tensor")
    beside, across = (me_dp, flip(me_t, 1)), (me_dp, flip(me_t, 2))

    def places(owner):
        return (wall.at[owner, 0], wall.at[owner, 1], ball.at[owner])

    def first_copies(peer, first):
        return [
            remote(src, dst, sends, recvs, first + k, peer)
            for k, (src, dst) in enumerate(zip((up, down, brow), places(me_t)))
        ]

    def second_copies():
        return [
            remote(ref, ref, sends, recvs, 6 + k, beside) for k, ref in enumerate(places(flip(me_t, 2)))
        ]

    def own_copies():
        return [
            pltpu.make_async_copy(src, dst, own.at[k])
            for k, (src, dst) in enumerate(zip((up, down, brow), places(me_t)))
        ]

    @pl.when(step == 0)
    def _():
        greet((beside, across))
        brow[...] = rows_where(0, row_of(ubias), 16, bf16)
        meet((beside, across))
        for copy in first_copies(across, 3) + first_copies(beside, 0) + own_copies():
            copy.start()

    @pl.when(step == steps - 2)
    def _():
        for copy in first_copies(across, 3):
            copy.wait()
        for copy in second_copies():
            copy.start()

    features = aw.shape[0]
    packed = aw.shape[1]
    rows = xl.shape[0]
    width = group * MAIN
    pairs = HEADS // 2
    heads = head_rows(rows, features)

    def first_norm(block):
        tokens = jnp.concatenate([block[g].T for g in range(group)], axis=1)
        normed, _ = norm_columns(tokens.astype(f32))
        return tokens, (normed * wide(cols[0], width) + wide(cols[1], width)).astype(bf16)

    def project(slot, part):
        span = slice(part * features, (part + 1) * features)
        qkv2[slot, span, :] = dot(awt[span, :], fia[...]).astype(bf16)

    @pl.when(step == 0)
    def _():
        ab = abias[...].astype(f32)
        for pair in range(pairs):
            for at in range(3):
                cut = slice(at * features + pair * 128, at * features + (pair + 1) * 128)
                to = parts_of(at, pair)
                scale = HEAD**-0.5 if at == 0 else 1.0
                awt[to, :features] = (aw[:, cut].astype(f32).T * scale).astype(bf16)
                if at == 1:
                    bias = jnp.zeros((1, 128), f32)
                else:
                    bias = ab[at // 2 : at // 2 + 1, pair * 128 : (pair + 1) * 128] * scale
                awt[to, features:] = rows_where(0, bias, 128, f32).T.astype(bf16)
        mwt[:, :features] = mw[...].astype(f32).T.astype(bf16)
        mwt[:, features:] = rows_where(0, row_of(mbias), 128, f32).T.astype(bf16)
        ones = rows_where(0, jnp.ones((1, fia.shape[1]), f32), 128, bf16)
        fia[features:, :] = ones
        atta[features:, :] = ones
        cols[0] = as_column(row_of(gain))
        cols[1] = as_column(row_of(shift))
        edges[...] = jnp.zeros_like(edges)
        take_left(left, xl, count)
        normed, _ = norm_rows(xl[...])
        fil = (normed * row_of(gain) + row_of(shift)).astype(bf16)
        fil_out[...] = fil.astype(f32)
        plain = dot(fil, aw[...])
        for pair in range(pairs):
            for at in range(3):
                cut = slice(at * features + pair * 128, at * features + (pair + 1) * 128)
                value = plain[:, cut]
                if at != 1:
                    value = value + ab[at // 2 : at // 2 + 1, pair * 128 : (pair + 1) * 128]
                value = value.astype(bf16).astype(f32)
                qkvl[:, parts_of(at, pair)] = value * (HEAD**-0.5) if at == 0 else value
        qkvl_out[...] = qkvl[...]
        attl[...] = jnp.zeros_like(attl)
        tokens, fi = first_norm(tok0)
        toks[0] = tokens
        fia[:features, :] = fi
        for part in range(3):
            project(0, part)

    def merge_branch():
        return dot(mwt[...], atta[...])

    def hidden_of(branch, index):
        tokens = toks[lax.rem(index, 3)].astype(f32)
        return tokens + lane_live(live, index * group, group) * branch

    @pl.when(step < steps)
    def _():
        now, later = lax.rem(step, 2), lax.rem(step + 1, 2)
        one_row = rows_where(0, jnp.ones((1, MAIN), f32), 16, bf16)
        held = {}
        units = [(g, h) for g in range(group) for h in range(HEADS)]

        def lanes_of(g):
            return slice(g * MAIN, (g + 1) * MAIN)

        def part(at, g, h):
            low = (h // 2) * 384 + at * 128 + (h % 2) * HEAD
            return qkv2[now, low : low + HEAD, lanes_of(g)]

        def all_heads(at, g):
            return jnp.concatenate(
                [qkv2[now, parts_of(at, pair), lanes_of(g)] for pair in range(pairs)], axis=0
            )

        def begin(g):
            image = step * group + g
            row = qkvl[pl.ds(image, 1), :]
            ql, kl, vl = (
                jnp.concatenate([row[:, parts_of(at, pair)] for pair in range(pairs)], axis=1)
                for at in range(3)
            )
            key_bias = jnp.where(pmask[pl.ds(image, 1), :] == 1, 0.0, MASKED)
            moved = pltpu.roll(key_bias, 1, axis=1)
            at = lax.broadcasted_iota(jnp.int32, moved.shape, 1)
            main_bias = jnp.where(at == 0, 0.0, moved)
            left_bias = moved[:, 0:1]
            held["bias", g] = rows_where(0, main_bias, 16, bf16)
            held["vl", g] = vl
            held["slk", g] = dot((heads * kl).astype(bf16), all_heads(0, g)) + left_bias
            held["sl", g] = dot((heads * ql).astype(bf16), all_heads(1, g)) + main_bias
            held["self", g] = jnp.sum(heads * (ql * kl), axis=1, keepdims=True) + left_bias

        def left_query(g):
            sl, self_score = held.pop(("sl", g)), held.pop(("self", g))
            peak = jnp.maximum(jnp.max(sl, axis=1, keepdims=True), self_score)
            raised = jnp.exp(sl - peak)
            raised_self = jnp.exp(self_score - peak)
            inv = 1.0 / (jnp.sum(raised, axis=1, keepdims=True) + raised_self)
            lp = raised * inv
            lself = raised_self * inv
            lp_out[g] = lp
            lself_out[g] = jnp.broadcast_to(lself, (rows, 128))
            mixed = dot(lp.astype(bf16), all_heads(2, g), NT) + lself * held["vl", g]
            image = step * group + g
            attl[pl.ds(image, 1), :] = (
                jnp.sum(mixed * heads, axis=0, keepdims=True).astype(bf16).astype(f32)
            )

        def scores(g, h):
            held["s", g, h] = dot(
                jnp.concatenate([part(1, g, h), held["bias", g]], axis=0),
                jnp.concatenate([part(0, g, h), one_row], axis=0),
                TN,
            )

        def soften(g, h):
            value = held.pop(("s", g, h))
            slk = held["slk", g][h : h + 1, :]
            peak = jnp.maximum(jnp.max(value, axis=0, keepdims=True), slk)
            raised = jnp.exp(value - peak).astype(bf16)
            probs_out[g, h] = raised
            held["e", g, h] = raised
            edge = jnp.exp(slk - peak)
            held["edge", g, h] = edge
            edges[g, h : h + 1, :] = edge

        def mix(g, h):
            held["o", g, h] = dot(
                jnp.concatenate([part(2, g, h), one_row], axis=0), held.pop(("e", g, h))
            )

        def add_left(g):
            edge_out[g] = edges[g]
            held["add", g] = dot((heads * held["vl", g]).astype(bf16), edges[g].astype(bf16), TN)

        def finish(g, h):
            out = held.pop(("o", g, h))
            span = slice(h * HEAD, (h + 1) * HEAD)
            inv = 1.0 / (out[HEAD : HEAD + 1, :] + held["edge", g, h])
            inv_out[g, h : h + 1, :] = inv
            mixed = ((out[:HEAD, :] + held["add", g][span]) * inv).astype(bf16)
            atta[span, lanes_of(g)] = mixed
            att_out[span, lanes_of(g)] = mixed

        count_units = len(units)
        for t in range(-2, count_units + 4):
            if t + 2 == 0:
                for g in range(group):
                    begin(g)
                held["branch"] = merge_branch()
            if 0 <= t + 2 < count_units:
                scores(*units[t + 2])
            if t == -1:
                hid_out[...] = hidden_of(held.pop("branch"), step - 1 + 3 * (1 - jnp.minimum(step, 1)))
                qkv_out[...] = qkv2[now]
                fi_out[:features, :] = fia[:features, :]
                fi_out[features:, :] = fia[features : features + 16, :]
                held["next"] = first_norm(tok)
            if t == 1:
                tokens, fi = held.pop("next")
                toks[lax.rem(step + 1, 3)] = tokens
                fia[:features, :] = fi
            if t in (2, 4, 6):
                project(later, (t - 2) // 2)
            if 0 <= t < count_units:
                soften(*units[t])
            if 0 <= t - 2 < count_units:
                mix(*units[t - 2])
            for g in range(group):
                if t == HEADS * g + 3:
                    left_query(g)
                if t == HEADS * (g + 1):
                    add_left(g)
                if t == HEADS * (g + 1) + 3:
                    for h in range(HEADS):
                        finish(g, h)

    @pl.when(step == steps)
    def _():
        hid_out[...] = hidden_of(merge_branch(), step - 1)
        attl_out[...] = attl[...]
        branch = dot(attl[...].astype(bf16), mw[...]) + row_of(mbias)
        hidl_out[...] = xl[...] + row_live(live, count, rows) * branch
        for copy in first_copies(beside, 0) + second_copies() + own_copies():
            copy.wait()


def feed_kernel(
    count, group, steps,
    hid, att, inv, cot, cleft, live, gain, shift, dbias, hidl, attl, wall, ball, mw,
    out, gh_out, gml_out, dots_out, ghl_out, gmleft_out, mine, beside, shared,
    upt, dnt, sia, atta, act, gpre, gb, cols, gsum, xl, outl, sil, gbl, actl, gprel,
    outp, gradp, up_acc, down_acc, merge_acc, sums, biases, kept, away, r1, across, r2, sends, recvs,
):
    step = pl.program_id(0)
    at_step = lax.rem(step, steps)
    second = step // steps
    features = mw.shape[0]
    rows = xl.shape[0]
    width = group * MAIN
    quarters = wall.shape[0]
    me_dp, me_t = lax.axis_index("dp"), lax.axis_index("tensor")
    core, chip = (me_dp, flip(me_t, 1)), (me_dp, flip(me_t, 2))
    first_of = (1 - second) * flip(me_t, 2) + second * me_t
    now = (first_of, flip(first_of, 1))

    def to_core():
        return remote(away, r1, sends, recvs, 0, core)

    def to_chip():
        return remote(across, r2, sends, recvs, 1, chip)

    @pl.when(step == 0)
    def _():
        greet((core, chip))
        gain_row, shift_row, dbias_row = row_of(gain), row_of(shift), row_of(dbias)
        for q in range(quarters):
            upt[q, :, :features] = wall[q, 0].astype(f32).T.astype(bf16)
            upt[q, :, features:] = rows_where(0, ball[q, 0:1, :].astype(f32), 128, f32).T.astype(bf16)
            dnt[q] = wall[q, 1].astype(f32).T.astype(bf16)
        ones = rows_where(0, jnp.ones((1, width), f32), 128, bf16)
        for k in range(steps):
            sia[k, features:, :] = ones
        atta[features:, :] = ones
        cols[0] = as_column(gain_row)
        cols[1] = as_column(shift_row)
        cols[2] = as_column(dbias_row)
        gsum[...] = jnp.zeros_like(gsum)
        biases[...] = jnp.zeros_like(biases)
        take_left(cleft, xl, count)
        alive = row_live(live, count, rows)
        normed, scale = norm_rows(hidl[...])
        si = (normed * gain_row + shift_row).astype(bf16)
        grad_branch = (alive * xl[...]).astype(bf16)
        total = hidl[...] + alive * dbias_row
        grad_second = jnp.zeros_like(total)
        for q in range(quarters):
            pre = dot(si, wall[q, 0]) + ball[q, 0:1, :].astype(f32)
            value, slope = gelu_both(pre)
            value = value.astype(bf16)
            actl[q] = value
            total = total + alive * dot(value, wall[q, 1])
            grad_pre = (dot(grad_branch, wall[q, 1], NT) * slope).astype(bf16)
            gprel[q] = grad_pre
            grad_second = grad_second + dot(grad_pre, wall[q, 0], NT)
        outl[...] = total
        grad_hidden = xl[...] + norm_back(grad_second * gain_row, normed, scale, 1)
        ghl_out[...] = grad_hidden
        grad_attn = (alive * grad_hidden).astype(bf16)
        gmleft_out[...] = dot(grad_attn, mw[...], NT).astype(bf16).astype(f32)
        one = jnp.ones((rows, 16), f32)
        sil[...] = jnp.concatenate([si.astype(f32), one], axis=1).astype(bf16)
        gbl[...] = grad_branch
        merge_acc[...] = dot(jnp.concatenate([attl[...], one], axis=1).astype(bf16), grad_attn, TN)
        sums[...] = jnp.zeros_like(sums)
        sums[0:1, :] = jnp.sum(grad_second * normed, axis=0, keepdims=True)
        sums[1:2, :] = jnp.sum(grad_second, axis=0, keepdims=True)
        sums[2:3, :] = jnp.sum(grad_branch.astype(f32), axis=0, keepdims=True)
        meet((core, chip))

    @pl.when(at_step == 0)
    def _():
        for c, q in enumerate(now):
            lanes = slice(c * features, (c + 1) * features)
            up_acc[:, lanes] = dot(sil[...], gprel[q], TN)
            down_acc[:, lanes] = dot(gbl[...], actl[q], TN)

    def rounded(ref, lanes, at):
        lanes = slice(lanes + at * 128, lanes + (at + 1) * 128)
        return jnp.concatenate([up_acc[:features, lanes], down_acc[:, lanes]], axis=0)

    @pl.when(step == steps + 1)
    def _():
        to_core().wait()
        for at in range(kept.shape[0]):
            across[at] = (kept[at] + r1[at].astype(f32)).astype(bf16)
        to_chip().start()

    pres, grads = {}, {}

    def into(c):
        pres[c] = dot(upt[now[c]], sia[at_step])
        grads[c] = dot(wall[now[c], 1], gb[at_step])

    def through(c):
        span = slice(c * features, (c + 1) * features)
        value, slope = gelu_both(pres.pop(c))
        act[span, :] = value.astype(bf16)
        gpre[span, :] = (grads.pop(c) * slope).astype(bf16)

    def both_of(ref, *more):
        return jnp.concatenate([ref[(q, *more)] for q in now], axis=1)

    def up_product():
        up_acc[...] += dot(sia[at_step, : up_acc.shape[0], :], gpre[...], NT)

    def down_product():
        down_acc[...] += dot(gb[at_step], act[...], NT)

    @pl.when(second == 0)
    def _():
        hidden = hid[...]
        normed, _ = norm_columns(hidden)
        sia[at_step, :features, :] = (normed * wide(cols[0], width) + wide(cols[1], width)).astype(bf16)
        alive = lane_live(live, at_step * group, group)
        cotangent = jnp.concatenate([cot[g].T for g in range(group)], axis=1).astype(f32)
        gb[at_step] = (cotangent * alive).astype(bf16)
        for c in range(2):
            into(c)
        for c in range(2):
            through(c)
        gradp[at_step] = dot(both_of(wall, 0), gpre[...])
        outp[at_step] = dot(both_of(dnt), act[...])
        up_product()
        down_product()

    @pl.when(second == 1)
    def _():
        alive = lane_live(live, at_step * group, group)
        for c in range(2):
            into(c)
        hidden = hid[...]
        normed, scale = norm_columns(hidden)
        cotangent = jnp.concatenate([cot[g].T for g in range(group)], axis=1).astype(f32)
        for c in range(2):
            through(c)
        grad_second = gradp[at_step] + dot(both_of(wall, 0), gpre[...])
        reduced = outp[at_step] + dot(both_of(dnt), act[...])
        up_product()
        grad_hidden = cotangent + norm_back(grad_second * wide(cols[0], width), normed, scale, 0)
        gh_out[...] = grad_hidden
        grad_attn = (alive * grad_hidden).astype(bf16)
        grad_mixed = dot(mw[...], grad_attn)
        down_product()
        result = hidden + alive * (reduced + wide(cols[2], width))
        for g in range(group):
            image = at_step * group + g
            out[g, :MAIN, :] = result[:, g * MAIN : (g + 1) * MAIN].astype(bf16).T
            out[g, MAIN : MAIN + 1, :] = outl[pl.ds(image, 1), :].astype(bf16)
        both = grad_second * normed
        for at in range(0, width, 128):
            gsum[0] += both[:, at : at + 128]
            gsum[1] += grad_second[:, at : at + 128]
        sums[2:3, :] += dot(jnp.ones((16, width), bf16), gb[at_step], NT)[0:1, :]
        atta[:features, :] = att[...]
        merge_acc[...] += dot(atta[: merge_acc.shape[0], :], grad_attn, NT)
        grad_mixed = grad_mixed.astype(bf16).astype(f32)
        both = grad_mixed * att[...].astype(f32)
        dots_out[...] = jnp.zeros_like(dots_out)
        for g in range(group):
            lanes = slice(g * MAIN, (g + 1) * MAIN)
            for h in range(HEADS):
                span = slice(h * HEAD, (h + 1) * HEAD)
                row_inv = inv[g, h : h + 1, :]
                gml_out[span, lanes] = (grad_mixed[span, lanes] * row_inv).astype(bf16)
                row_dot = jnp.sum(both[span, lanes], axis=0, keepdims=True) * row_inv
                dots_out[g, h : h + 1, :] = row_dot

    @pl.when(at_step == steps - 1)
    def _():
        for c, q in enumerate(now):
            biases[pl.ds(q, 1), :] = up_acc[features : features + 1, c * features : (c + 1) * features]

    @pl.when(step == steps - 1)
    def _():
        for at in range(kept.shape[0]):
            kept[at] = rounded(up_acc, 0, at)
            away[at] = rounded(up_acc, features, at).astype(bf16)
        to_core().start()

    @pl.when(step == 2 * steps - 1)
    def _():
        sums[0:1, :] += jnp.sum(gsum[0].T, axis=0, keepdims=True)
        sums[1:2, :] += jnp.sum(gsum[1].T, axis=0, keepdims=True)
        ends = jnp.concatenate([sums[...], biases[...]], axis=0)
        merged = jnp.concatenate([merge_acc[:features, :], merge_acc[features : features + 16, :], ends], axis=0)
        for at in range(features // 128):
            block = merged.shape[0]
            shared[at * block : (at + 1) * block] = merged[:, at * 128 : (at + 1) * 128].astype(bf16)
        rest = shared.shape[0] - (features // 128) * merged.shape[0]
        if rest:
            shared[shared.shape[0] - rest :] = jnp.zeros((rest, 128), bf16)
        for at in range(kept.shape[0]):
            beside[at] = rounded(up_acc, features, at).astype(bf16)
        to_chip().wait()
        for at in range(kept.shape[0]):
            mine[at] = (rounded(up_acc, 0, at) + r2[at].astype(f32)).astype(bf16)


def back_kernel(
    count, group, steps, late_group, late_steps, quarter, spread, plan,
    qkv, probs, edge, lp, lself, gml, dots, fi, fil, qkvl, attl, gmleft, aw, mine, beside, shared,
    tok, left, gh, ghl, gain, shift,
    out, quarter_out, spread_out, bias_out,
    gpa, acc, gpl, gplt, awp, cols, xl, outl, fis, own, *comm,
):
    step = pl.program_id(0)
    features = aw.shape[0]
    rows = xl.shape[0]
    pairs = HEADS // 2
    last = pairs * steps
    pair = lax.rem(step // steps, pairs)
    at_group = lax.rem(step, steps)
    used = len(quarter.scratch())
    quarter.bind(mine, beside, comm[:used])
    spread.bind(comm[used:])
    engines = {"quarter": quarter, "spread": spread}
    at = lax.broadcasted_iota(jnp.int32, (rows, 128), 0)
    heads = jnp.where(at == lax.broadcasted_iota(jnp.int32, (rows, 128), 1) // HEAD, 1.0, 0.0)

    def fi_copy(k):
        width = group * MAIN
        return pltpu.make_async_copy(fi.at[:, pl.ds(k * width, width)], fis.at[k], own.at[k])

    @pl.when(step == 0)
    def _():
        peers = [
            (quarter.me_dp, flip(quarter.me_t, 1)), *(spread.plane(j)[0] for j in (1, 2, 3)),
            *(spread.line(j) for j in range(1, spread.far)),
        ]
        greet(peers)
        for k in range(steps):
            fi_copy(k).start()
        spread.send[0] = shared[...]
        for part in range(pairs):
            for k in range(3):
                cut = slice(k * features + part * 128, k * features + (part + 1) * 128)
                awp[:, parts_of(k, part)] = aw[:, cut]
        cols[...] = as_column(row_of(gain))
        gpl[...] = jnp.zeros_like(gpl)
        meet(peers)
        for s in range(quarter.streams):
            quarter.start(1, s)
        spread.start(1, 0)

    for slot, name, phase, s in plan:
        if slot < last + late_steps:
            pl.when(step == slot)(functools.partial(engines[name].advance, phase, s))

    @pl.when(step < last)
    def _():
        at16 = lax.broadcasted_iota(jnp.int32, (16, MAIN), 0)
        minus = jnp.where(at16 < 2, -1.0, 0.0).astype(bf16)
        ends_row = jnp.where(lax.broadcasted_iota(jnp.int32, (1, 16), 1) < 2, -1.0, 0.0)
        gp = gpa.at[at_group, pl.ds(pl.multiple_of(pair * 384, 128), 384)]
        held = {}
        units = [(g, r) for g in range(group) for r in range(2)]

        @pl.when(at_group == 0)
        def _():
            acc[...] = jnp.zeros_like(acc)
            gplt[...] = jnp.zeros_like(gplt)

        def lanes_of(g):
            return slice(g * MAIN, (g + 1) * MAIN)

        def part(at, r, g):
            return qkv[at * 128 + r * HEAD : at * 128 + (r + 1) * HEAD, lanes_of(g)]

        def lower(value):
            return value.astype(bf16).astype(f32)

        def prepare(g):
            image = at_group * group + g
            row = qkvl[pl.ds(image, 1), :]
            ql, kl, vl = (row[:, at * 128 : (at + 1) * 128] for at in range(3))
            gm_row = gmleft[pl.ds(image, 1), :]
            row_dot = jnp.sum(heads * (gm_row * attl[pl.ds(image, 1), :]), axis=1, keepdims=True)
            prob = jnp.sum(heads * (gm_row * vl), axis=1, keepdims=True)
            held["cols", g] = tuple(as_column(v) for v in (ql, kl, gm_row))
            held["left", g] = (vl, row_dot, prob - row_dot)

        def change(g, r):
            row_dot = dots[g, pl.ds(2 * pair + r, 1), :]
            high = row_dot.astype(bf16).astype(f32)
            rest = jnp.where(at16 == 0, high, jnp.where(at16 == 1, row_dot - high, 0.0)).astype(bf16)
            values = jnp.concatenate([part(2, r, g), minus], axis=0).T
            vl = held["left", g][0][:, r * HEAD : (r + 1) * HEAD]
            last_row = rows_where(0, jnp.concatenate([vl, ends_row], axis=1), 16, bf16)
            held["z", g, r] = dot(
                jnp.concatenate([values, last_row], axis=0),
                jnp.concatenate([gml[r * HEAD : (r + 1) * HEAD, lanes_of(g)], rest], axis=0),
            )

        def left_unit(g, r, edge_change):
            image = at_group * group + g
            span = slice(r * HEAD, (r + 1) * HEAD)
            head = pl.ds(2 * pair + r, 1)
            colq, colk, colg = (wide(v[span], MAIN) for v in held["cols", g])
            _, row_dot, self_change = held["left", g]
            row_dot, self_change = row_dot[r : r + 1, :], self_change[r : r + 1, :]
            edge_row, lp_row, self_prob = edge[g, head, :], lp[g, head, :], lself[g, head, 0:1]
            edge_grad = lower(edge_row * edge_change)
            left_change = jnp.sum(colg * part(2, r, g).astype(f32), axis=0, keepdims=True) - row_dot
            left_grad = lower(lp_row * left_change)
            self_grad = lower(self_prob * self_change)
            held["add", g, r] = (colk * edge_grad, colq * left_grad, colg * lower(lp_row))
            grad_q = jnp.sum(part(1, r, g).astype(f32) * left_grad, axis=1, keepdims=True)
            grad_k = jnp.sum(part(0, r, g).astype(f32) * edge_grad, axis=1, keepdims=True)
            grad_v = jnp.sum(
                gml[span, lanes_of(g)].astype(f32) * lower(edge_row), axis=1, keepdims=True
            )
            values = (
                (grad_q + self_grad * colk[:, 0:1]) * HEAD**-0.5,
                grad_k + self_grad * colq[:, 0:1],
                grad_v + lower(self_prob) * colg[:, 0:1],
            )
            at = lax.broadcasted_iota(jnp.int32, (HEAD, 128), 1)
            for k, value in enumerate(values):
                to = slice(k * 128 + r * HEAD, k * 128 + (r + 1) * HEAD)
                gplt[to, :] = jnp.where(at == image, lower(value), gplt[to, :])

        def scores(g, r):
            raised = probs[g, r]
            value = held.pop(("z", g, r))
            held["ds", g, r] = (raised.astype(f32) * value[:MAIN]).astype(bf16)
            left_unit(g, r, value[MAIN : MAIN + 1])
            held["v", g, r] = dot(gml[r * HEAD : (r + 1) * HEAD, lanes_of(g)], raised, NT)

        def grads(g, r):
            ds = held.pop(("ds", g, r))
            held["q", g, r] = dot(part(1, r, g), ds)
            held["k", g, r] = dot(part(0, r, g), ds, NT)

        def store(g, r):
            span = slice(r * HEAD, (r + 1) * HEAD)
            add_q, add_k, add_v = held.pop(("add", g, r))
            values = (
                (held.pop(("q", g, r)) + add_q) * HEAD**-0.5,
                held.pop(("k", g, r)) + add_k,
                held.pop(("v", g, r)) + add_v,
            )
            for at, value in enumerate(values):
                gp[at * 128 + r * HEAD : at * 128 + (r + 1) * HEAD, lanes_of(g)] = value.astype(bf16)

        number = len(units)
        for t in range(-4, number + 4):
            for g in range(group):
                if t == 2 * g - 4:
                    prepare(g)
            if 0 <= t + 2 < number:
                change(*units[t + 2])
            if 0 <= t < number:
                scores(*units[t])
            if 0 <= t - 1 < number:
                grads(*units[t - 1])
            if 0 <= t - 3 < number:
                store(*units[t - 3])

        for k in range(steps):
            pl.when(step == k)(lambda k=k: fi_copy(k).wait())
        acc[...] += dot(fis[at_group], gp[...], NT)

        @pl.when(at_group == steps - 1)
        def _():
            one = jnp.ones((rows, 16), f32)
            gpl[pair] = gplt[...].T[:rows, :]
            acc[...] += dot(
                jnp.concatenate([fil[...], one], axis=1).astype(bf16), gpl[pair].astype(bf16), TN
            )
            weight = awp[:, pl.ds(pl.multiple_of(pair * 384, 128), 384)].astype(f32)
            by_gain = weight * acc[:features, :]
            by_shift = weight * acc[features : features + 1, :]
            fold = lambda v: jnp.sum((v[:, :128] + v[:, 128:256] + v[:, 256:]).T, axis=0, keepdims=True)
            shift_row = fold(by_shift)
            gain_row = (fold(by_gain) - row_of(shift) * shift_row) / row_of(gain)
            block = features + 32
            stream = pair + 1
            for k in range(3):
                lanes = slice(k * 128, (k + 1) * 128)
                spread.send[stream, k * block : k * block + features + 16] = acc[:, lanes].astype(bf16)
                ends = rows_where(0, gain_row[:, lanes], 16, f32) + rows_where(1, shift_row[:, lanes], 16, f32)
                spread.send[stream, k * block + features + 16 : (k + 1) * block] = ends.astype(bf16)
            rest = spread.send.shape[1] - 3 * block
            if rest:
                spread.send[stream, 3 * block :] = jnp.zeros((rest, 128), bf16)
            spread.start(1, stream)

    @pl.when(step == last)
    def _():
        take_left(left, xl, count)
        normed, scale = norm_rows(xl[...])
        packed = jnp.concatenate([gpl[p] for p in range(pairs)], axis=1).astype(bf16)
        grad_first = dot(packed, awp[...], NT)
        outl[...] = ghl[...] + norm_back(grad_first * row_of(gain), normed, scale, 1)

    @pl.when(step >= last)
    def _():
        held = {}
        first = (step - last) * late_group

        def product(g):
            image = first + g
            lanes = pl.ds(pl.multiple_of(lax.rem(image, group) * MAIN, MAIN), MAIN)
            held["grad", g] = dot(awp[...], gpa[image // group, :, lanes])

        def norm(g):
            held["norm", g] = norm_columns(tok[g].T.astype(f32))

        def finish(g):
            normed, scale = held.pop(("norm", g))
            grad = norm_back(held.pop(("grad", g)) * wide(cols[...], MAIN), normed, scale, 0)
            result = gh[:, g * MAIN : (g + 1) * MAIN] + grad
            out[g, :MAIN, :] = result.astype(bf16).T
            out[g, MAIN : MAIN + 1, :] = outl[pl.ds(first + g, 1), :].astype(bf16)

        product(0)
        norm(0)
        for g in range(late_group):
            if g + 1 < late_group:
                product(g + 1)
                norm(g + 1)
            finish(g)

    @pl.when(step == last + late_steps - 1)
    def _():
        for slot, name, phase, s in plan:
            if slot >= last + late_steps:
                engines[name].advance(phase, s)
        for s in range(quarter.streams):
            for side in range(2):
                quarter_out[s, side] = quarter.fin[s, side, : quarter.half]
        spread_out[...] = spread.out[...]
        block = features + 32
        for k in range(3):
            low = k * block + features + 16
            ends = spread.out[0, low : low + 16].astype(f32)
            at = lax.broadcasted_iota(jnp.int32, ends.shape, 0)
            row = jnp.sum(jnp.where(at == 8 + quarter.me_t, ends, 0.0), axis=0, keepdims=True)
            bias_out[:, k * 128 : (k + 1) * 128] = jnp.broadcast_to(row, (8, 128))


def place_kernel(
    pairs, parts, quarter, spread, bias, output, input_grad,
    output_to, input_to, first_gain, first_shift, attend, attend_bias, merge, merge_bias,
    second_gain, second_shift, up, up_bias, down, down_bias, held, sems,
):
    features = merge.shape[0]
    count = output.shape[0]
    ins, outs = [], []
    for k, (src, to) in enumerate(((output, output_to), (input_grad, input_to))):
        for image in range(count):
            ins.append(pltpu.make_async_copy(src.at[image], held.at[k, image], sems.at[0, k, image]))
            outs.append(pltpu.make_async_copy(held.at[k, image], to.at[image], sems.at[1, k, image]))
    for copy in ins:
        copy.start()
    for s in range(quarter.shape[0]):
        lanes = slice(s * 128, (s + 1) * 128)
        up[:, lanes] = quarter[s, 0].astype(f32)
        down[lanes, :] = quarter[s, 1].astype(f32).T
    up_bias[...] = bias[0:1, :].reshape(features)
    block = features + 32
    ends, firsts, seconds, merge_ends = [], [], [], []
    for k in range(3):
        merge[:, k * 128 : (k + 1) * 128] = spread[0, k * block : k * block + features].astype(f32)
        low = k * block + features
        merge_ends.append(spread[0, low : low + 16].astype(f32))
        seconds.append(spread[0, low + 16 : low + 32].astype(f32))
        total = jnp.zeros((16, 128), f32)
        for pair in range(pairs):
            lanes = slice(k * features + pair * 128, k * features + (pair + 1) * 128)
            attend[:, lanes] = spread[pair + 1, k * block : k * block + features].astype(f32)
            total = total + spread[pair + 1, low + 16 : low + 32].astype(f32)
        firsts.append(total)
    merge_ends, firsts, seconds = (jnp.concatenate(v, axis=1) for v in (merge_ends, firsts, seconds))
    merge_bias[...] = merge_ends[0:1, :].reshape(features)
    first_gain[...] = firsts[0:1, :].reshape(features)
    first_shift[...] = firsts[1:2, :].reshape(features)
    second_gain[...] = seconds[0:1, :].reshape(features)
    second_shift[...] = seconds[1:2, :].reshape(features)
    down_bias[...] = seconds[2:3, :].reshape(features)
    for to, k in ((0, 0), (1, 2)):
        rows = [
            spread[pair + 1, k * block + features : k * block + features + 16].astype(f32)[0:1, :]
            for pair in range(pairs)
        ]
        attend_bias[to : to + 1, :] = jnp.concatenate(rows, axis=1)
    for copy, on in zip(ins, outs):
        copy.wait()
        on.start()
    for copy in outs:
        copy.wait()


def transfers(streams, steps, last, late_steps):
    end = last + late_steps
    plan = [(1, "quarter", 1, s) for s in range(streams)] + [(1, "spread", 1, 0)]
    plan += [(min(3 + s // 2, last), "quarter", 2, s) for s in range(streams)]
    plan += [(min(5 + s // 2, last), "quarter", 3, s) for s in range(streams)]
    plan += [(3, "spread", 2, 0), (5, "spread", 3, 0), (last, "spread", 4, 0), (last + 2, "spread", 5, 0)]
    plan += [
        (steps + 1, "spread", 1, 1), (steps + 2, "spread", 2, 1), (last, "spread", 3, 1),
        (last + 2, "spread", 4, 1), (last + 4, "spread", 5, 1),
        (2 * steps + 1, "spread", 1, 2), (last, "spread", 2, 2), (last + 5, "spread", 3, 2),
        (3 * steps + 2, "spread", 1, 3),
    ]
    plan.sort(key=lambda item: item[0])
    plan += [
        (end, "spread", 2, 3), (end, "quarter", 4, 0), (end, "quarter", 4, 1), (end, "quarter", 4, 2),
        (end, "spread", 4, 2), (end, "spread", 3, 3), (end, "quarter", 5, 0), (end, "quarter", 5, 1),
        (end, "spread", 5, 2), (end, "spread", 4, 3), (end, "quarter", 5, 2), (end, "spread", 5, 3),
    ]
    return plan


def whole(*dims):
    return pl.BlockSpec(dims, lambda i: (0,) * len(dims))


def once(*dims):
    return pl.BlockSpec(dims, lambda i: (0,) * len(dims), pipeline_mode=pl.Buffered(1))


LIVE = pl.BlockSpec(memory_space=pltpu.SMEM)
ANY = pl.BlockSpec(memory_space=pl.ANY)


def params(**more):
    return pltpu.CompilerParams(
        vmem_limit_bytes=60 * 2**20, dimension_semantics=("arbitrary",), **more
    )


def shape(dtype, *dims):
    return jax.ShapeDtypeStruct(dims, dtype)


def shards(
    mesh_sizes, tokens, image_mask, patch_mask, first_gain, first_shift, attend_weight, attend_bias,
    merge_weight, merge_bias, second_gain, second_shift, up_weight, up_bias, down_weight,
    down_bias, cotangent,
):
    n, seq, d = tokens.shape
    packed = attend_weight.shape[1]
    rows = -(-n // 16) * 16
    group = 2 if n % 2 == 0 else 1
    steps = n // group
    width = group * MAIN
    pairs = HEADS // 2
    total = n * MAIN
    left = pl.BlockSpec((n, 16, d), lambda i: (0, MAIN // 16, 0), pipeline_mode=pl.Buffered(1))
    quarters, share = mesh_sizes[1], up_weight.shape[1]

    here = lambda i: jnp.minimum(i, steps - 1)
    cols = lambda r: pl.BlockSpec((r, width), lambda i: (0, here(i)))
    images = lambda *dims: pl.BlockSpec((group, *dims), lambda i: (here(i),) + (0,) * len(dims))
    fi, qkv, probs, edges, invs, lp, lself, att, hid, fil, qkvl, attl, hidl, wall, ball = pl.pallas_call(
        functools.partial(attend_kernel, n, group, steps),
        grid=(steps + 1,),
        in_specs=[
            once(group, MAIN, d),
            pl.BlockSpec((group, MAIN, d), lambda i: (here(i + 1), 0, 0)),
            left, whole(n, MAIN), LIVE, whole(d), whole(d), whole(2, d), whole(d),
            once(d, packed), once(d, d), ANY, whole(share), ANY,
        ],
        out_specs=[
            cols(d + 16), cols(packed), images(HEADS, MAIN, MAIN), images(16, MAIN),
            images(16, MAIN), images(16, MAIN), images(16, 128), cols(d),
            pl.BlockSpec((d, width), lambda i: (0, jnp.maximum(i, 1) - 1)),
            whole(rows, d), whole(rows, packed), whole(rows, d), whole(rows, d), ANY, ANY,
        ],
        out_shape=[
            shape(bf16, d + 16, total), shape(bf16, packed, total), shape(bf16, n, HEADS, MAIN, MAIN),
            shape(f32, n, 16, MAIN), shape(f32, n, 16, MAIN), shape(f32, n, 16, MAIN),
            shape(f32, n, 16, 128), shape(bf16, d, total), shape(f32, d, total),
            shape(f32, rows, d), shape(f32, rows, packed), shape(f32, rows, d), shape(f32, rows, d),
            shape(bf16, quarters, 2, d, share), shape(bf16, quarters, 16, share),
        ],
        scratch_shapes=[
            pltpu.VMEM((packed, d + 128), bf16), pltpu.VMEM((d, d + 128), bf16),
            pltpu.VMEM((d + 128, width), bf16), pltpu.VMEM((d + 128, width), bf16),
            pltpu.VMEM((2, d, 128), f32), pltpu.VMEM((group, 16, MAIN), f32),
            pltpu.VMEM((2, packed, width), bf16),
            pltpu.VMEM((3, d, width), bf16),
            pltpu.VMEM((rows, d), f32), pltpu.VMEM((rows, packed), f32), pltpu.VMEM((rows, d), f32),
            pltpu.VMEM((16, share), bf16), pltpu.SemaphoreType.DMA((9,)), pltpu.SemaphoreType.DMA((9,)),
            pltpu.SemaphoreType.DMA((3,)),
        ],
        compiler_params=params(collective_id=0, has_side_effects=True),
        name="attend",
    )(
        tokens, tokens, tokens, patch_mask, image_mask, first_gain, first_shift, attend_bias, merge_bias,
        attend_weight, merge_weight, up_weight, up_bias, down_weight,
    )

    streams = d // 128
    block = d + 32
    chunk = -(-3 * block // (8 * 16)) * 16
    half_images = lambda *dims: pl.BlockSpec((group, *dims), lambda i: (i % steps,) + (0,) * len(dims))
    late_images = lambda *dims: pl.BlockSpec(
        (group, *dims), lambda i: ((i // steps) * (i - steps),) + (0,) * len(dims)
    )
    late_cols = lambda r: pl.BlockSpec((r, width), lambda i: (0, (i // steps) * (i - steps)))
    quarter_vm = lambda dtype: pltpu.VMEM((streams, 2 * d, 128), dtype)
    output, gh, gml, dots, ghl, gmleft, mine, beside, shared = pl.pallas_call(
        functools.partial(feed_kernel, n, group, steps),
        grid=(2 * steps,),
        in_specs=[
            pl.BlockSpec((d, width), lambda i: (0, i % steps)), late_cols(d), late_images(16, MAIN),
            half_images(MAIN, d), left, LIVE, whole(d), whole(d), whole(d),
            whole(rows, d), whole(rows, d), once(quarters, 2, d, share), once(quarters, 16, share), once(d, d),
        ],
        out_specs=[
            late_images(seq, d), late_cols(d), late_cols(d), late_images(16, MAIN),
            whole(rows, d), whole(rows, d),
            once(streams, 2 * d, 128), once(streams, 2 * d, 128), once(8 * chunk, 128),
        ],
        out_shape=[
            shape(bf16, n, seq, d), shape(f32, d, total), shape(bf16, d, total),
            shape(f32, n, 16, MAIN), shape(f32, rows, d), shape(f32, rows, d),
            shape(bf16, streams, 2 * d, 128), shape(bf16, streams, 2 * d, 128), shape(bf16, 8 * chunk, 128),
        ],
        scratch_shapes=[
            pltpu.VMEM((quarters, share, d + 128), bf16), pltpu.VMEM((quarters, d, share), bf16),
            pltpu.VMEM((steps, d + 128, width), bf16), pltpu.VMEM((d + 128, width), bf16),
            pltpu.VMEM((2 * share, width), bf16), pltpu.VMEM((2 * share, width), bf16),
            pltpu.VMEM((steps, d, width), bf16), pltpu.VMEM((3, d, 128), f32), pltpu.VMEM((2, d, 128), f32),
            pltpu.VMEM((rows, d), f32), pltpu.VMEM((rows, d), f32),
            pltpu.VMEM((rows, d + 16), bf16), pltpu.VMEM((rows, d), bf16),
            pltpu.VMEM((quarters, rows, share), bf16), pltpu.VMEM((quarters, rows, share), bf16),
            pltpu.VMEM((steps, d, width), f32), pltpu.VMEM((steps, d, width), f32),
            pltpu.VMEM((d + 16, 2 * share), f32), pltpu.VMEM((d, 2 * share), f32),
            pltpu.VMEM((d + 16, d), f32), pltpu.VMEM((8, d), f32), pltpu.VMEM((8, d), f32),
            quarter_vm(f32), quarter_vm(bf16), quarter_vm(bf16), quarter_vm(bf16), quarter_vm(bf16),
            pltpu.SemaphoreType.DMA((2,)), pltpu.SemaphoreType.DMA((2,)),
        ],
        compiler_params=params(collective_id=1, has_side_effects=True),
        name="feed",
    )(
        hid, att, invs, cotangent, cotangent, image_mask, second_gain, second_shift, down_bias, hidl, attl,
        wall, ball, merge_weight,
    )

    late_group, late_steps = group, steps
    group = next(g for g in (7, 2, 1) if n % g == 0)
    steps = n // group
    width = group * MAIN
    last = pairs * steps
    quarter = Quarter(mesh_sizes[0], streams, 2 * d)
    spread = Spread(mesh_sizes, pairs + 1, chunk)
    plan = transfers(streams, steps, last, late_steps)
    side = lambda i: (i + late_steps) // (last + late_steps)
    early = lambda i: i - side(i) * (i - (last - 1))
    late = lambda i: side(i) * (i - last)
    by_pair = lambda r: pl.BlockSpec((r, width), lambda i: (early(i) // steps, early(i) % steps))
    early_images = lambda *dims: pl.BlockSpec((group, *dims), lambda i: (early(i) % steps,) + (0,) * len(dims))
    pair_lanes = lambda w: pl.BlockSpec((rows, w), lambda i: (0, early(i) // steps))
    late_images = lambda *dims: pl.BlockSpec((late_group, *dims), lambda i: (late(i),) + (0,) * len(dims))
    input_grad, quarter_sum, spread_sum, bias_sum = pl.pallas_call(
        functools.partial(back_kernel, n, group, steps, late_group, late_steps, quarter, spread, plan),
        grid=(last + late_steps,),
        in_specs=[
            by_pair(3 * 128),
            pl.BlockSpec((group, 2, MAIN, MAIN), lambda i: (early(i) % steps, early(i) // steps, 0, 0)),
            early_images(16, MAIN), early_images(16, MAIN), early_images(16, 128), by_pair(128),
            early_images(16, MAIN), ANY,
            whole(rows, d), pair_lanes(384), pair_lanes(128), pair_lanes(128), once(d, packed),
            once(streams, 2 * d, 128), once(streams, 2 * d, 128), once(8 * chunk, 128),
            late_images(MAIN, d), left, pl.BlockSpec((d, late_group * MAIN), lambda i: (0, late(i))),
            whole(rows, d), whole(d), whole(d),
        ],
        out_specs=[
            late_images(seq, d), once(streams, 2, d, 128), once(pairs + 1, 8 * chunk, 128), whole(8, d),
        ],
        out_shape=[
            shape(bf16, n, seq, d), shape(bf16, streams, 2, d, 128), shape(bf16, pairs + 1, 8 * chunk, 128),
            shape(f32, 8, d),
        ],
        scratch_shapes=[
            pltpu.VMEM((steps, packed, width), bf16), pltpu.VMEM((d + 16, 384), f32),
            pltpu.VMEM((pairs, rows, 384), f32), pltpu.VMEM((384, 128), f32),
            pltpu.VMEM((d, packed), bf16), pltpu.VMEM((d, 128), f32),
            pltpu.VMEM((rows, d), f32), pltpu.VMEM((rows, d), f32),
            pltpu.VMEM((steps, d + 16, width), bf16), pltpu.SemaphoreType.DMA((steps,)),
            *quarter.scratch(), *spread.scratch(),
        ],
        compiler_params=params(collective_id=2, has_side_effects=True),
        name="back",
    )(
        qkv, probs, edges, lp, lself, gml, dots, fi, fil, qkvl, attl, gmleft, attend_weight,
        mine, beside, shared, tokens, tokens, gh, ghl, first_gain, first_shift,
    )
    row = lambda: pl.BlockSpec(memory_space=pltpu.VMEM)
    return pl.pallas_call(
        functools.partial(place_kernel, pairs, quarters),
        in_specs=[row(), row(), row(), ANY, ANY],
        out_specs=[ANY, ANY] + [row()] * 12,
        out_shape=[
            shape(bf16, n, seq, d), shape(bf16, n, seq, d), shape(f32, d), shape(f32, d),
            shape(f32, d, packed), shape(f32, 2, d), shape(f32, d, d), shape(f32, d), shape(f32, d),
            shape(f32, d), shape(f32, d, share), shape(f32, share), shape(f32, share, d), shape(f32, d),
        ],
        scratch_shapes=[pltpu.VMEM((2, n, seq, d), bf16), pltpu.SemaphoreType.DMA((2, 2, n))],
        compiler_params=pltpu.CompilerParams(vmem_limit_bytes=60 * 2**20),
        name="place",
    )(quarter_sum, spread_sum, bias_sum, output, input_grad)


def solution(mesh):
    split = ("dp", "tensor")
    in_specs = (
        P(split, None, None), P(split), P(split, None), P(), P(), P(), P(), P(), P(), P(), P(),
        P(None, "tensor"), P("tensor"), P("tensor", None), P(), P(split, None, None),
    )
    out_specs = (
        P(split, None, None), P(split, None, None), P(), P(), P(), P(), P(), P(), P(), P(),
        P(None, "tensor"), P("tensor"), P("tensor", None), P(),
    )
    sizes = (mesh.shape["dp"], mesh.shape["tensor"])
    return jax.shard_map(functools.partial(shards, sizes), mesh=mesh, in_specs=in_specs, out_specs=out_specs, check_vma=False)
```

```python
import functools

import jax
import jax.numpy as jnp
from jax import lax
from jax.experimental import pallas as pl
from jax.experimental.pallas import tpu as pltpu
from jax.sharding import PartitionSpec as P

HEADS = 6
HEAD = 64
MAIN = 256
EPS = 1e-06
MASKED = -1e30
f32, bf16 = jnp.float32, jnp.bfloat16

NN = ((1,), (0,))
NT = ((1,), (1,))
TN = ((0,), (0,))


def dot(left, right, dims=NN):
    return lax.dot_general(left, right, (dims, ((), ())), preferred_element_type=f32)


def rows_where(index, value, rows, dtype):
    columns = value.shape[-1]
    at = lax.broadcasted_iota(jnp.int32, (rows, columns), 0)
    return jnp.where(at == index, value, 0.0).astype(dtype)


def wide(column, width):
    return jnp.concatenate([column] * (width // 128), axis=1)


def as_column(row):
    return jnp.broadcast_to(row, (128, row.shape[1])).T


def norm_columns(values):
    center = values - jnp.mean(values, axis=0, keepdims=True)
    scale = lax.rsqrt(jnp.mean(center * center, axis=0, keepdims=True) + EPS)
    return center * scale, scale


def norm_rows(values):
    center = values - jnp.mean(values, axis=1, keepdims=True)
    scale = lax.rsqrt(jnp.mean(center * center, axis=1, keepdims=True) + EPS)
    return center * scale, scale


def norm_back(grad, normed, scale, axis):
    mean_grad = jnp.mean(grad, axis=axis, keepdims=True)
    mean_both = jnp.mean(grad * normed, axis=axis, keepdims=True)
    return scale * (grad - mean_grad - normed * mean_both)


def gelu_both(pre):
    curve = 0.5 + 0.5 * lax.erf(pre * 0.7071067811865476)
    bell = 0.3989422804014327 * jnp.exp(-0.5 * pre * pre)
    return pre * curve, curve + pre * bell


def head_rows(rows, features):
    at = lax.broadcasted_iota(jnp.int32, (rows, features), 0)
    head = lax.broadcasted_iota(jnp.int32, (rows, features), 1) // HEAD
    return jnp.where(at == head, 1.0, 0.0)


def lane_live(live_ref, first, count):
    flags = [
        jnp.full((1, MAIN), live_ref[first + g].astype(f32)) for g in range(count)
    ]
    return jnp.concatenate(flags, axis=1)


def row_live(live_ref, count, rows):
    at = lax.broadcasted_iota(jnp.int32, (rows, 1), 0)
    flags = jnp.zeros((rows, 1), f32)
    for image in range(count):
        flags = jnp.where(at == image, live_ref[image].astype(f32), flags)
    return flags


def take_left(left_ref, to_ref, count):
    to_ref[...] = jnp.zeros_like(to_ref)
    for image in range(count):
        to_ref[image : image + 1, :] = left_ref[image].astype(f32)[0:1, :]


def flip(place, bits):
    if bits & 1:
        place = place + 1 - 2 * lax.rem(place, 2)
    if bits & 2:
        place = place + 2 - 4 * (place // 2)
    return place


def remote(src, dst, sends, recvs, index, peer):
    return pltpu.make_async_remote_copy(
        src_ref=src, dst_ref=dst, send_sem=sends.at[index], recv_sem=recvs.at[index],
        device_id=peer, device_id_type=pl.DeviceIdType.MESH,
    )


def greet(peers):
    barrier = pltpu.get_barrier_semaphore()
    for peer in peers:
        pl.semaphore_signal(barrier, inc=1, device_id=peer, device_id_type=pl.DeviceIdType.MESH)


def meet(peers):
    pl.semaphore_wait(pltpu.get_barrier_semaphore(), len(peers))


class Quarter:
    def __init__(self, dp, streams, rows):
        self.far = dp // 2
        self.streams, self.half = streams, rows // 2
        self.chunk = -(-self.half // (16 * self.far)) * 16
        self.padded = self.chunk * self.far
        self.copies = 3 + 2 * (self.far - 1)

    def scratch(self):
        s = self.streams
        vm = lambda *dims: pltpu.VMEM((s, *dims, 128), bf16)
        return [
            vm(2 * self.half), vm(2 * self.half), vm(self.half), vm(self.padded),
            vm(max(self.far - 1, 1), self.chunk), vm(2, self.padded),
            pltpu.SemaphoreType.DMA((s, self.copies)), pltpu.SemaphoreType.DMA((s, self.copies)),
        ]

    def bind(self, mine, beside, refs):
        self.mine, self.beside = mine, beside
        self.r1, self.work, self.r2, self.cur, self.r3, self.fin, self.sends, self.recvs = refs
        self.me_dp, self.me_t = lax.axis_index("dp"), lax.axis_index("tensor")
        self.x, self.z = lax.rem(self.me_dp, 2), self.me_dp // 2

    def line(self, j):
        return (lax.rem(self.z + j, self.far) * 2 + self.x, self.me_t)

    def copies_of(self, phase, s):
        across = (self.z * 2 + 1 - self.x, self.me_t)
        cp = lambda index, src, dst, peer: remote(src, dst, self.sends, self.recvs, (s, index), peer)
        if phase == 1:
            return [cp(0, self.beside.at[s], self.r1.at[s], (self.me_dp, flip(self.me_t, 1)))]
        if phase == 2:
            other = pl.ds(pl.multiple_of((1 - self.x) * self.half, 16), self.half)
            return [cp(1, self.work.at[s, other], self.r2.at[s], across)]
        found = []
        if phase == 3:
            for j in range(1, self.far):
                place = lax.rem(self.z + j, self.far)
                src = self.cur.at[s, pl.ds(pl.multiple_of(place * self.chunk, 16), self.chunk)]
                found.append(cp(1 + j, src, self.r3.at[s, j - 1], self.line(j)))
        if phase == 4:
            ref = self.fin.at[s, self.x, pl.ds(pl.multiple_of(self.z * self.chunk, 16), self.chunk)]
            for j in range(1, self.far):
                found.append(cp(self.far + j, ref, ref, self.line(j)))
        if phase == 5:
            ref = self.fin.at[s, self.x, pl.ds(0, self.half)]
            found.append(cp(2 * self.far, ref, ref, across))
        return found

    def start(self, phase, s):
        for copy in self.copies_of(phase, s):
            copy.start()

    def advance(self, phase, s):
        for copy in self.copies_of(phase, s):
            copy.wait()
        if phase == 1:
            self.work[s] = (self.mine[s].astype(f32) + self.r1[s].astype(f32)).astype(bf16)
        if phase == 2:
            kept = self.work[s, pl.ds(pl.multiple_of(self.x * self.half, 16), self.half)]
            self.cur[s, : self.half] = (kept.astype(f32) + self.r2[s].astype(f32)).astype(bf16)
            if self.padded > self.half:
                self.cur[s, self.half :] = jnp.zeros((self.padded - self.half, 128), bf16)
        if phase == 3:
            mine = pl.ds(pl.multiple_of(self.z * self.chunk, 16), self.chunk)
            total = self.cur[s, mine].astype(f32)
            for j in range(self.far - 1):
                total = total + self.r3[s, j].astype(f32)
            self.fin[s, self.x, mine] = total.astype(bf16)
        if phase < 5:
            self.start(phase + 1, s)


class Spread:
    def __init__(self, mesh_sizes, streams, chunk):
        self.dp, self.tensor = mesh_sizes
        self.far = self.dp // 2
        self.hops = self.far.bit_length() - 1
        self.streams, self.chunk = streams, chunk
        self.copies = 1 + 3 + (self.far - 1) + 3 + 1

    def phases(self, s):
        hops = ["line"] if s == self.streams - 1 else [("hop", k) for k in range(self.hops)]
        return ["core", "plane", *hops, "plane back", "core back"]

    def scratch(self):
        s, c = self.streams, self.chunk
        vm = lambda *dims: pltpu.VMEM((s, *dims, 128), bf16)
        return [
            vm(8 * c), vm(4 * c), vm(4 * c), vm(3, c), vm(self.far, c), vm(c), vm(8 * c),
            pltpu.SemaphoreType.DMA((s, self.copies)), pltpu.SemaphoreType.DMA((s, self.copies)),
        ]

    def bind(self, refs):
        self.send, self.r1, self.work, self.r2, self.r3, self.cur, self.out, self.ss, self.rs = refs
        self.me_dp, self.me_t = lax.axis_index("dp"), lax.axis_index("tensor")
        self.x, self.z = lax.rem(self.me_dp, 2), self.me_dp // 2
        self.c, self.y = lax.rem(self.me_t, 2), self.me_t // 2
        self.place = 2 * self.y + self.x

    def plane(self, j):
        x = 1 - self.x if j & 1 else self.x
        y = 1 - self.y if j & 2 else self.y
        return (self.z * 2 + x, 2 * y + self.c), 2 * y + x

    def core(self):
        return (self.me_dp, 2 * self.y + 1 - self.c)

    def line(self, j):
        return (lax.rem(self.z + j, self.far) * 2 + self.x, self.me_t)

    def hop(self, k):
        step = 1 << k
        there = self.z + step - 2 * step * lax.rem(self.z // step, 2)
        return (there * 2 + self.x, self.me_t)

    def rows(self, first, count):
        return pl.ds(pl.multiple_of(first * self.chunk, 16), count * self.chunk)

    def copies_of(self, kind, s):
        cp = lambda index, src, dst, peer: remote(src, dst, self.ss, self.rs, (s, index), peer)
        if kind == "core":
            return [cp(0, self.send.at[s, self.rows(4 * (1 - self.c), 4)], self.r1.at[s], self.core())]
        found = []
        if kind == "plane":
            for j in (1, 2, 3):
                peer, place = self.plane(j)
                found.append(cp(j, self.work.at[s, self.rows(place, 1)], self.r2.at[s, j - 1], peer))
        if kind == "line":
            for j in range(1, self.far):
                ref = self.r3.at[s, self.z]
                found.append(cp(3 + j, ref, ref, self.line(j)))
        if kind[0] == "hop":
            found.append(cp(4 + kind[1], self.cur.at[s], self.r3.at[s, kind[1]], self.hop(kind[1])))
        if kind == "plane back":
            mine = self.out.at[s, self.rows(4 * self.c + self.place, 1)]
            for j in (1, 2, 3):
                found.append(cp(2 + self.far + j, mine, mine, self.plane(j)[0]))
        if kind == "core back":
            ref = self.out.at[s, self.rows(4 * self.c, 4)]
            found.append(cp(6 + self.far, ref, ref, self.core()))
        return found

    def start(self, kind, s):
        for copy in self.copies_of(kind, s):
            copy.start()

    def advance(self, phase, s):
        phases = self.phases(s)
        kind = phases[phase - 1]
        for copy in self.copies_of(kind, s):
            copy.wait()
        mine = self.rows(4 * self.c + self.place, 1)
        if kind == "core":
            half = self.send[s, self.rows(4 * self.c, 4)].astype(f32)
            self.work[s] = (half + self.r1[s].astype(f32)).astype(bf16)
        if kind == "plane":
            total = self.work[s, self.rows(self.place, 1)].astype(f32)
            for j in range(3):
                total = total + self.r2[s, j].astype(f32)
            if phases[2] == "line":
                self.r3[s, self.z] = total.astype(bf16)
            else:
                self.cur[s] = total.astype(bf16)
        if kind == "line":
            total = self.r3[s, 0].astype(f32)
            for j in range(1, self.far):
                total = total + self.r3[s, j].astype(f32)
            self.out[s, mine] = total.astype(bf16)
        if kind[0] == "hop":
            total = (self.cur[s].astype(f32) + self.r3[s, kind[1]].astype(f32)).astype(bf16)
            self.cur[s] = total
            if kind[1] == self.hops - 1:
                self.out[s, mine] = total
        if phase < len(phases):
            self.start(phases[phase], s)


def row_of(ref):
    return ref[...].astype(f32).reshape(1, ref.shape[0])


def parts_of(at, pair):
    return slice(pair * 384 + at * 128, pair * 384 + (at + 1) * 128)


def attend_kernel(
    count, group, steps,
    tok0, tok, left, pmask, live, gain, shift, abias, mbias, aw, mw, up, ubias, down,
    fi_out, qkv_out, probs_out, edge_out, inv_out, lp_out, lself_out, att_out, hid_out,
    fil_out, qkvl_out, attl_out, hidl_out, wall, ball,
    awt, mwt, fia, atta, cols, edges, qkv2, toks, xl, qkvl, attl, brow, sends, recvs, own,
):
    step = pl.program_id(0)
    me_dp, me_t = lax.axis_index("dp"), lax.axis_index("tensor")
    beside, across = (me_dp, flip(me_t, 1)), (me_dp, flip(me_t, 2))

    def places(owner):
        return (wall.at[owner, 0], wall.at[owner, 1], ball.at[owner])

    def first_copies(peer, first):
        return [
            remote(src, dst, sends, recvs, first + k, peer)
            for k, (src, dst) in enumerate(zip((up, down, brow), places(me_t)))
        ]

    def second_copies():
        return [
            remote(ref, ref, sends, recvs, 6 + k, beside) for k, ref in enumerate(places(flip(me_t, 2)))
        ]

    def own_copies():
        return [
            pltpu.make_async_copy(src, dst, own.at[k])
            for k, (src, dst) in enumerate(zip((up, down, brow), places(me_t)))
        ]

    @pl.when(step == 0)
    def _():
        greet((beside, across))
        brow[...] = rows_where(0, row_of(ubias), 16, bf16)
        meet((beside, across))
        for copy in first_copies(across, 3) + first_copies(beside, 0) + own_copies():
            copy.start()

    @pl.when(step == steps - 2)
    def _():
        for copy in first_copies(across, 3):
            copy.wait()
        for copy in second_copies():
            copy.start()

    features = aw.shape[0]
    packed = aw.shape[1]
    rows = xl.shape[0]
    width = group * MAIN
    pairs = HEADS // 2
    heads = head_rows(rows, features)

    def first_norm(block):
        tokens = jnp.concatenate([block[g].T for g in range(group)], axis=1)
        normed, _ = norm_columns(tokens.astype(f32))
        return tokens, (normed * wide(cols[0], width) + wide(cols[1], width)).astype(bf16)

    def project(slot, part):
        span = slice(part * features, (part + 1) * features)
        qkv2[slot, span, :] = dot(awt[span, :], fia[...]).astype(bf16)

    @pl.when(step == 0)
    def _():
        ab = abias[...].astype(f32)
        for pair in range(pairs):
            for at in range(3):
                cut = slice(at * features + pair * 128, at * features + (pair + 1) * 128)
                to = parts_of(at, pair)
                scale = HEAD**-0.5 if at == 0 else 1.0
                awt[to, :features] = (aw[:, cut].astype(f32).T * scale).astype(bf16)
                if at == 1:
                    bias = jnp.zeros((1, 128), f32)
                else:
                    bias = ab[at // 2 : at // 2 + 1, pair * 128 : (pair + 1) * 128] * scale
                awt[to, features:] = rows_where(0, bias, 128, f32).T.astype(bf16)
        mwt[:, :features] = mw[...].astype(f32).T.astype(bf16)
        mwt[:, features:] = rows_where(0, row_of(mbias), 128, f32).T.astype(bf16)
        ones = rows_where(0, jnp.ones((1, fia.shape[1]), f32), 128, bf16)
        fia[features:, :] = ones
        atta[features:, :] = ones
        cols[0] = as_column(row_of(gain))
        cols[1] = as_column(row_of(shift))
        edges[...] = jnp.zeros_like(edges)
        take_left(left, xl, count)
        normed, _ = norm_rows(xl[...])
        fil = (normed * row_of(gain) + row_of(shift)).astype(bf16)
        fil_out[...] = fil.astype(f32)
        plain = dot(fil, aw[...])
        for pair in range(pairs):
            for at in range(3):
                cut = slice(at * features + pair * 128, at * features + (pair + 1) * 128)
                value = plain[:, cut]
                if at != 1:
                    value = value + ab[at // 2 : at // 2 + 1, pair * 128 : (pair + 1) * 128]
                value = value.astype(bf16).astype(f32)
                qkvl[:, parts_of(at, pair)] = value * (HEAD**-0.5) if at == 0 else value
        qkvl_out[...] = qkvl[...]
        attl[...] = jnp.zeros_like(attl)
        tokens, fi = first_norm(tok0)
        toks[0] = tokens
        fia[:features, :] = fi
        for part in range(3):
            project(0, part)

    def merge_branch():
        return dot(mwt[...], atta[...])

    def hidden_of(branch, index):
        tokens = toks[lax.rem(index, 3)].astype(f32)
        return tokens + lane_live(live, index * group, group) * branch

    @pl.when(step < steps)
    def _():
        now, later = lax.rem(step, 2), lax.rem(step + 1, 2)
        one_row = rows_where(0, jnp.ones((1, MAIN), f32), 16, bf16)
        held = {}
        units = [(g, h) for g in range(group) for h in range(HEADS)]

        def lanes_of(g):
            return slice(g * MAIN, (g + 1) * MAIN)

        def part(at, g, h):
            low = (h // 2) * 384 + at * 128 + (h % 2) * HEAD
            return qkv2[now, low : low + HEAD, lanes_of(g)]

        def all_heads(at, g):
            return jnp.concatenate(
                [qkv2[now, parts_of(at, pair), lanes_of(g)] for pair in range(pairs)], axis=0
            )

        def begin(g):
            image = step * group + g
            row = qkvl[pl.ds(image, 1), :]
            ql, kl, vl = (
                jnp.concatenate([row[:, parts_of(at, pair)] for pair in range(pairs)], axis=1)
                for at in range(3)
            )
            key_bias = jnp.where(pmask[pl.ds(image, 1), :] == 1, 0.0, MASKED)
            moved = pltpu.roll(key_bias, 1, axis=1)
            at = lax.broadcasted_iota(jnp.int32, moved.shape, 1)
            main_bias = jnp.where(at == 0, 0.0, moved)
            left_bias = moved[:, 0:1]
            held["bias", g] = rows_where(0, main_bias, 16, bf16)
            held["vl", g] = vl
            held["slk", g] = dot((heads * kl).astype(bf16), all_heads(0, g)) + left_bias
            held["sl", g] = dot((heads * ql).astype(bf16), all_heads(1, g)) + main_bias
            held["self", g] = jnp.sum(heads * (ql * kl), axis=1, keepdims=True) + left_bias

        def left_query(g):
            sl, self_score = held.pop(("sl", g)), held.pop(("self", g))
            peak = jnp.maximum(jnp.max(sl, axis=1, keepdims=True), self_score)
            raised = jnp.exp(sl - peak)
            raised_self = jnp.exp(self_score - peak)
            inv = 1.0 / (jnp.sum(raised, axis=1, keepdims=True) + raised_self)
            lp = raised * inv
            lself = raised_self * inv
            lp_out[g] = lp
            lself_out[g] = jnp.broadcast_to(lself, (rows, 128))
            mixed = dot(lp.astype(bf16), all_heads(2, g), NT) + lself * held["vl", g]
            image = step * group + g
            attl[pl.ds(image, 1), :] = (
                jnp.sum(mixed * heads, axis=0, keepdims=True).astype(bf16).astype(f32)
            )

        def scores(g, h):
            held["s", g, h] = dot(
                jnp.concatenate([part(1, g, h), held["bias", g]], axis=0),
                jnp.concatenate([part(0, g, h), one_row], axis=0),
                TN,
            )

        def soften(g, h):
            value = held.pop(("s", g, h))
            slk = held["slk", g][h : h + 1, :]
            peak = jnp.maximum(jnp.max(value, axis=0, keepdims=True), slk)
            raised = jnp.exp(value - peak).astype(bf16)
            probs_out[g, h] = raised
            held["e", g, h] = raised
            edge = jnp.exp(slk - peak)
            held["edge", g, h] = edge
            edges[g, h : h + 1, :] = edge

        def mix(g, h):
            held["o", g, h] = dot(
                jnp.concatenate([part(2, g, h), one_row], axis=0), held.pop(("e", g, h))
            )

        def add_left(g):
            edge_out[g] = edges[g]
            held["add", g] = dot((heads * held["vl", g]).astype(bf16), edges[g].astype(bf16), TN)

        def finish(g, h):
            out = held.pop(("o", g, h))
            span = slice(h * HEAD, (h + 1) * HEAD)
            inv = 1.0 / (out[HEAD : HEAD + 1, :] + held["edge", g, h])
            inv_out[g, h : h + 1, :] = inv
            mixed = ((out[:HEAD, :] + held["add", g][span]) * inv).astype(bf16)
            atta[span, lanes_of(g)] = mixed
            att_out[span, lanes_of(g)] = mixed

        count_units = len(units)
        for t in range(-2, count_units + 4):
            if t + 2 == 0:
                for g in range(group):
                    begin(g)
                held["branch"] = merge_branch()
            if 0 <= t + 2 < count_units:
                scores(*units[t + 2])
            if t == -1:
                hid_out[...] = hidden_of(held.pop("branch"), step - 1 + 3 * (1 - jnp.minimum(step, 1)))
                qkv_out[...] = qkv2[now]
                fi_out[:features, :] = fia[:features, :]
                fi_out[features:, :] = fia[features : features + 16, :]
                held["next"] = first_norm(tok)
            if t == 1:
                tokens, fi = held.pop("next")
                toks[lax.rem(step + 1, 3)] = tokens
                fia[:features, :] = fi
            if t in (2, 4, 6):
                project(later, (t - 2) // 2)
            if 0 <= t < count_units:
                soften(*units[t])
            if 0 <= t - 2 < count_units:
                mix(*units[t - 2])
            for g in range(group):
                if t == HEADS * g + 3:
                    left_query(g)
                if t == HEADS * (g + 1):
                    add_left(g)
                if t == HEADS * (g + 1) + 3:
                    for h in range(HEADS):
                        finish(g, h)

    @pl.when(step == steps)
    def _():
        hid_out[...] = hidden_of(merge_branch(), step - 1)
        attl_out[...] = attl[...]
        branch = dot(attl[...].astype(bf16), mw[...]) + row_of(mbias)
        hidl_out[...] = xl[...] + row_live(live, count, rows) * branch
        for copy in first_copies(beside, 0) + second_copies() + own_copies():
            copy.wait()


def feed_kernel(
    count, group, steps,
    hid0, hid, att, inv, cot0, cot, cleft, live, gain, shift, dbias, hidl, attl, wall, ball, mw,
    out, gh_out, gml_out, dots_out, ghl_out, gmleft_out, mine, beside, shared,
    upt, dnt, sia, atta, act, gpre, gb, gattn, cols, gsum, xl, outl, sil, gbl, actl, gprel,
    outp, gradp, up_acc, down_acc, merge_acc, sums, biases, kept, away, r1, across, r2, sends, recvs,
):
    step = pl.program_id(0)
    at_step = lax.rem(step, steps)
    second = step // steps
    features = mw.shape[0]
    rows = xl.shape[0]
    width = group * MAIN
    quarters = wall.shape[0]
    me_dp, me_t = lax.axis_index("dp"), lax.axis_index("tensor")
    core, chip = (me_dp, flip(me_t, 1)), (me_dp, flip(me_t, 2))
    first_of = (1 - second) * flip(me_t, 2) + second * me_t
    now = (first_of, flip(first_of, 1))

    def to_core():
        return remote(away, r1, sends, recvs, 0, core)

    def to_chip():
        return remote(across, r2, sends, recvs, 1, chip)

    @pl.when(step == 0)
    def _():
        greet((core, chip))
        gain_row, shift_row, dbias_row = row_of(gain), row_of(shift), row_of(dbias)
        for q in range(quarters):
            upt[q, :, :features] = wall[q, 0].astype(f32).T.astype(bf16)
            upt[q, :, features:] = rows_where(0, ball[q, 0:1, :].astype(f32), 128, f32).T.astype(bf16)
            dnt[q] = wall[q, 1].astype(f32).T.astype(bf16)
        ones = rows_where(0, jnp.ones((1, width), f32), 128, bf16)
        for k in range(steps):
            sia[k, features:, :] = ones
        atta[features:, :] = ones
        cols[0] = as_column(gain_row)
        cols[1] = as_column(shift_row)
        cols[2] = as_column(dbias_row)
        gsum[...] = jnp.zeros_like(gsum)
        biases[...] = jnp.zeros_like(biases)
        take_left(cleft, xl, count)
        alive = row_live(live, count, rows)
        normed, scale = norm_rows(hidl[...])
        si = (normed * gain_row + shift_row).astype(bf16)
        grad_branch = (alive * xl[...]).astype(bf16)
        total = hidl[...] + alive * dbias_row
        grad_second = jnp.zeros_like(total)
        pre_of = [dot(si, wall[q, 0]) + ball[q, 0:1, :].astype(f32) for q in range(quarters)]
        grad_of = [dot(grad_branch, wall[q, 1], NT) for q in range(quarters)]
        for q in range(quarters):
            value, slope = gelu_both(pre_of[q])
            actl[q] = value.astype(bf16)
            gprel[q] = (grad_of[q] * slope).astype(bf16)
        for q in range(quarters):
            total = total + alive * dot(actl[q], wall[q, 1])
            grad_second = grad_second + dot(gprel[q], wall[q, 0], NT)
        outl[...] = total
        grad_hidden = xl[...] + norm_back(grad_second * gain_row, normed, scale, 1)
        ghl_out[...] = grad_hidden
        grad_attn = (alive * grad_hidden).astype(bf16)
        gmleft_out[...] = dot(grad_attn, mw[...], NT).astype(bf16).astype(f32)
        one = jnp.ones((rows, 16), f32)
        sil[...] = jnp.concatenate([si.astype(f32), one], axis=1).astype(bf16)
        gbl[...] = grad_branch
        merge_acc[...] = dot(jnp.concatenate([attl[...], one], axis=1).astype(bf16), grad_attn, TN)
        sums[...] = jnp.zeros_like(sums)
        sums[0:1, :] = jnp.sum(grad_second * normed, axis=0, keepdims=True)
        sums[1:2, :] = jnp.sum(grad_second, axis=0, keepdims=True)
        sums[2:3, :] = jnp.sum(grad_branch.astype(f32), axis=0, keepdims=True)
        meet((core, chip))

    @pl.when(at_step == 0)
    def _():
        for c, q in enumerate(now):
            lanes = slice(c * features, (c + 1) * features)
            up_acc[:, lanes] = dot(sil[...], gprel[q], TN)
            down_acc[:, lanes] = dot(gbl[...], actl[q], TN)

    def rounded(ref, lanes, at):
        lanes = slice(lanes + at * 128, lanes + (at + 1) * 128)
        return jnp.concatenate([up_acc[:features, lanes], down_acc[:, lanes]], axis=0)

    @pl.when(step == steps + 1)
    def _():
        to_core().wait()
        for at in range(kept.shape[0]):
            across[at] = (kept[at] + r1[at].astype(f32)).astype(bf16)
        to_chip().start()

    pres, grads = {}, {}
    lanes_of = [slice(g * MAIN, (g + 1) * MAIN) for g in range(group)]

    def enter(hidden, cotangent, to):
        normed, _ = norm_columns(hidden[...])
        sia[to, :features, :] = (normed * wide(cols[0], width) + wide(cols[1], width)).astype(bf16)
        alive = lane_live(live, to * group, group)
        turned = jnp.concatenate([cotangent[g].T for g in range(group)], axis=1).astype(f32)
        gb[to] = (turned * alive).astype(bf16)

    def into(g):
        for c in range(2):
            pres[g, c] = dot(upt[now[c]], sia[at_step, :, lanes_of[g]])
            grads[g, c] = dot(wall[now[c], 1], gb[at_step, :, lanes_of[g]])

    def through(g):
        for c in range(2):
            span = slice(c * features, (c + 1) * features)
            value, slope = gelu_both(pres.pop((g, c)))
            act[span, lanes_of[g]] = value.astype(bf16)
            gpre[span, lanes_of[g]] = (grads.pop((g, c)) * slope).astype(bf16)

    def both_of(ref, *more):
        return jnp.concatenate([ref[(q, *more)] for q in now], axis=1)

    def second_sum(g):
        return dot(both_of(wall, 0), gpre[:, lanes_of[g]])

    def output_sum(g):
        return dot(both_of(dnt), act[:, lanes_of[g]])

    def up_product():
        up_acc[...] += dot(sia[at_step, : up_acc.shape[0], :], gpre[...], NT)

    def down_product():
        down_acc[...] += dot(gb[at_step], act[...], NT)

    @pl.when(step == 0)
    def _():
        enter(hid0, cot0, 0)

    @pl.when(second == 0)
    def _():
        for g in range(group):
            into(g)
        for g in range(group):
            through(g)
            gradp[at_step, :, lanes_of[g]] = second_sum(g)
            outp[at_step, :, lanes_of[g]] = output_sum(g)
        up_product()
        enter(hid, cot, at_step + 1 - (at_step + 1) // steps)
        down_product()

    @pl.when(second == 1)
    def _():
        held = {}
        for g in range(group):
            into(g)
        for g in range(group):
            hidden = hid[:, lanes_of[g]]
            held["norm", g] = norm_columns(hidden)
            held["cot", g] = cot[g].T.astype(f32)
        for g in range(group):
            through(g)
            held["second", g] = gradp[at_step, :, lanes_of[g]] + second_sum(g)
            held["out", g] = outp[at_step, :, lanes_of[g]] + output_sum(g)

        def back(g):
            grad_second = held["second", g]
            normed, scale = held["norm", g]
            grad = held["cot", g] + norm_back(grad_second * wide(cols[0], MAIN), normed, scale, 0)
            gh_out[:, lanes_of[g]] = grad
            alive = live[at_step * group + g].astype(f32)
            gattn[:, lanes_of[g]] = (alive * grad).astype(bf16)
            both = grad_second * normed
            for at in range(0, MAIN, 128):
                gsum[0] += both[:, at : at + 128]
                gsum[1] += grad_second[:, at : at + 128]

        def write(g):
            image = at_step * group + g
            alive = live[image].astype(f32)
            result = hid[:, lanes_of[g]] + alive * (held["out", g] + wide(cols[2], MAIN))
            out[g, :MAIN, :] = result.astype(bf16).T
            out[g, MAIN : MAIN + 1, :] = outl[pl.ds(image, 1), :].astype(bf16)

        def scale_rows(g):
            mixed = held["mixed", g].astype(bf16).astype(f32)
            both = mixed * att[:, lanes_of[g]].astype(f32)
            for h in range(HEADS):
                span = slice(h * HEAD, (h + 1) * HEAD)
                row_inv = inv[g, h : h + 1, :]
                gml_out[span, lanes_of[g]] = (mixed[span] * row_inv).astype(bf16)
                row_dot = jnp.sum(both[span], axis=0, keepdims=True) * row_inv
                dots_out[g, h : h + 1, :] = row_dot

        dots_out[...] = jnp.zeros_like(dots_out)
        atta[:features, :] = att[...]
        back(0)
        up_product()
        for g in range(1, group):
            back(g)
        for g in range(group):
            held["mixed", g] = dot(mw[...], gattn[:, lanes_of[g]])
        down_product()
        for g in range(group):
            scale_rows(g)
        merge_acc[...] += dot(atta[: merge_acc.shape[0], :], gattn[...], NT)
        sums[2:3, :] += dot(jnp.ones((16, width), bf16), gb[at_step], NT)[0:1, :]
        for g in range(group):
            write(g)

    @pl.when(at_step == steps - 1)
    def _():
        for c, q in enumerate(now):
            biases[pl.ds(q, 1), :] = up_acc[features : features + 1, c * features : (c + 1) * features]

    @pl.when(step == steps - 1)
    def _():
        for at in range(kept.shape[0]):
            kept[at] = rounded(up_acc, 0, at)
            away[at] = rounded(up_acc, features, at).astype(bf16)
        to_core().start()

    @pl.when(step == 2 * steps - 1)
    def _():
        sums[0:1, :] += jnp.sum(gsum[0].T, axis=0, keepdims=True)
        sums[1:2, :] += jnp.sum(gsum[1].T, axis=0, keepdims=True)
        ends = jnp.concatenate([sums[...], biases[...]], axis=0)
        merged = jnp.concatenate([merge_acc[:features, :], merge_acc[features : features + 16, :], ends], axis=0)
        for at in range(features // 128):
            block = merged.shape[0]
            shared[at * block : (at + 1) * block] = merged[:, at * 128 : (at + 1) * 128].astype(bf16)
        rest = shared.shape[0] - (features // 128) * merged.shape[0]
        if rest:
            shared[shared.shape[0] - rest :] = jnp.zeros((rest, 128), bf16)
        for at in range(kept.shape[0]):
            beside[at] = rounded(up_acc, features, at).astype(bf16)
        to_chip().wait()
        for at in range(kept.shape[0]):
            mine[at] = (rounded(up_acc, 0, at) + r2[at].astype(f32)).astype(bf16)


def back_kernel(
    count, group, steps, late_group, late_steps, quarter, spread, plan,
    qkv, probs, edge, lp, lself, gml, dots, fi, fil, qkvl, attl, gmleft, aw, mine, beside, shared,
    tok, left, gh, ghl, gain, shift,
    out, quarter_out, spread_out, bias_out,
    gpa, acc, gpl, gplt, awp, cols, xl, outl, fis, minev, own, *comm,
):
    step = pl.program_id(0)
    features = aw.shape[0]
    rows = xl.shape[0]
    pairs = HEADS // 2
    last = pairs * steps
    pair = lax.rem(step // steps, pairs)
    at_group = lax.rem(step, steps)
    used = len(quarter.scratch())
    quarter.bind(minev, beside, comm[:used])
    spread.bind(comm[used:])
    engines = {"quarter": quarter, "spread": spread}
    at = lax.broadcasted_iota(jnp.int32, (rows, 128), 0)
    heads = jnp.where(at == lax.broadcasted_iota(jnp.int32, (rows, 128), 1) // HEAD, 1.0, 0.0)

    def fi_copy(k):
        width = group * MAIN
        return pltpu.make_async_copy(fi.at[:, pl.ds(k * width, width)], fis.at[k], own.at[k])

    def shared_copy():
        return pltpu.make_async_copy(shared, spread.send.at[0], own.at[steps])

    def early_copies():
        found = [pltpu.make_async_copy(mine, minev, own.at[steps + 1])]
        for part in range(pairs):
            for k in range(3):
                cut = pl.ds(k * features + part * 128, 128)
                to = pl.ds(part * 384 + k * 128, 128)
                sem = own.at[steps + 2 + part * 3 + k]
                found.append(pltpu.make_async_copy(aw.at[:, cut], awp.at[:, to], sem))
        return found

    @pl.when(step == 0)
    def _():
        peers = [
            (quarter.me_dp, flip(quarter.me_t, 1)), *(spread.plane(j)[0] for j in (1, 2, 3)),
            *(spread.line(j) for j in range(1, spread.far)),
        ]
        greet(peers)
        shared_copy().start()
        for copy in early_copies():
            copy.start()
        for k in range(steps):
            fi_copy(k).start()
        cols[...] = as_column(row_of(gain))
        gpl[...] = jnp.zeros_like(gpl)
        gplt[...] = jnp.zeros_like(gplt)
        acc[...] = jnp.zeros_like(acc)
        meet(peers)
        for s in range(quarter.streams):
            quarter.start(1, s)
        shared_copy().wait()
        spread.start("core", 0)

    for k in range(steps):
        pl.when(step == k)(lambda k=k: fi_copy(k).wait())

    @pl.when(step == 1)
    def _():
        for copy in early_copies():
            copy.wait()

    def advance(slot):
        for at, name, phase, s in plan:
            if at == slot:
                engines[name].advance(phase, s)

    for slot in sorted({item[0] for item in plan if item[0] < last + late_steps}):
        pl.when(step == slot)(functools.partial(advance, slot))

    @pl.when(step < last)
    def _():
        at16 = lax.broadcasted_iota(jnp.int32, (16, MAIN), 0)
        minus = jnp.where(at16 < 2, -1.0, 0.0).astype(bf16)
        ends_row = jnp.where(lax.broadcasted_iota(jnp.int32, (1, 16), 1) < 2, -1.0, 0.0)
        gp = gpa.at[at_group, pl.ds(pl.multiple_of(pair * 384, 128), 384)]
        held = {}
        units = [(g, r) for g in range(group) for r in range(2)]

        def lanes_of(g):
            return slice(g * MAIN, (g + 1) * MAIN)

        def part(at, r, g):
            return qkv[at * 128 + r * HEAD : at * 128 + (r + 1) * HEAD, lanes_of(g)]

        def lower(value):
            return value.astype(bf16).astype(f32)

        def prepare(g):
            image = at_group * group + g
            row = qkvl[pl.ds(image, 1), :]
            ql, kl, vl = (row[:, at * 128 : (at + 1) * 128] for at in range(3))
            gm_row = gmleft[pl.ds(image, 1), :]
            row_dot = jnp.sum(heads * (gm_row * attl[pl.ds(image, 1), :]), axis=1, keepdims=True)
            prob = jnp.sum(heads * (gm_row * vl), axis=1, keepdims=True)
            held["cols", g] = tuple(as_column(v) for v in (ql, kl, gm_row))
            held["left", g] = (vl, row_dot, prob - row_dot)

        def change(g, r):
            row_dot = dots[g, pl.ds(2 * pair + r, 1), :]
            high = row_dot.astype(bf16).astype(f32)
            rest = jnp.where(at16 == 0, high, jnp.where(at16 == 1, row_dot - high, 0.0)).astype(bf16)
            values = jnp.concatenate([part(2, r, g), minus], axis=0).T
            vl = held["left", g][0][:, r * HEAD : (r + 1) * HEAD]
            last_row = rows_where(0, jnp.concatenate([vl, ends_row], axis=1), 16, bf16)
            held["z", g, r] = dot(
                jnp.concatenate([values, last_row], axis=0),
                jnp.concatenate([gml[r * HEAD : (r + 1) * HEAD, lanes_of(g)], rest], axis=0),
            )

        def left_unit(g, r, edge_change):
            image = at_group * group + g
            span = slice(r * HEAD, (r + 1) * HEAD)
            head = pl.ds(2 * pair + r, 1)
            colq, colk, colg = (wide(v[span], MAIN) for v in held["cols", g])
            _, row_dot, self_change = held["left", g]
            row_dot, self_change = row_dot[r : r + 1, :], self_change[r : r + 1, :]
            edge_row, lp_row, self_prob = edge[g, head, :], lp[g, head, :], lself[g, head, 0:1]
            edge_grad = lower(edge_row * edge_change)
            left_change = jnp.sum(colg * part(2, r, g).astype(f32), axis=0, keepdims=True) - row_dot
            left_grad = lower(lp_row * left_change)
            self_grad = lower(self_prob * self_change)
            held["add", g, r] = (colk * edge_grad, colq * left_grad, colg * lower(lp_row))
            grad_q = jnp.sum(part(1, r, g).astype(f32) * left_grad, axis=1, keepdims=True)
            grad_k = jnp.sum(part(0, r, g).astype(f32) * edge_grad, axis=1, keepdims=True)
            grad_v = jnp.sum(
                gml[span, lanes_of(g)].astype(f32) * lower(edge_row), axis=1, keepdims=True
            )
            values = (
                (grad_q + self_grad * colk[:, 0:1]) * HEAD**-0.5,
                grad_k + self_grad * colq[:, 0:1],
                grad_v + lower(self_prob) * colg[:, 0:1],
            )
            at = lax.broadcasted_iota(jnp.int32, (HEAD, 128), 1)
            for k, value in enumerate(values):
                to = slice(k * 128 + r * HEAD, k * 128 + (r + 1) * HEAD)
                gplt[to, :] = jnp.where(at == image, lower(value), gplt[to, :])

        def scores(g, r):
            raised = probs[g, r]
            value = held.pop(("z", g, r))
            held["ds", g, r] = (raised.astype(f32) * value[:MAIN]).astype(bf16)
            left_unit(g, r, value[MAIN : MAIN + 1])
            held["v", g, r] = dot(gml[r * HEAD : (r + 1) * HEAD, lanes_of(g)], raised, NT)

        def grads(g, r):
            ds = held.pop(("ds", g, r))
            held["q", g, r] = dot(part(1, r, g), ds)
            held["k", g, r] = dot(part(0, r, g), ds, NT)

        def store(g, r):
            span = slice(r * HEAD, (r + 1) * HEAD)
            add_q, add_k, add_v = held.pop(("add", g, r))
            values = (
                (held.pop(("q", g, r)) + add_q) * HEAD**-0.5,
                held.pop(("k", g, r)) + add_k,
                held.pop(("v", g, r)) + add_v,
            )
            for at, value in enumerate(values):
                gp[at * 128 + r * HEAD : at * 128 + (r + 1) * HEAD, lanes_of(g)] = value.astype(bf16)

        number = len(units)
        for t in range(-4, number + 4):
            for g in range(group):
                if t == 2 * g - 4:
                    prepare(g)
            if 0 <= t + 2 < number:
                change(*units[t + 2])
            if 0 <= t < number:
                scores(*units[t])
            if 0 <= t - 1 < number:
                grads(*units[t - 1])
            if 0 <= t - 3 < number:
                store(*units[t - 3])

        acc[...] = jnp.where(at_group == 0, 0.0, acc[...]) + dot(fis[at_group], gp[...], NT)

        @pl.when(at_group == steps - 1)
        def _():
            one = jnp.ones((rows, 16), f32)
            gpl[pair] = gplt[...].T[:rows, :]
            acc[...] += dot(
                jnp.concatenate([fil[...], one], axis=1).astype(bf16), gpl[pair].astype(bf16), TN
            )
            weight = awp[:, pl.ds(pl.multiple_of(pair * 384, 128), 384)].astype(f32)
            by_gain = weight * acc[:features, :]
            by_shift = weight * acc[features : features + 1, :]
            fold = lambda v: jnp.sum((v[:, :128] + v[:, 128:256] + v[:, 256:]).T, axis=0, keepdims=True)
            shift_row = fold(by_shift)
            gain_row = (fold(by_gain) - row_of(shift) * shift_row) / row_of(gain)
            block = features + 32
            stream = pair + 1
            for k in range(3):
                lanes = slice(k * 128, (k + 1) * 128)
                spread.send[stream, k * block : k * block + features + 16] = acc[:, lanes].astype(bf16)
                ends = rows_where(0, gain_row[:, lanes], 16, f32) + rows_where(1, shift_row[:, lanes], 16, f32)
                spread.send[stream, k * block + features + 16 : (k + 1) * block] = ends.astype(bf16)
            rest = spread.send.shape[1] - 3 * block
            if rest:
                spread.send[stream, 3 * block :] = jnp.zeros((rest, 128), bf16)
            spread.start("core", stream)

    @pl.when(step == last)
    def _():
        take_left(left, xl, count)
        normed, scale = norm_rows(xl[...])
        packed = jnp.concatenate([gpl[p] for p in range(pairs)], axis=1).astype(bf16)
        grad_first = dot(packed, awp[...], NT)
        outl[...] = ghl[...] + norm_back(grad_first * row_of(gain), normed, scale, 1)

    @pl.when(step >= last)
    def _():
        held = {}
        first = (step - last) * late_group

        def product(g):
            image = first + g
            lanes = pl.ds(pl.multiple_of(lax.rem(image, group) * MAIN, MAIN), MAIN)
            held["grad", g] = dot(awp[...], gpa[image // group, :, lanes])

        def norm(g):
            held["norm", g] = norm_columns(tok[g].T.astype(f32))

        def finish(g):
            normed, scale = held.pop(("norm", g))
            grad = norm_back(held.pop(("grad", g)) * wide(cols[...], MAIN), normed, scale, 0)
            result = gh[:, g * MAIN : (g + 1) * MAIN] + grad
            out[g, :MAIN, :] = result.astype(bf16).T
            out[g, MAIN : MAIN + 1, :] = outl[pl.ds(first + g, 1), :].astype(bf16)

        product(0)
        norm(0)
        for g in range(late_group):
            if g + 1 < late_group:
                product(g + 1)
                norm(g + 1)
            finish(g)

    @pl.when(step == last + late_steps - 1)
    def _():
        for slot, name, phase, s in plan:
            if slot >= last + late_steps:
                engines[name].advance(phase, s)
        for s in range(quarter.streams):
            for side in range(2):
                quarter_out[s, side] = quarter.fin[s, side, : quarter.half]
        spread_out[...] = spread.out[...]
        block = features + 32
        for k in range(3):
            low = k * block + features + 16
            ends = spread.out[0, low : low + 16].astype(f32)
            at = lax.broadcasted_iota(jnp.int32, ends.shape, 0)
            row = jnp.sum(jnp.where(at == 8 + quarter.me_t, ends, 0.0), axis=0, keepdims=True)
            bias_out[:, k * 128 : (k + 1) * 128] = jnp.broadcast_to(row, (8, 128))


def place_kernel(
    pairs, quarter_in, spread_in, bias, output, input_grad,
    output_to, input_to, first_gain, first_shift, attend_to, attend_bias, merge_to, merge_bias,
    second_gain, second_shift, up_to, up_bias, down_to, down_bias,
    held, quarter, spread, attend, merge, up, down, sems, small,
):
    features = merge.shape[0]
    count = output.shape[0]
    got = [
        pltpu.make_async_copy(quarter_in, quarter, small.at[0]),
        pltpu.make_async_copy(spread_in, spread, small.at[1]),
    ]
    ins, outs = [], []
    for k, (src, to) in enumerate(((output, output_to), (input_grad, input_to))):
        for image in range(count):
            ins.append(pltpu.make_async_copy(src.at[image], held.at[k, image], sems.at[0, k, image]))
            outs.append(pltpu.make_async_copy(held.at[k, image], to.at[image], sems.at[1, k, image]))
    for copy in got + ins:
        copy.start()
    for copy in got:
        copy.wait()
    for s in range(quarter.shape[0]):
        lanes = slice(s * 128, (s + 1) * 128)
        up[:, lanes] = quarter[s, 0].astype(f32)
        down[lanes, :] = quarter[s, 1].astype(f32).T
    block = features + 32
    firsts, seconds, merge_ends = [], [], []
    for k in range(3):
        merge[:, k * 128 : (k + 1) * 128] = spread[0, k * block : k * block + features].astype(f32)
        low = k * block + features
        merge_ends.append(spread[0, low : low + 16].astype(f32))
        seconds.append(spread[0, low + 16 : low + 32].astype(f32))
        total = jnp.zeros((16, 128), f32)
        for pair in range(pairs):
            lanes = slice(k * features + pair * 128, k * features + (pair + 1) * 128)
            attend[:, lanes] = spread[pair + 1, k * block : k * block + features].astype(f32)
            total = total + spread[pair + 1, low + 16 : low + 32].astype(f32)
        firsts.append(total)
    puts = [
        pltpu.make_async_copy(src, to, small.at[2 + k])
        for k, (src, to) in enumerate(((attend, attend_to), (merge, merge_to), (up, up_to), (down, down_to)))
    ]
    for copy in puts:
        copy.start()
    merge_ends, firsts, seconds = (jnp.concatenate(v, axis=1) for v in (merge_ends, firsts, seconds))
    up_bias[...] = bias[0:1, :].reshape(features)
    merge_bias[...] = merge_ends[0:1, :].reshape(features)
    first_gain[...] = firsts[0:1, :].reshape(features)
    first_shift[...] = firsts[1:2, :].reshape(features)
    second_gain[...] = seconds[0:1, :].reshape(features)
    second_shift[...] = seconds[1:2, :].reshape(features)
    down_bias[...] = seconds[2:3, :].reshape(features)
    for to, k in ((0, 0), (1, 2)):
        rows = [
            spread[pair + 1, k * block + features : k * block + features + 16].astype(f32)[0:1, :]
            for pair in range(pairs)
        ]
        attend_bias[to : to + 1, :] = jnp.concatenate(rows, axis=1)
    for copy, on in zip(ins, outs):
        copy.wait()
        on.start()
    for copy in outs + puts:
        copy.wait()


def transfers(quarter, spread, steps, last, late_steps):
    end = last + late_steps
    when = {
        ("quarter", 0): [1, 3, 5, last + 6, end + 0.4],
        ("quarter", 1): [1, 3, 5, last + 6, end + 0.4],
        ("quarter", 2): [1, 4, last, end + 0.1, end + 0.45],
        ("spread", 0): [1, 3, 4, 5, last, last + 2],
        ("spread", 1): [steps + 1, steps + 2, steps + 3, last + 1, last + 4, last + 6],
        ("spread", 2): [2 * steps + 1, last + 1, last + 4, end + 0.2, end + 0.35, end + 0.6],
        ("spread", 3): [last + 1, last + 5, end + 0.3, end + 0.5, end + 0.7],
    }
    plan = []
    for (name, s), times in when.items():
        phases = 5 if name == "quarter" else len(spread.phases(s))
        times = times[:2] + [times[2]] * (phases - len(times)) + times[2:]
        plan += [(time, name, phase + 1, s) for phase, time in enumerate(times)]
    plan.sort(key=lambda item: item[0])
    return [(int(time), *rest) for time, *rest in plan]


def whole(*dims):
    return pl.BlockSpec(dims, lambda i: (0,) * len(dims))


def once(*dims):
    return pl.BlockSpec(dims, lambda i: (0,) * len(dims), pipeline_mode=pl.Buffered(1))


LIVE = pl.BlockSpec(memory_space=pltpu.SMEM)
ANY = pl.BlockSpec(memory_space=pl.ANY)


def params(**more):
    return pltpu.CompilerParams(
        vmem_limit_bytes=60 * 2**20, dimension_semantics=("arbitrary",), **more
    )


def shape(dtype, *dims):
    return jax.ShapeDtypeStruct(dims, dtype)


def shards(
    mesh_sizes, tokens, image_mask, patch_mask, first_gain, first_shift, attend_weight, attend_bias,
    merge_weight, merge_bias, second_gain, second_shift, up_weight, up_bias, down_weight,
    down_bias, cotangent,
):
    n, seq, d = tokens.shape
    packed = attend_weight.shape[1]
    rows = -(-n // 16) * 16
    group = 2 if n % 2 == 0 else 1
    steps = n // group
    width = group * MAIN
    pairs = HEADS // 2
    total = n * MAIN
    left = pl.BlockSpec((n, 16, d), lambda i: (0, MAIN // 16, 0), pipeline_mode=pl.Buffered(1))
    quarters, share = mesh_sizes[1], up_weight.shape[1]

    here = lambda i: jnp.minimum(i, steps - 1)
    cols = lambda r: pl.BlockSpec((r, width), lambda i: (0, here(i)))
    images = lambda *dims: pl.BlockSpec((group, *dims), lambda i: (here(i),) + (0,) * len(dims))
    fi, qkv, probs, edges, invs, lp, lself, att, hid, fil, qkvl, attl, hidl, wall, ball = pl.pallas_call(
        functools.partial(attend_kernel, n, group, steps),
        grid=(steps + 1,),
        in_specs=[
            once(group, MAIN, d),
            pl.BlockSpec((group, MAIN, d), lambda i: (here(i + 1), 0, 0)),
            left, whole(n, MAIN), LIVE, whole(d), whole(d), whole(2, d), whole(d),
            once(d, packed), once(d, d), ANY, whole(share), ANY,
        ],
        out_specs=[
            cols(d + 16), cols(packed), images(HEADS, MAIN, MAIN), images(16, MAIN),
            images(16, MAIN), images(16, MAIN), images(16, 128), cols(d),
            pl.BlockSpec((d, width), lambda i: (0, jnp.maximum(i, 1) - 1)),
            whole(rows, d), whole(rows, packed), whole(rows, d), whole(rows, d), ANY, ANY,
        ],
        out_shape=[
            shape(bf16, d + 16, total), shape(bf16, packed, total), shape(bf16, n, HEADS, MAIN, MAIN),
            shape(f32, n, 16, MAIN), shape(f32, n, 16, MAIN), shape(f32, n, 16, MAIN),
            shape(f32, n, 16, 128), shape(bf16, d, total), shape(f32, d, total),
            shape(f32, rows, d), shape(f32, rows, packed), shape(f32, rows, d), shape(f32, rows, d),
            shape(bf16, quarters, 2, d, share), shape(bf16, quarters, 16, share),
        ],
        scratch_shapes=[
            pltpu.VMEM((packed, d + 128), bf16), pltpu.VMEM((d, d + 128), bf16),
            pltpu.VMEM((d + 128, width), bf16), pltpu.VMEM((d + 128, width), bf16),
            pltpu.VMEM((2, d, 128), f32), pltpu.VMEM((group, 16, MAIN), f32),
            pltpu.VMEM((2, packed, width), bf16),
            pltpu.VMEM((3, d, width), bf16),
            pltpu.VMEM((rows, d), f32), pltpu.VMEM((rows, packed), f32), pltpu.VMEM((rows, d), f32),
            pltpu.VMEM((16, share), bf16), pltpu.SemaphoreType.DMA((9,)), pltpu.SemaphoreType.DMA((9,)),
            pltpu.SemaphoreType.DMA((3,)),
        ],
        compiler_params=params(collective_id=0, has_side_effects=True),
        name="attend",
    )(
        tokens, tokens, tokens, patch_mask, image_mask, first_gain, first_shift, attend_bias, merge_bias,
        attend_weight, merge_weight, up_weight, up_bias, down_weight,
    )

    streams = d // 128
    block = d + 32
    chunk = -(-3 * block // (8 * 16)) * 16
    ahead = lambda i: (i // steps) * (i - steps) + (1 - i // steps) * (i + 1 - (i + 1) // steps)
    late_images = lambda *dims: pl.BlockSpec(
        (group, *dims), lambda i: ((i // steps) * (i - steps),) + (0,) * len(dims)
    )
    late_cols = lambda r: pl.BlockSpec((r, width), lambda i: (0, (i // steps) * (i - steps)))
    quarter_vm = lambda dtype: pltpu.VMEM((streams, 2 * d, 128), dtype)
    output, gh, gml, dots, ghl, gmleft, mine, beside, shared = pl.pallas_call(
        functools.partial(feed_kernel, n, group, steps),
        grid=(2 * steps,),
        in_specs=[
            once(d, width), pl.BlockSpec((d, width), lambda i: (0, ahead(i))), late_cols(d), late_images(16, MAIN),
            once(group, MAIN, d), pl.BlockSpec((group, MAIN, d), lambda i: (ahead(i), 0, 0)), left, LIVE, whole(d), whole(d), whole(d),
            whole(rows, d), whole(rows, d), once(quarters, 2, d, share), once(quarters, 16, share), once(d, d),
        ],
        out_specs=[
            late_images(seq, d), late_cols(d), late_cols(d), late_images(16, MAIN),
            whole(rows, d), whole(rows, d),
            once(streams, 2 * d, 128), once(streams, 2 * d, 128), once(8 * chunk, 128),
        ],
        out_shape=[
            shape(bf16, n, seq, d), shape(f32, d, total), shape(bf16, d, total),
            shape(f32, n, 16, MAIN), shape(f32, rows, d), shape(f32, rows, d),
            shape(bf16, streams, 2 * d, 128), shape(bf16, streams, 2 * d, 128), shape(bf16, 8 * chunk, 128),
        ],
        scratch_shapes=[
            pltpu.VMEM((quarters, share, d + 128), bf16), pltpu.VMEM((quarters, d, share), bf16),
            pltpu.VMEM((steps, d + 128, width), bf16), pltpu.VMEM((d + 128, width), bf16),
            pltpu.VMEM((2 * share, width), bf16), pltpu.VMEM((2 * share, width), bf16),
            pltpu.VMEM((steps, d, width), bf16), pltpu.VMEM((d, width), bf16),
            pltpu.VMEM((3, d, 128), f32), pltpu.VMEM((2, d, 128), f32),
            pltpu.VMEM((rows, d), f32), pltpu.VMEM((rows, d), f32),
            pltpu.VMEM((rows, d + 16), bf16), pltpu.VMEM((rows, d), bf16),
            pltpu.VMEM((quarters, rows, share), bf16), pltpu.VMEM((quarters, rows, share), bf16),
            pltpu.VMEM((steps, d, width), f32), pltpu.VMEM((steps, d, width), f32),
            pltpu.VMEM((d + 16, 2 * share), f32), pltpu.VMEM((d, 2 * share), f32),
            pltpu.VMEM((d + 16, d), f32), pltpu.VMEM((8, d), f32), pltpu.VMEM((8, d), f32),
            quarter_vm(f32), quarter_vm(bf16), quarter_vm(bf16), quarter_vm(bf16), quarter_vm(bf16),
            pltpu.SemaphoreType.DMA((2,)), pltpu.SemaphoreType.DMA((2,)),
        ],
        compiler_params=params(collective_id=1, has_side_effects=True),
        name="feed",
    )(
        hid, hid, att, invs, cotangent, cotangent, cotangent, image_mask, second_gain, second_shift, down_bias, hidl, attl,
        wall, ball, merge_weight,
    )

    late_group, late_steps = group, steps
    group = next(g for g in (7, 2, 1) if n % g == 0)
    steps = n // group
    width = group * MAIN
    last = pairs * steps
    quarter = Quarter(mesh_sizes[0], streams, 2 * d)
    spread = Spread(mesh_sizes, pairs + 1, chunk)
    plan = transfers(quarter, spread, steps, last, late_steps)
    side = lambda i: (i + late_steps) // (last + late_steps)
    early = lambda i: i - side(i) * (i - (last - 1))
    late = lambda i: side(i) * (i - last)
    by_pair = lambda r: pl.BlockSpec((r, width), lambda i: (early(i) // steps, early(i) % steps))
    early_images = lambda *dims: pl.BlockSpec((group, *dims), lambda i: (early(i) % steps,) + (0,) * len(dims))
    pair_lanes = lambda w: pl.BlockSpec((rows, w), lambda i: (0, early(i) // steps))
    late_images = lambda *dims: pl.BlockSpec((late_group, *dims), lambda i: (late(i),) + (0,) * len(dims))
    input_grad, quarter_sum, spread_sum, bias_sum = pl.pallas_call(
        functools.partial(back_kernel, n, group, steps, late_group, late_steps, quarter, spread, plan),
        grid=(last + late_steps,),
        in_specs=[
            by_pair(3 * 128),
            pl.BlockSpec((group, 2, MAIN, MAIN), lambda i: (early(i) % steps, early(i) // steps, 0, 0)),
            early_images(16, MAIN), early_images(16, MAIN), early_images(16, 128), by_pair(128),
            early_images(16, MAIN), ANY,
            whole(rows, d), pair_lanes(384), pair_lanes(128), pair_lanes(128), ANY, ANY, ANY, ANY,
            late_images(MAIN, d), left, pl.BlockSpec((d, late_group * MAIN), lambda i: (0, late(i))),
            whole(rows, d), whole(d), whole(d),
        ],
        out_specs=[
            late_images(seq, d), once(streams, 2, d, 128), once(pairs + 1, 8 * chunk, 128), whole(8, d),
        ],
        out_shape=[
            shape(bf16, n, seq, d), shape(bf16, streams, 2, d, 128), shape(bf16, pairs + 1, 8 * chunk, 128),
            shape(f32, 8, d),
        ],
        scratch_shapes=[
            pltpu.VMEM((steps, packed, width), bf16), pltpu.VMEM((d + 16, 384), f32),
            pltpu.VMEM((pairs, rows, 384), f32), pltpu.VMEM((384, 128), f32),
            pltpu.VMEM((d, packed), bf16), pltpu.VMEM((d, 128), f32),
            pltpu.VMEM((rows, d), f32), pltpu.VMEM((rows, d), f32),
            pltpu.VMEM((steps, d + 16, width), bf16), pltpu.VMEM((streams, 2 * d, 128), bf16),
            pltpu.SemaphoreType.DMA((steps + 2 + 3 * pairs,)),
            *quarter.scratch(), *spread.scratch(),
        ],
        compiler_params=params(collective_id=2, has_side_effects=True),
        name="back",
    )(
        qkv, probs, edges, lp, lself, gml, dots, fi, fil, qkvl, attl, gmleft, attend_weight,
        mine, beside, shared, tokens, tokens, gh, ghl, first_gain, first_shift,
    )
    row = lambda: pl.BlockSpec(memory_space=pltpu.VMEM)
    return pl.pallas_call(
        functools.partial(place_kernel, pairs),
        in_specs=[ANY, ANY, row(), ANY, ANY],
        out_specs=[
            ANY, ANY, row(), row(), ANY, row(), ANY, row(), row(), row(), ANY, row(), ANY, row(),
        ],
        out_shape=[
            shape(bf16, n, seq, d), shape(bf16, n, seq, d), shape(f32, d), shape(f32, d),
            shape(f32, d, packed), shape(f32, 2, d), shape(f32, d, d), shape(f32, d), shape(f32, d),
            shape(f32, d), shape(f32, d, share), shape(f32, share), shape(f32, share, d), shape(f32, d),
        ],
        scratch_shapes=[
            pltpu.VMEM((2, n, seq, d), bf16), pltpu.VMEM((streams, 2, d, 128), bf16),
            pltpu.VMEM((pairs + 1, 8 * chunk, 128), bf16), pltpu.VMEM((d, packed), f32), pltpu.VMEM((d, d), f32),
            pltpu.VMEM((d, share), f32), pltpu.VMEM((share, d), f32),
            pltpu.SemaphoreType.DMA((2, 2, n)), pltpu.SemaphoreType.DMA((6,)),
        ],
        compiler_params=pltpu.CompilerParams(vmem_limit_bytes=60 * 2**20),
        name="place",
    )(quarter_sum, spread_sum, bias_sum, output, input_grad)


def solution(mesh):
    split = ("dp", "tensor")
    in_specs = (
        P(split, None, None), P(split), P(split, None), P(), P(), P(), P(), P(), P(), P(), P(),
        P(None, "tensor"), P("tensor"), P("tensor", None), P(), P(split, None, None),
    )
    out_specs = (
        P(split, None, None), P(split, None, None), P(), P(), P(), P(), P(), P(), P(), P(),
        P(None, "tensor"), P("tensor"), P("tensor", None), P(),
    )
    sizes = (mesh.shape["dp"], mesh.shape["tensor"])
    return jax.shard_map(functools.partial(shards, sizes), mesh=mesh, in_specs=in_specs, out_specs=out_specs, check_vma=False)
```

```python
import functools

import jax
import jax.numpy as jnp
from jax import lax
from jax.experimental import pallas as pl
from jax.experimental.pallas import tpu as pltpu
from jax.sharding import PartitionSpec as P

HEADS = 6
HEAD = 64
MAIN = 256
EPS = 1e-06
MASKED = -1e30
f32, bf16 = jnp.float32, jnp.bfloat16

NN = ((1,), (0,))
NT = ((1,), (1,))
TN = ((0,), (0,))


def dot(left, right, dims=NN):
    return lax.dot_general(left, right, (dims, ((), ())), preferred_element_type=f32)


def rows_where(index, value, rows, dtype):
    columns = value.shape[-1]
    at = lax.broadcasted_iota(jnp.int32, (rows, columns), 0)
    return jnp.where(at == index, value, 0.0).astype(dtype)


def wide(column, width):
    return jnp.concatenate([column] * (width // 128), axis=1)


def as_column(row):
    return jnp.broadcast_to(row, (128, row.shape[1])).T


def norm_columns(values):
    center = values - jnp.mean(values, axis=0, keepdims=True)
    scale = lax.rsqrt(jnp.mean(center * center, axis=0, keepdims=True) + EPS)
    return center * scale, scale


def norm_rows(values):
    center = values - jnp.mean(values, axis=1, keepdims=True)
    scale = lax.rsqrt(jnp.mean(center * center, axis=1, keepdims=True) + EPS)
    return center * scale, scale


def norm_back(grad, normed, scale, axis):
    mean_grad = jnp.mean(grad, axis=axis, keepdims=True)
    mean_both = jnp.mean(grad * normed, axis=axis, keepdims=True)
    return scale * (grad - mean_grad - normed * mean_both)


def gelu_both(pre):
    curve = 0.5 + 0.5 * lax.erf(pre * 0.7071067811865476)
    bell = 0.3989422804014327 * jnp.exp(-0.5 * pre * pre)
    return pre * curve, curve + pre * bell


def head_rows(rows, features):
    at = lax.broadcasted_iota(jnp.int32, (rows, features), 0)
    head = lax.broadcasted_iota(jnp.int32, (rows, features), 1) // HEAD
    return jnp.where(at == head, 1.0, 0.0)


def lane_live(live_ref, first, count):
    flags = [
        jnp.full((1, MAIN), live_ref[first + g].astype(f32)) for g in range(count)
    ]
    return jnp.concatenate(flags, axis=1)


def row_live(live_ref, count, rows):
    at = lax.broadcasted_iota(jnp.int32, (rows, 1), 0)
    flags = jnp.zeros((rows, 1), f32)
    for image in range(count):
        flags = jnp.where(at == image, live_ref[image].astype(f32), flags)
    return flags


def take_left(left_ref, to_ref, count):
    to_ref[...] = jnp.zeros_like(to_ref)
    for image in range(count):
        to_ref[image : image + 1, :] = left_ref[image].astype(f32)[0:1, :]


def flip(place, bits):
    if bits & 1:
        place = place + 1 - 2 * lax.rem(place, 2)
    if bits & 2:
        place = place + 2 - 4 * (place // 2)
    return place


def remote(src, dst, sends, recvs, index, peer):
    return pltpu.make_async_remote_copy(
        src_ref=src, dst_ref=dst, send_sem=sends.at[index], recv_sem=recvs.at[index],
        device_id=peer, device_id_type=pl.DeviceIdType.MESH,
    )


def greet(peers):
    barrier = pltpu.get_barrier_semaphore()
    for peer in peers:
        pl.semaphore_signal(barrier, inc=1, device_id=peer, device_id_type=pl.DeviceIdType.MESH)


def meet(peers):
    pl.semaphore_wait(pltpu.get_barrier_semaphore(), len(peers))


class Quarter:
    def __init__(self, dp, streams, rows):
        self.far = dp // 2
        self.streams, self.half = streams, rows // 2
        self.chunk = -(-self.half // (16 * self.far)) * 16
        self.padded = self.chunk * self.far
        self.copies = 3 + 2 * (self.far - 1)

    def scratch(self):
        s = self.streams
        vm = lambda *dims: pltpu.VMEM((s, *dims, 128), bf16)
        return [
            vm(2 * self.half), vm(2 * self.half), vm(self.half), vm(self.padded),
            vm(max(self.far - 1, 1), self.chunk), vm(2, self.padded),
            pltpu.SemaphoreType.DMA((s, self.copies)), pltpu.SemaphoreType.DMA((s, self.copies)),
        ]

    def bind(self, mine, beside, refs):
        self.mine, self.beside = mine, beside
        self.r1, self.work, self.r2, self.cur, self.r3, self.fin, self.sends, self.recvs = refs
        self.me_dp, self.me_t = lax.axis_index("dp"), lax.axis_index("tensor")
        self.x, self.z = lax.rem(self.me_dp, 2), self.me_dp // 2

    def line(self, j):
        return (lax.rem(self.z + j, self.far) * 2 + self.x, self.me_t)

    def copies_of(self, phase, s):
        across = (self.z * 2 + 1 - self.x, self.me_t)
        cp = lambda index, src, dst, peer: remote(src, dst, self.sends, self.recvs, (s, index), peer)
        if phase == 1:
            return [cp(0, self.beside.at[s], self.r1.at[s], (self.me_dp, flip(self.me_t, 1)))]
        if phase == 2:
            other = pl.ds(pl.multiple_of((1 - self.x) * self.half, 16), self.half)
            return [cp(1, self.work.at[s, other], self.r2.at[s], across)]
        found = []
        if phase == 3:
            for j in range(1, self.far):
                place = lax.rem(self.z + j, self.far)
                src = self.cur.at[s, pl.ds(pl.multiple_of(place * self.chunk, 16), self.chunk)]
                found.append(cp(1 + j, src, self.r3.at[s, j - 1], self.line(j)))
        if phase == 4:
            ref = self.fin.at[s, self.x, pl.ds(pl.multiple_of(self.z * self.chunk, 16), self.chunk)]
            for j in range(1, self.far):
                found.append(cp(self.far + j, ref, ref, self.line(j)))
        if phase == 5:
            ref = self.fin.at[s, self.x, pl.ds(0, self.half)]
            found.append(cp(2 * self.far, ref, ref, across))
        return found

    def start(self, phase, s):
        for copy in self.copies_of(phase, s):
            copy.start()

    def advance(self, phase, s):
        for copy in self.copies_of(phase, s):
            copy.wait()
        if phase == 1:
            self.work[s] = (self.mine[s].astype(f32) + self.r1[s].astype(f32)).astype(bf16)
        if phase == 2:
            kept = self.work[s, pl.ds(pl.multiple_of(self.x * self.half, 16), self.half)]
            self.cur[s, : self.half] = (kept.astype(f32) + self.r2[s].astype(f32)).astype(bf16)
            if self.padded > self.half:
                self.cur[s, self.half :] = jnp.zeros((self.padded - self.half, 128), bf16)
        if phase == 3:
            mine = pl.ds(pl.multiple_of(self.z * self.chunk, 16), self.chunk)
            total = self.cur[s, mine].astype(f32)
            for j in range(self.far - 1):
                total = total + self.r3[s, j].astype(f32)
            self.fin[s, self.x, mine] = total.astype(bf16)
        if phase < 5:
            self.start(phase + 1, s)


class Spread:
    def __init__(self, mesh_sizes, streams, chunk):
        self.dp, self.tensor = mesh_sizes
        self.far = self.dp // 2
        self.hops = self.far.bit_length() - 1
        self.streams, self.chunk = streams, chunk
        self.copies = 1 + 3 + (self.far - 1) + 3 + 1

    def phases(self, s):
        hops = ["line"] if s == self.streams - 1 else [("hop", k) for k in range(self.hops)]
        return ["core", "plane", *hops, "plane back", "core back"]

    def scratch(self):
        s, c = self.streams, self.chunk
        vm = lambda *dims: pltpu.VMEM((s, *dims, 128), bf16)
        return [
            vm(8 * c), vm(4 * c), vm(4 * c), vm(3, c), vm(self.far, c), vm(c), vm(8 * c),
            pltpu.SemaphoreType.DMA((s, self.copies)), pltpu.SemaphoreType.DMA((s, self.copies)),
        ]

    def bind(self, refs):
        self.send, self.r1, self.work, self.r2, self.r3, self.cur, self.out, self.ss, self.rs = refs
        self.me_dp, self.me_t = lax.axis_index("dp"), lax.axis_index("tensor")
        self.x, self.z = lax.rem(self.me_dp, 2), self.me_dp // 2
        self.c, self.y = lax.rem(self.me_t, 2), self.me_t // 2
        self.place = 2 * self.y + self.x

    def plane(self, j):
        x = 1 - self.x if j & 1 else self.x
        y = 1 - self.y if j & 2 else self.y
        return (self.z * 2 + x, 2 * y + self.c), 2 * y + x

    def core(self):
        return (self.me_dp, 2 * self.y + 1 - self.c)

    def line(self, j):
        return (lax.rem(self.z + j, self.far) * 2 + self.x, self.me_t)

    def hop(self, k):
        step = 1 << k
        there = self.z + step - 2 * step * lax.rem(self.z // step, 2)
        return (there * 2 + self.x, self.me_t)

    def rows(self, first, count):
        return pl.ds(pl.multiple_of(first * self.chunk, 16), count * self.chunk)

    def copies_of(self, kind, s):
        cp = lambda index, src, dst, peer: remote(src, dst, self.ss, self.rs, (s, index), peer)
        if kind == "core":
            return [cp(0, self.send.at[s, self.rows(4 * (1 - self.c), 4)], self.r1.at[s], self.core())]
        found = []
        if kind == "plane":
            for j in (1, 2, 3):
                peer, place = self.plane(j)
                found.append(cp(j, self.work.at[s, self.rows(place, 1)], self.r2.at[s, j - 1], peer))
        if kind == "line":
            for j in range(1, self.far):
                ref = self.r3.at[s, self.z]
                found.append(cp(3 + j, ref, ref, self.line(j)))
        if kind[0] == "hop":
            found.append(cp(4 + kind[1], self.cur.at[s], self.r3.at[s, kind[1]], self.hop(kind[1])))
        if kind == "plane back":
            mine = self.out.at[s, self.rows(4 * self.c + self.place, 1)]
            for j in (1, 2, 3):
                found.append(cp(2 + self.far + j, mine, mine, self.plane(j)[0]))
        if kind == "core back":
            ref = self.out.at[s, self.rows(4 * self.c, 4)]
            found.append(cp(6 + self.far, ref, ref, self.core()))
        return found

    def start(self, kind, s):
        for copy in self.copies_of(kind, s):
            copy.start()

    def advance(self, phase, s):
        phases = self.phases(s)
        kind = phases[phase - 1]
        for copy in self.copies_of(kind, s):
            copy.wait()
        mine = self.rows(4 * self.c + self.place, 1)
        if kind == "core":
            half = self.send[s, self.rows(4 * self.c, 4)].astype(f32)
            self.work[s] = (half + self.r1[s].astype(f32)).astype(bf16)
        if kind == "plane":
            total = self.work[s, self.rows(self.place, 1)].astype(f32)
            for j in range(3):
                total = total + self.r2[s, j].astype(f32)
            if phases[2] == "line":
                self.r3[s, self.z] = total.astype(bf16)
            else:
                self.cur[s] = total.astype(bf16)
        if kind == "line":
            total = self.r3[s, 0].astype(f32)
            for j in range(1, self.far):
                total = total + self.r3[s, j].astype(f32)
            self.out[s, mine] = total.astype(bf16)
        if kind[0] == "hop":
            total = (self.cur[s].astype(f32) + self.r3[s, kind[1]].astype(f32)).astype(bf16)
            self.cur[s] = total
            if kind[1] == self.hops - 1:
                self.out[s, mine] = total
        if phase < len(phases):
            self.start(phases[phase], s)


def row_of(ref):
    return ref[...].astype(f32).reshape(1, ref.shape[0])


def parts_of(at, pair):
    return slice(pair * 384 + at * 128, pair * 384 + (at + 1) * 128)


def attend_kernel(
    count, group, steps,
    tok0, tok, left, pmask, live, gain, shift, abias, mbias, aw, mw, up, ubias, down,
    fi_out, qkv_out, probs_out, edge_out, inv_out, lp_out, lself_out, att_out, hid_out,
    fil_out, qkvl_out, attl_out, hidl_out, wall, ball,
    awt, mwt, fia, atta, cols, edges, qkv2, toks, xl, qkvl, attl, brow, sends, recvs, own,
):
    step = pl.program_id(0)
    me_dp, me_t = lax.axis_index("dp"), lax.axis_index("tensor")
    beside, across = (me_dp, flip(me_t, 1)), (me_dp, flip(me_t, 2))

    def places(owner):
        return (wall.at[owner, 0], wall.at[owner, 1], ball.at[owner])

    def first_copies(peer, first):
        return [
            remote(src, dst, sends, recvs, first + k, peer)
            for k, (src, dst) in enumerate(zip((up, down, brow), places(me_t)))
        ]

    def second_copies():
        return [
            remote(ref, ref, sends, recvs, 6 + k, beside) for k, ref in enumerate(places(flip(me_t, 2)))
        ]

    def own_copies():
        return [
            pltpu.make_async_copy(src, dst, own.at[k])
            for k, (src, dst) in enumerate(zip((up, down, brow), places(me_t)))
        ]

    @pl.when(step == 0)
    def _():
        greet((beside, across))
        brow[...] = rows_where(0, row_of(ubias), 16, bf16)
        meet((beside, across))
        for copy in first_copies(across, 3) + first_copies(beside, 0) + own_copies():
            copy.start()

    @pl.when(step == steps - 2)
    def _():
        for copy in first_copies(across, 3):
            copy.wait()
        for copy in second_copies():
            copy.start()

    features = aw.shape[0]
    packed = aw.shape[1]
    rows = xl.shape[0]
    width = group * MAIN
    pairs = HEADS // 2
    heads = head_rows(rows, features)

    def first_norm(block):
        tokens = jnp.concatenate([block[g].T for g in range(group)], axis=1)
        normed, _ = norm_columns(tokens.astype(f32))
        return tokens, (normed * wide(cols[0], width) + wide(cols[1], width)).astype(bf16)

    def project(slot, part):
        span = slice(part * features, (part + 1) * features)
        qkv2[slot, span, :] = dot(awt[span, :], fia[...]).astype(bf16)

    @pl.when(step == 0)
    def _():
        ab = abias[...].astype(f32)
        for pair in range(pairs):
            for at in range(3):
                cut = slice(at * features + pair * 128, at * features + (pair + 1) * 128)
                to = parts_of(at, pair)
                scale = HEAD**-0.5 if at == 0 else 1.0
                awt[to, :features] = (aw[:, cut].astype(f32).T * scale).astype(bf16)
                if at == 1:
                    bias = jnp.zeros((1, 128), f32)
                else:
                    bias = ab[at // 2 : at // 2 + 1, pair * 128 : (pair + 1) * 128] * scale
                awt[to, features:] = rows_where(0, bias, 128, f32).T.astype(bf16)
        mwt[:, :features] = mw[...].astype(f32).T.astype(bf16)
        mwt[:, features:] = rows_where(0, row_of(mbias), 128, f32).T.astype(bf16)
        ones = rows_where(0, jnp.ones((1, fia.shape[1]), f32), 128, bf16)
        fia[features:, :] = ones
        atta[features:, :] = ones
        cols[0] = as_column(row_of(gain))
        cols[1] = as_column(row_of(shift))
        edges[...] = jnp.zeros_like(edges)
        take_left(left, xl, count)
        normed, _ = norm_rows(xl[...])
        fil = (normed * row_of(gain) + row_of(shift)).astype(bf16)
        fil_out[...] = fil.astype(f32)
        plain = dot(fil, aw[...])
        for pair in range(pairs):
            for at in range(3):
                cut = slice(at * features + pair * 128, at * features + (pair + 1) * 128)
                value = plain[:, cut]
                if at != 1:
                    value = value + ab[at // 2 : at // 2 + 1, pair * 128 : (pair + 1) * 128]
                value = value.astype(bf16).astype(f32)
                qkvl[:, parts_of(at, pair)] = value * (HEAD**-0.5) if at == 0 else value
        qkvl_out[...] = qkvl[...]
        attl[...] = jnp.zeros_like(attl)
        tokens, fi = first_norm(tok0)
        toks[0] = tokens
        fia[:features, :] = fi
        for part in range(3):
            project(0, part)

    def merge_branch():
        return dot(mwt[...], atta[...])

    def hidden_of(branch, index):
        tokens = toks[lax.rem(index, 3)].astype(f32)
        return tokens + lane_live(live, index * group, group) * branch

    @pl.when(step < steps)
    def _():
        now, later = lax.rem(step, 2), lax.rem(step + 1, 2)
        one_row = rows_where(0, jnp.ones((1, MAIN), f32), 16, bf16)
        held = {}
        units = [(g, h) for g in range(group) for h in range(HEADS)]

        def lanes_of(g):
            return slice(g * MAIN, (g + 1) * MAIN)

        def part(at, g, h):
            low = (h // 2) * 384 + at * 128 + (h % 2) * HEAD
            return qkv2[now, low : low + HEAD, lanes_of(g)]

        def all_heads(at, g):
            return jnp.concatenate(
                [qkv2[now, parts_of(at, pair), lanes_of(g)] for pair in range(pairs)], axis=0
            )

        def begin(g):
            image = step * group + g
            row = qkvl[pl.ds(image, 1), :]
            ql, kl, vl = (
                jnp.concatenate([row[:, parts_of(at, pair)] for pair in range(pairs)], axis=1)
                for at in range(3)
            )
            key_bias = jnp.where(pmask[pl.ds(image, 1), :] == 1, 0.0, MASKED)
            moved = pltpu.roll(key_bias, 1, axis=1)
            at = lax.broadcasted_iota(jnp.int32, moved.shape, 1)
            main_bias = jnp.where(at == 0, 0.0, moved)
            left_bias = moved[:, 0:1]
            held["bias", g] = rows_where(0, main_bias, 16, bf16)
            held["vl", g] = vl
            held["slk", g] = dot((heads * kl).astype(bf16), all_heads(0, g)) + left_bias
            held["sl", g] = dot((heads * ql).astype(bf16), all_heads(1, g)) + main_bias
            held["self", g] = jnp.sum(heads * (ql * kl), axis=1, keepdims=True) + left_bias

        def left_query(g):
            sl, self_score = held.pop(("sl", g)), held.pop(("self", g))
            peak = jnp.maximum(jnp.max(sl, axis=1, keepdims=True), self_score)
            raised = jnp.exp(sl - peak)
            raised_self = jnp.exp(self_score - peak)
            inv = 1.0 / (jnp.sum(raised, axis=1, keepdims=True) + raised_self)
            lp = raised * inv
            lself = raised_self * inv
            lp_out[g] = lp
            lself_out[g] = jnp.broadcast_to(lself, (rows, 128))
            mixed = dot(lp.astype(bf16), all_heads(2, g), NT) + lself * held["vl", g]
            image = step * group + g
            attl[pl.ds(image, 1), :] = (
                jnp.sum(mixed * heads, axis=0, keepdims=True).astype(bf16).astype(f32)
            )

        def scores(g, h):
            held["s", g, h] = dot(
                jnp.concatenate([part(1, g, h), held["bias", g]], axis=0),
                jnp.concatenate([part(0, g, h), one_row], axis=0),
                TN,
            )

        def soften(g, h):
            value = held.pop(("s", g, h))
            slk = held["slk", g][h : h + 1, :]
            peak = jnp.maximum(jnp.max(value, axis=0, keepdims=True), slk)
            raised = jnp.exp(value - peak).astype(bf16)
            probs_out[g, h] = raised
            held["e", g, h] = raised
            edge = jnp.exp(slk - peak)
            held["edge", g, h] = edge
            edges[g, h : h + 1, :] = edge

        def mix(g, h):
            held["o", g, h] = dot(
                jnp.concatenate([part(2, g, h), one_row], axis=0), held.pop(("e", g, h))
            )

        def add_left(g):
            edge_out[g] = edges[g]
            held["add", g] = dot((heads * held["vl", g]).astype(bf16), edges[g].astype(bf16), TN)

        def finish(g, h):
            out = held.pop(("o", g, h))
            span = slice(h * HEAD, (h + 1) * HEAD)
            inv = 1.0 / (out[HEAD : HEAD + 1, :] + held["edge", g, h])
            inv_out[g, h : h + 1, :] = inv
            mixed = ((out[:HEAD, :] + held["add", g][span]) * inv).astype(bf16)
            atta[span, lanes_of(g)] = mixed
            att_out[span, lanes_of(g)] = mixed

        count_units = len(units)
        for t in range(-2, count_units + 4):
            if t + 2 == 0:
                for g in range(group):
                    begin(g)
                held["branch"] = merge_branch()
            if 0 <= t + 2 < count_units:
                scores(*units[t + 2])
            if t == -1:
                hid_out[...] = hidden_of(held.pop("branch"), step - 1 + 3 * (1 - jnp.minimum(step, 1)))
                qkv_out[...] = qkv2[now]
                fi_out[:features, :] = fia[:features, :]
                fi_out[features:, :] = fia[features : features + 16, :]
                held["next"] = first_norm(tok)
            if t == 1:
                tokens, fi = held.pop("next")
                toks[lax.rem(step + 1, 3)] = tokens
                fia[:features, :] = fi
            if t in (5, 7, 9):
                project(later, (t - 5) // 2)
            if 0 <= t < count_units:
                soften(*units[t])
            if 0 <= t - 2 < count_units:
                mix(*units[t - 2])
            for g in range(group):
                if t == HEADS * g + 3:
                    left_query(g)
                if t == HEADS * (g + 1):
                    add_left(g)
                if t == HEADS * (g + 1) + 3:
                    for h in range(HEADS):
                        finish(g, h)

    @pl.when(step == steps)
    def _():
        hid_out[...] = hidden_of(merge_branch(), step - 1)
        attl_out[...] = attl[...]
        branch = dot(attl[...].astype(bf16), mw[...]) + row_of(mbias)
        hidl_out[...] = xl[...] + row_live(live, count, rows) * branch
        for copy in first_copies(beside, 0) + second_copies() + own_copies():
            copy.wait()


def feed_kernel(
    count, group, steps,
    hid0, hid, att, inv, cot0, cot, cleft, live, gain, shift, dbias, hidl, attl, wall, ball, mw,
    out, gh_out, gml_out, dots_out, ghl_out, gmleft_out, mine, beside, shared,
    upt, dnt, sia, atta, act, gpre, gb, gattn, cols, gsum, xl, outl, sil, gbl, actl, gprel,
    outp, gradp, up_acc, down_acc, merge_acc, sums, biases, kept, away, r1, across, r2, sends, recvs,
):
    step = pl.program_id(0)
    at_step = lax.rem(step, steps)
    second = step // steps
    features = mw.shape[0]
    rows = xl.shape[0]
    width = group * MAIN
    quarters = wall.shape[0]
    me_dp, me_t = lax.axis_index("dp"), lax.axis_index("tensor")
    core, chip = (me_dp, flip(me_t, 1)), (me_dp, flip(me_t, 2))
    first_of = (1 - second) * flip(me_t, 2) + second * me_t
    now = (first_of, flip(first_of, 1))

    def to_core():
        return remote(away, r1, sends, recvs, 0, core)

    def to_chip():
        return remote(across, r2, sends, recvs, 1, chip)

    @pl.when(step == 0)
    def _():
        greet((core, chip))
        gain_row, shift_row, dbias_row = row_of(gain), row_of(shift), row_of(dbias)
        for q in range(quarters):
            upt[q, :, :features] = wall[q, 0].astype(f32).T.astype(bf16)
            upt[q, :, features:] = rows_where(0, ball[q, 0:1, :].astype(f32), 128, f32).T.astype(bf16)
            dnt[q] = wall[q, 1].astype(f32).T.astype(bf16)
        ones = rows_where(0, jnp.ones((1, width), f32), 128, bf16)
        for k in range(steps):
            sia[k, features:, :] = ones
        atta[features:, :] = ones
        cols[0] = as_column(gain_row)
        cols[1] = as_column(shift_row)
        cols[2] = as_column(dbias_row)
        gsum[...] = jnp.zeros_like(gsum)
        biases[...] = jnp.zeros_like(biases)
        take_left(cleft, xl, count)
        alive = row_live(live, count, rows)
        normed, scale = norm_rows(hidl[...])
        si = (normed * gain_row + shift_row).astype(bf16)
        grad_branch = (alive * xl[...]).astype(bf16)
        total = hidl[...] + alive * dbias_row
        grad_second = jnp.zeros_like(total)
        pre_of = [dot(si, wall[q, 0]) + ball[q, 0:1, :].astype(f32) for q in range(quarters)]
        grad_of = [dot(grad_branch, wall[q, 1], NT) for q in range(quarters)]
        for q in range(quarters):
            value, slope = gelu_both(pre_of[q])
            actl[q] = value.astype(bf16)
            gprel[q] = (grad_of[q] * slope).astype(bf16)
        for q in range(quarters):
            total = total + alive * dot(actl[q], wall[q, 1])
            grad_second = grad_second + dot(gprel[q], wall[q, 0], NT)
        outl[...] = total
        grad_hidden = xl[...] + norm_back(grad_second * gain_row, normed, scale, 1)
        ghl_out[...] = grad_hidden
        grad_attn = (alive * grad_hidden).astype(bf16)
        gmleft_out[...] = dot(grad_attn, mw[...], NT).astype(bf16).astype(f32)
        one = jnp.ones((rows, 16), f32)
        sil[...] = jnp.concatenate([si.astype(f32), one], axis=1).astype(bf16)
        gbl[...] = grad_branch
        merge_acc[...] = dot(jnp.concatenate([attl[...], one], axis=1).astype(bf16), grad_attn, TN)
        sums[...] = jnp.zeros_like(sums)
        sums[0:1, :] = jnp.sum(grad_second * normed, axis=0, keepdims=True)
        sums[1:2, :] = jnp.sum(grad_second, axis=0, keepdims=True)
        sums[2:3, :] = jnp.sum(grad_branch.astype(f32), axis=0, keepdims=True)
        meet((core, chip))

    @pl.when(at_step == 0)
    def _():
        for c, q in enumerate(now):
            lanes = slice(c * features, (c + 1) * features)
            up_acc[:, lanes] = dot(sil[...], gprel[q], TN)
            down_acc[:, lanes] = dot(gbl[...], actl[q], TN)

    def rounded(ref, lanes, at):
        lanes = slice(lanes + at * 128, lanes + (at + 1) * 128)
        return jnp.concatenate([up_acc[:features, lanes], down_acc[:, lanes]], axis=0)

    @pl.when(step == steps + 1)
    def _():
        to_core().wait()
        for at in range(kept.shape[0]):
            across[at] = (kept[at] + r1[at].astype(f32)).astype(bf16)
        to_chip().start()

    pres, grads = {}, {}
    lanes_of = [slice(g * MAIN, (g + 1) * MAIN) for g in range(group)]

    def enter(hidden, cotangent, to):
        normed, _ = norm_columns(hidden[...])
        sia[to, :features, :] = (normed * wide(cols[0], width) + wide(cols[1], width)).astype(bf16)
        alive = lane_live(live, to * group, group)
        turned = jnp.concatenate([cotangent[g].T for g in range(group)], axis=1).astype(f32)
        gb[to] = (turned * alive).astype(bf16)

    def into(g):
        for c in range(2):
            pres[g, c] = dot(upt[now[c]], sia[at_step, :, lanes_of[g]])
            grads[g, c] = dot(wall[now[c], 1], gb[at_step, :, lanes_of[g]])

    def through(g):
        for c in range(2):
            span = slice(c * features, (c + 1) * features)
            value, slope = gelu_both(pres.pop((g, c)))
            act[span, lanes_of[g]] = value.astype(bf16)
            gpre[span, lanes_of[g]] = (grads.pop((g, c)) * slope).astype(bf16)

    def both_of(ref, *more):
        return jnp.concatenate([ref[(q, *more)] for q in now], axis=1)

    def second_sum(g):
        return dot(both_of(wall, 0), gpre[:, lanes_of[g]])

    def output_sum(g):
        return dot(both_of(dnt), act[:, lanes_of[g]])

    def up_product():
        up_acc[...] += dot(sia[at_step, : up_acc.shape[0], :], gpre[...], NT)

    def down_product():
        down_acc[...] += dot(gb[at_step], act[...], NT)

    @pl.when(step == 0)
    def _():
        enter(hid0, cot0, 0)

    @pl.when(second == 0)
    def _():
        for g in range(group):
            into(g)
        for g in range(group):
            through(g)
            gradp[at_step, :, lanes_of[g]] = second_sum(g)
            outp[at_step, :, lanes_of[g]] = output_sum(g)
        up_product()
        enter(hid, cot, at_step + 1 - (at_step + 1) // steps)
        down_product()

    @pl.when(second == 1)
    def _():
        held = {}
        for g in range(group):
            into(g)
        for g in range(group):
            hidden = hid[:, lanes_of[g]]
            held["norm", g] = norm_columns(hidden)
            held["cot", g] = cot[g].T.astype(f32)
        for g in range(group):
            through(g)
            held["second", g] = gradp[at_step, :, lanes_of[g]] + second_sum(g)
            held["out", g] = outp[at_step, :, lanes_of[g]] + output_sum(g)

        def back(g):
            grad_second = held["second", g]
            normed, scale = held["norm", g]
            grad = held["cot", g] + norm_back(grad_second * wide(cols[0], MAIN), normed, scale, 0)
            gh_out[:, lanes_of[g]] = grad
            alive = live[at_step * group + g].astype(f32)
            gattn[:, lanes_of[g]] = (alive * grad).astype(bf16)
            both = grad_second * normed
            for at in range(0, MAIN, 128):
                gsum[0] += both[:, at : at + 128]
                gsum[1] += grad_second[:, at : at + 128]

        def write(g):
            image = at_step * group + g
            alive = live[image].astype(f32)
            result = hid[:, lanes_of[g]] + alive * (held["out", g] + wide(cols[2], MAIN))
            out[g, :MAIN, :] = result.astype(bf16).T
            out[g, MAIN : MAIN + 1, :] = outl[pl.ds(image, 1), :].astype(bf16)

        def scale_rows(g):
            mixed = held["mixed", g].astype(bf16).astype(f32)
            both = mixed * att[:, lanes_of[g]].astype(f32)
            for h in range(HEADS):
                span = slice(h * HEAD, (h + 1) * HEAD)
                row_inv = inv[g, h : h + 1, :]
                gml_out[span, lanes_of[g]] = (mixed[span] * row_inv).astype(bf16)
                row_dot = jnp.sum(both[span], axis=0, keepdims=True) * row_inv
                dots_out[g, h : h + 1, :] = row_dot

        dots_out[...] = jnp.zeros_like(dots_out)
        atta[:features, :] = att[...]
        back(0)
        up_product()
        for g in range(1, group):
            back(g)
        for g in range(group):
            held["mixed", g] = dot(mw[...], gattn[:, lanes_of[g]])
        down_product()
        for g in range(group):
            scale_rows(g)
        merge_acc[...] += dot(atta[: merge_acc.shape[0], :], gattn[...], NT)
        sums[2:3, :] += dot(jnp.ones((16, width), bf16), gb[at_step], NT)[0:1, :]
        for g in range(group):
            write(g)

    @pl.when(at_step == steps - 1)
    def _():
        for c, q in enumerate(now):
            biases[pl.ds(q, 1), :] = up_acc[features : features + 1, c * features : (c + 1) * features]

    @pl.when(step == steps - 1)
    def _():
        for at in range(kept.shape[0]):
            kept[at] = rounded(up_acc, 0, at)
            away[at] = rounded(up_acc, features, at).astype(bf16)
        to_core().start()

    @pl.when(step == 2 * steps - 1)
    def _():
        sums[0:1, :] += jnp.sum(gsum[0].T, axis=0, keepdims=True)
        sums[1:2, :] += jnp.sum(gsum[1].T, axis=0, keepdims=True)
        ends = jnp.concatenate([sums[...], biases[...]], axis=0)
        merged = jnp.concatenate([merge_acc[:features, :], merge_acc[features : features + 16, :], ends], axis=0)
        for at in range(features // 128):
            block = merged.shape[0]
            shared[at * block : (at + 1) * block] = merged[:, at * 128 : (at + 1) * 128].astype(bf16)
        rest = shared.shape[0] - (features // 128) * merged.shape[0]
        if rest:
            shared[shared.shape[0] - rest :] = jnp.zeros((rest, 128), bf16)
        for at in range(kept.shape[0]):
            beside[at] = rounded(up_acc, features, at).astype(bf16)
        to_chip().wait()
        for at in range(kept.shape[0]):
            mine[at] = (rounded(up_acc, 0, at) + r2[at].astype(f32)).astype(bf16)


def back_kernel(
    count, group, steps, late_group, late_steps, quarter, spread, plan,
    qkv, probs, edge, lp, lself, gml, dots, fi, fil, qkvl, attl, gmleft, aw, mine, beside, shared,
    tok, left, gh, ghl, gain, shift,
    out, quarter_out, spread_out, bias_out,
    gpa, acc, gpl, gplt, awp, cols, xl, outl, fis, minev, own, *comm,
):
    step = pl.program_id(0)
    features = aw.shape[0]
    rows = xl.shape[0]
    pairs = HEADS // 2
    last = pairs * steps
    pair = lax.rem(step // steps, pairs)
    at_group = lax.rem(step, steps)
    used = len(quarter.scratch())
    quarter.bind(minev, beside, comm[:used])
    spread.bind(comm[used:])
    engines = {"quarter": quarter, "spread": spread}
    at = lax.broadcasted_iota(jnp.int32, (rows, 128), 0)
    heads = jnp.where(at == lax.broadcasted_iota(jnp.int32, (rows, 128), 1) // HEAD, 1.0, 0.0)

    def fi_copy(k):
        width = group * MAIN
        return pltpu.make_async_copy(fi.at[:, pl.ds(k * width, width)], fis.at[k], own.at[k])

    def shared_copy():
        return pltpu.make_async_copy(shared, spread.send.at[0], own.at[steps])

    def early_copies():
        found = [pltpu.make_async_copy(mine, minev, own.at[steps + 1])]
        for part in range(pairs):
            for k in range(3):
                cut = pl.ds(k * features + part * 128, 128)
                to = pl.ds(part * 384 + k * 128, 128)
                sem = own.at[steps + 2 + part * 3 + k]
                found.append(pltpu.make_async_copy(aw.at[:, cut], awp.at[:, to], sem))
        return found

    @pl.when(step == 0)
    def _():
        peers = [
            (quarter.me_dp, flip(quarter.me_t, 1)), *(spread.plane(j)[0] for j in (1, 2, 3)),
            *(spread.line(j) for j in range(1, spread.far)),
        ]
        greet(peers)
        shared_copy().start()
        for copy in early_copies():
            copy.start()
        for k in range(steps):
            fi_copy(k).start()
        cols[...] = as_column(row_of(gain))
        gpl[...] = jnp.zeros_like(gpl)
        gplt[...] = jnp.zeros_like(gplt)
        acc[...] = jnp.zeros_like(acc)
        meet(peers)
        for s in range(quarter.streams):
            quarter.start(1, s)
        shared_copy().wait()
        spread.start("core", 0)

    for k in range(steps):
        pl.when(step == k)(lambda k=k: fi_copy(k).wait())

    @pl.when(step == 1)
    def _():
        for copy in early_copies():
            copy.wait()

    def advance(slot):
        for at, name, phase, s in plan:
            if at == slot:
                engines[name].advance(phase, s)

    for slot in sorted({item[0] for item in plan if item[0] < last + late_steps}):
        pl.when(step == slot)(functools.partial(advance, slot))

    @pl.when(step < last)
    def _():
        at16 = lax.broadcasted_iota(jnp.int32, (16, MAIN), 0)
        minus = jnp.where(at16 < 2, -1.0, 0.0).astype(bf16)
        ends_row = jnp.where(lax.broadcasted_iota(jnp.int32, (1, 16), 1) < 2, -1.0, 0.0)
        gp = gpa.at[at_group, pl.ds(pl.multiple_of(pair * 384, 128), 384)]
        held = {}
        units = [(g, r) for g in range(group) for r in range(2)]

        def lanes_of(g):
            return slice(g * MAIN, (g + 1) * MAIN)

        def part(at, r, g):
            return qkv[at * 128 + r * HEAD : at * 128 + (r + 1) * HEAD, lanes_of(g)]

        def lower(value):
            return value.astype(bf16).astype(f32)

        def prepare(g):
            image = at_group * group + g
            row = qkvl[pl.ds(image, 1), :]
            ql, kl, vl = (row[:, at * 128 : (at + 1) * 128] for at in range(3))
            gm_row = gmleft[pl.ds(image, 1), :]
            row_dot = jnp.sum(heads * (gm_row * attl[pl.ds(image, 1), :]), axis=1, keepdims=True)
            prob = jnp.sum(heads * (gm_row * vl), axis=1, keepdims=True)
            held["cols", g] = tuple(as_column(v) for v in (ql, kl, gm_row))
            held["left", g] = (vl, row_dot, prob - row_dot)

        def change(g, r):
            row_dot = dots[g, pl.ds(2 * pair + r, 1), :]
            high = row_dot.astype(bf16).astype(f32)
            rest = jnp.where(at16 == 0, high, jnp.where(at16 == 1, row_dot - high, 0.0)).astype(bf16)
            values = jnp.concatenate([part(2, r, g), minus], axis=0).T
            vl = held["left", g][0][:, r * HEAD : (r + 1) * HEAD]
            last_row = rows_where(0, jnp.concatenate([vl, ends_row], axis=1), 16, bf16)
            held["z", g, r] = dot(
                jnp.concatenate([values, last_row], axis=0),
                jnp.concatenate([gml[r * HEAD : (r + 1) * HEAD, lanes_of(g)], rest], axis=0),
            )

        def left_unit(g, r, edge_change):
            image = at_group * group + g
            span = slice(r * HEAD, (r + 1) * HEAD)
            head = pl.ds(2 * pair + r, 1)
            colq, colk, colg = (wide(v[span], MAIN) for v in held["cols", g])
            _, row_dot, self_change = held["left", g]
            row_dot, self_change = row_dot[r : r + 1, :], self_change[r : r + 1, :]
            edge_row, lp_row, self_prob = edge[g, head, :], lp[g, head, :], lself[g, head, 0:1]
            edge_grad = lower(edge_row * edge_change)
            left_change = jnp.sum(colg * part(2, r, g).astype(f32), axis=0, keepdims=True) - row_dot
            left_grad = lower(lp_row * left_change)
            self_grad = lower(self_prob * self_change)
            held["add", g, r] = (colk * edge_grad, colq * left_grad, colg * lower(lp_row))
            grad_q = jnp.sum(part(1, r, g).astype(f32) * left_grad, axis=1, keepdims=True)
            grad_k = jnp.sum(part(0, r, g).astype(f32) * edge_grad, axis=1, keepdims=True)
            grad_v = jnp.sum(
                gml[span, lanes_of(g)].astype(f32) * lower(edge_row), axis=1, keepdims=True
            )
            values = (
                (grad_q + self_grad * colk[:, 0:1]) * HEAD**-0.5,
                grad_k + self_grad * colq[:, 0:1],
                grad_v + lower(self_prob) * colg[:, 0:1],
            )
            at = lax.broadcasted_iota(jnp.int32, (HEAD, 128), 1)
            for k, value in enumerate(values):
                to = slice(k * 128 + r * HEAD, k * 128 + (r + 1) * HEAD)
                gplt[to, :] = jnp.where(at == image, lower(value), gplt[to, :])

        def scores(g, r):
            raised = probs[g, r]
            value = held.pop(("z", g, r))
            held["ds", g, r] = (raised.astype(f32) * value[:MAIN]).astype(bf16)
            left_unit(g, r, value[MAIN : MAIN + 1])
            held["v", g, r] = dot(gml[r * HEAD : (r + 1) * HEAD, lanes_of(g)], raised, NT)

        def grads(g, r):
            ds = held.pop(("ds", g, r))
            held["q", g, r] = dot(part(1, r, g), ds)
            held["k", g, r] = dot(part(0, r, g), ds, NT)

        def store(g, r):
            span = slice(r * HEAD, (r + 1) * HEAD)
            add_q, add_k, add_v = held.pop(("add", g, r))
            values = (
                (held.pop(("q", g, r)) + add_q) * HEAD**-0.5,
                held.pop(("k", g, r)) + add_k,
                held.pop(("v", g, r)) + add_v,
            )
            for at, value in enumerate(values):
                gp[at * 128 + r * HEAD : at * 128 + (r + 1) * HEAD, lanes_of(g)] = value.astype(bf16)

        number = len(units)
        thirds = sorted({0, -(-group // 3), -(-2 * group // 3), group})
        cuts = list(zip(thirds[:-1], thirds[1:]))

        def add_product(low, high):
            lanes = slice(low * MAIN, high * MAIN)
            before = jnp.where(at_group == 0, 0.0, acc[...]) if low == 0 else acc[...]
            acc[...] = before + dot(fis[at_group, :, lanes], gp[:, lanes], NT)

        for t in range(-4, number + 4):
            for g in range(group):
                if t == 2 * g - 4:
                    prepare(g)
            if 0 <= t + 2 < number:
                change(*units[t + 2])
            if 0 <= t < number:
                scores(*units[t])
            if 0 <= t - 1 < number:
                grads(*units[t - 1])
            if 0 <= t - 3 < number:
                store(*units[t - 3])
            for low, high in cuts[:-1]:
                if t - 3 == 2 * high - 1:
                    add_product(low, high)

        add_product(*cuts[-1])

        @pl.when(at_group == steps - 1)
        def _():
            one = jnp.ones((rows, 16), f32)
            gpl[pair] = gplt[...].T[:rows, :]
            acc[...] += dot(
                jnp.concatenate([fil[...], one], axis=1).astype(bf16), gpl[pair].astype(bf16), TN
            )
            weight = awp[:, pl.ds(pl.multiple_of(pair * 384, 128), 384)].astype(f32)
            by_gain = weight * acc[:features, :]
            by_shift = weight * acc[features : features + 1, :]
            fold = lambda v: jnp.sum((v[:, :128] + v[:, 128:256] + v[:, 256:]).T, axis=0, keepdims=True)
            shift_row = fold(by_shift)
            gain_row = (fold(by_gain) - row_of(shift) * shift_row) / row_of(gain)
            block = features + 32
            stream = pair + 1
            for k in range(3):
                lanes = slice(k * 128, (k + 1) * 128)
                spread.send[stream, k * block : k * block + features + 16] = acc[:, lanes].astype(bf16)
                ends = rows_where(0, gain_row[:, lanes], 16, f32) + rows_where(1, shift_row[:, lanes], 16, f32)
                spread.send[stream, k * block + features + 16 : (k + 1) * block] = ends.astype(bf16)
            rest = spread.send.shape[1] - 3 * block
            if rest:
                spread.send[stream, 3 * block :] = jnp.zeros((rest, 128), bf16)
            spread.start("core", stream)

    @pl.when(step == last)
    def _():
        take_left(left, xl, count)
        normed, scale = norm_rows(xl[...])
        packed = jnp.concatenate([gpl[p] for p in range(pairs)], axis=1).astype(bf16)
        grad_first = dot(packed, awp[...], NT)
        outl[...] = ghl[...] + norm_back(grad_first * row_of(gain), normed, scale, 1)

    @pl.when(step >= last)
    def _():
        held = {}
        first = (step - last) * late_group

        def product(g):
            image = first + g
            lanes = pl.ds(pl.multiple_of(lax.rem(image, group) * MAIN, MAIN), MAIN)
            held["grad", g] = dot(awp[...], gpa[image // group, :, lanes])

        def norm(g):
            held["norm", g] = norm_columns(tok[g].T.astype(f32))

        def finish(g):
            normed, scale = held.pop(("norm", g))
            grad = norm_back(held.pop(("grad", g)) * wide(cols[...], MAIN), normed, scale, 0)
            result = gh[:, g * MAIN : (g + 1) * MAIN] + grad
            out[g, :MAIN, :] = result.astype(bf16).T
            out[g, MAIN : MAIN + 1, :] = outl[pl.ds(first + g, 1), :].astype(bf16)

        product(0)
        norm(0)
        for g in range(late_group):
            if g + 1 < late_group:
                product(g + 1)
                norm(g + 1)
            finish(g)

    @pl.when(step == last + late_steps - 1)
    def _():
        for slot, name, phase, s in plan:
            if slot >= last + late_steps:
                engines[name].advance(phase, s)
        for s in range(quarter.streams):
            for side in range(2):
                quarter_out[s, side] = quarter.fin[s, side, : quarter.half]
        spread_out[...] = spread.out[...]
        block = features + 32
        for k in range(3):
            low = k * block + features + 16
            ends = spread.out[0, low : low + 16].astype(f32)
            at = lax.broadcasted_iota(jnp.int32, ends.shape, 0)
            row = jnp.sum(jnp.where(at == 8 + quarter.me_t, ends, 0.0), axis=0, keepdims=True)
            bias_out[:, k * 128 : (k + 1) * 128] = jnp.broadcast_to(row, (8, 128))


def place_kernel(
    pairs, quarter_in, spread_in, bias, output, input_grad,
    output_to, input_to, first_gain, first_shift, attend_to, attend_bias, merge_to, merge_bias,
    second_gain, second_shift, up_to, up_bias, down_to, down_bias,
    held, quarter, spread, attend, merge, up, down, sems, small,
):
    features = merge.shape[0]
    count = output.shape[0]
    got = [
        pltpu.make_async_copy(quarter_in, quarter, small.at[0]),
        pltpu.make_async_copy(spread_in, spread, small.at[1]),
    ]
    ins, outs = [], []
    for k, (src, to) in enumerate(((output, output_to), (input_grad, input_to))):
        for image in range(count):
            ins.append(pltpu.make_async_copy(src.at[image], held.at[k, image], sems.at[0, k, image]))
            outs.append(pltpu.make_async_copy(held.at[k, image], to.at[image], sems.at[1, k, image]))
    for copy in got + ins:
        copy.start()
    for copy in got:
        copy.wait()
    for s in range(quarter.shape[0]):
        lanes = slice(s * 128, (s + 1) * 128)
        up[:, lanes] = quarter[s, 0].astype(f32)
        down[lanes, :] = quarter[s, 1].astype(f32).T
    block = features + 32
    firsts, seconds, merge_ends = [], [], []
    for k in range(3):
        merge[:, k * 128 : (k + 1) * 128] = spread[0, k * block : k * block + features].astype(f32)
        low = k * block + features
        merge_ends.append(spread[0, low : low + 16].astype(f32))
        seconds.append(spread[0, low + 16 : low + 32].astype(f32))
        total = jnp.zeros((16, 128), f32)
        for pair in range(pairs):
            lanes = slice(k * features + pair * 128, k * features + (pair + 1) * 128)
            attend[:, lanes] = spread[pair + 1, k * block : k * block + features].astype(f32)
            total = total + spread[pair + 1, low + 16 : low + 32].astype(f32)
        firsts.append(total)
    puts = [
        pltpu.make_async_copy(src, to, small.at[2 + k])
        for k, (src, to) in enumerate(((attend, attend_to), (merge, merge_to), (up, up_to), (down, down_to)))
    ]
    for copy in puts:
        copy.start()
    merge_ends, firsts, seconds = (jnp.concatenate(v, axis=1) for v in (merge_ends, firsts, seconds))
    up_bias[...] = bias[0:1, :].reshape(features)
    merge_bias[...] = merge_ends[0:1, :].reshape(features)
    first_gain[...] = firsts[0:1, :].reshape(features)
    first_shift[...] = firsts[1:2, :].reshape(features)
    second_gain[...] = seconds[0:1, :].reshape(features)
    second_shift[...] = seconds[1:2, :].reshape(features)
    down_bias[...] = seconds[2:3, :].reshape(features)
    for to, k in ((0, 0), (1, 2)):
        rows = [
            spread[pair + 1, k * block + features : k * block + features + 16].astype(f32)[0:1, :]
            for pair in range(pairs)
        ]
        attend_bias[to : to + 1, :] = jnp.concatenate(rows, axis=1)
    for copy, on in zip(ins, outs):
        copy.wait()
        on.start()
    for copy in outs + puts:
        copy.wait()


def transfers(quarter, spread, steps, last, late_steps):
    end = last + late_steps
    when = {
        ("quarter", 0): [1, 3, 5, last + 6, end + 0.4],
        ("quarter", 1): [1, 3, 5, last + 6, end + 0.4],
        ("quarter", 2): [1, 4, last, end + 0.1, end + 0.45],
        ("spread", 0): [2, 4, last, last + 2, last + 4, end + 0.01],
        ("spread", 1): [4, last, last + 2, last + 5, end + 0.02, end + 0.15],
        ("spread", 2): [last, last + 3, end + 0.05, end + 0.31, end + 0.51, end + 0.6],
        ("spread", 3): [last + 1, last + 5, end + 0.3, end + 0.5, end + 0.7],
    }
    plan = []
    for (name, s), times in when.items():
        phases = 5 if name == "quarter" else len(spread.phases(s))
        times = times[:2] + [times[2]] * (phases - len(times)) + times[2:]
        plan += [(time, name, phase + 1, s) for phase, time in enumerate(times)]
    plan.sort(key=lambda item: item[0])
    return [(int(time), *rest) for time, *rest in plan]


def whole(*dims):
    return pl.BlockSpec(dims, lambda i: (0,) * len(dims))


def once(*dims):
    return pl.BlockSpec(dims, lambda i: (0,) * len(dims), pipeline_mode=pl.Buffered(1))


LIVE = pl.BlockSpec(memory_space=pltpu.SMEM)
ANY = pl.BlockSpec(memory_space=pl.ANY)


def params(**more):
    return pltpu.CompilerParams(
        vmem_limit_bytes=60 * 2**20, dimension_semantics=("arbitrary",), **more
    )


def shape(dtype, *dims):
    return jax.ShapeDtypeStruct(dims, dtype)


def shards(
    mesh_sizes, tokens, image_mask, patch_mask, first_gain, first_shift, attend_weight, attend_bias,
    merge_weight, merge_bias, second_gain, second_shift, up_weight, up_bias, down_weight,
    down_bias, cotangent,
):
    n, seq, d = tokens.shape
    packed = attend_weight.shape[1]
    rows = -(-n // 16) * 16
    group = 2 if n % 2 == 0 else 1
    steps = n // group
    width = group * MAIN
    pairs = HEADS // 2
    total = n * MAIN
    left = pl.BlockSpec((n, 16, d), lambda i: (0, MAIN // 16, 0), pipeline_mode=pl.Buffered(1))
    quarters, share = mesh_sizes[1], up_weight.shape[1]

    here = lambda i: jnp.minimum(i, steps - 1)
    cols = lambda r: pl.BlockSpec((r, width), lambda i: (0, here(i)))
    images = lambda *dims: pl.BlockSpec((group, *dims), lambda i: (here(i),) + (0,) * len(dims))
    fi, qkv, probs, edges, invs, lp, lself, att, hid, fil, qkvl, attl, hidl, wall, ball = pl.pallas_call(
        functools.partial(attend_kernel, n, group, steps),
        grid=(steps + 1,),
        in_specs=[
            once(group, MAIN, d),
            pl.BlockSpec((group, MAIN, d), lambda i: (here(i + 1), 0, 0)),
            left, whole(n, MAIN), LIVE, whole(d), whole(d), whole(2, d), whole(d),
            once(d, packed), once(d, d), ANY, whole(share), ANY,
        ],
        out_specs=[
            cols(d + 16), cols(packed), images(HEADS, MAIN, MAIN), images(16, MAIN),
            images(16, MAIN), images(16, MAIN), images(16, 128), cols(d),
            pl.BlockSpec((d, width), lambda i: (0, jnp.maximum(i, 1) - 1)),
            whole(rows, d), whole(rows, packed), whole(rows, d), whole(rows, d), ANY, ANY,
        ],
        out_shape=[
            shape(bf16, d + 16, total), shape(bf16, packed, total), shape(bf16, n, HEADS, MAIN, MAIN),
            shape(f32, n, 16, MAIN), shape(f32, n, 16, MAIN), shape(f32, n, 16, MAIN),
            shape(f32, n, 16, 128), shape(bf16, d, total), shape(f32, d, total),
            shape(f32, rows, d), shape(f32, rows, packed), shape(f32, rows, d), shape(f32, rows, d),
            shape(bf16, quarters, 2, d, share), shape(bf16, quarters, 16, share),
        ],
        scratch_shapes=[
            pltpu.VMEM((packed, d + 128), bf16), pltpu.VMEM((d, d + 128), bf16),
            pltpu.VMEM((d + 128, width), bf16), pltpu.VMEM((d + 128, width), bf16),
            pltpu.VMEM((2, d, 128), f32), pltpu.VMEM((group, 16, MAIN), f32),
            pltpu.VMEM((2, packed, width), bf16),
            pltpu.VMEM((3, d, width), bf16),
            pltpu.VMEM((rows, d), f32), pltpu.VMEM((rows, packed), f32), pltpu.VMEM((rows, d), f32),
            pltpu.VMEM((16, share), bf16), pltpu.SemaphoreType.DMA((9,)), pltpu.SemaphoreType.DMA((9,)),
            pltpu.SemaphoreType.DMA((3,)),
        ],
        compiler_params=params(collective_id=0, has_side_effects=True),
        name="attend",
    )(
        tokens, tokens, tokens, patch_mask, image_mask, first_gain, first_shift, attend_bias, merge_bias,
        attend_weight, merge_weight, up_weight, up_bias, down_weight,
    )

    streams = d // 128
    block = d + 32
    chunk = -(-3 * block // (8 * 16)) * 16
    ahead = lambda i: (i // steps) * (i - steps) + (1 - i // steps) * (i + 1 - (i + 1) // steps)
    late_images = lambda *dims: pl.BlockSpec(
        (group, *dims), lambda i: ((i // steps) * (i - steps),) + (0,) * len(dims)
    )
    late_cols = lambda r: pl.BlockSpec((r, width), lambda i: (0, (i // steps) * (i - steps)))
    quarter_vm = lambda dtype: pltpu.VMEM((streams, 2 * d, 128), dtype)
    output, gh, gml, dots, ghl, gmleft, mine, beside, shared = pl.pallas_call(
        functools.partial(feed_kernel, n, group, steps),
        grid=(2 * steps,),
        in_specs=[
            once(d, width), pl.BlockSpec((d, width), lambda i: (0, ahead(i))), late_cols(d), late_images(16, MAIN),
            once(group, MAIN, d), pl.BlockSpec((group, MAIN, d), lambda i: (ahead(i), 0, 0)), left, LIVE, whole(d), whole(d), whole(d),
            whole(rows, d), whole(rows, d), once(quarters, 2, d, share), once(quarters, 16, share), once(d, d),
        ],
        out_specs=[
            late_images(seq, d), late_cols(d), late_cols(d), late_images(16, MAIN),
            whole(rows, d), whole(rows, d),
            once(streams, 2 * d, 128), once(streams, 2 * d, 128), once(8 * chunk, 128),
        ],
        out_shape=[
            shape(bf16, n, seq, d), shape(f32, d, total), shape(bf16, d, total),
            shape(f32, n, 16, MAIN), shape(f32, rows, d), shape(f32, rows, d),
            shape(bf16, streams, 2 * d, 128), shape(bf16, streams, 2 * d, 128), shape(bf16, 8 * chunk, 128),
        ],
        scratch_shapes=[
            pltpu.VMEM((quarters, share, d + 128), bf16), pltpu.VMEM((quarters, d, share), bf16),
            pltpu.VMEM((steps, d + 128, width), bf16), pltpu.VMEM((d + 128, width), bf16),
            pltpu.VMEM((2 * share, width), bf16), pltpu.VMEM((2 * share, width), bf16),
            pltpu.VMEM((steps, d, width), bf16), pltpu.VMEM((d, width), bf16),
            pltpu.VMEM((3, d, 128), f32), pltpu.VMEM((2, d, 128), f32),
            pltpu.VMEM((rows, d), f32), pltpu.VMEM((rows, d), f32),
            pltpu.VMEM((rows, d + 16), bf16), pltpu.VMEM((rows, d), bf16),
            pltpu.VMEM((quarters, rows, share), bf16), pltpu.VMEM((quarters, rows, share), bf16),
            pltpu.VMEM((steps, d, width), f32), pltpu.VMEM((steps, d, width), f32),
            pltpu.VMEM((d + 16, 2 * share), f32), pltpu.VMEM((d, 2 * share), f32),
            pltpu.VMEM((d + 16, d), f32), pltpu.VMEM((8, d), f32), pltpu.VMEM((8, d), f32),
            quarter_vm(f32), quarter_vm(bf16), quarter_vm(bf16), quarter_vm(bf16), quarter_vm(bf16),
            pltpu.SemaphoreType.DMA((2,)), pltpu.SemaphoreType.DMA((2,)),
        ],
        compiler_params=params(collective_id=1, has_side_effects=True),
        name="feed",
    )(
        hid, hid, att, invs, cotangent, cotangent, cotangent, image_mask, second_gain, second_shift, down_bias, hidl, attl,
        wall, ball, merge_weight,
    )

    late_group, late_steps = group, steps
    group = next(g for g in (7, 2, 1) if n % g == 0)
    steps = n // group
    width = group * MAIN
    last = pairs * steps
    quarter = Quarter(mesh_sizes[0], streams, 2 * d)
    spread = Spread(mesh_sizes, pairs + 1, chunk)
    plan = transfers(quarter, spread, steps, last, late_steps)
    side = lambda i: (i + late_steps) // (last + late_steps)
    early = lambda i: i - side(i) * (i - (last - 1))
    late = lambda i: side(i) * (i - last)
    by_pair = lambda r: pl.BlockSpec((r, width), lambda i: (early(i) // steps, early(i) % steps))
    early_images = lambda *dims: pl.BlockSpec((group, *dims), lambda i: (early(i) % steps,) + (0,) * len(dims))
    pair_lanes = lambda w: pl.BlockSpec((rows, w), lambda i: (0, early(i) // steps))
    late_images = lambda *dims: pl.BlockSpec((late_group, *dims), lambda i: (late(i),) + (0,) * len(dims))
    input_grad, quarter_sum, spread_sum, bias_sum = pl.pallas_call(
        functools.partial(back_kernel, n, group, steps, late_group, late_steps, quarter, spread, plan),
        grid=(last + late_steps,),
        in_specs=[
            by_pair(3 * 128),
            pl.BlockSpec((group, 2, MAIN, MAIN), lambda i: (early(i) % steps, early(i) // steps, 0, 0)),
            early_images(16, MAIN), early_images(16, MAIN), early_images(16, 128), by_pair(128),
            early_images(16, MAIN), ANY,
            whole(rows, d), pair_lanes(384), pair_lanes(128), pair_lanes(128), ANY, ANY, ANY, ANY,
            late_images(MAIN, d), left, pl.BlockSpec((d, late_group * MAIN), lambda i: (0, late(i))),
            whole(rows, d), whole(d), whole(d),
        ],
        out_specs=[
            late_images(seq, d), once(streams, 2, d, 128), once(pairs + 1, 8 * chunk, 128), whole(8, d),
        ],
        out_shape=[
            shape(bf16, n, seq, d), shape(bf16, streams, 2, d, 128), shape(bf16, pairs + 1, 8 * chunk, 128),
            shape(f32, 8, d),
        ],
        scratch_shapes=[
            pltpu.VMEM((steps, packed, width), bf16), pltpu.VMEM((d + 16, 384), f32),
            pltpu.VMEM((pairs, rows, 384), f32), pltpu.VMEM((384, 128), f32),
            pltpu.VMEM((d, packed), bf16), pltpu.VMEM((d, 128), f32),
            pltpu.VMEM((rows, d), f32), pltpu.VMEM((rows, d), f32),
            pltpu.VMEM((steps, d + 16, width), bf16), pltpu.VMEM((streams, 2 * d, 128), bf16),
            pltpu.SemaphoreType.DMA((steps + 2 + 3 * pairs,)),
            *quarter.scratch(), *spread.scratch(),
        ],
        compiler_params=params(collective_id=2, has_side_effects=True),
        name="back",
    )(
        qkv, probs, edges, lp, lself, gml, dots, fi, fil, qkvl, attl, gmleft, attend_weight,
        mine, beside, shared, tokens, tokens, gh, ghl, first_gain, first_shift,
    )
    row = lambda: pl.BlockSpec(memory_space=pltpu.VMEM)
    return pl.pallas_call(
        functools.partial(place_kernel, pairs),
        in_specs=[ANY, ANY, row(), ANY, ANY],
        out_specs=[
            ANY, ANY, row(), row(), ANY, row(), ANY, row(), row(), row(), ANY, row(), ANY, row(),
        ],
        out_shape=[
            shape(bf16, n, seq, d), shape(bf16, n, seq, d), shape(f32, d), shape(f32, d),
            shape(f32, d, packed), shape(f32, 2, d), shape(f32, d, d), shape(f32, d), shape(f32, d),
            shape(f32, d), shape(f32, d, share), shape(f32, share), shape(f32, share, d), shape(f32, d),
        ],
        scratch_shapes=[
            pltpu.VMEM((2, n, seq, d), bf16), pltpu.VMEM((streams, 2, d, 128), bf16),
            pltpu.VMEM((pairs + 1, 8 * chunk, 128), bf16), pltpu.VMEM((d, packed), f32), pltpu.VMEM((d, d), f32),
            pltpu.VMEM((d, share), f32), pltpu.VMEM((share, d), f32),
            pltpu.SemaphoreType.DMA((2, 2, n)), pltpu.SemaphoreType.DMA((6,)),
        ],
        compiler_params=pltpu.CompilerParams(vmem_limit_bytes=60 * 2**20),
        name="place",
    )(quarter_sum, spread_sum, bias_sum, output, input_grad)


def solution(mesh):
    split = ("dp", "tensor")
    in_specs = (
        P(split, None, None), P(split), P(split, None), P(), P(), P(), P(), P(), P(), P(), P(),
        P(None, "tensor"), P("tensor"), P("tensor", None), P(), P(split, None, None),
    )
    out_specs = (
        P(split, None, None), P(split, None, None), P(), P(), P(), P(), P(), P(), P(), P(),
        P(None, "tensor"), P("tensor"), P("tensor", None), P(),
    )
    sizes = (mesh.shape["dp"], mesh.shape["tensor"])
    return jax.shard_map(functools.partial(shards, sizes), mesh=mesh, in_specs=in_specs, out_specs=out_specs, check_vma=False)
```

```python
import functools

import jax
import jax.numpy as jnp
from jax import lax
from jax.experimental import pallas as pl
from jax.experimental.pallas import tpu as pltpu
from jax.sharding import PartitionSpec as P

HEADS = 6
HEAD = 64
MAIN = 256
EPS = 1e-06
MASKED = -1e30
f32, bf16 = jnp.float32, jnp.bfloat16

NN = ((1,), (0,))
NT = ((1,), (1,))
TN = ((0,), (0,))


def dot(left, right, dims=NN):
    return lax.dot_general(left, right, (dims, ((), ())), preferred_element_type=f32)


def rows_where(index, value, rows, dtype):
    columns = value.shape[-1]
    at = lax.broadcasted_iota(jnp.int32, (rows, columns), 0)
    return jnp.where(at == index, value, 0.0).astype(dtype)


def wide(column, width):
    return jnp.concatenate([column] * (width // 128), axis=1)


def as_column(row):
    return jnp.broadcast_to(row, (128, row.shape[1])).T


def norm_columns(values):
    center = values - jnp.mean(values, axis=0, keepdims=True)
    scale = lax.rsqrt(jnp.mean(center * center, axis=0, keepdims=True) + EPS)
    return center * scale, scale


def norm_rows(values):
    center = values - jnp.mean(values, axis=1, keepdims=True)
    scale = lax.rsqrt(jnp.mean(center * center, axis=1, keepdims=True) + EPS)
    return center * scale, scale


def norm_back(grad, normed, scale, axis):
    mean_grad = jnp.mean(grad, axis=axis, keepdims=True)
    mean_both = jnp.mean(grad * normed, axis=axis, keepdims=True)
    return scale * (grad - mean_grad - normed * mean_both)


def gelu_both(pre):
    curve = 0.5 + 0.5 * lax.erf(pre * 0.7071067811865476)
    bell = 0.3989422804014327 * jnp.exp(-0.5 * pre * pre)
    return pre * curve, curve + pre * bell


def head_rows(rows, features):
    at = lax.broadcasted_iota(jnp.int32, (rows, features), 0)
    head = lax.broadcasted_iota(jnp.int32, (rows, features), 1) // HEAD
    return jnp.where(at == head, 1.0, 0.0)


def lane_live(live_ref, first, count):
    flags = [
        jnp.full((1, MAIN), live_ref[first + g].astype(f32)) for g in range(count)
    ]
    return jnp.concatenate(flags, axis=1)


def row_live(live_ref, count, rows):
    at = lax.broadcasted_iota(jnp.int32, (rows, 1), 0)
    flags = jnp.zeros((rows, 1), f32)
    for image in range(count):
        flags = jnp.where(at == image, live_ref[image].astype(f32), flags)
    return flags


def take_left(left_ref, to_ref, count):
    to_ref[...] = jnp.zeros_like(to_ref)
    for image in range(count):
        to_ref[image : image + 1, :] = left_ref[image].astype(f32)[0:1, :]


def flip(place, bits):
    if bits & 1:
        place = place + 1 - 2 * lax.rem(place, 2)
    if bits & 2:
        place = place + 2 - 4 * (place // 2)
    return place


def remote(src, dst, sends, recvs, index, peer):
    return pltpu.make_async_remote_copy(
        src_ref=src, dst_ref=dst, send_sem=sends.at[index], recv_sem=recvs.at[index],
        device_id=peer, device_id_type=pl.DeviceIdType.MESH,
    )


def greet(peers):
    barrier = pltpu.get_barrier_semaphore()
    for peer in peers:
        pl.semaphore_signal(barrier, inc=1, device_id=peer, device_id_type=pl.DeviceIdType.MESH)


def meet(peers):
    pl.semaphore_wait(pltpu.get_barrier_semaphore(), len(peers))


class Quarter:
    def __init__(self, dp, streams, rows):
        self.far = dp // 2
        self.streams, self.half = streams, rows // 2
        self.chunk = -(-self.half // (16 * self.far)) * 16
        self.padded = self.chunk * self.far
        self.copies = 3 + 2 * (self.far - 1)

    def scratch(self):
        s = self.streams
        vm = lambda *dims: pltpu.VMEM((s, *dims, 128), bf16)
        return [
            vm(2 * self.half), vm(2 * self.half), vm(self.half), vm(self.padded),
            vm(max(self.far - 1, 1), self.chunk), vm(2, self.padded),
            pltpu.SemaphoreType.DMA((s, self.copies)), pltpu.SemaphoreType.DMA((s, self.copies)),
        ]

    def bind(self, mine, beside, refs):
        self.mine, self.beside = mine, beside
        self.r1, self.work, self.r2, self.cur, self.r3, self.fin, self.sends, self.recvs = refs
        self.me_dp, self.me_t = lax.axis_index("dp"), lax.axis_index("tensor")
        self.x, self.z = lax.rem(self.me_dp, 2), self.me_dp // 2

    def line(self, j):
        return (lax.rem(self.z + j, self.far) * 2 + self.x, self.me_t)

    def copies_of(self, phase, s):
        across = (self.z * 2 + 1 - self.x, self.me_t)
        cp = lambda index, src, dst, peer: remote(src, dst, self.sends, self.recvs, (s, index), peer)
        if phase == 1:
            return [cp(0, self.beside.at[s], self.r1.at[s], (self.me_dp, flip(self.me_t, 1)))]
        if phase == 2:
            other = pl.ds(pl.multiple_of((1 - self.x) * self.half, 16), self.half)
            return [cp(1, self.work.at[s, other], self.r2.at[s], across)]
        found = []
        if phase == 3:
            for j in range(1, self.far):
                place = lax.rem(self.z + j, self.far)
                src = self.cur.at[s, pl.ds(pl.multiple_of(place * self.chunk, 16), self.chunk)]
                found.append(cp(1 + j, src, self.r3.at[s, j - 1], self.line(j)))
        if phase == 4:
            ref = self.fin.at[s, self.x, pl.ds(pl.multiple_of(self.z * self.chunk, 16), self.chunk)]
            for j in range(1, self.far):
                found.append(cp(self.far + j, ref, ref, self.line(j)))
        if phase == 5:
            ref = self.fin.at[s, self.x, pl.ds(0, self.half)]
            found.append(cp(2 * self.far, ref, ref, across))
        return found

    def start(self, phase, s):
        for copy in self.copies_of(phase, s):
            copy.start()

    def advance(self, phase, s):
        for copy in self.copies_of(phase, s):
            copy.wait()
        if phase == 1:
            self.work[s] = (self.mine[s].astype(f32) + self.r1[s].astype(f32)).astype(bf16)
        if phase == 2:
            kept = self.work[s, pl.ds(pl.multiple_of(self.x * self.half, 16), self.half)]
            self.cur[s, : self.half] = (kept.astype(f32) + self.r2[s].astype(f32)).astype(bf16)
            if self.padded > self.half:
                self.cur[s, self.half :] = jnp.zeros((self.padded - self.half, 128), bf16)
        if phase == 3:
            mine = pl.ds(pl.multiple_of(self.z * self.chunk, 16), self.chunk)
            total = self.cur[s, mine].astype(f32)
            for j in range(self.far - 1):
                total = total + self.r3[s, j].astype(f32)
            self.fin[s, self.x, mine] = total.astype(bf16)
        if phase < 5:
            self.start(phase + 1, s)


class Spread:
    def __init__(self, mesh_sizes, streams, chunk):
        self.dp, self.tensor = mesh_sizes
        self.far = self.dp // 2
        self.hops = self.far.bit_length() - 1
        self.streams, self.chunk = streams, chunk
        self.copies = 1 + 3 + (self.far - 1) + 3 + 1

    def phases(self, s):
        hops = ["line"] if s == self.streams - 1 else [("hop", k) for k in range(self.hops)]
        return ["core", "plane", *hops, "plane back", "core back"]

    def scratch(self):
        s, c = self.streams, self.chunk
        vm = lambda *dims: pltpu.VMEM((s, *dims, 128), bf16)
        return [
            vm(8 * c), vm(4 * c), vm(4 * c), vm(3, c), vm(self.far, c), vm(c), vm(8 * c),
            pltpu.SemaphoreType.DMA((s, self.copies)), pltpu.SemaphoreType.DMA((s, self.copies)),
        ]

    def bind(self, refs):
        self.send, self.r1, self.work, self.r2, self.r3, self.cur, self.out, self.ss, self.rs = refs
        self.me_dp, self.me_t = lax.axis_index("dp"), lax.axis_index("tensor")
        self.x, self.z = lax.rem(self.me_dp, 2), self.me_dp // 2
        self.c, self.y = lax.rem(self.me_t, 2), self.me_t // 2
        self.place = 2 * self.y + self.x

    def plane(self, j):
        x = 1 - self.x if j & 1 else self.x
        y = 1 - self.y if j & 2 else self.y
        return (self.z * 2 + x, 2 * y + self.c), 2 * y + x

    def core(self):
        return (self.me_dp, 2 * self.y + 1 - self.c)

    def line(self, j):
        return (lax.rem(self.z + j, self.far) * 2 + self.x, self.me_t)

    def hop(self, k):
        step = 1 << k
        there = self.z + step - 2 * step * lax.rem(self.z // step, 2)
        return (there * 2 + self.x, self.me_t)

    def rows(self, first, count):
        return pl.ds(pl.multiple_of(first * self.chunk, 16), count * self.chunk)

    def copies_of(self, kind, s):
        cp = lambda index, src, dst, peer: remote(src, dst, self.ss, self.rs, (s, index), peer)
        if kind == "core":
            return [cp(0, self.send.at[s, self.rows(4 * (1 - self.c), 4)], self.r1.at[s], self.core())]
        found = []
        if kind == "plane":
            for j in (1, 2, 3):
                peer, place = self.plane(j)
                found.append(cp(j, self.work.at[s, self.rows(place, 1)], self.r2.at[s, j - 1], peer))
        if kind == "line":
            for j in range(1, self.far):
                ref = self.r3.at[s, self.z]
                found.append(cp(3 + j, ref, ref, self.line(j)))
        if kind[0] == "hop":
            found.append(cp(4 + kind[1], self.cur.at[s], self.r3.at[s, kind[1]], self.hop(kind[1])))
        if kind == "plane back":
            mine = self.out.at[s, self.rows(4 * self.c + self.place, 1)]
            for j in (1, 2, 3):
                found.append(cp(2 + self.far + j, mine, mine, self.plane(j)[0]))
        if kind == "core back":
            ref = self.out.at[s, self.rows(4 * self.c, 4)]
            found.append(cp(6 + self.far, ref, ref, self.core()))
        return found

    def start(self, kind, s):
        for copy in self.copies_of(kind, s):
            copy.start()

    def advance(self, phase, s):
        phases = self.phases(s)
        kind = phases[phase - 1]
        for copy in self.copies_of(kind, s):
            copy.wait()
        mine = self.rows(4 * self.c + self.place, 1)
        if kind == "core":
            half = self.send[s, self.rows(4 * self.c, 4)].astype(f32)
            self.work[s] = (half + self.r1[s].astype(f32)).astype(bf16)
        if kind == "plane":
            total = self.work[s, self.rows(self.place, 1)].astype(f32)
            for j in range(3):
                total = total + self.r2[s, j].astype(f32)
            if phases[2] == "line":
                self.r3[s, self.z] = total.astype(bf16)
            else:
                self.cur[s] = total.astype(bf16)
        if kind == "line":
            total = self.r3[s, 0].astype(f32)
            for j in range(1, self.far):
                total = total + self.r3[s, j].astype(f32)
            self.out[s, mine] = total.astype(bf16)
        if kind[0] == "hop":
            total = (self.cur[s].astype(f32) + self.r3[s, kind[1]].astype(f32)).astype(bf16)
            self.cur[s] = total
            if kind[1] == self.hops - 1:
                self.out[s, mine] = total
        if phase < len(phases):
            self.start(phases[phase], s)


def row_of(ref):
    return ref[...].astype(f32).reshape(1, ref.shape[0])


def parts_of(at, pair):
    return slice(pair * 384 + at * 128, pair * 384 + (at + 1) * 128)


def attend_kernel(
    count, group, steps,
    tok0, tok, left, pmask, live, gain, shift, abias, mbias, aw, mw, up, ubias, down,
    fi_out, qkv_out, probs_out, edge_out, inv_out, lp_out, lself_out, att_out, hid_out,
    fil_out, qkvl_out, attl_out, hidl_out, wall, ball,
    awt, mwt, fia, atta, cols, edges, qkv2, toks, xl, qkvl, attl, brow, sends, recvs, own, leave,
):
    step = pl.program_id(0)
    me_dp, me_t = lax.axis_index("dp"), lax.axis_index("tensor")
    beside, across = (me_dp, flip(me_t, 1)), (me_dp, flip(me_t, 2))

    def places(owner):
        return (wall.at[owner, 0], wall.at[owner, 1], ball.at[owner])

    def first_copies(peer, first):
        return [
            remote(src, dst, sends, recvs, first + k, peer)
            for k, (src, dst) in enumerate(zip((up, down, brow), places(me_t)))
        ]

    def second_copies():
        return [
            remote(ref, ref, sends, recvs, 6 + k, beside) for k, ref in enumerate(places(flip(me_t, 2)))
        ]

    def own_copies():
        return [
            pltpu.make_async_copy(src, dst, own.at[k])
            for k, (src, dst) in enumerate(zip((up, down, brow), places(me_t)))
        ]

    @pl.when(step == 0)
    def _():
        greet((beside, across))
        brow[...] = rows_where(0, row_of(ubias), 16, bf16)
        meet((beside, across))
        for copy in first_copies(across, 3) + first_copies(beside, 0) + own_copies():
            copy.start()

    @pl.when(step == steps - 2)
    def _():
        for copy in first_copies(across, 3):
            copy.wait()
        for copy in second_copies():
            copy.start()

    features = aw.shape[0]
    packed = aw.shape[1]
    rows = xl.shape[0]
    width = group * MAIN
    pairs = HEADS // 2
    heads = head_rows(rows, features)

    def first_norm(block):
        tokens = jnp.concatenate([block[g].T for g in range(group)], axis=1)
        normed, _ = norm_columns(tokens.astype(f32))
        return tokens, (normed * wide(cols[0], width) + wide(cols[1], width)).astype(bf16)

    def project(slot, part):
        span = slice(part * features, (part + 1) * features)
        qkv2[slot, span, :] = dot(awt[span, :], fia[...]).astype(bf16)

    @pl.when(step == 0)
    def _():
        ab = abias[...].astype(f32)
        for pair in range(pairs):
            for at in range(3):
                cut = slice(at * features + pair * 128, at * features + (pair + 1) * 128)
                to = parts_of(at, pair)
                scale = HEAD**-0.5 if at == 0 else 1.0
                awt[to, :features] = (aw[:, cut].astype(f32).T * scale).astype(bf16)
                if at == 1:
                    bias = jnp.zeros((1, 128), f32)
                else:
                    bias = ab[at // 2 : at // 2 + 1, pair * 128 : (pair + 1) * 128] * scale
                awt[to, features:] = rows_where(0, bias, 128, f32).T.astype(bf16)
        mwt[:, :features] = mw[...].astype(f32).T.astype(bf16)
        mwt[:, features:] = rows_where(0, row_of(mbias), 128, f32).T.astype(bf16)
        ones = rows_where(0, jnp.ones((1, fia.shape[1]), f32), 128, bf16)
        fia[features:, :] = ones
        atta[features:, :] = ones
        cols[0] = as_column(row_of(gain))
        cols[1] = as_column(row_of(shift))
        edges[...] = jnp.zeros_like(edges)
        take_left(left, xl, count)
        normed, _ = norm_rows(xl[...])
        fil = (normed * row_of(gain) + row_of(shift)).astype(bf16)
        fil_out[...] = fil.astype(f32)
        plain = dot(fil, aw[...])
        for pair in range(pairs):
            for at in range(3):
                cut = slice(at * features + pair * 128, at * features + (pair + 1) * 128)
                value = plain[:, cut]
                if at != 1:
                    value = value + ab[at // 2 : at // 2 + 1, pair * 128 : (pair + 1) * 128]
                value = value.astype(bf16).astype(f32)
                qkvl[:, parts_of(at, pair)] = value * (HEAD**-0.5) if at == 0 else value
        qkvl_out[...] = qkvl[...]
        attl[...] = jnp.zeros_like(attl)
        tokens, fi = first_norm(tok0)
        toks[0] = tokens
        fia[:features, :] = fi
        for part in range(3):
            project(0, part)

    def qkv_copy(index):
        slot = lax.rem(index, 2)
        lanes = pl.ds(pl.multiple_of(index * width, 128), width)
        return pltpu.make_async_copy(qkv2.at[slot], qkv_out.at[:, lanes], leave.at[slot])

    @pl.when(step > 0)
    def _():
        qkv_copy(step - 1).wait()

    def merge_branch():
        return dot(mwt[...], atta[...])

    def hidden_of(branch, index):
        tokens = toks[lax.rem(index, 3)].astype(f32)
        return tokens + lane_live(live, index * group, group) * branch

    @pl.when(step < steps)
    def _():
        now, later = lax.rem(step, 2), lax.rem(step + 1, 2)
        qkv_copy(step).start()
        one_row = rows_where(0, jnp.ones((1, MAIN), f32), 16, bf16)
        held = {}
        units = [(g, h) for g in range(group) for h in range(HEADS)]

        def lanes_of(g):
            return slice(g * MAIN, (g + 1) * MAIN)

        def part(at, g, h):
            low = (h // 2) * 384 + at * 128 + (h % 2) * HEAD
            return qkv2[now, low : low + HEAD, lanes_of(g)]

        def all_heads(at, g):
            return jnp.concatenate(
                [qkv2[now, parts_of(at, pair), lanes_of(g)] for pair in range(pairs)], axis=0
            )

        def begin(g):
            image = step * group + g
            row = qkvl[pl.ds(image, 1), :]
            ql, kl, vl = (
                jnp.concatenate([row[:, parts_of(at, pair)] for pair in range(pairs)], axis=1)
                for at in range(3)
            )
            key_bias = jnp.where(pmask[pl.ds(image, 1), :] == 1, 0.0, MASKED)
            moved = pltpu.roll(key_bias, 1, axis=1)
            at = lax.broadcasted_iota(jnp.int32, moved.shape, 1)
            main_bias = jnp.where(at == 0, 0.0, moved)
            left_bias = moved[:, 0:1]
            held["bias", g] = rows_where(0, main_bias, 16, bf16)
            held["vl", g] = vl
            held["slk", g] = dot((heads * kl).astype(bf16), all_heads(0, g)) + left_bias
            held["sl", g] = dot((heads * ql).astype(bf16), all_heads(1, g)) + main_bias
            held["self", g] = jnp.sum(heads * (ql * kl), axis=1, keepdims=True) + left_bias

        def left_query(g):
            sl, self_score = held.pop(("sl", g)), held.pop(("self", g))
            peak = jnp.maximum(jnp.max(sl, axis=1, keepdims=True), self_score)
            raised = jnp.exp(sl - peak)
            raised_self = jnp.exp(self_score - peak)
            inv = 1.0 / (jnp.sum(raised, axis=1, keepdims=True) + raised_self)
            lp = raised * inv
            lself = raised_self * inv
            lp_out[g] = lp
            lself_out[g] = jnp.broadcast_to(lself, (rows, 128))
            mixed = dot(lp.astype(bf16), all_heads(2, g), NT) + lself * held["vl", g]
            image = step * group + g
            attl[pl.ds(image, 1), :] = (
                jnp.sum(mixed * heads, axis=0, keepdims=True).astype(bf16).astype(f32)
            )

        def scores(g, h):
            held["s", g, h] = dot(
                jnp.concatenate([part(1, g, h), held["bias", g]], axis=0),
                jnp.concatenate([part(0, g, h), one_row], axis=0),
                TN,
            )

        def soften(g, h):
            value = held.pop(("s", g, h))
            slk = held["slk", g][h : h + 1, :]
            peak = jnp.maximum(jnp.max(value, axis=0, keepdims=True), slk)
            raised = jnp.exp(value - peak).astype(bf16)
            probs_out[g, h] = raised
            held["e", g, h] = raised
            edge = jnp.exp(slk - peak)
            held["edge", g, h] = edge
            edges[g, h : h + 1, :] = edge

        def mix(g, h):
            held["o", g, h] = dot(
                jnp.concatenate([part(2, g, h), one_row], axis=0), held.pop(("e", g, h))
            )

        def add_left(g):
            edge_out[g] = edges[g]
            held["add", g] = dot((heads * held["vl", g]).astype(bf16), edges[g].astype(bf16), TN)

        def finish(g, h):
            out = held.pop(("o", g, h))
            span = slice(h * HEAD, (h + 1) * HEAD)
            inv = 1.0 / (out[HEAD : HEAD + 1, :] + held["edge", g, h])
            inv_out[g, h : h + 1, :] = inv
            mixed = ((out[:HEAD, :] + held["add", g][span]) * inv).astype(bf16)
            atta[span, lanes_of(g)] = mixed
            att_out[span, lanes_of(g)] = mixed

        count_units = len(units)
        for t in range(-2, count_units + 4):
            if t + 2 == 0:
                for g in range(group):
                    begin(g)
                    held["branch"] = merge_branch()
                att_out[features:, :] = atta[features : features + 16, :]
            if 0 <= t + 2 < count_units:
                scores(*units[t + 2])
            if t == -1:
                hid_out[...] = hidden_of(held.pop("branch"), step - 1 + 3 * (1 - jnp.minimum(step, 1)))
                fi_out[:features, :] = fia[:features, :]
                fi_out[features:, :] = fia[features : features + 16, :]
                held["next"] = first_norm(tok)
            if t == 1:
                tokens, fi = held.pop("next")
                toks[lax.rem(step + 1, 3)] = tokens
                fia[:features, :] = fi
            if t in (5, 7, 9):
                project(later, (t - 5) // 2)
            if 0 <= t < count_units:
                soften(*units[t])
            if 0 <= t - 2 < count_units:
                mix(*units[t - 2])
            for g in range(group):
                if t == HEADS * g + 3:
                    left_query(g)
                if t == HEADS * (g + 1):
                    add_left(g)
                if t == HEADS * (g + 1) + 3:
                    for h in range(HEADS):
                        finish(g, h)

    @pl.when(step == steps)
    def _():
        hid_out[...] = hidden_of(merge_branch(), step - 1)
        attl_out[...] = attl[...]
        branch = dot(attl[...].astype(bf16), mw[...]) + row_of(mbias)
        hidl_out[...] = xl[...] + row_live(live, count, rows) * branch
        for copy in first_copies(beside, 0) + second_copies() + own_copies():
            copy.wait()


def feed_kernel(
    count, group, steps,
    hid0, hid, att, inv, cot0, cot, cleft, live, gain, shift, dbias, hidl, attl, wall, ball, mw,
    out, gh_out, gml_out, dots_out, ghl_out, gmleft_out, mine, beside, shared,
    upt, dnt, sia, act, gpre, gb, gattn, cols, gsum, xl, outl, sil, gbl, actl, gprel,
    outp, gradp, up_acc, down_acc, merge_acc, sums, biases, kept, away, r1, across, r2, sends, recvs,
):
    step = pl.program_id(0)
    at_step = lax.rem(step, steps)
    second = step // steps
    features = mw.shape[0]
    rows = xl.shape[0]
    width = group * MAIN
    quarters = wall.shape[0]
    me_dp, me_t = lax.axis_index("dp"), lax.axis_index("tensor")
    core, chip = (me_dp, flip(me_t, 1)), (me_dp, flip(me_t, 2))
    first_of = (1 - second) * flip(me_t, 2) + second * me_t
    now = (first_of, flip(first_of, 1))

    def to_core():
        return remote(away, r1, sends, recvs, 0, core)

    def to_chip():
        return remote(across, r2, sends, recvs, 1, chip)

    @pl.when(step == 0)
    def _():
        greet((core, chip))
        gain_row, shift_row, dbias_row = row_of(gain), row_of(shift), row_of(dbias)
        for q in range(quarters):
            upt[q, :, :features] = wall[q, 0].astype(f32).T.astype(bf16)
            upt[q, :, features:] = rows_where(0, ball[q, 0:1, :].astype(f32), 128, f32).T.astype(bf16)
            dnt[q] = wall[q, 1].astype(f32).T.astype(bf16)
        ones = rows_where(0, jnp.ones((1, width), f32), 128, bf16)
        for k in range(steps):
            sia[k, features:, :] = ones
        cols[0] = as_column(gain_row)
        cols[1] = as_column(shift_row)
        cols[2] = as_column(dbias_row)
        gsum[...] = jnp.zeros_like(gsum)
        biases[...] = jnp.zeros_like(biases)
        take_left(cleft, xl, count)
        alive = row_live(live, count, rows)
        normed, scale = norm_rows(hidl[...])
        si = (normed * gain_row + shift_row).astype(bf16)
        grad_branch = (alive * xl[...]).astype(bf16)
        total = hidl[...] + alive * dbias_row
        grad_second = jnp.zeros_like(total)
        pre_of = [dot(si, wall[q, 0]) + ball[q, 0:1, :].astype(f32) for q in range(quarters)]
        grad_of = [dot(grad_branch, wall[q, 1], NT) for q in range(quarters)]
        for q in range(quarters):
            value, slope = gelu_both(pre_of[q])
            actl[q] = value.astype(bf16)
            gprel[q] = (grad_of[q] * slope).astype(bf16)
        for q in range(quarters):
            total = total + alive * dot(actl[q], wall[q, 1])
            grad_second = grad_second + dot(gprel[q], wall[q, 0], NT)
        outl[...] = total
        grad_hidden = xl[...] + norm_back(grad_second * gain_row, normed, scale, 1)
        ghl_out[...] = grad_hidden
        grad_attn = (alive * grad_hidden).astype(bf16)
        gmleft_out[...] = dot(grad_attn, mw[...], NT).astype(bf16).astype(f32)
        one = jnp.ones((rows, 16), f32)
        sil[...] = jnp.concatenate([si.astype(f32), one], axis=1).astype(bf16)
        gbl[...] = grad_branch
        merge_acc[...] = dot(jnp.concatenate([attl[...], one], axis=1).astype(bf16), grad_attn, TN)
        sums[...] = jnp.zeros_like(sums)
        sums[0:1, :] = jnp.sum(grad_second * normed, axis=0, keepdims=True)
        sums[1:2, :] = jnp.sum(grad_second, axis=0, keepdims=True)
        sums[2:3, :] = jnp.sum(grad_branch.astype(f32), axis=0, keepdims=True)
        meet((core, chip))

    @pl.when(at_step == 0)
    def _():
        for c, q in enumerate(now):
            lanes = slice(c * features, (c + 1) * features)
            up_acc[:, lanes] = dot(sil[...], gprel[q], TN)
            down_acc[:, lanes] = dot(gbl[...], actl[q], TN)

    def rounded(ref, lanes, at):
        lanes = slice(lanes + at * 128, lanes + (at + 1) * 128)
        return jnp.concatenate([up_acc[:features, lanes], down_acc[:, lanes]], axis=0)

    @pl.when(step == steps + 1)
    def _():
        to_core().wait()
        for at in range(kept.shape[0]):
            across[at] = (kept[at] + r1[at].astype(f32)).astype(bf16)
        to_chip().start()

    pres, grads = {}, {}
    lanes_of = [slice(g * MAIN, (g + 1) * MAIN) for g in range(group)]

    def enter(hidden, cotangent, to):
        normed, _ = norm_columns(hidden[...])
        sia[to, :features, :] = (normed * wide(cols[0], width) + wide(cols[1], width)).astype(bf16)
        alive = lane_live(live, to * group, group)
        turned = jnp.concatenate([cotangent[g].T for g in range(group)], axis=1).astype(f32)
        gb[to] = (turned * alive).astype(bf16)

    def into(g):
        for c in range(2):
            pres[g, c] = dot(upt[now[c]], sia[at_step, :, lanes_of[g]])
            grads[g, c] = dot(wall[now[c], 1], gb[at_step, :, lanes_of[g]])

    def through(g):
        for c in range(2):
            span = slice(c * features, (c + 1) * features)
            value, slope = gelu_both(pres.pop((g, c)))
            act[span, lanes_of[g]] = value.astype(bf16)
            gpre[span, lanes_of[g]] = (grads.pop((g, c)) * slope).astype(bf16)

    def both_of(ref, *more):
        return jnp.concatenate([ref[(q, *more)] for q in now], axis=1)

    def second_sum(g):
        return dot(both_of(wall, 0), gpre[:, lanes_of[g]])

    def output_sum(g):
        return dot(both_of(dnt), act[:, lanes_of[g]])

    def up_product():
        up_acc[...] += dot(sia[at_step, : up_acc.shape[0], :], gpre[...], NT)

    def down_product():
        down_acc[...] += dot(gb[at_step], act[...], NT)

    @pl.when(step == 0)
    def _():
        enter(hid0, cot0, 0)

    @pl.when(second == 0)
    def _():
        for g in range(group):
            into(g)
        for g in range(group):
            through(g)
            gradp[at_step, :, lanes_of[g]] = second_sum(g)
            outp[at_step, :, lanes_of[g]] = output_sum(g)
        up_product()
        enter(hid, cot, at_step + 1 - (at_step + 1) // steps)
        down_product()

    @pl.when(second == 1)
    def _():
        held = {}
        for g in range(group):
            into(g)
        for g in range(group):
            hidden = hid[:, lanes_of[g]]
            held["norm", g] = norm_columns(hidden)
            held["cot", g] = cot[g].T.astype(f32)
        for g in range(group):
            through(g)
            held["second", g] = gradp[at_step, :, lanes_of[g]] + second_sum(g)
            held["out", g] = outp[at_step, :, lanes_of[g]] + output_sum(g)

        def back(g):
            grad_second = held["second", g]
            normed, scale = held["norm", g]
            grad = held["cot", g] + norm_back(grad_second * wide(cols[0], MAIN), normed, scale, 0)
            gh_out[:, lanes_of[g]] = grad
            alive = live[at_step * group + g].astype(f32)
            gattn[:, lanes_of[g]] = (alive * grad).astype(bf16)
            both = grad_second * normed
            for at in range(0, MAIN, 128):
                gsum[0] += both[:, at : at + 128]
                gsum[1] += grad_second[:, at : at + 128]

        def write(g):
            image = at_step * group + g
            alive = live[image].astype(f32)
            result = hid[:, lanes_of[g]] + alive * (held["out", g] + wide(cols[2], MAIN))
            out[g, :MAIN, :] = result.astype(bf16).T
            out[g, MAIN : MAIN + 1, :] = outl[pl.ds(image, 1), :].astype(bf16)

        def scale_rows(g):
            mixed = held["mixed", g].astype(bf16).astype(f32)
            both = mixed * att[:features, lanes_of[g]].astype(f32)
            for h in range(HEADS):
                span = slice(h * HEAD, (h + 1) * HEAD)
                row_inv = inv[g, h : h + 1, :]
                gml_out[span, lanes_of[g]] = (mixed[span] * row_inv).astype(bf16)
                row_dot = jnp.sum(both[span], axis=0, keepdims=True) * row_inv
                dots_out[g, h : h + 1, :] = row_dot

        dots_out[...] = jnp.zeros_like(dots_out)
        back(0)
        up_product()
        for g in range(1, group):
            back(g)
        for g in range(group):
            held["mixed", g] = dot(mw[...], gattn[:, lanes_of[g]])
        down_product()
        for g in range(group):
            scale_rows(g)
        merge_acc[...] += dot(att[...], gattn[...], NT)
        sums[2:3, :] += dot(jnp.ones((16, width), bf16), gb[at_step], NT)[0:1, :]
        for g in range(group):
            write(g)

    @pl.when(at_step == steps - 1)
    def _():
        for c, q in enumerate(now):
            biases[pl.ds(q, 1), :] = up_acc[features : features + 1, c * features : (c + 1) * features]

    @pl.when(step == steps - 1)
    def _():
        for at in range(kept.shape[0]):
            kept[at] = rounded(up_acc, 0, at)
            away[at] = rounded(up_acc, features, at).astype(bf16)
        to_core().start()

    @pl.when(step == 2 * steps - 1)
    def _():
        sums[0:1, :] += jnp.sum(gsum[0].T, axis=0, keepdims=True)
        sums[1:2, :] += jnp.sum(gsum[1].T, axis=0, keepdims=True)
        ends = jnp.concatenate([sums[...], biases[...]], axis=0)
        merged = jnp.concatenate([merge_acc[:features, :], merge_acc[features : features + 16, :], ends], axis=0)
        for at in range(features // 128):
            block = merged.shape[0]
            shared[at * block : (at + 1) * block] = merged[:, at * 128 : (at + 1) * 128].astype(bf16)
        rest = shared.shape[0] - (features // 128) * merged.shape[0]
        if rest:
            shared[shared.shape[0] - rest :] = jnp.zeros((rest, 128), bf16)
        for at in range(kept.shape[0]):
            beside[at] = rounded(up_acc, features, at).astype(bf16)
        to_chip().wait()
        for at in range(kept.shape[0]):
            mine[at] = (rounded(up_acc, 0, at) + r2[at].astype(f32)).astype(bf16)


def back_kernel(
    count, group, steps, late_group, late_steps, quarter, spread, plan,
    qkv, probs, edge, lp, lself, gml, dots, fi, fil, qkvl, attl, gmleft, aw, mine, beside, shared,
    tok, left, gh, ghl, gain, shift,
    out, quarter_out, spread_out, bias_out,
    gpa, acc, gpl, gplt, awp, cols, xl, outl, fis, minev, own, *comm,
):
    step = pl.program_id(0)
    features = aw.shape[0]
    rows = xl.shape[0]
    pairs = HEADS // 2
    last = pairs * steps
    pair = lax.rem(step // steps, pairs)
    at_group = lax.rem(step, steps)
    used = len(quarter.scratch())
    quarter.bind(minev, beside, comm[:used])
    spread.bind(comm[used:])
    engines = {"quarter": quarter, "spread": spread}
    at = lax.broadcasted_iota(jnp.int32, (rows, 128), 0)
    heads = jnp.where(at == lax.broadcasted_iota(jnp.int32, (rows, 128), 1) // HEAD, 1.0, 0.0)

    def fi_copy(k):
        width = group * MAIN
        return pltpu.make_async_copy(fi.at[:, pl.ds(k * width, width)], fis.at[k], own.at[k])

    def shared_copy():
        return pltpu.make_async_copy(shared, spread.send.at[0], own.at[steps])

    def early_copies():
        found = [pltpu.make_async_copy(mine, minev, own.at[steps + 1])]
        for part in range(pairs):
            for k in range(3):
                cut = pl.ds(k * features + part * 128, 128)
                to = pl.ds(part * 384 + k * 128, 128)
                sem = own.at[steps + 2 + part * 3 + k]
                found.append(pltpu.make_async_copy(aw.at[:, cut], awp.at[:, to], sem))
        return found

    @pl.when(step == 0)
    def _():
        peers = [
            (quarter.me_dp, flip(quarter.me_t, 1)), *(spread.plane(j)[0] for j in (1, 2, 3)),
            *(spread.line(j) for j in range(1, spread.far)),
        ]
        greet(peers)
        shared_copy().start()
        for copy in early_copies():
            copy.start()
        for k in range(steps):
            fi_copy(k).start()
        cols[...] = as_column(row_of(gain))
        gpl[...] = jnp.zeros_like(gpl)
        gplt[...] = jnp.zeros_like(gplt)
        acc[...] = jnp.zeros_like(acc)
        meet(peers)
        for s in range(quarter.streams):
            quarter.start(1, s)
        shared_copy().wait()
        spread.start("core", 0)

    for k in range(steps):
        pl.when(step == k)(lambda k=k: fi_copy(k).wait())

    @pl.when(step == 1)
    def _():
        for copy in early_copies():
            copy.wait()

    def advance(slot):
        for at, name, phase, s in plan:
            if at == slot:
                engines[name].advance(phase, s)

    for slot in sorted({item[0] for item in plan if item[0] < last + late_steps}):
        pl.when(step == slot)(functools.partial(advance, slot))

    @pl.when(step < last)
    def _():
        at16 = lax.broadcasted_iota(jnp.int32, (16, MAIN), 0)
        minus = jnp.where(at16 < 2, -1.0, 0.0).astype(bf16)
        ends_row = jnp.where(lax.broadcasted_iota(jnp.int32, (1, 16), 1) < 2, -1.0, 0.0)
        gp = gpa.at[at_group, pl.ds(pl.multiple_of(pair * 384, 128), 384)]
        held = {}
        units = [(g, r) for g in range(group) for r in range(2)]

        def lanes_of(g):
            return slice(g * MAIN, (g + 1) * MAIN)

        def part(at, r, g):
            return qkv[at * 128 + r * HEAD : at * 128 + (r + 1) * HEAD, lanes_of(g)]

        def lower(value):
            return value.astype(bf16).astype(f32)

        def prepare(g):
            image = at_group * group + g
            row = qkvl[pl.ds(image, 1), :]
            ql, kl, vl = (row[:, at * 128 : (at + 1) * 128] for at in range(3))
            gm_row = gmleft[pl.ds(image, 1), :]
            row_dot = jnp.sum(heads * (gm_row * attl[pl.ds(image, 1), :]), axis=1, keepdims=True)
            prob = jnp.sum(heads * (gm_row * vl), axis=1, keepdims=True)
            held["cols", g] = tuple(as_column(v) for v in (ql, kl, gm_row))
            held["left", g] = (vl, row_dot, prob - row_dot)

        def change(g, r):
            row_dot = dots[g, pl.ds(2 * pair + r, 1), :]
            high = row_dot.astype(bf16).astype(f32)
            rest = jnp.where(at16 == 0, high, jnp.where(at16 == 1, row_dot - high, 0.0)).astype(bf16)
            values = jnp.concatenate([part(2, r, g), minus], axis=0).T
            vl = held["left", g][0][:, r * HEAD : (r + 1) * HEAD]
            last_row = rows_where(0, jnp.concatenate([vl, ends_row], axis=1), 16, bf16)
            held["z", g, r] = dot(
                jnp.concatenate([values, last_row], axis=0),
                jnp.concatenate([gml[r * HEAD : (r + 1) * HEAD, lanes_of(g)], rest], axis=0),
            )

        def left_unit(g, r, edge_change):
            image = at_group * group + g
            span = slice(r * HEAD, (r + 1) * HEAD)
            head = pl.ds(2 * pair + r, 1)
            colq, colk, colg = (wide(v[span], MAIN) for v in held["cols", g])
            _, row_dot, self_change = held["left", g]
            row_dot, self_change = row_dot[r : r + 1, :], self_change[r : r + 1, :]
            edge_row, lp_row, self_prob = edge[g, head, :], lp[g, head, :], lself[g, head, 0:1]
            edge_grad = lower(edge_row * edge_change)
            left_change = jnp.sum(colg * part(2, r, g).astype(f32), axis=0, keepdims=True) - row_dot
            left_grad = lower(lp_row * left_change)
            self_grad = lower(self_prob * self_change)
            held["add", g, r] = (colk * edge_grad, colq * left_grad, colg * lower(lp_row))
            grad_q = jnp.sum(part(1, r, g).astype(f32) * left_grad, axis=1, keepdims=True)
            grad_k = jnp.sum(part(0, r, g).astype(f32) * edge_grad, axis=1, keepdims=True)
            grad_v = jnp.sum(
                gml[span, lanes_of(g)].astype(f32) * lower(edge_row), axis=1, keepdims=True
            )
            values = (
                (grad_q + self_grad * colk[:, 0:1]) * HEAD**-0.5,
                grad_k + self_grad * colq[:, 0:1],
                grad_v + lower(self_prob) * colg[:, 0:1],
            )
            at = lax.broadcasted_iota(jnp.int32, (HEAD, 128), 1)
            for k, value in enumerate(values):
                to = slice(k * 128 + r * HEAD, k * 128 + (r + 1) * HEAD)
                gplt[to, :] = jnp.where(at == image, lower(value), gplt[to, :])

        def scores(g, r):
            raised = probs[g, r]
            value = held.pop(("z", g, r))
            held["ds", g, r] = (raised.astype(f32) * value[:MAIN]).astype(bf16)
            left_unit(g, r, value[MAIN : MAIN + 1])
            held["v", g, r] = dot(gml[r * HEAD : (r + 1) * HEAD, lanes_of(g)], raised, NT)

        def grads(g, r):
            ds = held.pop(("ds", g, r))
            held["q", g, r] = dot(part(1, r, g), ds)
            held["k", g, r] = dot(part(0, r, g), ds, NT)

        def store(g, r):
            span = slice(r * HEAD, (r + 1) * HEAD)
            add_q, add_k, add_v = held.pop(("add", g, r))
            values = (
                (held.pop(("q", g, r)) + add_q) * HEAD**-0.5,
                held.pop(("k", g, r)) + add_k,
                held.pop(("v", g, r)) + add_v,
            )
            for at, value in enumerate(values):
                gp[at * 128 + r * HEAD : at * 128 + (r + 1) * HEAD, lanes_of(g)] = value.astype(bf16)

        number = len(units)
        thirds = sorted({0, -(-group // 3), -(-2 * group // 3), group})
        cuts = list(zip(thirds[:-1], thirds[1:]))

        def add_product(low, high):
            lanes = slice(low * MAIN, high * MAIN)
            before = jnp.where(at_group == 0, 0.0, acc[...]) if low == 0 else acc[...]
            acc[...] = before + dot(fis[at_group, :, lanes], gp[:, lanes], NT)

        for t in range(-4, number + 4):
            for g in range(group):
                if t == 2 * g - 4:
                    prepare(g)
            if 0 <= t + 2 < number:
                change(*units[t + 2])
            if 0 <= t < number:
                scores(*units[t])
            if 0 <= t - 1 < number:
                grads(*units[t - 1])
            if 0 <= t - 3 < number:
                store(*units[t - 3])
            for low, high in cuts[:-1]:
                if t - 3 == 2 * high - 1:
                    add_product(low, high)

        add_product(*cuts[-1])

        @pl.when(at_group == steps - 1)
        def _():
            one = jnp.ones((rows, 16), f32)
            gpl[pair] = gplt[...].T[:rows, :]
            acc[...] += dot(
                jnp.concatenate([fil[...], one], axis=1).astype(bf16), gpl[pair].astype(bf16), TN
            )
            weight = awp[:, pl.ds(pl.multiple_of(pair * 384, 128), 384)].astype(f32)
            by_gain = weight * acc[:features, :]
            by_shift = weight * acc[features : features + 1, :]
            fold = lambda v: jnp.sum((v[:, :128] + v[:, 128:256] + v[:, 256:]).T, axis=0, keepdims=True)
            shift_row = fold(by_shift)
            gain_row = (fold(by_gain) - row_of(shift) * shift_row) / row_of(gain)
            block = features + 32
            stream = pair + 1
            for k in range(3):
                lanes = slice(k * 128, (k + 1) * 128)
                spread.send[stream, k * block : k * block + features + 16] = acc[:, lanes].astype(bf16)
                ends = rows_where(0, gain_row[:, lanes], 16, f32) + rows_where(1, shift_row[:, lanes], 16, f32)
                spread.send[stream, k * block + features + 16 : (k + 1) * block] = ends.astype(bf16)
            rest = spread.send.shape[1] - 3 * block
            if rest:
                spread.send[stream, 3 * block :] = jnp.zeros((rest, 128), bf16)
            spread.start("core", stream)

    @pl.when(step == last)
    def _():
        take_left(left, xl, count)
        normed, scale = norm_rows(xl[...])
        packed = jnp.concatenate([gpl[p] for p in range(pairs)], axis=1).astype(bf16)
        grad_first = dot(packed, awp[...], NT)
        outl[...] = ghl[...] + norm_back(grad_first * row_of(gain), normed, scale, 1)

    @pl.when(step >= last)
    def _():
        held = {}
        first = (step - last) * late_group

        def product(g):
            image = first + g
            lanes = pl.ds(pl.multiple_of(lax.rem(image, group) * MAIN, MAIN), MAIN)
            held["grad", g] = dot(awp[...], gpa[image // group, :, lanes])

        def norm(g):
            held["norm", g] = norm_columns(tok[g].T.astype(f32))

        def finish(g):
            normed, scale = held.pop(("norm", g))
            grad = norm_back(held.pop(("grad", g)) * wide(cols[...], MAIN), normed, scale, 0)
            result = gh[:, g * MAIN : (g + 1) * MAIN] + grad
            out[g, :MAIN, :] = result.astype(bf16).T
            out[g, MAIN : MAIN + 1, :] = outl[pl.ds(first + g, 1), :].astype(bf16)

        product(0)
        norm(0)
        for g in range(late_group):
            if g + 1 < late_group:
                product(g + 1)
                norm(g + 1)
            finish(g)

    @pl.when(step == last + late_steps - 1)
    def _():
        for slot, name, phase, s in plan:
            if slot >= last + late_steps:
                engines[name].advance(phase, s)
        for s in range(quarter.streams):
            for side in range(2):
                quarter_out[s, side] = quarter.fin[s, side, : quarter.half]
        spread_out[...] = spread.out[...]
        block = features + 32
        for k in range(3):
            low = k * block + features + 16
            ends = spread.out[0, low : low + 16].astype(f32)
            at = lax.broadcasted_iota(jnp.int32, ends.shape, 0)
            row = jnp.sum(jnp.where(at == 8 + quarter.me_t, ends, 0.0), axis=0, keepdims=True)
            bias_out[:, k * 128 : (k + 1) * 128] = jnp.broadcast_to(row, (8, 128))


def place_kernel(
    pairs, quarter_in, spread_in, bias, output, input_grad,
    output_to, input_to, first_gain, first_shift, attend_to, attend_bias, merge_to, merge_bias,
    second_gain, second_shift, up_to, up_bias, down_to, down_bias,
    held, quarter, spread, attend, merge, up, down, sems, small,
):
    features = merge.shape[0]
    count = output.shape[0]
    got = [
        pltpu.make_async_copy(quarter_in, quarter, small.at[0]),
        pltpu.make_async_copy(spread_in, spread, small.at[1]),
    ]
    ins, outs = [], []
    for k, (src, to) in enumerate(((output, output_to), (input_grad, input_to))):
        for image in range(count):
            ins.append(pltpu.make_async_copy(src.at[image], held.at[k, image], sems.at[0, k, image]))
            outs.append(pltpu.make_async_copy(held.at[k, image], to.at[image], sems.at[1, k, image]))
    for copy in got + ins:
        copy.start()
    for copy in got:
        copy.wait()
    for s in range(quarter.shape[0]):
        lanes = slice(s * 128, (s + 1) * 128)
        up[:, lanes] = quarter[s, 0].astype(f32)
        down[lanes, :] = quarter[s, 1].astype(f32).T
    block = features + 32
    firsts, seconds, merge_ends = [], [], []
    for k in range(3):
        merge[:, k * 128 : (k + 1) * 128] = spread[0, k * block : k * block + features].astype(f32)
        low = k * block + features
        merge_ends.append(spread[0, low : low + 16].astype(f32))
        seconds.append(spread[0, low + 16 : low + 32].astype(f32))
        total = jnp.zeros((16, 128), f32)
        for pair in range(pairs):
            lanes = slice(k * features + pair * 128, k * features + (pair + 1) * 128)
            attend[:, lanes] = spread[pair + 1, k * block : k * block + features].astype(f32)
            total = total + spread[pair + 1, low + 16 : low + 32].astype(f32)
        firsts.append(total)
    puts = [
        pltpu.make_async_copy(src, to, small.at[2 + k])
        for k, (src, to) in enumerate(((attend, attend_to), (merge, merge_to), (up, up_to), (down, down_to)))
    ]
    for copy in puts:
        copy.start()
    merge_ends, firsts, seconds = (jnp.concatenate(v, axis=1) for v in (merge_ends, firsts, seconds))
    up_bias[...] = bias[0:1, :].reshape(features)
    merge_bias[...] = merge_ends[0:1, :].reshape(features)
    first_gain[...] = firsts[0:1, :].reshape(features)
    first_shift[...] = firsts[1:2, :].reshape(features)
    second_gain[...] = seconds[0:1, :].reshape(features)
    second_shift[...] = seconds[1:2, :].reshape(features)
    down_bias[...] = seconds[2:3, :].reshape(features)
    for to, k in ((0, 0), (1, 2)):
        rows = [
            spread[pair + 1, k * block + features : k * block + features + 16].astype(f32)[0:1, :]
            for pair in range(pairs)
        ]
        attend_bias[to : to + 1, :] = jnp.concatenate(rows, axis=1)
    for copy, on in zip(ins, outs):
        copy.wait()
        on.start()
    for copy in outs + puts:
        copy.wait()


def transfers(quarter, spread, steps, last, late_steps):
    end = last + late_steps
    when = {
        ("quarter", 0): [1, 3, 5, last + 6, end + 0.4],
        ("quarter", 1): [1, 3, 5, last + 6, end + 0.4],
        ("quarter", 2): [1, 4, last, end + 0.1, end + 0.45],
        ("spread", 0): [2, 4, last, last + 2, last + 4, end + 0.01],
        ("spread", 1): [4, last, last + 2, last + 5, end + 0.02, end + 0.15],
        ("spread", 2): [last, last + 3, end + 0.05, end + 0.31, end + 0.51, end + 0.6],
        ("spread", 3): [last + 1, last + 5, end + 0.3, end + 0.5, end + 0.7],
    }
    plan = []
    for (name, s), times in when.items():
        phases = 5 if name == "quarter" else len(spread.phases(s))
        times = times[:2] + [times[2]] * (phases - len(times)) + times[2:]
        plan += [(time, name, phase + 1, s) for phase, time in enumerate(times)]
    plan.sort(key=lambda item: item[0])
    return [(int(time), *rest) for time, *rest in plan]


def whole(*dims):
    return pl.BlockSpec(dims, lambda i: (0,) * len(dims))


def once(*dims):
    return pl.BlockSpec(dims, lambda i: (0,) * len(dims), pipeline_mode=pl.Buffered(1))


LIVE = pl.BlockSpec(memory_space=pltpu.SMEM)
ANY = pl.BlockSpec(memory_space=pl.ANY)


def params(**more):
    return pltpu.CompilerParams(
        vmem_limit_bytes=60 * 2**20, dimension_semantics=("arbitrary",), **more
    )


def shape(dtype, *dims):
    return jax.ShapeDtypeStruct(dims, dtype)


def shards(
    mesh_sizes, tokens, image_mask, patch_mask, first_gain, first_shift, attend_weight, attend_bias,
    merge_weight, merge_bias, second_gain, second_shift, up_weight, up_bias, down_weight,
    down_bias, cotangent,
):
    n, seq, d = tokens.shape
    packed = attend_weight.shape[1]
    rows = -(-n // 16) * 16
    group = 2 if n % 2 == 0 else 1
    steps = n // group
    width = group * MAIN
    pairs = HEADS // 2
    total = n * MAIN
    left = pl.BlockSpec((n, 16, d), lambda i: (0, MAIN // 16, 0), pipeline_mode=pl.Buffered(1))
    quarters, share = mesh_sizes[1], up_weight.shape[1]

    here = lambda i: jnp.minimum(i, steps - 1)
    cols = lambda r: pl.BlockSpec((r, width), lambda i: (0, here(i)))
    images = lambda *dims: pl.BlockSpec((group, *dims), lambda i: (here(i),) + (0,) * len(dims))
    fi, qkv, probs, edges, invs, lp, lself, att, hid, fil, qkvl, attl, hidl, wall, ball = pl.pallas_call(
        functools.partial(attend_kernel, n, group, steps),
        grid=(steps + 1,),
        in_specs=[
            once(group, MAIN, d),
            pl.BlockSpec((group, MAIN, d), lambda i: (here(i + 1), 0, 0)),
            left, whole(n, MAIN), LIVE, whole(d), whole(d), whole(2, d), whole(d),
            once(d, packed), once(d, d), ANY, whole(share), ANY,
        ],
        out_specs=[
            cols(d + 16), ANY, images(HEADS, MAIN, MAIN), images(16, MAIN),
            images(16, MAIN), images(16, MAIN), images(16, 128), cols(d + 16),
            pl.BlockSpec((d, width), lambda i: (0, jnp.maximum(i, 1) - 1)),
            whole(rows, d), whole(rows, packed), whole(rows, d), whole(rows, d), ANY, ANY,
        ],
        out_shape=[
            shape(bf16, d + 16, total), shape(bf16, packed, total), shape(bf16, n, HEADS, MAIN, MAIN),
            shape(f32, n, 16, MAIN), shape(f32, n, 16, MAIN), shape(f32, n, 16, MAIN),
            shape(f32, n, 16, 128), shape(bf16, d + 16, total), shape(f32, d, total),
            shape(f32, rows, d), shape(f32, rows, packed), shape(f32, rows, d), shape(f32, rows, d),
            shape(bf16, quarters, 2, d, share), shape(bf16, quarters, 16, share),
        ],
        scratch_shapes=[
            pltpu.VMEM((packed, d + 128), bf16), pltpu.VMEM((d, d + 128), bf16),
            pltpu.VMEM((d + 128, width), bf16), pltpu.VMEM((d + 128, width), bf16),
            pltpu.VMEM((2, d, 128), f32), pltpu.VMEM((group, 16, MAIN), f32),
            pltpu.VMEM((2, packed, width), bf16),
            pltpu.VMEM((3, d, width), bf16),
            pltpu.VMEM((rows, d), f32), pltpu.VMEM((rows, packed), f32), pltpu.VMEM((rows, d), f32),
            pltpu.VMEM((16, share), bf16), pltpu.SemaphoreType.DMA((9,)), pltpu.SemaphoreType.DMA((9,)),
            pltpu.SemaphoreType.DMA((3,)), pltpu.SemaphoreType.DMA((2,)),
        ],
        compiler_params=params(collective_id=0, has_side_effects=True),
        name="attend",
    )(
        tokens, tokens, tokens, patch_mask, image_mask, first_gain, first_shift, attend_bias, merge_bias,
        attend_weight, merge_weight, up_weight, up_bias, down_weight,
    )

    streams = d // 128
    block = d + 32
    chunk = -(-3 * block // (8 * 16)) * 16
    ahead = lambda i: (i // steps) * (i - steps) + (1 - i // steps) * (i + 1 - (i + 1) // steps)
    late_images = lambda *dims: pl.BlockSpec(
        (group, *dims), lambda i: ((i // steps) * (i - steps),) + (0,) * len(dims)
    )
    late_cols = lambda r: pl.BlockSpec((r, width), lambda i: (0, (i // steps) * (i - steps)))
    quarter_vm = lambda dtype: pltpu.VMEM((streams, 2 * d, 128), dtype)
    output, gh, gml, dots, ghl, gmleft, mine, beside, shared = pl.pallas_call(
        functools.partial(feed_kernel, n, group, steps),
        grid=(2 * steps,),
        in_specs=[
            once(d, width), pl.BlockSpec((d, width), lambda i: (0, ahead(i))), late_cols(d + 16), late_images(16, MAIN),
            once(group, MAIN, d), pl.BlockSpec((group, MAIN, d), lambda i: (ahead(i), 0, 0)), left, LIVE, whole(d), whole(d), whole(d),
            whole(rows, d), whole(rows, d), once(quarters, 2, d, share), once(quarters, 16, share), once(d, d),
        ],
        out_specs=[
            late_images(seq, d), late_cols(d), late_cols(d), late_images(16, MAIN),
            whole(rows, d), whole(rows, d),
            once(streams, 2 * d, 128), once(streams, 2 * d, 128), once(8 * chunk, 128),
        ],
        out_shape=[
            shape(bf16, n, seq, d), shape(f32, d, total), shape(bf16, d, total),
            shape(f32, n, 16, MAIN), shape(f32, rows, d), shape(f32, rows, d),
            shape(bf16, streams, 2 * d, 128), shape(bf16, streams, 2 * d, 128), shape(bf16, 8 * chunk, 128),
        ],
        scratch_shapes=[
            pltpu.VMEM((quarters, share, d + 128), bf16), pltpu.VMEM((quarters, d, share), bf16),
            pltpu.VMEM((steps, d + 128, width), bf16),
            pltpu.VMEM((2 * share, width), bf16), pltpu.VMEM((2 * share, width), bf16),
            pltpu.VMEM((steps, d, width), bf16), pltpu.VMEM((d, width), bf16),
            pltpu.VMEM((3, d, 128), f32), pltpu.VMEM((2, d, 128), f32),
            pltpu.VMEM((rows, d), f32), pltpu.VMEM((rows, d), f32),
            pltpu.VMEM((rows, d + 16), bf16), pltpu.VMEM((rows, d), bf16),
            pltpu.VMEM((quarters, rows, share), bf16), pltpu.VMEM((quarters, rows, share), bf16),
            pltpu.VMEM((steps, d, width), f32), pltpu.VMEM((steps, d, width), f32),
            pltpu.VMEM((d + 16, 2 * share), f32), pltpu.VMEM((d, 2 * share), f32),
            pltpu.VMEM((d + 16, d), f32), pltpu.VMEM((8, d), f32), pltpu.VMEM((8, d), f32),
            quarter_vm(f32), quarter_vm(bf16), quarter_vm(bf16), quarter_vm(bf16), quarter_vm(bf16),
            pltpu.SemaphoreType.DMA((2,)), pltpu.SemaphoreType.DMA((2,)),
        ],
        compiler_params=params(collective_id=1, has_side_effects=True),
        name="feed",
    )(
        hid, hid, att, invs, cotangent, cotangent, cotangent, image_mask, second_gain, second_shift, down_bias, hidl, attl,
        wall, ball, merge_weight,
    )

    late_group, late_steps = group, steps
    group = next(g for g in (7, 2, 1) if n % g == 0)
    steps = n // group
    width = group * MAIN
    last = pairs * steps
    quarter = Quarter(mesh_sizes[0], streams, 2 * d)
    spread = Spread(mesh_sizes, pairs + 1, chunk)
    plan = transfers(quarter, spread, steps, last, late_steps)
    side = lambda i: (i + late_steps) // (last + late_steps)
    early = lambda i: i - side(i) * (i - (last - 1))
    late = lambda i: side(i) * (i - last)
    by_pair = lambda r: pl.BlockSpec((r, width), lambda i: (early(i) // steps, early(i) % steps))
    early_images = lambda *dims: pl.BlockSpec((group, *dims), lambda i: (early(i) % steps,) + (0,) * len(dims))
    pair_lanes = lambda w: pl.BlockSpec((rows, w), lambda i: (0, early(i) // steps))
    late_images = lambda *dims: pl.BlockSpec((late_group, *dims), lambda i: (late(i),) + (0,) * len(dims))
    input_grad, quarter_sum, spread_sum, bias_sum = pl.pallas_call(
        functools.partial(back_kernel, n, group, steps, late_group, late_steps, quarter, spread, plan),
        grid=(last + late_steps,),
        in_specs=[
            by_pair(3 * 128),
            pl.BlockSpec((group, 2, MAIN, MAIN), lambda i: (early(i) % steps, early(i) // steps, 0, 0)),
            early_images(16, MAIN), early_images(16, MAIN), early_images(16, 128), by_pair(128),
            early_images(16, MAIN), ANY,
            whole(rows, d), pair_lanes(384), pair_lanes(128), pair_lanes(128), ANY, ANY, ANY, ANY,
            late_images(MAIN, d), left, pl.BlockSpec((d, late_group * MAIN), lambda i: (0, late(i))),
            whole(rows, d), whole(d), whole(d),
        ],
        out_specs=[
            late_images(seq, d), once(streams, 2, d, 128), once(pairs + 1, 8 * chunk, 128), whole(8, d),
        ],
        out_shape=[
            shape(bf16, n, seq, d), shape(bf16, streams, 2, d, 128), shape(bf16, pairs + 1, 8 * chunk, 128),
            shape(f32, 8, d),
        ],
        scratch_shapes=[
            pltpu.VMEM((steps, packed, width), bf16), pltpu.VMEM((d + 16, 384), f32),
            pltpu.VMEM((pairs, rows, 384), f32), pltpu.VMEM((384, 128), f32),
            pltpu.VMEM((d, packed), bf16), pltpu.VMEM((d, 128), f32),
            pltpu.VMEM((rows, d), f32), pltpu.VMEM((rows, d), f32),
            pltpu.VMEM((steps, d + 16, width), bf16), pltpu.VMEM((streams, 2 * d, 128), bf16),
            pltpu.SemaphoreType.DMA((steps + 2 + 3 * pairs,)),
            *quarter.scratch(), *spread.scratch(),
        ],
        compiler_params=params(collective_id=2, has_side_effects=True),
        name="back",
    )(
        qkv, probs, edges, lp, lself, gml, dots, fi, fil, qkvl, attl, gmleft, attend_weight,
        mine, beside, shared, tokens, tokens, gh, ghl, first_gain, first_shift,
    )
    row = lambda: pl.BlockSpec(memory_space=pltpu.VMEM)
    return pl.pallas_call(
        functools.partial(place_kernel, pairs),
        in_specs=[ANY, ANY, row(), ANY, ANY],
        out_specs=[
            ANY, ANY, row(), row(), ANY, row(), ANY, row(), row(), row(), ANY, row(), ANY, row(),
        ],
        out_shape=[
            shape(bf16, n, seq, d), shape(bf16, n, seq, d), shape(f32, d), shape(f32, d),
            shape(f32, d, packed), shape(f32, 2, d), shape(f32, d, d), shape(f32, d), shape(f32, d),
            shape(f32, d), shape(f32, d, share), shape(f32, share), shape(f32, share, d), shape(f32, d),
        ],
        scratch_shapes=[
            pltpu.VMEM((2, n, seq, d), bf16), pltpu.VMEM((streams, 2, d, 128), bf16),
            pltpu.VMEM((pairs + 1, 8 * chunk, 128), bf16), pltpu.VMEM((d, packed), f32), pltpu.VMEM((d, d), f32),
            pltpu.VMEM((d, share), f32), pltpu.VMEM((share, d), f32),
            pltpu.SemaphoreType.DMA((2, 2, n)), pltpu.SemaphoreType.DMA((6,)),
        ],
        compiler_params=pltpu.CompilerParams(vmem_limit_bytes=60 * 2**20),
        name="place",
    )(quarter_sum, spread_sum, bias_sum, output, input_grad)


def solution(mesh):
    split = ("dp", "tensor")
    in_specs = (
        P(split, None, None), P(split), P(split, None), P(), P(), P(), P(), P(), P(), P(), P(),
        P(None, "tensor"), P("tensor"), P("tensor", None), P(), P(split, None, None),
    )
    out_specs = (
        P(split, None, None), P(split, None, None), P(), P(), P(), P(), P(), P(), P(), P(),
        P(None, "tensor"), P("tensor"), P("tensor", None), P(),
    )
    sizes = (mesh.shape["dp"], mesh.shape["tensor"])
    return jax.shard_map(functools.partial(shards, sizes), mesh=mesh, in_specs=in_specs, out_specs=out_specs, check_vma=False)
```

```python
import functools

import jax
import jax.numpy as jnp
from jax import lax
from jax.experimental import pallas as pl
from jax.experimental.pallas import tpu as pltpu
from jax.sharding import PartitionSpec as P

HEADS = 6
HEAD = 64
MAIN = 256
EPS = 1e-06
MASKED = -1e30
f32, bf16 = jnp.float32, jnp.bfloat16

NN = ((1,), (0,))
NT = ((1,), (1,))
TN = ((0,), (0,))


def dot(left, right, dims=NN):
    return lax.dot_general(left, right, (dims, ((), ())), preferred_element_type=f32)


def rows_where(index, value, rows, dtype):
    columns = value.shape[-1]
    at = lax.broadcasted_iota(jnp.int32, (rows, columns), 0)
    return jnp.where(at == index, value, 0.0).astype(dtype)


def wide(column, width):
    return jnp.concatenate([column] * (width // 128), axis=1)


def as_column(row):
    return jnp.broadcast_to(row, (128, row.shape[1])).T


def norm_columns(values):
    center = values - jnp.mean(values, axis=0, keepdims=True)
    scale = lax.rsqrt(jnp.mean(center * center, axis=0, keepdims=True) + EPS)
    return center * scale, scale


def norm_rows(values):
    center = values - jnp.mean(values, axis=1, keepdims=True)
    scale = lax.rsqrt(jnp.mean(center * center, axis=1, keepdims=True) + EPS)
    return center * scale, scale


def norm_back(grad, normed, scale, axis):
    mean_grad = jnp.mean(grad, axis=axis, keepdims=True)
    mean_both = jnp.mean(grad * normed, axis=axis, keepdims=True)
    return scale * (grad - mean_grad - normed * mean_both)


def gelu_both(pre):
    curve = 0.5 + 0.5 * lax.erf(pre * 0.7071067811865476)
    bell = 0.3989422804014327 * jnp.exp(-0.5 * pre * pre)
    return pre * curve, curve + pre * bell


def head_rows(rows, features):
    at = lax.broadcasted_iota(jnp.int32, (rows, features), 0)
    head = lax.broadcasted_iota(jnp.int32, (rows, features), 1) // HEAD
    return jnp.where(at == head, 1.0, 0.0)


def lane_live(live_ref, first, count):
    flags = [
        jnp.full((1, MAIN), live_ref[first + g].astype(f32)) for g in range(count)
    ]
    return jnp.concatenate(flags, axis=1)


def row_live(live_ref, count, rows):
    at = lax.broadcasted_iota(jnp.int32, (rows, 1), 0)
    flags = jnp.zeros((rows, 1), f32)
    for image in range(count):
        flags = jnp.where(at == image, live_ref[image].astype(f32), flags)
    return flags


def take_left(left_ref, to_ref, count):
    to_ref[...] = jnp.zeros_like(to_ref)
    for image in range(count):
        to_ref[image : image + 1, :] = left_ref[image].astype(f32)[0:1, :]


def flip(place, bits):
    if bits & 1:
        place = place + 1 - 2 * lax.rem(place, 2)
    if bits & 2:
        place = place + 2 - 4 * (place // 2)
    return place


def remote(src, dst, sends, recvs, index, peer):
    return pltpu.make_async_remote_copy(
        src_ref=src, dst_ref=dst, send_sem=sends.at[index], recv_sem=recvs.at[index],
        device_id=peer, device_id_type=pl.DeviceIdType.MESH,
    )


def greet(peers):
    barrier = pltpu.get_barrier_semaphore()
    for peer in peers:
        pl.semaphore_signal(barrier, inc=1, device_id=peer, device_id_type=pl.DeviceIdType.MESH)


def meet(peers):
    pl.semaphore_wait(pltpu.get_barrier_semaphore(), len(peers))


class Quarter:
    def __init__(self, dp, streams, rows):
        self.far = dp // 2
        self.streams, self.half = streams, rows // 2
        self.chunk = -(-self.half // (16 * self.far)) * 16
        self.padded = self.chunk * self.far
        self.copies = 3 + 2 * (self.far - 1)

    def scratch(self):
        s = self.streams
        vm = lambda *dims: pltpu.VMEM((s, *dims, 128), bf16)
        return [
            vm(2 * self.half), vm(2 * self.half), vm(self.half), vm(self.padded),
            vm(max(self.far - 1, 1), self.chunk), vm(2, self.padded),
            pltpu.SemaphoreType.DMA((s, self.copies)), pltpu.SemaphoreType.DMA((s, self.copies)),
        ]

    def bind(self, mine, beside, refs):
        self.mine, self.beside = mine, beside
        self.r1, self.work, self.r2, self.cur, self.r3, self.fin, self.sends, self.recvs = refs
        self.me_dp, self.me_t = lax.axis_index("dp"), lax.axis_index("tensor")
        self.x, self.z = lax.rem(self.me_dp, 2), self.me_dp // 2

    def line(self, j):
        return (lax.rem(self.z + j, self.far) * 2 + self.x, self.me_t)

    def copies_of(self, phase, s):
        across = (self.z * 2 + 1 - self.x, self.me_t)
        cp = lambda index, src, dst, peer: remote(src, dst, self.sends, self.recvs, (s, index), peer)
        if phase == 1:
            return [cp(0, self.beside.at[s], self.r1.at[s], (self.me_dp, flip(self.me_t, 1)))]
        if phase == 2:
            other = pl.ds(pl.multiple_of((1 - self.x) * self.half, 16), self.half)
            return [cp(1, self.work.at[s, other], self.r2.at[s], across)]
        found = []
        if phase == 3:
            for j in range(1, self.far):
                place = lax.rem(self.z + j, self.far)
                src = self.cur.at[s, pl.ds(pl.multiple_of(place * self.chunk, 16), self.chunk)]
                found.append(cp(1 + j, src, self.r3.at[s, j - 1], self.line(j)))
        if phase == 4:
            ref = self.fin.at[s, self.x, pl.ds(pl.multiple_of(self.z * self.chunk, 16), self.chunk)]
            for j in range(1, self.far):
                found.append(cp(self.far + j, ref, ref, self.line(j)))
        if phase == 5:
            ref = self.fin.at[s, self.x, pl.ds(0, self.half)]
            found.append(cp(2 * self.far, ref, ref, across))
        return found

    def start(self, phase, s):
        for copy in self.copies_of(phase, s):
            copy.start()

    def advance(self, phase, s):
        for copy in self.copies_of(phase, s):
            copy.wait()
        if phase == 1:
            self.work[s] = (self.mine[s].astype(f32) + self.r1[s].astype(f32)).astype(bf16)
        if phase == 2:
            kept = self.work[s, pl.ds(pl.multiple_of(self.x * self.half, 16), self.half)]
            self.cur[s, : self.half] = (kept.astype(f32) + self.r2[s].astype(f32)).astype(bf16)
            if self.padded > self.half:
                self.cur[s, self.half :] = jnp.zeros((self.padded - self.half, 128), bf16)
        if phase == 3:
            mine = pl.ds(pl.multiple_of(self.z * self.chunk, 16), self.chunk)
            total = self.cur[s, mine].astype(f32)
            for j in range(self.far - 1):
                total = total + self.r3[s, j].astype(f32)
            self.fin[s, self.x, mine] = total.astype(bf16)
        if phase < 5:
            self.start(phase + 1, s)


class Spread:
    def __init__(self, mesh_sizes, streams, chunk):
        self.dp, self.tensor = mesh_sizes
        self.far = self.dp // 2
        self.hops = self.far.bit_length() - 1
        self.streams, self.chunk = streams, chunk
        self.copies = 1 + 3 + (self.far - 1) + 3 + 1

    def phases(self, s):
        hops = ["line"] if s == self.streams - 1 else [("hop", k) for k in range(self.hops)]
        return ["core", "plane", *hops, "plane back", "core back"]

    def scratch(self):
        s, c = self.streams, self.chunk
        vm = lambda *dims: pltpu.VMEM((s, *dims, 128), bf16)
        return [
            vm(8 * c), vm(4 * c), vm(4 * c), vm(3, c), vm(self.far, c), vm(c), vm(8 * c),
            pltpu.SemaphoreType.DMA((s, self.copies)), pltpu.SemaphoreType.DMA((s, self.copies)),
        ]

    def bind(self, refs):
        self.send, self.r1, self.work, self.r2, self.r3, self.cur, self.out, self.ss, self.rs = refs
        self.me_dp, self.me_t = lax.axis_index("dp"), lax.axis_index("tensor")
        self.x, self.z = lax.rem(self.me_dp, 2), self.me_dp // 2
        self.c, self.y = lax.rem(self.me_t, 2), self.me_t // 2
        self.place = 2 * self.y + self.x

    def plane(self, j):
        x = 1 - self.x if j & 1 else self.x
        y = 1 - self.y if j & 2 else self.y
        return (self.z * 2 + x, 2 * y + self.c), 2 * y + x

    def core(self):
        return (self.me_dp, 2 * self.y + 1 - self.c)

    def line(self, j):
        return (lax.rem(self.z + j, self.far) * 2 + self.x, self.me_t)

    def hop(self, k):
        step = 1 << k
        there = self.z + step - 2 * step * lax.rem(self.z // step, 2)
        return (there * 2 + self.x, self.me_t)

    def rows(self, first, count):
        return pl.ds(pl.multiple_of(first * self.chunk, 16), count * self.chunk)

    def copies_of(self, kind, s):
        cp = lambda index, src, dst, peer: remote(src, dst, self.ss, self.rs, (s, index), peer)
        if kind == "core":
            return [cp(0, self.send.at[s, self.rows(4 * (1 - self.c), 4)], self.r1.at[s], self.core())]
        found = []
        if kind == "plane":
            for j in (1, 2, 3):
                peer, place = self.plane(j)
                found.append(cp(j, self.work.at[s, self.rows(place, 1)], self.r2.at[s, j - 1], peer))
        if kind == "line":
            for j in range(1, self.far):
                ref = self.r3.at[s, self.z]
                found.append(cp(3 + j, ref, ref, self.line(j)))
        if kind[0] == "hop":
            found.append(cp(4 + kind[1], self.cur.at[s], self.r3.at[s, kind[1]], self.hop(kind[1])))
        if kind == "plane back":
            mine = self.out.at[s, self.rows(4 * self.c + self.place, 1)]
            for j in (1, 2, 3):
                found.append(cp(2 + self.far + j, mine, mine, self.plane(j)[0]))
        if kind == "core back":
            ref = self.out.at[s, self.rows(4 * self.c, 4)]
            found.append(cp(6 + self.far, ref, ref, self.core()))
        return found

    def start(self, kind, s):
        for copy in self.copies_of(kind, s):
            copy.start()

    def advance(self, phase, s):
        phases = self.phases(s)
        kind = phases[phase - 1]
        for copy in self.copies_of(kind, s):
            copy.wait()
        mine = self.rows(4 * self.c + self.place, 1)
        if kind == "core":
            half = self.send[s, self.rows(4 * self.c, 4)].astype(f32)
            self.work[s] = (half + self.r1[s].astype(f32)).astype(bf16)
        if kind == "plane":
            total = self.work[s, self.rows(self.place, 1)].astype(f32)
            for j in range(3):
                total = total + self.r2[s, j].astype(f32)
            if phases[2] == "line":
                self.r3[s, self.z] = total.astype(bf16)
            else:
                self.cur[s] = total.astype(bf16)
        if kind == "line":
            total = self.r3[s, 0].astype(f32)
            for j in range(1, self.far):
                total = total + self.r3[s, j].astype(f32)
            self.out[s, mine] = total.astype(bf16)
        if kind[0] == "hop":
            total = (self.cur[s].astype(f32) + self.r3[s, kind[1]].astype(f32)).astype(bf16)
            self.cur[s] = total
            if kind[1] == self.hops - 1:
                self.out[s, mine] = total
        if phase < len(phases):
            self.start(phases[phase], s)


def row_of(ref):
    return ref[...].astype(f32).reshape(1, ref.shape[0])


def parts_of(at, pair):
    return slice(pair * 384 + at * 128, pair * 384 + (at + 1) * 128)


def attend_kernel(
    count, group, steps,
    tok0, tok, left, pmask, live, gain, shift, abias, mbias, aw, mw, up, ubias, down,
    fi_out, qkv_out, probs_out, edge_out, inv_out, lp_out, lself_out, att_out, hid_out,
    fil_out, qkvl_out, attl_out, hidl_out, wall, ball,
    awt, mwt, fia, atta, cols, edges, qkv2, toks, xl, qkvl, attl, brow, sends, recvs, own, leave,
):
    step = pl.program_id(0)
    me_dp, me_t = lax.axis_index("dp"), lax.axis_index("tensor")
    beside, across = (me_dp, flip(me_t, 1)), (me_dp, flip(me_t, 2))

    def places(owner):
        return (wall.at[owner, 0], wall.at[owner, 1], ball.at[owner])

    def first_copies(peer, first):
        return [
            remote(src, dst, sends, recvs, first + k, peer)
            for k, (src, dst) in enumerate(zip((up, down, brow), places(me_t)))
        ]

    def second_copies():
        return [
            remote(ref, ref, sends, recvs, 6 + k, beside) for k, ref in enumerate(places(flip(me_t, 2)))
        ]

    def own_copies():
        return [
            pltpu.make_async_copy(src, dst, own.at[k])
            for k, (src, dst) in enumerate(zip((up, down, brow), places(me_t)))
        ]

    @pl.when(step == 0)
    def _():
        greet((beside, across))
        brow[...] = rows_where(0, row_of(ubias), 16, bf16)
        meet((beside, across))
        for copy in first_copies(across, 3) + first_copies(beside, 0) + own_copies():
            copy.start()

    @pl.when(step == steps - 2)
    def _():
        for copy in first_copies(across, 3):
            copy.wait()
        for copy in second_copies():
            copy.start()

    features = aw.shape[0]
    packed = aw.shape[1]
    rows = xl.shape[0]
    width = group * MAIN
    pairs = HEADS // 2
    heads = head_rows(rows, features)

    def first_norm(block):
        tokens = jnp.concatenate([block[g].T for g in range(group)], axis=1)
        normed, _ = norm_columns(tokens.astype(f32))
        return tokens, (normed * wide(cols[0], width) + wide(cols[1], width)).astype(bf16)

    def project(slot, part):
        span = slice(part * features, (part + 1) * features)
        qkv2[slot, span, :] = dot(awt[span, :], fia[slot]).astype(bf16)

    @pl.when(step == 0)
    def _():
        ab = abias[...].astype(f32)
        for pair in range(pairs):
            for at in range(3):
                cut = slice(at * features + pair * 128, at * features + (pair + 1) * 128)
                to = parts_of(at, pair)
                scale = HEAD**-0.5 if at == 0 else 1.0
                awt[to, :features] = (aw[:, cut].astype(f32).T * scale).astype(bf16)
                if at == 1:
                    bias = jnp.zeros((1, 128), f32)
                else:
                    bias = ab[at // 2 : at // 2 + 1, pair * 128 : (pair + 1) * 128] * scale
                awt[to, features:] = rows_where(0, bias, 128, f32).T.astype(bf16)
        mwt[:, :features] = mw[...].astype(f32).T.astype(bf16)
        mwt[:, features:] = rows_where(0, row_of(mbias), 128, f32).T.astype(bf16)
        ones = rows_where(0, jnp.ones((1, width), f32), 128, bf16)
        fia[0, features:, :] = ones
        fia[1, features:, :] = ones
        atta[features:, :] = ones
        cols[0] = as_column(row_of(gain))
        cols[1] = as_column(row_of(shift))
        edges[...] = jnp.zeros_like(edges)
        take_left(left, xl, count)
        normed, _ = norm_rows(xl[...])
        fil = (normed * row_of(gain) + row_of(shift)).astype(bf16)
        fil_out[...] = fil.astype(f32)
        plain = dot(fil, aw[...])
        for pair in range(pairs):
            for at in range(3):
                cut = slice(at * features + pair * 128, at * features + (pair + 1) * 128)
                value = plain[:, cut]
                if at != 1:
                    value = value + ab[at // 2 : at // 2 + 1, pair * 128 : (pair + 1) * 128]
                value = value.astype(bf16).astype(f32)
                qkvl[:, parts_of(at, pair)] = value * (HEAD**-0.5) if at == 0 else value
        qkvl_out[...] = qkvl[...]
        attl[...] = jnp.zeros_like(attl)
        tokens, fi = first_norm(tok0)
        toks[0] = tokens
        fia[0, :features, :] = fi
        for part in range(3):
            project(0, part)

    def qkv_copy(index):
        slot = lax.rem(index, 2)
        lanes = pl.ds(pl.multiple_of(index * width, 128), width)
        return pltpu.make_async_copy(qkv2.at[slot], qkv_out.at[:, lanes], leave.at[slot])

    def fi_copy(index):
        slot = lax.rem(index, 2)
        lanes = pl.ds(pl.multiple_of(index * width, 128), width)
        src = fia.at[slot, pl.ds(0, features + 16)]
        return pltpu.make_async_copy(src, fi_out.at[:, lanes], leave.at[2 + slot])

    @pl.when(step > 0)
    def _():
        qkv_copy(step - 1).wait()
        fi_copy(step - 1).wait()

    def merge_branch():
        return dot(mwt[...], atta[...])

    def hidden_of(branch, index):
        tokens = toks[lax.rem(index, 3)].astype(f32)
        return tokens + lane_live(live, index * group, group) * branch

    @pl.when(step < steps)
    def _():
        now, later = lax.rem(step, 2), lax.rem(step + 1, 2)
        qkv_copy(step).start()
        fi_copy(step).start()
        one_row = rows_where(0, jnp.ones((1, MAIN), f32), 16, bf16)
        held = {}
        units = [(g, h) for g in range(group) for h in range(HEADS)]

        def lanes_of(g):
            return slice(g * MAIN, (g + 1) * MAIN)

        def part(at, g, h):
            low = (h // 2) * 384 + at * 128 + (h % 2) * HEAD
            return qkv2[now, low : low + HEAD, lanes_of(g)]

        def all_heads(at, g):
            return jnp.concatenate(
                [qkv2[now, parts_of(at, pair), lanes_of(g)] for pair in range(pairs)], axis=0
            )

        def begin(g):
            image = step * group + g
            row = qkvl[pl.ds(image, 1), :]
            ql, kl, vl = (
                jnp.concatenate([row[:, parts_of(at, pair)] for pair in range(pairs)], axis=1)
                for at in range(3)
            )
            key_bias = jnp.where(pmask[pl.ds(image, 1), :] == 1, 0.0, MASKED)
            moved = pltpu.roll(key_bias, 1, axis=1)
            at = lax.broadcasted_iota(jnp.int32, moved.shape, 1)
            main_bias = jnp.where(at == 0, 0.0, moved)
            left_bias = moved[:, 0:1]
            held["bias", g] = rows_where(0, main_bias, 16, bf16)
            held["vl", g] = vl
            held["slk", g] = dot((heads * kl).astype(bf16), all_heads(0, g)) + left_bias
            held["sl", g] = dot((heads * ql).astype(bf16), all_heads(1, g)) + main_bias
            held["self", g] = jnp.sum(heads * (ql * kl), axis=1, keepdims=True) + left_bias

        def left_query(g):
            sl, self_score = held.pop(("sl", g)), held.pop(("self", g))
            peak = jnp.maximum(jnp.max(sl, axis=1, keepdims=True), self_score)
            raised = jnp.exp(sl - peak)
            raised_self = jnp.exp(self_score - peak)
            inv = 1.0 / (jnp.sum(raised, axis=1, keepdims=True) + raised_self)
            lp = raised * inv
            lself = raised_self * inv
            lp_out[g] = lp
            lself_out[g] = jnp.broadcast_to(lself, (rows, 128))
            mixed = dot(lp.astype(bf16), all_heads(2, g), NT) + lself * held["vl", g]
            image = step * group + g
            attl[pl.ds(image, 1), :] = (
                jnp.sum(mixed * heads, axis=0, keepdims=True).astype(bf16).astype(f32)
            )

        def scores(g, h):
            held["s", g, h] = dot(
                jnp.concatenate([part(1, g, h), held["bias", g]], axis=0),
                jnp.concatenate([part(0, g, h), one_row], axis=0),
                TN,
            )

        def soften(g, h):
            value = held.pop(("s", g, h))
            slk = held["slk", g][h : h + 1, :]
            peak = jnp.maximum(jnp.max(value, axis=0, keepdims=True), slk)
            raised = jnp.exp(value - peak).astype(bf16)
            probs_out[g, h] = raised
            held["e", g, h] = raised
            edge = jnp.exp(slk - peak)
            held["edge", g, h] = edge
            edges[g, h : h + 1, :] = edge

        def mix(g, h):
            held["o", g, h] = dot(
                jnp.concatenate([part(2, g, h), one_row], axis=0), held.pop(("e", g, h))
            )

        def add_left(g):
            edge_out[g] = edges[g]
            held["add", g] = dot((heads * held["vl", g]).astype(bf16), edges[g].astype(bf16), TN)

        def finish(g, h):
            out = held.pop(("o", g, h))
            span = slice(h * HEAD, (h + 1) * HEAD)
            inv = 1.0 / (out[HEAD : HEAD + 1, :] + held["edge", g, h])
            inv_out[g, h : h + 1, :] = inv
            mixed = ((out[:HEAD, :] + held["add", g][span]) * inv).astype(bf16)
            atta[span, lanes_of(g)] = mixed
            att_out[span, lanes_of(g)] = mixed

        count_units = len(units)
        for t in range(-2, count_units + 4):
            if t + 2 == 0:
                for g in range(group):
                    begin(g)
                    held["branch"] = merge_branch()
                att_out[features:, :] = atta[features : features + 16, :]
            if 0 <= t + 2 < count_units:
                scores(*units[t + 2])
            if t == -1:
                hid_out[...] = hidden_of(held.pop("branch"), step - 1 + 3 * (1 - jnp.minimum(step, 1)))
                held["next"] = first_norm(tok)
            if t == 1:
                tokens, fi = held.pop("next")
                toks[lax.rem(step + 1, 3)] = tokens
                fia[later, :features, :] = fi
            if t in (5, 7, 9):
                project(later, (t - 5) // 2)
            if 0 <= t < count_units:
                soften(*units[t])
            if 0 <= t - 2 < count_units:
                mix(*units[t - 2])
            for g in range(group):
                if t == HEADS * g + 3:
                    left_query(g)
                if t == HEADS * (g + 1):
                    add_left(g)
                if t == HEADS * (g + 1) + 3:
                    for h in range(HEADS):
                        finish(g, h)

    @pl.when(step == steps)
    def _():
        hid_out[...] = hidden_of(merge_branch(), step - 1)
        attl_out[...] = attl[...]
        branch = dot(attl[...].astype(bf16), mw[...]) + row_of(mbias)
        hidl_out[...] = xl[...] + row_live(live, count, rows) * branch
        for copy in first_copies(beside, 0) + second_copies() + own_copies():
            copy.wait()


def feed_kernel(
    count, group, steps,
    hid0, hid, att, inv, cot0, cot, cleft, live, gain, shift, dbias, hidl, attl, wall, ball, mw,
    out, gh_out, gml_out, dots_out, ghl_out, gmleft_out, mine, beside, shared,
    upt, dnt, sia, act, gpre, gb, gattn, cols, gsum, xl, outl, sil, gbl, actl, gprel,
    outp, gradp, up_acc, down_acc, merge_acc, sums, biases, kept, away, r1, across, r2, sends, recvs,
):
    step = pl.program_id(0)
    at_step = lax.rem(step, steps)
    second = step // steps
    features = mw.shape[0]
    rows = xl.shape[0]
    width = group * MAIN
    quarters = wall.shape[0]
    me_dp, me_t = lax.axis_index("dp"), lax.axis_index("tensor")
    core, chip = (me_dp, flip(me_t, 1)), (me_dp, flip(me_t, 2))
    first_of = (1 - second) * flip(me_t, 2) + second * me_t
    now = (first_of, flip(first_of, 1))

    def to_core():
        return remote(away, r1, sends, recvs, 0, core)

    def to_chip():
        return remote(across, r2, sends, recvs, 1, chip)

    @pl.when(step == 0)
    def _():
        greet((core, chip))
        gain_row, shift_row, dbias_row = row_of(gain), row_of(shift), row_of(dbias)
        for q in range(quarters):
            upt[q, :, :features] = wall[q, 0].astype(f32).T.astype(bf16)
            upt[q, :, features:] = rows_where(0, ball[q, 0:1, :].astype(f32), 128, f32).T.astype(bf16)
            dnt[q] = wall[q, 1].astype(f32).T.astype(bf16)
        ones = rows_where(0, jnp.ones((1, width), f32), 128, bf16)
        for k in range(steps):
            sia[k, features:, :] = ones
        cols[0] = as_column(gain_row)
        cols[1] = as_column(shift_row)
        cols[2] = as_column(dbias_row)
        gsum[...] = jnp.zeros_like(gsum)
        biases[...] = jnp.zeros_like(biases)
        take_left(cleft, xl, count)
        alive = row_live(live, count, rows)
        normed, scale = norm_rows(hidl[...])
        si = (normed * gain_row + shift_row).astype(bf16)
        grad_branch = (alive * xl[...]).astype(bf16)
        total = hidl[...] + alive * dbias_row
        grad_second = jnp.zeros_like(total)
        pre_of = [dot(si, wall[q, 0]) + ball[q, 0:1, :].astype(f32) for q in range(quarters)]
        grad_of = [dot(grad_branch, wall[q, 1], NT) for q in range(quarters)]
        for q in range(quarters):
            value, slope = gelu_both(pre_of[q])
            actl[q] = value.astype(bf16)
            gprel[q] = (grad_of[q] * slope).astype(bf16)
        for q in range(quarters):
            total = total + alive * dot(actl[q], wall[q, 1])
            grad_second = grad_second + dot(gprel[q], wall[q, 0], NT)
        outl[...] = total
        grad_hidden = xl[...] + norm_back(grad_second * gain_row, normed, scale, 1)
        ghl_out[...] = grad_hidden
        grad_attn = (alive * grad_hidden).astype(bf16)
        gmleft_out[...] = dot(grad_attn, mw[...], NT).astype(bf16).astype(f32)
        one = jnp.ones((rows, 16), f32)
        sil[...] = jnp.concatenate([si.astype(f32), one], axis=1).astype(bf16)
        gbl[...] = grad_branch
        merge_acc[...] = dot(jnp.concatenate([attl[...], one], axis=1).astype(bf16), grad_attn, TN)
        sums[...] = jnp.zeros_like(sums)
        sums[0:1, :] = jnp.sum(grad_second * normed, axis=0, keepdims=True)
        sums[1:2, :] = jnp.sum(grad_second, axis=0, keepdims=True)
        sums[2:3, :] = jnp.sum(grad_branch.astype(f32), axis=0, keepdims=True)
        meet((core, chip))

    @pl.when(at_step == 0)
    def _():
        for c, q in enumerate(now):
            lanes = slice(c * features, (c + 1) * features)
            up_acc[:, lanes] = dot(sil[...], gprel[q], TN)
            down_acc[:, lanes] = dot(gbl[...], actl[q], TN)

    def rounded(ref, lanes, at):
        lanes = slice(lanes + at * 128, lanes + (at + 1) * 128)
        return jnp.concatenate([up_acc[:features, lanes], down_acc[:, lanes]], axis=0)

    @pl.when(step == steps + 1)
    def _():
        to_core().wait()
        for at in range(kept.shape[0]):
            across[at] = (kept[at] + r1[at].astype(f32)).astype(bf16)
        to_chip().start()

    pres, grads = {}, {}
    lanes_of = [slice(g * MAIN, (g + 1) * MAIN) for g in range(group)]

    def enter(hidden, cotangent, to):
        normed, _ = norm_columns(hidden[...])
        sia[to, :features, :] = (normed * wide(cols[0], width) + wide(cols[1], width)).astype(bf16)
        alive = lane_live(live, to * group, group)
        turned = jnp.concatenate([cotangent[g].T for g in range(group)], axis=1).astype(f32)
        gb[to] = (turned * alive).astype(bf16)

    def into(g):
        for c in range(2):
            pres[g, c] = dot(upt[now[c]], sia[at_step, :, lanes_of[g]])
            grads[g, c] = dot(wall[now[c], 1], gb[at_step, :, lanes_of[g]])

    def through(g):
        for c in range(2):
            span = slice(c * features, (c + 1) * features)
            value, slope = gelu_both(pres.pop((g, c)))
            act[span, lanes_of[g]] = value.astype(bf16)
            gpre[span, lanes_of[g]] = (grads.pop((g, c)) * slope).astype(bf16)

    def both_of(ref, *more):
        return jnp.concatenate([ref[(q, *more)] for q in now], axis=1)

    def second_sum(g):
        return dot(both_of(wall, 0), gpre[:, lanes_of[g]])

    def output_sum(g):
        return dot(both_of(dnt), act[:, lanes_of[g]])

    def up_product():
        up_acc[...] += dot(sia[at_step, : up_acc.shape[0], :], gpre[...], NT)

    def down_product():
        down_acc[...] += dot(gb[at_step], act[...], NT)

    @pl.when(step == 0)
    def _():
        enter(hid0, cot0, 0)

    @pl.when(second == 0)
    def _():
        for g in range(group):
            into(g)
        for g in range(group):
            through(g)
            gradp[at_step, :, lanes_of[g]] = second_sum(g)
            outp[at_step, :, lanes_of[g]] = output_sum(g)
        up_product()
        enter(hid, cot, at_step + 1 - (at_step + 1) // steps)
        down_product()

    @pl.when(second == 1)
    def _():
        held = {}
        for g in range(group):
            into(g)
        for g in range(group):
            hidden = hid[:, lanes_of[g]]
            held["norm", g] = norm_columns(hidden)
            held["cot", g] = cot[g].T.astype(f32)
        for g in range(group):
            through(g)
            held["second", g] = gradp[at_step, :, lanes_of[g]] + second_sum(g)
            held["out", g] = outp[at_step, :, lanes_of[g]] + output_sum(g)

        def back(g):
            grad_second = held["second", g]
            normed, scale = held["norm", g]
            grad = held["cot", g] + norm_back(grad_second * wide(cols[0], MAIN), normed, scale, 0)
            gh_out[:, lanes_of[g]] = grad
            alive = live[at_step * group + g].astype(f32)
            gattn[:, lanes_of[g]] = (alive * grad).astype(bf16)
            both = grad_second * normed
            for at in range(0, MAIN, 128):
                gsum[0] += both[:, at : at + 128]
                gsum[1] += grad_second[:, at : at + 128]

        def write(g):
            image = at_step * group + g
            alive = live[image].astype(f32)
            result = hid[:, lanes_of[g]] + alive * (held["out", g] + wide(cols[2], MAIN))
            out[g, :MAIN, :] = result.astype(bf16).T
            out[g, MAIN : MAIN + 1, :] = outl[pl.ds(image, 1), :].astype(bf16)

        def scale_rows(g):
            mixed = held["mixed", g].astype(bf16).astype(f32)
            both = mixed * att[:features, lanes_of[g]].astype(f32)
            for h in range(HEADS):
                span = slice(h * HEAD, (h + 1) * HEAD)
                row_inv = inv[g, h : h + 1, :]
                gml_out[span, lanes_of[g]] = (mixed[span] * row_inv).astype(bf16)
                row_dot = jnp.sum(both[span], axis=0, keepdims=True) * row_inv
                dots_out[g, h : h + 1, :] = row_dot

        dots_out[...] = jnp.zeros_like(dots_out)
        back(0)
        up_product()
        for g in range(1, group):
            back(g)
        for g in range(group):
            held["mixed", g] = dot(mw[...], gattn[:, lanes_of[g]])
        down_product()
        for g in range(group):
            scale_rows(g)
        merge_acc[...] += dot(att[...], gattn[...], NT)
        sums[2:3, :] += dot(jnp.ones((16, width), bf16), gb[at_step], NT)[0:1, :]
        for g in range(group):
            write(g)

    @pl.when(at_step == steps - 1)
    def _():
        for c, q in enumerate(now):
            biases[pl.ds(q, 1), :] = up_acc[features : features + 1, c * features : (c + 1) * features]

    @pl.when(step == steps - 1)
    def _():
        for at in range(kept.shape[0]):
            kept[at] = rounded(up_acc, 0, at)
            away[at] = rounded(up_acc, features, at).astype(bf16)
        to_core().start()

    @pl.when(step == 2 * steps - 1)
    def _():
        sums[0:1, :] += jnp.sum(gsum[0].T, axis=0, keepdims=True)
        sums[1:2, :] += jnp.sum(gsum[1].T, axis=0, keepdims=True)
        ends = jnp.concatenate([sums[...], biases[...]], axis=0)
        merged = jnp.concatenate([merge_acc[:features, :], merge_acc[features : features + 16, :], ends], axis=0)
        for at in range(features // 128):
            block = merged.shape[0]
            shared[at * block : (at + 1) * block] = merged[:, at * 128 : (at + 1) * 128].astype(bf16)
        rest = shared.shape[0] - (features // 128) * merged.shape[0]
        if rest:
            shared[shared.shape[0] - rest :] = jnp.zeros((rest, 128), bf16)
        for at in range(kept.shape[0]):
            beside[at] = rounded(up_acc, features, at).astype(bf16)
        to_chip().wait()
        for at in range(kept.shape[0]):
            mine[at] = (rounded(up_acc, 0, at) + r2[at].astype(f32)).astype(bf16)


def back_kernel(
    count, group, steps, late_group, late_steps, quarter, spread, plan,
    qkv, probs, edge, lp, lself, gml, dots, fi, fil, qkvl, attl, gmleft, aw, mine, beside, shared,
    tok, left, gh, ghl, gain, shift,
    out, quarter_out, spread_out, bias_out,
    gpa, acc, gpl, gplt, awp, cols, xl, outl, fis, minev, own, *comm,
):
    step = pl.program_id(0)
    features = aw.shape[0]
    rows = xl.shape[0]
    pairs = HEADS // 2
    last = pairs * steps
    pair = lax.rem(step // steps, pairs)
    at_group = lax.rem(step, steps)
    used = len(quarter.scratch())
    quarter.bind(minev, beside, comm[:used])
    spread.bind(comm[used:])
    engines = {"quarter": quarter, "spread": spread}
    at = lax.broadcasted_iota(jnp.int32, (rows, 128), 0)
    heads = jnp.where(at == lax.broadcasted_iota(jnp.int32, (rows, 128), 1) // HEAD, 1.0, 0.0)

    def fi_copy(k):
        width = group * MAIN
        return pltpu.make_async_copy(fi.at[:, pl.ds(k * width, width)], fis.at[k], own.at[k])

    def shared_copy():
        return pltpu.make_async_copy(shared, spread.send.at[0], own.at[steps])

    def early_copies():
        found = [pltpu.make_async_copy(mine, minev, own.at[steps + 1])]
        for part in range(pairs):
            for k in range(3):
                cut = pl.ds(k * features + part * 128, 128)
                to = pl.ds(part * 384 + k * 128, 128)
                sem = own.at[steps + 2 + part * 3 + k]
                found.append(pltpu.make_async_copy(aw.at[:, cut], awp.at[:, to], sem))
        return found

    @pl.when(step == 0)
    def _():
        peers = [
            (quarter.me_dp, flip(quarter.me_t, 1)), *(spread.plane(j)[0] for j in (1, 2, 3)),
            *(spread.line(j) for j in range(1, spread.far)),
        ]
        greet(peers)
        shared_copy().start()
        for copy in early_copies():
            copy.start()
        for k in range(steps):
            fi_copy(k).start()
        cols[...] = as_column(row_of(gain))
        gpl[...] = jnp.zeros_like(gpl)
        gplt[...] = jnp.zeros_like(gplt)
        acc[...] = jnp.zeros_like(acc)
        meet(peers)
        for s in range(quarter.streams):
            quarter.start(1, s)
        shared_copy().wait()
        spread.start("core", 0)

    for k in range(steps):
        pl.when(step == k)(lambda k=k: fi_copy(k).wait())

    @pl.when(step == 1)
    def _():
        for copy in early_copies():
            copy.wait()

    def advance(slot):
        for at, name, phase, s in plan:
            if at == slot:
                engines[name].advance(phase, s)

    for slot in sorted({item[0] for item in plan if item[0] < last + late_steps}):
        pl.when(step == slot)(functools.partial(advance, slot))

    @pl.when(step < last)
    def _():
        at16 = lax.broadcasted_iota(jnp.int32, (16, MAIN), 0)
        minus = jnp.where(at16 < 2, -1.0, 0.0).astype(bf16)
        ends_row = jnp.where(lax.broadcasted_iota(jnp.int32, (1, 16), 1) < 2, -1.0, 0.0)
        gp = gpa.at[at_group, pl.ds(pl.multiple_of(pair * 384, 128), 384)]
        held = {}
        units = [(g, r) for g in range(group) for r in range(2)]

        def lanes_of(g):
            return slice(g * MAIN, (g + 1) * MAIN)

        def part(at, r, g):
            return qkv[at * 128 + r * HEAD : at * 128 + (r + 1) * HEAD, lanes_of(g)]

        def lower(value):
            return value.astype(bf16).astype(f32)

        def prepare(g):
            image = at_group * group + g
            row = qkvl[pl.ds(image, 1), :]
            ql, kl, vl = (row[:, at * 128 : (at + 1) * 128] for at in range(3))
            gm_row = gmleft[pl.ds(image, 1), :]
            row_dot = jnp.sum(heads * (gm_row * attl[pl.ds(image, 1), :]), axis=1, keepdims=True)
            prob = jnp.sum(heads * (gm_row * vl), axis=1, keepdims=True)
            held["cols", g] = tuple(as_column(v) for v in (ql, kl, gm_row))
            held["left", g] = (vl, row_dot, prob - row_dot)

        def change(g, r):
            row_dot = dots[g, pl.ds(2 * pair + r, 1), :]
            high = row_dot.astype(bf16).astype(f32)
            rest = jnp.where(at16 == 0, high, jnp.where(at16 == 1, row_dot - high, 0.0)).astype(bf16)
            values = jnp.concatenate([part(2, r, g), minus], axis=0).T
            vl = held["left", g][0][:, r * HEAD : (r + 1) * HEAD]
            last_row = rows_where(0, jnp.concatenate([vl, ends_row], axis=1), 16, bf16)
            held["z", g, r] = dot(
                jnp.concatenate([values, last_row], axis=0),
                jnp.concatenate([gml[r * HEAD : (r + 1) * HEAD, lanes_of(g)], rest], axis=0),
            )

        def left_unit(g, r, edge_change):
            image = at_group * group + g
            span = slice(r * HEAD, (r + 1) * HEAD)
            head = pl.ds(2 * pair + r, 1)
            colq, colk, colg = (wide(v[span], MAIN) for v in held["cols", g])
            _, row_dot, self_change = held["left", g]
            row_dot, self_change = row_dot[r : r + 1, :], self_change[r : r + 1, :]
            edge_row, lp_row, self_prob = edge[g, head, :], lp[g, head, :], lself[g, head, 0:1]
            edge_grad = lower(edge_row * edge_change)
            left_change = jnp.sum(colg * part(2, r, g).astype(f32), axis=0, keepdims=True) - row_dot
            left_grad = lower(lp_row * left_change)
            self_grad = lower(self_prob * self_change)
            held["add", g, r] = (colk * edge_grad, colq * left_grad, colg * lower(lp_row))
            grad_q = jnp.sum(part(1, r, g).astype(f32) * left_grad, axis=1, keepdims=True)
            grad_k = jnp.sum(part(0, r, g).astype(f32) * edge_grad, axis=1, keepdims=True)
            grad_v = jnp.sum(
                gml[span, lanes_of(g)].astype(f32) * lower(edge_row), axis=1, keepdims=True
            )
            values = (
                (grad_q + self_grad * colk[:, 0:1]) * HEAD**-0.5,
                grad_k + self_grad * colq[:, 0:1],
                grad_v + lower(self_prob) * colg[:, 0:1],
            )
            at = lax.broadcasted_iota(jnp.int32, (HEAD, 128), 1)
            for k, value in enumerate(values):
                to = slice(k * 128 + r * HEAD, k * 128 + (r + 1) * HEAD)
                gplt[to, :] = jnp.where(at == image, lower(value), gplt[to, :])

        def scores(g, r):
            raised = probs[g, r]
            value = held.pop(("z", g, r))
            held["ds", g, r] = (raised.astype(f32) * value[:MAIN]).astype(bf16)
            left_unit(g, r, value[MAIN : MAIN + 1])
            held["v", g, r] = dot(gml[r * HEAD : (r + 1) * HEAD, lanes_of(g)], raised, NT)

        def grads(g, r):
            ds = held.pop(("ds", g, r))
            held["q", g, r] = dot(part(1, r, g), ds)
            held["k", g, r] = dot(part(0, r, g), ds, NT)

        def store(g, r):
            span = slice(r * HEAD, (r + 1) * HEAD)
            add_q, add_k, add_v = held.pop(("add", g, r))
            values = (
                (held.pop(("q", g, r)) + add_q) * HEAD**-0.5,
                held.pop(("k", g, r)) + add_k,
                held.pop(("v", g, r)) + add_v,
            )
            for at, value in enumerate(values):
                gp[at * 128 + r * HEAD : at * 128 + (r + 1) * HEAD, lanes_of(g)] = value.astype(bf16)

        number = len(units)
        thirds = sorted({0, -(-group // 3), -(-2 * group // 3), group})
        cuts = list(zip(thirds[:-1], thirds[1:]))

        def add_product(low, high):
            lanes = slice(low * MAIN, high * MAIN)
            before = jnp.where(at_group == 0, 0.0, acc[...]) if low == 0 else acc[...]
            acc[...] = before + dot(fis[at_group, :, lanes], gp[:, lanes], NT)

        for t in range(-4, number + 4):
            for g in range(group):
                if t == 2 * g - 4:
                    prepare(g)
            if 0 <= t + 2 < number:
                change(*units[t + 2])
            if 0 <= t < number:
                scores(*units[t])
            if 0 <= t - 1 < number:
                grads(*units[t - 1])
            if 0 <= t - 3 < number:
                store(*units[t - 3])
            for low, high in cuts[:-1]:
                if t - 3 == 2 * high - 1:
                    add_product(low, high)

        add_product(*cuts[-1])

        @pl.when(at_group == steps - 1)
        def _():
            one = jnp.ones((rows, 16), f32)
            gpl[pair] = gplt[...].T[:rows, :]
            acc[...] += dot(
                jnp.concatenate([fil[...], one], axis=1).astype(bf16), gpl[pair].astype(bf16), TN
            )
            weight = awp[:, pl.ds(pl.multiple_of(pair * 384, 128), 384)].astype(f32)
            by_gain = weight * acc[:features, :]
            by_shift = weight * acc[features : features + 1, :]
            fold = lambda v: jnp.sum((v[:, :128] + v[:, 128:256] + v[:, 256:]).T, axis=0, keepdims=True)
            shift_row = fold(by_shift)
            gain_row = (fold(by_gain) - row_of(shift) * shift_row) / row_of(gain)
            block = features + 32
            stream = pair + 1
            for k in range(3):
                lanes = slice(k * 128, (k + 1) * 128)
                spread.send[stream, k * block : k * block + features + 16] = acc[:, lanes].astype(bf16)
                ends = rows_where(0, gain_row[:, lanes], 16, f32) + rows_where(1, shift_row[:, lanes], 16, f32)
                spread.send[stream, k * block + features + 16 : (k + 1) * block] = ends.astype(bf16)
            rest = spread.send.shape[1] - 3 * block
            if rest:
                spread.send[stream, 3 * block :] = jnp.zeros((rest, 128), bf16)
            spread.start("core", stream)

    @pl.when(step == last)
    def _():
        take_left(left, xl, count)
        normed, scale = norm_rows(xl[...])
        packed = jnp.concatenate([gpl[p] for p in range(pairs)], axis=1).astype(bf16)
        grad_first = dot(packed, awp[...], NT)
        outl[...] = ghl[...] + norm_back(grad_first * row_of(gain), normed, scale, 1)

    @pl.when(step >= last)
    def _():
        held = {}
        first = (step - last) * late_group

        def product(g):
            image = first + g
            lanes = pl.ds(pl.multiple_of(lax.rem(image, group) * MAIN, MAIN), MAIN)
            held["grad", g] = dot(awp[...], gpa[image // group, :, lanes])

        def norm(g):
            held["norm", g] = norm_columns(tok[g].T.astype(f32))

        def finish(g):
            normed, scale = held.pop(("norm", g))
            grad = norm_back(held.pop(("grad", g)) * wide(cols[...], MAIN), normed, scale, 0)
            result = gh[:, g * MAIN : (g + 1) * MAIN] + grad
            out[g, :MAIN, :] = result.astype(bf16).T
            out[g, MAIN : MAIN + 1, :] = outl[pl.ds(first + g, 1), :].astype(bf16)

        product(0)
        norm(0)
        for g in range(late_group):
            if g + 1 < late_group:
                product(g + 1)
                norm(g + 1)
            finish(g)

    @pl.when(step == last + late_steps - 1)
    def _():
        for slot, name, phase, s in plan:
            if slot >= last + late_steps:
                engines[name].advance(phase, s)
        for s in range(quarter.streams):
            for side in range(2):
                quarter_out[s, side] = quarter.fin[s, side, : quarter.half]
        spread_out[...] = spread.out[...]
        block = features + 32
        for k in range(3):
            low = k * block + features + 16
            ends = spread.out[0, low : low + 16].astype(f32)
            at = lax.broadcasted_iota(jnp.int32, ends.shape, 0)
            row = jnp.sum(jnp.where(at == 8 + quarter.me_t, ends, 0.0), axis=0, keepdims=True)
            bias_out[:, k * 128 : (k + 1) * 128] = jnp.broadcast_to(row, (8, 128))


def place_kernel(
    pairs, quarter_in, spread_in, bias, output, input_grad,
    output_to, input_to, first_gain, first_shift, attend_to, attend_bias, merge_to, merge_bias,
    second_gain, second_shift, up_to, up_bias, down_to, down_bias,
    held, quarter, spread, attend, merge, up, down, sems, small,
):
    features = merge.shape[0]
    count = output.shape[0]
    got = [
        pltpu.make_async_copy(quarter_in, quarter, small.at[0]),
        pltpu.make_async_copy(spread_in, spread, small.at[1]),
    ]
    ins, outs = [], []
    for k, (src, to) in enumerate(((output, output_to), (input_grad, input_to))):
        for image in range(count):
            ins.append(pltpu.make_async_copy(src.at[image], held.at[k, image], sems.at[0, k, image]))
            outs.append(pltpu.make_async_copy(held.at[k, image], to.at[image], sems.at[1, k, image]))
    for copy in got + ins:
        copy.start()
    for copy in got:
        copy.wait()
    for s in range(quarter.shape[0]):
        lanes = slice(s * 128, (s + 1) * 128)
        up[:, lanes] = quarter[s, 0].astype(f32)
        down[lanes, :] = quarter[s, 1].astype(f32).T
    block = features + 32
    firsts, seconds, merge_ends = [], [], []
    for k in range(3):
        merge[:, k * 128 : (k + 1) * 128] = spread[0, k * block : k * block + features].astype(f32)
        low = k * block + features
        merge_ends.append(spread[0, low : low + 16].astype(f32))
        seconds.append(spread[0, low + 16 : low + 32].astype(f32))
        total = jnp.zeros((16, 128), f32)
        for pair in range(pairs):
            lanes = slice(k * features + pair * 128, k * features + (pair + 1) * 128)
            attend[:, lanes] = spread[pair + 1, k * block : k * block + features].astype(f32)
            total = total + spread[pair + 1, low + 16 : low + 32].astype(f32)
        firsts.append(total)
    puts = [
        pltpu.make_async_copy(src, to, small.at[2 + k])
        for k, (src, to) in enumerate(((attend, attend_to), (merge, merge_to), (up, up_to), (down, down_to)))
    ]
    for copy in puts:
        copy.start()
    merge_ends, firsts, seconds = (jnp.concatenate(v, axis=1) for v in (merge_ends, firsts, seconds))
    up_bias[...] = bias[0:1, :].reshape(features)
    merge_bias[...] = merge_ends[0:1, :].reshape(features)
    first_gain[...] = firsts[0:1, :].reshape(features)
    first_shift[...] = firsts[1:2, :].reshape(features)
    second_gain[...] = seconds[0:1, :].reshape(features)
    second_shift[...] = seconds[1:2, :].reshape(features)
    down_bias[...] = seconds[2:3, :].reshape(features)
    for to, k in ((0, 0), (1, 2)):
        rows = [
            spread[pair + 1, k * block + features : k * block + features + 16].astype(f32)[0:1, :]
            for pair in range(pairs)
        ]
        attend_bias[to : to + 1, :] = jnp.concatenate(rows, axis=1)
    for copy, on in zip(ins, outs):
        copy.wait()
        on.start()
    for copy in outs + puts:
        copy.wait()


def transfers(quarter, spread, steps, last, late_steps):
    end = last + late_steps
    when = {
        ("quarter", 0): [1, 3, 5, last + 6, end + 0.4],
        ("quarter", 1): [1, 3, 5, last + 6, end + 0.4],
        ("quarter", 2): [1, 4, last, end + 0.1, end + 0.45],
        ("spread", 0): [2, 4, last, last + 2, last + 4, end + 0.01],
        ("spread", 1): [4, last, last + 2, last + 5, end + 0.02, end + 0.15],
        ("spread", 2): [last, last + 3, end + 0.05, end + 0.31, end + 0.51, end + 0.6],
        ("spread", 3): [last + 1, last + 5, end + 0.3, end + 0.5, end + 0.7],
    }
    plan = []
    for (name, s), times in when.items():
        phases = 5 if name == "quarter" else len(spread.phases(s))
        times = times[:2] + [times[2]] * (phases - len(times)) + times[2:]
        plan += [(time, name, phase + 1, s) for phase, time in enumerate(times)]
    plan.sort(key=lambda item: item[0])
    return [(int(time), *rest) for time, *rest in plan]


def whole(*dims):
    return pl.BlockSpec(dims, lambda i: (0,) * len(dims))


def once(*dims):
    return pl.BlockSpec(dims, lambda i: (0,) * len(dims), pipeline_mode=pl.Buffered(1))


LIVE = pl.BlockSpec(memory_space=pltpu.SMEM)
ANY = pl.BlockSpec(memory_space=pl.ANY)


def params(**more):
    return pltpu.CompilerParams(
        vmem_limit_bytes=60 * 2**20, dimension_semantics=("arbitrary",), **more
    )


def shape(dtype, *dims):
    return jax.ShapeDtypeStruct(dims, dtype)


def shards(
    mesh_sizes, tokens, image_mask, patch_mask, first_gain, first_shift, attend_weight, attend_bias,
    merge_weight, merge_bias, second_gain, second_shift, up_weight, up_bias, down_weight,
    down_bias, cotangent,
):
    n, seq, d = tokens.shape
    packed = attend_weight.shape[1]
    rows = -(-n // 16) * 16
    group = 2 if n % 2 == 0 else 1
    steps = n // group
    width = group * MAIN
    pairs = HEADS // 2
    total = n * MAIN
    left = pl.BlockSpec((n, 16, d), lambda i: (0, MAIN // 16, 0), pipeline_mode=pl.Buffered(1))
    quarters, share = mesh_sizes[1], up_weight.shape[1]

    here = lambda i: jnp.minimum(i, steps - 1)
    cols = lambda r: pl.BlockSpec((r, width), lambda i: (0, here(i)))
    images = lambda *dims: pl.BlockSpec((group, *dims), lambda i: (here(i),) + (0,) * len(dims))
    fi, qkv, probs, edges, invs, lp, lself, att, hid, fil, qkvl, attl, hidl, wall, ball = pl.pallas_call(
        functools.partial(attend_kernel, n, group, steps),
        grid=(steps + 1,),
        in_specs=[
            once(group, MAIN, d),
            pl.BlockSpec((group, MAIN, d), lambda i: (here(i + 1), 0, 0)),
            left, whole(n, MAIN), LIVE, whole(d), whole(d), whole(2, d), whole(d),
            once(d, packed), once(d, d), ANY, whole(share), ANY,
        ],
        out_specs=[
            ANY, ANY, images(HEADS, MAIN, MAIN), images(16, MAIN),
            images(16, MAIN), images(16, MAIN), images(16, 128), cols(d + 16),
            pl.BlockSpec((d, width), lambda i: (0, jnp.maximum(i, 1) - 1)),
            whole(rows, d), whole(rows, packed), whole(rows, d), whole(rows, d), ANY, ANY,
        ],
        out_shape=[
            shape(bf16, d + 16, total), shape(bf16, packed, total), shape(bf16, n, HEADS, MAIN, MAIN),
            shape(f32, n, 16, MAIN), shape(f32, n, 16, MAIN), shape(f32, n, 16, MAIN),
            shape(f32, n, 16, 128), shape(bf16, d + 16, total), shape(f32, d, total),
            shape(f32, rows, d), shape(f32, rows, packed), shape(f32, rows, d), shape(f32, rows, d),
            shape(bf16, quarters, 2, d, share), shape(bf16, quarters, 16, share),
        ],
        scratch_shapes=[
            pltpu.VMEM((packed, d + 128), bf16), pltpu.VMEM((d, d + 128), bf16),
            pltpu.VMEM((2, d + 128, width), bf16), pltpu.VMEM((d + 128, width), bf16),
            pltpu.VMEM((2, d, 128), f32), pltpu.VMEM((group, 16, MAIN), f32),
            pltpu.VMEM((2, packed, width), bf16),
            pltpu.VMEM((3, d, width), bf16),
            pltpu.VMEM((rows, d), f32), pltpu.VMEM((rows, packed), f32), pltpu.VMEM((rows, d), f32),
            pltpu.VMEM((16, share), bf16), pltpu.SemaphoreType.DMA((9,)), pltpu.SemaphoreType.DMA((9,)),
            pltpu.SemaphoreType.DMA((3,)), pltpu.SemaphoreType.DMA((4,)),
        ],
        compiler_params=params(collective_id=0, has_side_effects=True),
        name="attend",
    )(
        tokens, tokens, tokens, patch_mask, image_mask, first_gain, first_shift, attend_bias, merge_bias,
        attend_weight, merge_weight, up_weight, up_bias, down_weight,
    )

    streams = d // 128
    block = d + 32
    chunk = -(-3 * block // (8 * 16)) * 16
    ahead = lambda i: (i // steps) * (i - steps) + (1 - i // steps) * (i + 1 - (i + 1) // steps)
    late_images = lambda *dims: pl.BlockSpec(
        (group, *dims), lambda i: ((i // steps) * (i - steps),) + (0,) * len(dims)
    )
    late_cols = lambda r: pl.BlockSpec((r, width), lambda i: (0, (i // steps) * (i - steps)))
    quarter_vm = lambda dtype: pltpu.VMEM((streams, 2 * d, 128), dtype)
    output, gh, gml, dots, ghl, gmleft, mine, beside, shared = pl.pallas_call(
        functools.partial(feed_kernel, n, group, steps),
        grid=(2 * steps,),
        in_specs=[
            once(d, width), pl.BlockSpec((d, width), lambda i: (0, ahead(i))), late_cols(d + 16), late_images(16, MAIN),
            once(group, MAIN, d), pl.BlockSpec((group, MAIN, d), lambda i: (ahead(i), 0, 0)), left, LIVE, whole(d), whole(d), whole(d),
            whole(rows, d), whole(rows, d), once(quarters, 2, d, share), once(quarters, 16, share), once(d, d),
        ],
        out_specs=[
            late_images(seq, d), late_cols(d), late_cols(d), late_images(16, MAIN),
            whole(rows, d), whole(rows, d),
            once(streams, 2 * d, 128), once(streams, 2 * d, 128), once(8 * chunk, 128),
        ],
        out_shape=[
            shape(bf16, n, seq, d), shape(f32, d, total), shape(bf16, d, total),
            shape(f32, n, 16, MAIN), shape(f32, rows, d), shape(f32, rows, d),
            shape(bf16, streams, 2 * d, 128), shape(bf16, streams, 2 * d, 128), shape(bf16, 8 * chunk, 128),
        ],
        scratch_shapes=[
            pltpu.VMEM((quarters, share, d + 128), bf16), pltpu.VMEM((quarters, d, share), bf16),
            pltpu.VMEM((steps, d + 128, width), bf16),
            pltpu.VMEM((2 * share, width), bf16), pltpu.VMEM((2 * share, width), bf16),
            pltpu.VMEM((steps, d, width), bf16), pltpu.VMEM((d, width), bf16),
            pltpu.VMEM((3, d, 128), f32), pltpu.VMEM((2, d, 128), f32),
            pltpu.VMEM((rows, d), f32), pltpu.VMEM((rows, d), f32),
            pltpu.VMEM((rows, d + 16), bf16), pltpu.VMEM((rows, d), bf16),
            pltpu.VMEM((quarters, rows, share), bf16), pltpu.VMEM((quarters, rows, share), bf16),
            pltpu.VMEM((steps, d, width), f32), pltpu.VMEM((steps, d, width), f32),
            pltpu.VMEM((d + 16, 2 * share), f32), pltpu.VMEM((d, 2 * share), f32),
            pltpu.VMEM((d + 16, d), f32), pltpu.VMEM((8, d), f32), pltpu.VMEM((8, d), f32),
            quarter_vm(f32), quarter_vm(bf16), quarter_vm(bf16), quarter_vm(bf16), quarter_vm(bf16),
            pltpu.SemaphoreType.DMA((2,)), pltpu.SemaphoreType.DMA((2,)),
        ],
        compiler_params=params(collective_id=1, has_side_effects=True),
        name="feed",
    )(
        hid, hid, att, invs, cotangent, cotangent, cotangent, image_mask, second_gain, second_shift, down_bias, hidl, attl,
        wall, ball, merge_weight,
    )

    late_group, late_steps = group, steps
    group = next(g for g in (7, 2, 1) if n % g == 0)
    steps = n // group
    width = group * MAIN
    last = pairs * steps
    quarter = Quarter(mesh_sizes[0], streams, 2 * d)
    spread = Spread(mesh_sizes, pairs + 1, chunk)
    plan = transfers(quarter, spread, steps, last, late_steps)
    side = lambda i: (i + late_steps) // (last + late_steps)
    early = lambda i: i - side(i) * (i - (last - 1))
    late = lambda i: side(i) * (i - last)
    by_pair = lambda r: pl.BlockSpec((r, width), lambda i: (early(i) // steps, early(i) % steps))
    early_images = lambda *dims: pl.BlockSpec((group, *dims), lambda i: (early(i) % steps,) + (0,) * len(dims))
    pair_lanes = lambda w: pl.BlockSpec((rows, w), lambda i: (0, early(i) // steps))
    late_images = lambda *dims: pl.BlockSpec((late_group, *dims), lambda i: (late(i),) + (0,) * len(dims))
    input_grad, quarter_sum, spread_sum, bias_sum = pl.pallas_call(
        functools.partial(back_kernel, n, group, steps, late_group, late_steps, quarter, spread, plan),
        grid=(last + late_steps,),
        in_specs=[
            by_pair(3 * 128),
            pl.BlockSpec((group, 2, MAIN, MAIN), lambda i: (early(i) % steps, early(i) // steps, 0, 0)),
            early_images(16, MAIN), early_images(16, MAIN), early_images(16, 128), by_pair(128),
            early_images(16, MAIN), ANY,
            whole(rows, d), pair_lanes(384), pair_lanes(128), pair_lanes(128), ANY, ANY, ANY, ANY,
            late_images(MAIN, d), left, pl.BlockSpec((d, late_group * MAIN), lambda i: (0, late(i))),
            whole(rows, d), whole(d), whole(d),
        ],
        out_specs=[
            late_images(seq, d), once(streams, 2, d, 128), once(pairs + 1, 8 * chunk, 128), whole(8, d),
        ],
        out_shape=[
            shape(bf16, n, seq, d), shape(bf16, streams, 2, d, 128), shape(bf16, pairs + 1, 8 * chunk, 128),
            shape(f32, 8, d),
        ],
        scratch_shapes=[
            pltpu.VMEM((steps, packed, width), bf16), pltpu.VMEM((d + 16, 384), f32),
            pltpu.VMEM((pairs, rows, 384), f32), pltpu.VMEM((384, 128), f32),
            pltpu.VMEM((d, packed), bf16), pltpu.VMEM((d, 128), f32),
            pltpu.VMEM((rows, d), f32), pltpu.VMEM((rows, d), f32),
            pltpu.VMEM((steps, d + 16, width), bf16), pltpu.VMEM((streams, 2 * d, 128), bf16),
            pltpu.SemaphoreType.DMA((steps + 2 + 3 * pairs,)),
            *quarter.scratch(), *spread.scratch(),
        ],
        compiler_params=params(collective_id=2, has_side_effects=True),
        name="back",
    )(
        qkv, probs, edges, lp, lself, gml, dots, fi, fil, qkvl, attl, gmleft, attend_weight,
        mine, beside, shared, tokens, tokens, gh, ghl, first_gain, first_shift,
    )
    row = lambda: pl.BlockSpec(memory_space=pltpu.VMEM)
    return pl.pallas_call(
        functools.partial(place_kernel, pairs),
        in_specs=[ANY, ANY, row(), ANY, ANY],
        out_specs=[
            ANY, ANY, row(), row(), ANY, row(), ANY, row(), row(), row(), ANY, row(), ANY, row(),
        ],
        out_shape=[
            shape(bf16, n, seq, d), shape(bf16, n, seq, d), shape(f32, d), shape(f32, d),
            shape(f32, d, packed), shape(f32, 2, d), shape(f32, d, d), shape(f32, d), shape(f32, d),
            shape(f32, d), shape(f32, d, share), shape(f32, share), shape(f32, share, d), shape(f32, d),
        ],
        scratch_shapes=[
            pltpu.VMEM((2, n, seq, d), bf16), pltpu.VMEM((streams, 2, d, 128), bf16),
            pltpu.VMEM((pairs + 1, 8 * chunk, 128), bf16), pltpu.VMEM((d, packed), f32), pltpu.VMEM((d, d), f32),
            pltpu.VMEM((d, share), f32), pltpu.VMEM((share, d), f32),
            pltpu.SemaphoreType.DMA((2, 2, n)), pltpu.SemaphoreType.DMA((6,)),
        ],
        compiler_params=pltpu.CompilerParams(vmem_limit_bytes=60 * 2**20),
        name="place",
    )(quarter_sum, spread_sum, bias_sum, output, input_grad)


def solution(mesh):
    split = ("dp", "tensor")
    in_specs = (
        P(split, None, None), P(split), P(split, None), P(), P(), P(), P(), P(), P(), P(), P(),
        P(None, "tensor"), P("tensor"), P("tensor", None), P(), P(split, None, None),
    )
    out_specs = (
        P(split, None, None), P(split, None, None), P(), P(), P(), P(), P(), P(), P(), P(),
        P(None, "tensor"), P("tensor"), P("tensor", None), P(),
    )
    sizes = (mesh.shape["dp"], mesh.shape["tensor"])
    return jax.shard_map(functools.partial(shards, sizes), mesh=mesh, in_specs=in_specs, out_specs=out_specs, check_vma=False)
```
